32 devices in a mesh: groups: 2 (over y), expert: 8 (over z, core), helper: 2 (over x), dp: 1.
Axes of the slice: x: 2, y: 2, z: 4, core: 2. Of those that a mesh axis runs over, the one named last changes fastest.
Arguments:
- tokens: bfloat16 [2048, 2048], P(('groups', 'expert', 'dp')), parts along dimension 0, may hold values from -6 to 6
- expert_ids: int32 [2048, 4], P(('groups', 'expert', 'dp')), parts along dimension 0, may hold values from 0 to 7, all different within a row; in each aligned block of 128 rows (0 to 127, 128 to 255, ...) at most 80 rows name the same one
- pick_counts: int32 [2048], P(('groups', 'expert', 'dp')), parts along dimension 0, may hold values from 1 to 4
- gate_scores: float32 [2048, 4], P(('groups', 'expert', 'dp')), parts along dimension 0, may hold values from 0.05 to 1
- w_gate: bfloat16 [8, 2048, 2048], P('expert', None, 'helper'), may hold values from -0.125 to 0.125
- w_up: bfloat16 [8, 2048, 2048], P('expert', None, 'helper'), may hold values from -0.125 to 0.125
- w_down: bfloat16 [8, 2048, 2048], P('expert', 'helper'), may hold values from -0.125 to 0.125
- grad_out: bfloat16 [2048, 2048], P(('groups', 'expert', 'dp')), parts along dimension 0, may hold values from -6 to 6
Outputs:
- outputs: bfloat16 [2048, 2048], P(('groups', 'expert', 'dp'), 'helper'), parts along dimension 0
- input_grads: bfloat16 [2048, 2048], P(('groups', 'expert', 'dp'), 'helper'), parts along dimension 0
- d_scores: float32 [2048, 4], P(('groups', 'expert', 'dp')), parts along dimension 0
- grad_w_gate: bfloat16 [16, 2048, 2048], P(('groups', 'expert'), 'dp', 'helper'), parts along dimension 0
- grad_w_up: bfloat16 [16, 2048, 2048], P(('groups', 'expert'), 'dp', 'helper'), parts along dimension 0
- grad_w_down: bfloat16 [16, 2048, 2048], P(('groups', 'expert'), 'helper', 'dp'), parts along dimension 0
The draws below stay inside these ranges and needn't reach their ends.
There are 2 independent parts, one for each index of `groups`. The reference program is written for one: setup_inputs(seed, part) draws one part's arguments, and reference() takes and returns one part's arrays. A program takes and returns all parts, laid end to end along the dimension named above; an argument that names none is the same for every part. Nothing has to cross between parts.
Inputs may be any that keep to these rules, and one draw needn't show every extreme that they name: `expert_ids`: in each aligned block of 128 rows (the rows of one device), no expert is named by more than 80 rows over all 4 columns; the entries of a row are distinct.
All inputs are finite; a program needn't handle non-finite values.
Results may differ from the reference program's by a relative error of at most 0.015.
Values may be sent and summed in bfloat16 or wider, within the bound.
No kernel may reach another device: no remote copies, remote signals or barrier semaphores. Data moves between devices by JAX's collectives and lax.ppermute only.
A program may use at most 128 MiB of HBM per device.

```python
import math
import jax
import jax.numpy as jnp
import numpy as np
from jax import lax

D = 2048
F = 2048
TOPK = 4
TOK_DEV = 128
EXPERTS = 8
FH = 1024
CAP = 80
TOKENS = 1024
N_HELPER = 2


def place_ends(array, own_key, low, top_value):
    extent = array.shape
    index_at = [jax.random.randint(jax.random.fold_in(own_key, axis), (), 0, extent[axis]) for axis in range(len(extent))]
    array = array.at[tuple(index_at)].set(low)
    longest = extent.index(max(extent))
    index_at[longest] = (index_at[longest] + 1) % extent[longest]
    return array.at[tuple(index_at)].set(top_value)


def block_levels(rng, dims, cuts, low, largest):
    def one(axis_at, blocks):
        heights = jax.random.uniform(jax.random.fold_in(jax.random.fold_in(rng, 6), axis_at), (blocks,), jnp.float32, low / len(cuts), largest / len(cuts))
        return jnp.repeat(jnp.exp(heights), dims[axis_at] // blocks).reshape((-1,) + (1,) * (len(dims) - axis_at - 1))

    level = one(*cuts[0])
    for cut in cuts[1:]:
        level = level * one(*cut)
    return level


def deal_out(own_key, own, number, rows, number_of, top, limit, skew):
    ranking = jax.random.permutation(own_key, number_of)
    heavy_load, usual = load_shares(number_of, rows * top, limit, skew, True), load_shares(number_of, rows * top, limit, skew, False)
    places = jnp.arange(number_of)

    def named(tallies, rotation):
        used = int((tallies > 0).sum())
        fixed = max(1, used // 4)
        passed = fixed + (places - fixed + rotation * (used - fixed)) % max(1, number_of - fixed)
        return jnp.zeros((number_of,), jnp.int32).at[ranking[jnp.where(places < fixed, places, passed)]].set(jnp.asarray(tallies, jnp.int32))

    tallies = jnp.where(number % 4 == 0, named(heavy_load, number // 4), named(usual, number - number // 4 - 1))
    mixed = jax.random.permutation(jax.random.fold_in(own, 3), number_of)
    source_of, sink = mixed[0:number_of // 2 * 2:2], mixed[1:number_of // 2 * 2:2]
    slack = jnp.minimum(tallies[source_of] - 1, limit - tallies[sink]) // 2
    slack = jnp.where((source_of == ranking[0]) | (sink == ranking[0]) | (tallies[sink] == 0), 0, jnp.maximum(slack, 0))
    passed = jax.random.randint(jax.random.fold_in(own, 4), (number_of // 2,), 0, 1 << 20) % (slack + 1)
    tallies = tallies.at[source_of].add(-passed).at[sink].add(passed)
    labels = jnp.searchsorted(jnp.cumsum(tallies), jnp.arange(rows * top), side="right").astype(jnp.int32)
    grid = labels.reshape(top, rows).T
    grid = grid[jax.random.permutation(jax.random.fold_in(own, 1), rows)]
    rotation = jax.random.randint(jax.random.fold_in(own, 2), (rows, 1), 0, top)
    return jnp.take_along_axis(grid, (jnp.arange(top)[None, :] + rotation) % top, axis=1)


def load_shares(amount, total, reach, skew, full):
    loads = [(1 << 20) // math.isqrt(standing ** skew) + 1 for standing in range(1, amount + 1)]
    largest = reach if full else min(reach, max(-(-total // amount), total * loads[0] // sum(loads)))
    least = 1 if total - largest >= amount - 1 else 0
    given, surplus = [largest] + [least] * (amount - 1), total - largest - least * (amount - 1)
    while surplus > 0:
        candidates = [i for i in range(1, amount) if given[i] < largest] or [i for i in range(1, amount) if given[i] < reach]
        mass, left = sum([loads[i] for i in candidates]), surplus
        for i in candidates:
            addition = min(reach - given[i], max(1, left * loads[i] // mass), surplus)
            given[i] = given[i] + addition
            surplus = surplus - addition
    return np.array(given)


def normal_values(stream_key, extent, scale, limit, shards=(), kind=jnp.bfloat16):
    result = jax.random.normal(stream_key, extent, jnp.float32) * scale
    if len(shards) > 0:
        result = block_levels(stream_key, extent, shards, -0.22, 0.18) * result
    return jnp.clip(result, min=-limit, max=limit).astype(kind)


def setup_inputs(seed: int = 0, part: int = 0) -> dict:
    splits = jax.random.split(jax.random.key(seed), 9)
    part_keys = jax.random.split(jax.random.fold_in(splits[8], part), 9)
    tokens = normal_values(part_keys[0], (TOKENS, D), 1.0, 6.0, ((0, 8),))
    expert_ids_keys = jax.random.split(jax.random.fold_in(part_keys[1], 1), TOKENS // TOK_DEV)
    expert_ids_turns = jax.random.permutation(jax.random.fold_in(part_keys[1], 3), TOKENS // TOK_DEV)
    expert_ids = jax.vmap(lambda own, number: deal_out(jax.random.fold_in(part_keys[1], 2), own, number, TOK_DEV, EXPERTS, TOPK, CAP, 2))(expert_ids_keys, expert_ids_turns).reshape((TOKENS, TOPK))
    pick_counts = place_ends(jax.random.randint(part_keys[2], (TOKENS,), 1, TOPK + 1), jax.random.fold_in(part_keys[2], 1), 1, TOPK).astype(jnp.int32)
    gate_scores = jnp.clip(jnp.exp(math.log(1.0) - 2.9957323 * jax.random.uniform(part_keys[3], (TOKENS, TOPK), jnp.float32) ** block_levels(part_keys[3], (TOKENS, TOPK), ((0, 8),), -0.2, 0.2)), 0.05, 1.0)
    w_gate = normal_values(splits[4], (EXPERTS, D, F), D ** -0.5, 0.125, ((0, 8), (2, 2)))
    w_up = normal_values(splits[5], (EXPERTS, D, F), D ** -0.5, 0.125, ((0, 8), (2, 2)))
    w_down = normal_values(splits[6], (EXPERTS, F, D), F ** -0.5, 0.125, ((0, 8), (1, 2)))
    grad_out = normal_values(part_keys[7], (TOKENS, D), 1.0, 6.0, ((0, 8),))
    return dict(tokens=tokens, expert_ids=expert_ids, pick_counts=pick_counts, gate_scores=gate_scores, w_gate=w_gate, w_up=w_up, w_down=w_down, grad_out=grad_out)


def silu_parts(argument):
    sigmoid_part = jax.nn.sigmoid(argument)
    return argument * sigmoid_part, sigmoid_part * (1.0 + argument * (1.0 - sigmoid_part))


def reference(tokens, expert_ids, pick_counts, gate_scores, w_gate, w_up, w_down, grad_out):
    pick_total = TOKENS * TOPK
    max_rows = (TOKENS // TOK_DEV) * CAP
    active_mask = jnp.arange(TOPK, dtype=jnp.int32)[None, :] < pick_counts[:, None]
    active_float = active_mask.astype(jnp.float32)
    weighted = gate_scores * active_float
    score_sum = jnp.sum(weighted, axis=1, keepdims=True)
    gate_weights = weighted / score_sum
    flat_ids = jnp.where(active_mask, expert_ids, EXPERTS).reshape(-1).astype(jnp.int32)
    flat_gates = jnp.concatenate([gate_weights.reshape(-1), jnp.zeros((1,), jnp.float32)])
    padded_tokens = jnp.concatenate([tokens, jnp.zeros((1, D), tokens.dtype)], axis=0)
    padded_grad = jnp.concatenate([grad_out, jnp.zeros((1, D), grad_out.dtype)], axis=0)

    def one_expert(expert_index):
        chosen = jnp.nonzero(flat_ids == expert_index, size=max_rows, fill_value=pick_total)[0].astype(jnp.int32)
        row_token = (chosen // TOPK).astype(jnp.int32)
        token_rows = padded_tokens[row_token]
        gate_rows = flat_gates[chosen]
        d_out = (gate_rows[:, None] * padded_grad[row_token].astype(jnp.float32)).astype(jnp.bfloat16)
        gate_mat = w_gate[expert_index]
        up_mat = w_up[expert_index]
        down_mat = w_down[expert_index]
        pre_gate = jnp.dot(token_rows, gate_mat, preferred_element_type=jnp.float32)
        pre_up = jnp.dot(token_rows, up_mat, preferred_element_type=jnp.float32)
        silu_value, silu_slope = silu_parts(pre_gate)
        hidden_act = (silu_value * pre_up).astype(jnp.bfloat16)
        act_blocks = hidden_act.astype(jnp.float32).reshape(max_rows, N_HELPER, FH)
        down_blocks = down_mat.astype(jnp.float32).reshape(N_HELPER, FH, D)
        block_out = jnp.einsum("rbf,bfd->rbd", act_blocks, down_blocks).astype(jnp.bfloat16)
        expert_out = jnp.sum(lax.optimization_barrier(block_out).astype(jnp.float32), axis=1)
        d_act = jnp.dot(d_out, down_mat.T, preferred_element_type=jnp.float32)
        d_pre_gate = (d_act * pre_up * silu_slope).astype(jnp.bfloat16)
        d_pre_up = (d_act * silu_value).astype(jnp.bfloat16)
        gate_blocks = gate_mat.astype(jnp.float32).reshape(D, N_HELPER, FH)
        up_blocks = up_mat.astype(jnp.float32).reshape(D, N_HELPER, FH)
        gate_part = jnp.einsum("rbf,dbf->rbd", d_pre_gate.astype(jnp.float32).reshape(max_rows, N_HELPER, FH), gate_blocks)
        up_part = jnp.einsum("rbf,dbf->rbd", d_pre_up.astype(jnp.float32).reshape(max_rows, N_HELPER, FH), up_blocks)
        block_in = (gate_part + up_part).astype(jnp.bfloat16)
        input_rows = jnp.sum(lax.optimization_barrier(block_in).astype(jnp.float32), axis=1)
        grad_gate = jnp.dot(token_rows.T, d_pre_gate, preferred_element_type=jnp.float32).astype(jnp.bfloat16)
        grad_up = jnp.dot(token_rows.T, d_pre_up, preferred_element_type=jnp.float32).astype(jnp.bfloat16)
        grad_down = jnp.dot(hidden_act.T, d_out, preferred_element_type=jnp.float32).astype(jnp.bfloat16)
        return expert_out, input_rows, chosen, grad_gate, grad_up, grad_down

    expert_out, input_rows, chosen, grad_w_gate, grad_w_up, grad_w_down = lax.map(
        one_expert, jnp.arange(EXPERTS, dtype=jnp.int32))
    flat_chosen = chosen.reshape(-1).astype(jnp.int32)
    pick_out = jnp.zeros((pick_total + 1, D), jnp.float32).at[flat_chosen].add(expert_out.reshape(-1, D))
    pick_out = pick_out[:pick_total].reshape(TOKENS, TOPK, D)
    token_in = jnp.zeros((TOKENS + 1, D), jnp.float32).at[(flat_chosen // TOPK).astype(jnp.int32)].add(
        input_rows.reshape(-1, D))[:TOKENS]
    outputs = jnp.sum(gate_weights[:, :, None] * pick_out, axis=1).astype(jnp.bfloat16)
    d_gates = jnp.einsum("td,tkd->tk", grad_out.astype(jnp.float32), pick_out)
    d_scores = active_float * (d_gates - jnp.sum(gate_weights * d_gates, axis=1, keepdims=True)) / score_sum
    return outputs, token_in.astype(jnp.bfloat16), d_scores, grad_w_gate, grad_w_up, grad_w_down
```

```python
import jax
import jax.numpy as jnp
from jax import lax
from jax.sharding import PartitionSpec as P


def product(first_mat, second_mat):
    return jnp.dot(first_mat, second_mat, preferred_element_type=jnp.float32)


def transposed_product(first_mat, second_mat):
    return lax.dot_general(
        first_mat, second_mat, (((0,), (0,)), ((), ())), preferred_element_type=jnp.float32
    )


def right_transposed(first_mat, second_mat):
    return lax.dot_general(
        first_mat, second_mat, (((1,), (1,)), ((), ())), preferred_element_type=jnp.float32
    )


def swap_halves(rows):
    half = rows.shape[-2] // 2
    return jnp.concatenate([rows[..., half:, :], rows[..., :half, :]], axis=-2)


class WholeAxis:
    def __init__(self, tok_rows):
        self.tok_rows = tok_rows

    def dispatch(self, rows):
        return lax.all_gather(rows, "expert", tiled=True)

    def order(self, by_device):
        return by_device.reshape(-1)

    def unorder(self, rows):
        return rows.reshape(-1, self.tok_rows)

    def combine(self, partial):
        summed = lax.psum_scatter(partial, "expert", scatter_dimension=0, tiled=True)
        return lax.psum_scatter(summed, "helper", scatter_dimension=1, tiled=True)


class FourChips:
    def __init__(self, tok_rows):
        self.tok_rows = tok_rows
        self.half = tok_rows // 2
        me = lax.axis_index("expert")
        self.chip, self.core = me // 2, me % 2
        self.side = lax.axis_index("helper")
        both = lambda pairs: [(2 * a + c, 2 * b + c) for a, b in pairs for c in (0, 1)]
        self.near = both([(z, z ^ 1) for z in range(4)])
        self.far = both([(z, z ^ 2) for z in range(4)])
        self.middle = both([(1, 2), (2, 1)])
        self.outward = both([(1, 0), (2, 3)])
        self.inward = both([(0, 1), (3, 2)])
        self.cores = [(i, i ^ 1) for i in range(8)]
        self.sides = [(0, 1), (1, 0)]

    def own_first(self, rows):
        return jnp.where(self.side == 0, rows, swap_halves(rows))

    def dispatch(self, rows):
        own = lax.dynamic_slice_in_dim(rows, self.side * self.half, self.half, 0)
        far = lax.ppermute(own, "expert", self.far)
        near = lax.ppermute(own, "expert", self.near)
        middle = lax.ppermute(own, "expert", self.middle)
        last = middle + lax.ppermute(far, "expert", self.outward)
        pieces = [self.own_first(rows)]
        for piece in (near, far, last):
            pieces = pieces + [piece, lax.ppermute(piece, "helper", self.sides)]
        own_core = jnp.concatenate(pieces, axis=0)
        other_core = lax.ppermute(own_core, "expert", self.cores)
        return jnp.concatenate([own_core, other_core], axis=0)

    def devices(self):
        slot = jnp.arange(4)
        return jnp.concatenate([(self.chip ^ slot) * 2 + self.core, (self.chip ^ slot) * 2 + 1 - self.core])

    def order(self, by_device):
        rows = by_device[self.devices()][..., None]
        return self.own_first(rows).reshape(-1)

    def unorder(self, rows):
        rows = self.own_first(rows.reshape(8, self.tok_rows, 1))[..., 0]
        everyone = jnp.arange(8)
        place = (everyone % 2 != self.core) * 4 + (everyone // 2 ^ self.chip)
        return rows[place]

    def combine(self, partial):
        rows, width = partial.shape
        received = lax.ppermute(partial[rows // 2 :], "expert", self.cores)
        kept = partial[: rows // 2]
        columns = width // 2

        def part_of(side):
            first = lax.dynamic_slice_in_dim(kept, side * columns, columns, 1)
            second = lax.dynamic_slice_in_dim(received, side * columns, columns, 1)
            total = first.astype(jnp.float32) + second.astype(jnp.float32)
            return total.reshape(4, self.tok_rows, columns)

        sent = part_of(1 - self.side).astype(jnp.bfloat16)
        mine = part_of(self.side)
        slots = [None] * 4
        for s in (3, 2, 1, 0):
            arrived = swap_halves(lax.ppermute(sent[s], "helper", self.sides))
            slots[s] = mine[s] + arrived.astype(jnp.float32)
        relay = lax.ppermute(slots[3].astype(jnp.bfloat16), "expert", self.inward)
        far = lax.ppermute(
            (slots[2] + relay.astype(jnp.float32)).astype(jnp.bfloat16), "expert", self.far
        )
        near = lax.ppermute(slots[1].astype(jnp.bfloat16), "expert", self.near)
        middle = lax.ppermute(slots[3].astype(jnp.bfloat16), "expert", self.middle)
        total = slots[0] + far.astype(jnp.float32) + near.astype(jnp.float32) + middle.astype(jnp.float32)
        return self.own_first(total).astype(jnp.bfloat16)


def on_device(tokens, expert_ids, pick_counts, gate_scores, w_gate, w_up, w_down, grad_out):
    tok_rows = tokens.shape[0]
    pick_width = expert_ids.shape[1]
    experts = lax.axis_size("expert")
    lined = experts == 8 and lax.axis_size("helper") == 2 and lax.axis_size("dp") == 1
    plan = FourChips(tok_rows) if lined else WholeAxis(tok_rows)
    gate_local, up_local, down_local = w_gate[0], w_up[0], w_down[0]
    active_mask = lax.broadcasted_iota(jnp.int32, (tok_rows, pick_width), 1) < pick_counts[:, None]
    active_float = active_mask.astype(jnp.float32)
    weighted = gate_scores * active_float
    score_sum = jnp.sum(weighted, axis=1, keepdims=True)
    gate_weights = weighted / score_sum
    picked = (expert_ids[:, :, None] == lax.broadcasted_iota(jnp.int32, (1, 1, experts), 2)).astype(
        jnp.float32
    )
    gate_table = jnp.sum(gate_weights[:, :, None] * picked, axis=1)

    rows = plan.dispatch(tokens)
    tables = lax.all_gather(gate_table.T, "expert", tiled=False)
    gates = plan.order(jnp.take(tables, lax.axis_index("expert"), axis=1))[:, None]
    grads = plan.dispatch(grad_out)

    pre_gate = product(rows, gate_local)
    pre_up = product(rows, up_local)
    sigmoid_part = jax.nn.sigmoid(pre_gate)
    silu_value = pre_gate * sigmoid_part
    silu_slope = sigmoid_part * (1.0 + pre_gate * (1.0 - sigmoid_part))
    hidden_act = silu_value * pre_up
    gated_act = (gates * hidden_act).astype(jnp.bfloat16)
    partial_out = product(gated_act, down_local).astype(jnp.bfloat16)
    output_cols = plan.combine(partial_out)

    raw_act = right_transposed(grads, down_local)
    gate_part = jnp.sum(raw_act * hidden_act, axis=1)
    d_act = gates * raw_act
    d_pre_gate = (d_act * pre_up * silu_slope).astype(jnp.bfloat16)
    d_pre_up = (d_act * silu_value).astype(jnp.bfloat16)
    partial_in = (
        right_transposed(d_pre_gate, gate_local) + right_transposed(d_pre_up, up_local)
    ).astype(jnp.bfloat16)
    input_cols = plan.combine(partial_in)

    gate_parts = lax.all_gather(plan.unorder(gate_part), ("expert", "helper"), tiled=False)
    own_parts = jnp.take(gate_parts, lax.axis_index("expert"), axis=1)
    by_expert = jnp.sum(own_parts.reshape(experts, -1, tok_rows), axis=1).T
    d_gates = jnp.sum(by_expert[:, None, :] * picked, axis=2)
    d_scores = (
        active_float
        * (d_gates - jnp.sum(gate_weights * d_gates, axis=1, keepdims=True))
        / score_sum
    )

    def over_dp(product_of, dimension):
        product_of = product_of.astype(jnp.bfloat16)
        if lax.axis_size("dp") > 1:
            product_of = lax.psum_scatter(
                product_of, "dp", scatter_dimension=dimension, tiled=True
            )
        return product_of[None]

    grad_w_gate = over_dp(transposed_product(rows, d_pre_gate), 0)
    grad_w_up = over_dp(transposed_product(rows, d_pre_up), 0)
    grad_w_down = over_dp(transposed_product(gated_act, grads), 1)
    return output_cols, input_cols, d_scores, grad_w_gate, grad_w_up, grad_w_down


def solution(mesh):
    in_specs = (
        P(("groups", "expert", "dp"), None),
        P(("groups", "expert", "dp"), None),
        P(("groups", "expert", "dp")),
        P(("groups", "expert", "dp"), None),
        P("expert", None, "helper"),
        P("expert", None, "helper"),
        P("expert", "helper", None),
        P(("groups", "expert", "dp"), None),
    )
    out_specs = (
        P(("groups", "expert", "dp"), "helper"),
        P(("groups", "expert", "dp"), "helper"),
        P(("groups", "expert", "dp"), None),
        P(("groups", "expert"), "dp", "helper"),
        P(("groups", "expert"), "dp", "helper"),
        P(("groups", "expert"), "helper", "dp"),
    )
    return jax.shard_map(
        on_device, mesh=mesh, in_specs=in_specs, out_specs=out_specs, check_vma=False
    )
```

```python
import functools

import jax
import jax.numpy as jnp
from jax import lax
from jax.experimental import pallas as pl
from jax.experimental.pallas import tpu as pltpu
from jax.sharding import PartitionSpec as P

LANES = 128
VMEM_BYTES = 56 * 2**20
ANY = pl.BlockSpec(memory_space=pl.ANY)
SCALARS = pl.BlockSpec(memory_space=pltpu.SMEM)


def product(first_mat, second_mat):
    return jnp.dot(first_mat, second_mat, preferred_element_type=jnp.float32)


def transposed_product(first_mat, second_mat):
    return lax.dot_general(
        first_mat, second_mat, (((0,), (0,)), ((), ())), preferred_element_type=jnp.float32
    )


def right_transposed(first_mat, second_mat):
    return lax.dot_general(
        first_mat, second_mat, (((1,), (1,)), ((), ())), preferred_element_type=jnp.float32
    )


def silu_parts(argument):
    sigmoid_part = jax.nn.sigmoid(argument)
    return argument * sigmoid_part, sigmoid_part * (1.0 + argument * (1.0 - sigmoid_part))


def params(steps=1):
    return pltpu.CompilerParams(
        dimension_semantics=("arbitrary",) * steps, vmem_limit_bytes=VMEM_BYTES
    )


def cost(flops, moved):
    return pl.CostEstimate(flops=flops, bytes_accessed=moved, transcendentals=0)


def lanes_of(rows):
    return lax.broadcasted_iota(jnp.int32, (rows, LANES), 1)


def hi_lo(values, is_high):
    high = values.astype(jnp.bfloat16).astype(jnp.float32)
    return jnp.where(is_high, high, values - high).astype(jnp.bfloat16)


def gate_columns(counts, scores):
    used = [(counts > k).astype(jnp.float32) for k in range(scores.shape[1])]
    weighted = [scores[:, k : k + 1] * used[k] for k in range(scores.shape[1])]
    score_sum = functools.reduce(jnp.add, weighted)
    return [w / score_sum for w in weighted], used, score_sum


def prepare_rows_kernel(experts, place, ids, counts, scores, rows, own, other):
    total, width = rows.shape
    half = total // 2
    lane = lanes_of(total)
    gates, _, _ = gate_columns(counts[...], scores[...])
    table = jnp.zeros((total, LANES), jnp.float32)
    for k, gate in enumerate(gates):
        named = ids[:, k : k + 1]
        table = table + jnp.where((lane == named) | (lane == named + experts), gate, 0.0)
    table = hi_lo(table, lane < experts)
    first = place[0] == 0

    @pl.when(first)
    def _():
        own[:, :width], other[:, :width] = rows[:half, :], rows[half:, :]
        own[:, width:], other[:, width:] = table[:half], table[half:]

    @pl.when(jnp.logical_not(first))
    def _():
        own[:, :width], other[:, :width] = rows[half:, :], rows[:half, :]
        own[:, width:], other[:, width:] = table[half:], table[:half]


def prepare_rows(place, ids, counts, scores, rows, experts):
    total, width = rows.shape
    piece = jax.ShapeDtypeStruct((total // 2, width + LANES), jnp.bfloat16)
    vmem = pl.BlockSpec(memory_space=pltpu.VMEM)
    return pl.pallas_call(
        functools.partial(prepare_rows_kernel, experts),
        out_shape=(piece, piece),
        in_specs=[SCALARS] + [vmem] * 4,
        out_specs=(vmem, vmem),
        compiler_params=pltpu.CompilerParams(vmem_limit_bytes=VMEM_BYTES),
        name="prepare_rows",
    )(place, ids, counts, scores, rows)


def prepare_grads_kernel(place, rows, after, own, other):
    half = rows.shape[0] // 2
    first = place[0] == 0

    @pl.when(first)
    def _():
        own[...], other[...] = rows[:half, :], rows[half:, :]

    @pl.when(jnp.logical_not(first))
    def _():
        own[...], other[...] = rows[half:, :], rows[:half, :]


def prepare_grads(place, rows, after):
    total, width = rows.shape
    piece = jax.ShapeDtypeStruct((total // 2, width), jnp.bfloat16)
    vmem = pl.BlockSpec(memory_space=pltpu.VMEM)
    return pl.pallas_call(
        prepare_grads_kernel,
        out_shape=(piece, piece),
        in_specs=[SCALARS, vmem, ANY],
        out_specs=(vmem, vmem),
        compiler_params=pltpu.CompilerParams(vmem_limit_bytes=VMEM_BYTES),
        name="prepare_grads",
    )(place, rows, after)


def bring_pieces(pieces, columns, target, sems):
    rows = pieces[0].shape[0]
    return [
        pltpu.make_async_copy(
            piece.at[:, columns], target.at[pl.ds(i * rows, rows), :], sems.at[i]
        )
        for i, piece in enumerate(pieces)
    ]


def forward_kernel(tiles, experts, place, *refs):
    pieces, refs = refs[:8], refs[8:]
    gate_mat, up_mat, down_mat, pre_gate, pre_up, gated, own, other = refs[:8]
    rows, gates, down, row_sems, gate_sems, down_sems = refs[8:]
    step = pl.program_id(0)
    width = rows.shape[1]
    half = width // 2
    tile = gate_mat.shape[1]
    kept = gated.shape[0] // 2

    def down_copy(i):
        side = place[0] if i == 1 else 1 - place[0]
        start = pl.multiple_of(side * half, half)
        return pltpu.make_async_copy(
            down_mat.at[:, pl.ds(start, half)], down.at[i], down_sems.at[i]
        )

    @pl.when(step == 0)
    def _():
        copies = bring_pieces(pieces, pl.ds(0, width), rows, row_sems)
        copies = copies + bring_pieces(pieces, pl.ds(width, LANES), gates, gate_sems)
        for copy in copies:
            copy.start()
        for i in range(2):
            down_copy(i).start()
        for copy in copies:
            copy.wait()

    @pl.when(step < tiles)
    def _():
        gate_part = product(rows[...], gate_mat[...])
        up_part = product(rows[...], up_mat[...])
        lane = lanes_of(gates.shape[0])
        mine = (lane == place[1]) | (lane == place[1] + experts)
        gate = jnp.sum(jnp.where(mine, gates[...].astype(jnp.float32), 0.0), axis=1, keepdims=True)
        silu_value, _ = silu_parts(gate_part)
        pre_gate[...] = gate_part
        pre_up[...] = up_part
        columns = pl.ds(pl.multiple_of(step * tile, tile), tile)
        gated[:, columns] = (gate * silu_value * up_part).astype(jnp.bfloat16)

    for i in range(2):

        @pl.when(step == tiles + i)
        def _(i=i):
            down_copy(i).wait()
            out = product(gated[...], down[i]).astype(jnp.bfloat16)
            own[0] = out[:kept]
            other[0] = out[kept:]


def forward(place, pieces, gate_mat, up_mat, down_mat, experts):
    width, hidden = gate_mat.shape
    total = 8 * pieces[0].shape[0]
    tile = 256
    tiles = hidden // tile
    early = lambda s: (0, jnp.minimum(s, tiles - 1))
    late = lambda s: (jnp.maximum(s - tiles, 0), 0, 0)
    pre = jax.ShapeDtypeStruct((total, hidden), jnp.float32)
    act = jax.ShapeDtypeStruct((total, hidden), jnp.bfloat16)
    sums = jax.ShapeDtypeStruct((2, total // 2, width // 2), jnp.bfloat16)
    return pl.pallas_call(
        functools.partial(forward_kernel, tiles, experts),
        grid=(tiles + 2,),
        out_shape=(pre, pre, act, sums, sums),
        in_specs=[SCALARS]
        + [ANY] * 8
        + [pl.BlockSpec((width, tile), early), pl.BlockSpec((width, tile), early), ANY],
        out_specs=(
            pl.BlockSpec((total, tile), early),
            pl.BlockSpec((total, tile), early),
            pl.BlockSpec((total, hidden), lambda s: (0, 0)),
            pl.BlockSpec((1, total // 2, width // 2), late),
            pl.BlockSpec((1, total // 2, width // 2), late),
        ),
        scratch_shapes=[
            pltpu.VMEM((total, width), jnp.bfloat16),
            pltpu.VMEM((total, LANES), jnp.bfloat16),
            pltpu.VMEM((2, hidden, width // 2), jnp.bfloat16),
            pltpu.SemaphoreType.DMA((8,)),
            pltpu.SemaphoreType.DMA((8,)),
            pltpu.SemaphoreType.DMA((2,)),
        ],
        compiler_params=params(),
        cost_estimate=cost(6 * total * width * hidden, 16 * 2**20),
        name="forward",
    )(place, *pieces, gate_mat, up_mat, down_mat)


def backward_kernel(tiles, experts, place, *refs):
    pieces, gate_pieces, refs = refs[:8], refs[8:16], refs[16:]
    down_mat, pre_gate, pre_up, gate_mat, up_mat, after = refs[:6]
    d_gate, d_up, own, other = refs[6:10]
    grads, gates, gate_half, up_half, parts, row_sems, gate_sems, mat_sems = refs[10:]
    step = pl.program_id(0)
    width = grads.shape[1]
    half = width // 2
    tile = down_mat.shape[0]
    total = grads.shape[0]
    kept = total // 2

    def mat_copy(i, which):
        side = place[0] if i == 1 else 1 - place[0]
        start = pl.multiple_of(side * half, half)
        source, target = ((gate_mat, gate_half), (up_mat, up_half))[which]
        return pltpu.make_async_copy(
            source.at[pl.ds(start, half), :], target.at[i], mat_sems.at[i, which]
        )

    @pl.when(step == 0)
    def _():
        copies = bring_pieces(pieces, pl.ds(0, width), grads, row_sems)
        copies = copies + bring_pieces(gate_pieces, pl.ds(width, LANES), gates, gate_sems)
        for copy in copies:
            copy.start()
        for i in range(2):
            for which in range(2):
                mat_copy(i, which).start()
        for copy in copies:
            copy.wait()
        parts[...] = jnp.zeros_like(parts)

    @pl.when(step < tiles)
    def _():
        raw = right_transposed(grads[...], down_mat[...])
        lane = lanes_of(total)
        mine = (lane == place[1]) | (lane == place[1] + experts)
        gate = jnp.sum(jnp.where(mine, gates[...].astype(jnp.float32), 0.0), axis=1, keepdims=True)
        up_part = pre_up[...]
        silu_value, silu_slope = silu_parts(pre_gate[...])
        shares = raw * silu_value * up_part
        parts[...] += functools.reduce(
            jnp.add, [shares[:, c : c + LANES] for c in range(0, tile, LANES)]
        )
        d_act = gate * raw
        columns = pl.ds(pl.multiple_of(step * tile, tile), tile)
        d_gate[:, columns] = (d_act * up_part * silu_slope).astype(jnp.bfloat16)
        d_up[:, columns] = (d_act * silu_value).astype(jnp.bfloat16)

    for i in range(2):

        @pl.when(step == tiles + i)
        def _(i=i):
            for which in range(2):
                mat_copy(i, which).wait()
            back = right_transposed(d_gate[...], gate_half[i]) + right_transposed(
                d_up[...], up_half[i]
            )
            back = back.astype(jnp.bfloat16)
            own[0, :, :half] = back[:kept]
            other[0, :, :half] = back[kept:]
            lane = lanes_of(total)
            high = 2 * place[1] + place[0]
            value = jnp.sum(parts[...], axis=1, keepdims=True)
            value = jnp.where((lane == high) | (lane == high + 2 * experts), value, 0.0)
            value = hi_lo(value, lane < 2 * experts)
            own[0, :, half:] = value[:kept]
            other[0, :, half:] = value[kept:]


def backward(place, pieces, gate_pieces, pre_gate, pre_up, gate_mat, up_mat, down_mat, after, experts):
    width, hidden = gate_mat.shape
    total = pre_gate.shape[0]
    tile = 256
    tiles = hidden // tile
    early = lambda s: (0, jnp.minimum(s, tiles - 1))
    late = lambda s: (jnp.maximum(s - tiles, 0), 0, 0)
    act = jax.ShapeDtypeStruct((total, hidden), jnp.bfloat16)
    sums = jax.ShapeDtypeStruct((2, total // 2, width // 2 + LANES), jnp.bfloat16)
    return pl.pallas_call(
        functools.partial(backward_kernel, tiles, experts),
        grid=(tiles + 2,),
        out_shape=(act, act, sums, sums),
        in_specs=[SCALARS]
        + [ANY] * 16
        + [
            pl.BlockSpec((tile, width), lambda s: (jnp.minimum(s, tiles - 1), 0)),
            pl.BlockSpec((total, tile), early),
            pl.BlockSpec((total, tile), early),
            ANY,
            ANY,
            ANY,
        ],
        out_specs=(
            pl.BlockSpec((total, hidden), lambda s: (0, 0)),
            pl.BlockSpec((total, hidden), lambda s: (0, 0)),
            pl.BlockSpec((1, total // 2, width // 2 + LANES), late),
            pl.BlockSpec((1, total // 2, width // 2 + LANES), late),
        ),
        scratch_shapes=[
            pltpu.VMEM((total, width), jnp.bfloat16),
            pltpu.VMEM((total, LANES), jnp.bfloat16),
            pltpu.VMEM((2, width // 2, hidden), jnp.bfloat16),
            pltpu.VMEM((2, width // 2, hidden), jnp.bfloat16),
            pltpu.VMEM((total, LANES), jnp.float32),
            pltpu.SemaphoreType.DMA((8,)),
            pltpu.SemaphoreType.DMA((8,)),
            pltpu.SemaphoreType.DMA((2, 2)),
        ],
        compiler_params=params(),
        cost_estimate=cost(6 * total * width * hidden, 20 * 2**20),
        name="backward",
    )(place, *pieces, *gate_pieces, down_mat, pre_gate, pre_up, gate_mat, up_mat, after)


def input_weights_kernel(*refs):
    pieces, refs = refs[:16], refs[16:]
    gates, ups, refs = refs[:2], refs[2:4], refs[4:]
    after, grad_gate, grad_up, gate_all, up_all = refs
    rows = gates[0].shape[0]

    @pl.when(pl.program_id(0) == 0)
    def _():
        for i in range(2):
            gate_all[pl.ds(i * rows, rows), :] = gates[i][...]
            up_all[pl.ds(i * rows, rows), :] = ups[i][...]

    tokens = jnp.concatenate([piece[...] for piece in pieces], axis=0)
    grad_gate[...] = transposed_product(tokens, gate_all[...]).astype(jnp.bfloat16)
    grad_up[...] = transposed_product(tokens, up_all[...]).astype(jnp.bfloat16)


def input_weights(pieces, gates, ups, after, width):
    rows, hidden = gates[0].shape
    tile = 256
    whole = pl.BlockSpec((rows, hidden), lambda s: (0, 0))
    grad = jax.ShapeDtypeStruct((width, hidden), jnp.bfloat16)
    return pl.pallas_call(
        input_weights_kernel,
        grid=(width // tile,),
        out_shape=(grad, grad),
        in_specs=[pl.BlockSpec((pieces[0].shape[0], tile), lambda s: (0, s))] * 16
        + [whole] * 4
        + [ANY],
        out_specs=(pl.BlockSpec((tile, hidden), lambda s: (s, 0)),) * 2,
        scratch_shapes=[pltpu.VMEM((2 * rows, hidden), jnp.bfloat16)] * 2,
        compiler_params=params(),
        cost_estimate=cost(8 * rows * width * hidden, 16 * 2**20),
        name="input_weights",
    )(*pieces, *gates, *ups, after)


def output_weights_kernel(*refs):
    pieces, refs = refs[:16], refs[16:]
    first, second, after, grad_down, grads, sems = refs

    @pl.when(pl.program_id(0) == 0)
    def _():
        copies = bring_pieces(pieces, pl.ds(0, grads.shape[1]), grads, sems)
        for copy in copies:
            copy.start()
        for copy in copies:
            copy.wait()

    acts = jnp.concatenate([first[...], second[...]], axis=0)
    grad_down[...] = transposed_product(acts, grads[...]).astype(jnp.bfloat16)


def output_weights(pieces, acts, after):
    rows, hidden = acts[0].shape
    width = pieces[0].shape[1]
    tile = 256
    column = pl.BlockSpec((rows, tile), lambda s: (0, s))
    return pl.pallas_call(
        output_weights_kernel,
        grid=(hidden // tile,),
        out_shape=jax.ShapeDtypeStruct((hidden, width), jnp.bfloat16),
        in_specs=[ANY] * 16 + [column, column, ANY],
        out_specs=pl.BlockSpec((tile, width), lambda s: (s, 0)),
        scratch_shapes=[
            pltpu.VMEM((2 * rows, width), jnp.bfloat16),
            pltpu.SemaphoreType.DMA((16,)),
        ],
        compiler_params=params(),
        cost_estimate=cost(4 * rows * width * hidden, 12 * 2**20),
        name="output_weights",
    )(*pieces, *acts, after)


def finish_kernel(experts, place, ids, counts, scores, own, far, near, middle, columns, d_scores):
    total = own.shape[0]
    half = total // 2
    width = columns.shape[1]
    total_sum = functools.reduce(
        jnp.add, [ref[...].astype(jnp.float32) for ref in (own, far, near, middle)]
    )
    swapped = jnp.concatenate([total_sum[half:], total_sum[:half]], axis=0)
    total_sum = jnp.where(place[0] == 0, total_sum, swapped)
    columns[...] = total_sum[:, :width].astype(jnp.bfloat16)
    table = total_sum[:, width:]
    lane = lanes_of(total)
    named_by = (lane % (2 * experts)) // 2
    gates, used, score_sum = gate_columns(counts[...], scores[...])
    d_gates = []
    for k in range(len(gates)):
        hit = (named_by == ids[:, k : k + 1]) & (lane < 4 * experts)
        d_gates.append(jnp.sum(jnp.where(hit, table, 0.0), axis=1, keepdims=True))
    mean = functools.reduce(jnp.add, [g * d for g, d in zip(gates, d_gates)])
    pick = lax.broadcasted_iota(jnp.int32, d_scores.shape, 1)
    result = jnp.zeros(d_scores.shape, jnp.float32)
    for k in range(len(gates)):
        result = jnp.where(pick == k, used[k] * (d_gates[k] - mean) / score_sum, result)
    d_scores[...] = result


def finish(place, ids, counts, scores, own, far, near, middle, experts):
    total, width = own.shape
    vmem = pl.BlockSpec(memory_space=pltpu.VMEM)
    return pl.pallas_call(
        functools.partial(finish_kernel, experts),
        out_shape=(
            jax.ShapeDtypeStruct((total, width - LANES), jnp.bfloat16),
            jax.ShapeDtypeStruct(scores.shape, jnp.float32),
        ),
        in_specs=[SCALARS] + [vmem] * 7,
        out_specs=(vmem, vmem),
        compiler_params=pltpu.CompilerParams(vmem_limit_bytes=VMEM_BYTES),
        name="finish",
    )(place, ids, counts, scores, own, far, near, middle)


class FourChips:
    def __init__(self):
        both = lambda pairs: [(2 * a + c, 2 * b + c) for a, b in pairs for c in (0, 1)]
        self.near = both([(z, z ^ 1) for z in range(4)])
        self.far = both([(z, z ^ 2) for z in range(4)])
        self.middle = both([(1, 2), (2, 1)])
        self.outward = both([(1, 0), (2, 3)])
        self.inward = both([(0, 1), (3, 2)])
        self.cores = [(i, i ^ 1) for i in range(8)]
        self.sides = [(0, 1), (1, 0)]

    def line(self, array, pairs):
        return lax.ppermute(array, "expert", pairs)

    def across(self, array):
        return lax.ppermute(array, "helper", self.sides)

    def dispatch(self, own, other):
        far = self.line(own, self.far)
        near = self.line(own, self.near)
        middle = self.line(own, self.middle)
        last = middle + self.line(far, self.outward)
        near_pieces = [own, other, near, self.across(near)]
        far_pieces = [far, self.across(far), last, self.across(last)]
        near_pieces = near_pieces + [self.line(p, self.cores) for p in near_pieces]
        far_pieces = far_pieces + [self.line(p, self.cores) for p in far_pieces]
        return near_pieces, far_pieces, far

    def two_slots(self, own, other):
        received = self.line(other, self.cores)
        sent = own[0] + received[0]
        arrived = self.across(sent)
        rows = sent.shape[0] // 4
        arrived = arrived.reshape(2, 2, rows, -1)[:, ::-1].reshape(4 * rows, -1)
        total = (
            own[1].astype(jnp.float32)
            + received[1].astype(jnp.float32)
            + arrived.astype(jnp.float32)
        ).astype(jnp.bfloat16)
        return total[: 2 * rows], total[2 * rows :], sent

    def combine(self, near_chunk, far_chunk):
        far_slot, last_slot, far_sent = self.two_slots(*far_chunk)
        own_slot, near_slot, near_sent = self.two_slots(*near_chunk)
        far_slot = far_slot + self.line(last_slot, self.inward)
        middle = self.line(last_slot, self.middle)
        far = self.line(far_slot, self.far)
        near = self.line(near_slot, self.near)
        return (own_slot, far, near, middle), near_sent


def lined_up(tokens, expert_ids, pick_counts, gate_scores, gate_local, up_local, down_local, grad_out):
    experts = lax.axis_size("expert")
    width = tokens.shape[1]
    plan = FourChips()
    side = lax.axis_index("helper")
    place = jnp.stack([side, lax.axis_index("expert")]).astype(jnp.int32)
    counts = pick_counts[:, None]
    own, other = prepare_rows(place, expert_ids, counts, gate_scores, tokens, experts)
    near_rows, far_rows, far_token = plan.dispatch(own, other)
    own, other = prepare_grads(place, grad_out, far_token)
    near_grads, far_grads, _ = plan.dispatch(own, other)

    near_gate, near_up, near_act, *near_out = forward(
        place, near_rows, gate_local, up_local, down_local, experts
    )
    far_gate, far_up, far_act, *far_out = forward(
        place, far_rows, gate_local, up_local, down_local, experts
    )
    out_sums, _ = plan.combine(near_out, far_out)

    far_d_gate, far_d_up, *far_in = backward(
        place, far_grads, far_rows, far_gate, far_up, gate_local, up_local, down_local, place, experts
    )
    near_d_gate, near_d_up, *near_in = backward(
        place, near_grads, near_rows, near_gate, near_up, gate_local, up_local, down_local, far_d_gate, experts
    )
    in_sums, sent = plan.combine(near_in, far_in)
    grad_down = output_weights(near_grads + far_grads, (near_act, far_act), near_d_gate)
    grad_gate, grad_up = input_weights(
        near_rows + far_rows, (near_d_gate, far_d_gate), (near_d_up, far_d_up), sent, width
    )

    total = functools.reduce(jnp.add, [s.astype(jnp.float32) for s in out_sums])
    half = total.shape[0] // 2
    swapped = jnp.concatenate([total[half:], total[:half]], axis=0)
    output_cols = jnp.where(side == 0, total, swapped).astype(jnp.bfloat16)
    input_cols, d_scores = finish(
        place, expert_ids, counts, gate_scores, *in_sums, experts
    )
    return output_cols, input_cols, d_scores, grad_gate[None], grad_up[None], grad_down[None]


def any_mesh(tokens, expert_ids, pick_counts, gate_scores, gate_local, up_local, down_local, grad_out):
    tok_rows = tokens.shape[0]
    pick_width = expert_ids.shape[1]
    experts = lax.axis_size("expert")
    active_mask = lax.broadcasted_iota(jnp.int32, (tok_rows, pick_width), 1) < pick_counts[:, None]
    active_float = active_mask.astype(jnp.float32)
    weighted = gate_scores * active_float
    score_sum = jnp.sum(weighted, axis=1, keepdims=True)
    gate_weights = weighted / score_sum
    picked = (expert_ids[:, :, None] == lax.broadcasted_iota(jnp.int32, (1, 1, experts), 2)).astype(
        jnp.float32
    )
    gate_table = jnp.sum(gate_weights[:, :, None] * picked, axis=1)

    def combine(partial):
        summed = lax.psum_scatter(partial, "expert", scatter_dimension=0, tiled=True)
        return lax.psum_scatter(summed, "helper", scatter_dimension=1, tiled=True)

    rows = lax.all_gather(tokens, "expert", tiled=True)
    tables = lax.all_gather(gate_table.T, "expert", tiled=False)
    gates = jnp.take(tables, lax.axis_index("expert"), axis=1).reshape(-1, 1)
    grads = lax.all_gather(grad_out, "expert", tiled=True)

    pre_gate = product(rows, gate_local)
    pre_up = product(rows, up_local)
    silu_value, silu_slope = silu_parts(pre_gate)
    hidden_act = silu_value * pre_up
    gated_act = (gates * hidden_act).astype(jnp.bfloat16)
    output_cols = combine(product(gated_act, down_local).astype(jnp.bfloat16))

    raw_act = right_transposed(grads, down_local)
    gate_part = jnp.sum(raw_act * hidden_act, axis=1)
    d_act = gates * raw_act
    d_pre_gate = (d_act * pre_up * silu_slope).astype(jnp.bfloat16)
    d_pre_up = (d_act * silu_value).astype(jnp.bfloat16)
    input_cols = combine(
        (right_transposed(d_pre_gate, gate_local) + right_transposed(d_pre_up, up_local)).astype(
            jnp.bfloat16
        )
    )

    gate_parts = lax.all_gather(
        gate_part.reshape(-1, tok_rows), ("expert", "helper"), tiled=False
    )
    own_parts = jnp.take(gate_parts, lax.axis_index("expert"), axis=1)
    by_expert = jnp.sum(own_parts.reshape(experts, -1, tok_rows), axis=1).T
    d_gates = jnp.sum(by_expert[:, None, :] * picked, axis=2)
    d_scores = (
        active_float
        * (d_gates - jnp.sum(gate_weights * d_gates, axis=1, keepdims=True))
        / score_sum
    )

    def over_dp(whole, dimension):
        return lax.psum_scatter(
            whole.astype(jnp.bfloat16), "dp", scatter_dimension=dimension, tiled=True
        )[None]

    grad_w_gate = over_dp(transposed_product(rows, d_pre_gate), 0)
    grad_w_up = over_dp(transposed_product(rows, d_pre_up), 0)
    grad_w_down = over_dp(transposed_product(gated_act, grads), 1)
    return output_cols, input_cols, d_scores, grad_w_gate, grad_w_up, grad_w_down


def on_device(tokens, expert_ids, pick_counts, gate_scores, w_gate, w_up, w_down, grad_out):
    sizes = tuple(lax.axis_size(axis) for axis in ("expert", "helper", "dp"))
    layer = lined_up if sizes == (8, 2, 1) else any_mesh
    return layer(
        tokens, expert_ids, pick_counts, gate_scores, w_gate[0], w_up[0], w_down[0], grad_out
    )


def solution(mesh):
    in_specs = (
        P(("groups", "expert", "dp"), None),
        P(("groups", "expert", "dp"), None),
        P(("groups", "expert", "dp")),
        P(("groups", "expert", "dp"), None),
        P("expert", None, "helper"),
        P("expert", None, "helper"),
        P("expert", "helper", None),
        P(("groups", "expert", "dp"), None),
    )
    out_specs = (
        P(("groups", "expert", "dp"), "helper"),
        P(("groups", "expert", "dp"), "helper"),
        P(("groups", "expert", "dp"), None),
        P(("groups", "expert"), "dp", "helper"),
        P(("groups", "expert"), "dp", "helper"),
        P(("groups", "expert"), "helper", "dp"),
    )
    return jax.shard_map(
        on_device, mesh=mesh, in_specs=in_specs, out_specs=out_specs, check_vma=False
    )
```

```python
import functools

import jax
import jax.numpy as jnp
from jax import lax
from jax.experimental import pallas as pl
from jax.experimental.pallas import tpu as pltpu
from jax.sharding import PartitionSpec as P

LANES = 128
VMEM = pl.BlockSpec(memory_space=pltpu.VMEM)


def product(first_mat, second_mat):
    return jnp.dot(first_mat, second_mat, preferred_element_type=jnp.float32)


def transposed_product(first_mat, second_mat):
    return lax.dot_general(
        first_mat, second_mat, (((0,), (0,)), ((), ())), preferred_element_type=jnp.float32
    )


def right_transposed(first_mat, second_mat):
    return lax.dot_general(
        first_mat, second_mat, (((1,), (1,)), ((), ())), preferred_element_type=jnp.float32
    )


def silu_parts(argument):
    sigmoid_part = jax.nn.sigmoid(argument)
    return argument * sigmoid_part, sigmoid_part * (1.0 + argument * (1.0 - sigmoid_part))


def total_of(terms):
    return functools.reduce(jnp.add, terms)


def call(kernel, name, operands, out_shape, scratch=(), flops=0, moved=0, mebibytes=16):
    return pl.pallas_call(
        kernel,
        out_shape=out_shape,
        in_specs=[VMEM] * len(operands),
        out_specs=jax.tree.map(lambda _: VMEM, out_shape),
        scratch_shapes=scratch,
        compiler_params=pltpu.CompilerParams(vmem_limit_bytes=mebibytes * 2**20),
        cost_estimate=pl.CostEstimate(
            flops=flops, bytes_accessed=moved, transcendentals=0
        ),
        name=name,
    )(*operands)


def half_at(array, which):
    rows = array.shape[0] // 2
    return array[which * rows : (which + 1) * rows]


def swap_halves(array):
    return jnp.concatenate([half_at(array, 1), half_at(array, 0)], axis=0)


def hi_lo(values, is_high):
    high = values.astype(jnp.bfloat16).astype(jnp.float32)
    return jnp.where(is_high, high, values - high).astype(jnp.bfloat16)


def gate_rows(counts, scores):
    used = [(counts > k).astype(jnp.float32) for k in range(scores.shape[0])]
    weighted = [scores[k : k + 1] * used[k] for k in range(scores.shape[0])]
    score_sum = total_of(weighted)
    return [w / score_sum for w in weighted], used, score_sum


def prepare_rows_kernel(experts, ids, counts, scores, rows, own, other, clock):
    total, width = rows.shape
    clock[...] = jnp.zeros_like(clock)
    lane = lax.broadcasted_iota(jnp.int32, (LANES, total), 0)
    gates, _, _ = gate_rows(counts[...], scores[...])
    table = jnp.zeros((LANES, total), jnp.float32)
    for k, gate in enumerate(gates):
        named = ids[k : k + 1, :]
        table = table + jnp.where((lane == named) | (lane == named + experts), gate, 0.0)
    table = table.T
    table = hi_lo(table, lax.broadcasted_iota(jnp.int32, table.shape, 1) < experts)
    for side in range(2):

        @pl.when(lax.axis_index("helper") == side)
        def _(side=side):
            for target, which in ((own, side), (other, 1 - side)):
                target[:, :width] = half_at(rows, which)
                target[:, width:] = half_at(table, which)


def prepare_rows(ids, counts, scores, rows, experts):
    total, width = rows.shape
    piece = jax.ShapeDtypeStruct((total // 2, width + LANES), jnp.bfloat16)
    return call(
        functools.partial(prepare_rows_kernel, experts),
        "prepare_rows",
        (ids, counts, scores, rows),
        (piece, piece, jax.ShapeDtypeStruct((8, LANES), jnp.float32)),
    )


def prepare_grads_kernel(rows, own, other):
    for side in range(2):

        @pl.when(lax.axis_index("helper") == side)
        def _(side=side):
            own[...] = half_at(rows, side)
            other[...] = half_at(rows, 1 - side)


def prepare_grads(rows):
    total, width = rows.shape
    piece = jax.ShapeDtypeStruct((total // 2, width), jnp.bfloat16)
    return call(prepare_grads_kernel, "prepare_grads", (rows,), (piece, piece))


def lay_out(pieces, target, columns):
    rows = pieces[0].shape[0]
    for i, piece in enumerate(pieces):
        target[i * rows : (i + 1) * rows, :] = piece[:, columns]


def gate_column(experts, pieces, width):
    table = jnp.concatenate([piece[:, width:] for piece in pieces], axis=0)
    lane = lax.broadcasted_iota(jnp.int32, table.shape, 1)
    expert = lax.axis_index("expert")
    mine = (lane == expert) | (lane == expert + experts)
    return jnp.sum(jnp.where(mine, table.astype(jnp.float32), 0.0), axis=1, keepdims=True)


def forward_kernel(experts, tile, *refs):
    pieces, refs = refs[:8], refs[8:]
    gate_mat, up_mat, down_mat, pre_gate, pre_up, gated, own, other, rows = refs
    width = rows.shape[1]
    half = width // 2
    lay_out(pieces, rows, slice(0, width))
    gate = gate_column(experts, pieces, width)
    for start in range(0, gated.shape[1], tile):
        columns = slice(start, start + tile)
        gate_part = product(rows[...], gate_mat[:, columns])
        up_part = product(rows[...], up_mat[:, columns])
        silu_value, _ = silu_parts(gate_part)
        pre_gate[:, columns] = gate_part
        pre_up[:, columns] = up_part
        gated[:, columns] = (gate * silu_value * up_part).astype(jnp.bfloat16)
    for which in range(2):
        stays = (lax.axis_index("helper") == which).astype(jnp.int32)
        for start in range(0, half, tile):
            columns = slice(start, start + tile)
            first = which * half + start
            out = product(gated[...], down_mat[:, first : first + tile]).astype(jnp.bfloat16)
            own[stays, :, columns] = half_at(out, 0)
            other[stays, :, columns] = half_at(out, 1)


def forward(pieces, gate_mat, up_mat, down_mat, experts):
    width, hidden = gate_mat.shape
    total = 8 * pieces[0].shape[0]
    pre = jax.ShapeDtypeStruct((total, hidden), jnp.float32)
    act = jax.ShapeDtypeStruct((total, hidden), jnp.bfloat16)
    sums = jax.ShapeDtypeStruct((2, total // 2, width // 2), jnp.bfloat16)
    return call(
        functools.partial(forward_kernel, experts, 256),
        "forward",
        (*pieces, gate_mat, up_mat, down_mat),
        (pre, pre, act, sums, sums),
        [pltpu.VMEM((total, width), jnp.bfloat16)],
        flops=6 * total * width * hidden,
    )


def backward_kernel(experts, tile, *refs):
    pieces, gate_pieces, refs = refs[:8], refs[8:16], refs[16:]
    down_mat, pre_gate, pre_up, gate_mat, up_mat = refs[:5]
    d_gate, d_up, own, other, grads = refs[5:]
    total, width = grads.shape
    half = width // 2
    lay_out(pieces, grads, slice(0, width))
    gate = gate_column(experts, gate_pieces, width)
    shares = []
    for start in range(0, d_gate.shape[1], tile):
        columns = slice(start, start + tile)
        raw = right_transposed(grads[...], down_mat[columns, :])
        up_part = pre_up[:, columns]
        silu_value, silu_slope = silu_parts(pre_gate[:, columns])
        share = raw * silu_value * up_part
        shares = shares + [share[:, c : c + LANES] for c in range(0, tile, LANES)]
        d_act = gate * raw
        d_gate[:, columns] = (d_act * up_part * silu_slope).astype(jnp.bfloat16)
        d_up[:, columns] = (d_act * silu_value).astype(jnp.bfloat16)
    value = jnp.sum(total_of(shares), axis=1, keepdims=True)
    lane = lax.broadcasted_iota(jnp.int32, (total, LANES), 1)
    high = 2 * lax.axis_index("expert") + lax.axis_index("helper")
    value = jnp.where((lane == high) | (lane == high + 2 * experts), value, 0.0)
    value = hi_lo(value, lane < 2 * experts)
    for which in range(2):
        own[which, :, half:] = half_at(value, 0)
        other[which, :, half:] = half_at(value, 1)
    for which in range(2):
        stays = (lax.axis_index("helper") == which).astype(jnp.int32)
        for start in range(0, half, tile):
            columns = slice(start, start + tile)
            first = which * half + start
            back = right_transposed(d_gate[...], gate_mat[first : first + tile, :])
            back = back + right_transposed(d_up[...], up_mat[first : first + tile, :])
            back = back.astype(jnp.bfloat16)
            own[stays, :, columns] = half_at(back, 0)
            other[stays, :, columns] = half_at(back, 1)


def backward(pieces, gate_pieces, pre_gate, pre_up, gate_mat, up_mat, down_mat, experts):
    width, hidden = gate_mat.shape
    total = pre_gate.shape[0]
    act = jax.ShapeDtypeStruct((total, hidden), jnp.bfloat16)
    sums = jax.ShapeDtypeStruct((2, total // 2, width // 2 + LANES), jnp.bfloat16)
    return call(
        functools.partial(backward_kernel, experts, 256),
        "backward",
        (*pieces, *gate_pieces, down_mat, pre_gate, pre_up, gate_mat, up_mat),
        (act, act, sums, sums),
        [pltpu.VMEM((total, width), jnp.bfloat16)],
        flops=6 * total * width * hidden,
    )


def weights_kernel(width, hidden, tile, *refs):
    pieces, refs = refs[:16], refs[16:]
    first, second, grad, rows, acts = refs
    lay_out(pieces, rows, slice(0, width))
    lay_out((first, second), acts, slice(0, hidden))
    left, right = (acts, rows) if grad.shape[0] == hidden else (rows, acts)
    for start in range(0, grad.shape[0], tile):
        columns = slice(start, start + tile)
        grad[columns, :] = transposed_product(left[:, columns], right[...]).astype(jnp.bfloat16)


def weights(name, pieces, acts, width, by_hidden):
    rows, hidden = acts[0].shape
    shape = (hidden, width) if by_hidden else (width, hidden)
    return call(
        functools.partial(weights_kernel, width, hidden, 256),
        name,
        (*pieces, *acts),
        jax.ShapeDtypeStruct(shape, jnp.bfloat16),
        [
            pltpu.VMEM((2 * rows, width), jnp.bfloat16),
            pltpu.VMEM((2 * rows, hidden), jnp.bfloat16),
        ],
        flops=4 * rows * width * hidden,
    )


def send_kernel(own, received, sent):
    sent[...] = own[0] + received[0]


def slots_kernel(own, received, arrived, first, second):
    rows = first.shape[0]
    half = rows // 2
    for slot, target in enumerate((first, second)):
        for which in range(2):
            here = slice(slot * rows + which * half, slot * rows + (which + 1) * half)
            there = slice(slot * rows + (1 - which) * half, slot * rows + (2 - which) * half)
            terms = (own[1, here, :], received[1, here, :], arrived[there, :])
            target[which * half : (which + 1) * half, :] = total_of(
                [term.astype(jnp.float32) for term in terms]
            ).astype(jnp.bfloat16)


def finish_outputs_kernel(*refs):
    columns = refs[-1]
    whole = total_of([ref[...].astype(jnp.float32) for ref in refs[:-1]])
    whole = jnp.where(lax.axis_index("helper") == 0, whole, swap_halves(whole))
    columns[...] = whole.astype(jnp.bfloat16)


def finish_inputs_kernel(experts, ids, counts, scores, clock, *refs):
    columns, d_scores = refs[-2:]
    width = columns.shape[1]
    whole = total_of([ref[...].astype(jnp.float32) for ref in refs[:-2]])
    whole = jnp.where(lax.axis_index("helper") == 0, whole, swap_halves(whole))
    columns[...] = whole[:, :width].astype(jnp.bfloat16)
    table = whole[:, width:].T
    lane = lax.broadcasted_iota(jnp.int32, table.shape, 0)
    named_by = (lane % (2 * experts)) // 2
    gates, used, score_sum = gate_rows(counts[...], scores[...])
    d_gates = []
    for k in range(len(gates)):
        hit = (named_by == ids[k : k + 1, :]) & (lane < 4 * experts)
        d_gates.append(jnp.sum(jnp.where(hit, table, 0.0), axis=0, keepdims=True))
    mean = total_of([gate * d_gate for gate, d_gate in zip(gates, d_gates)])
    for k, d_gate in enumerate(d_gates):
        d_scores[k : k + 1, :] = used[k] * (d_gate - mean) / score_sum


class FourChips:
    def __init__(self, label):
        self.label = label
        both = lambda pairs: [(2 * a + c, 2 * b + c) for a, b in pairs for c in (0, 1)]
        self.near = both([(z, z ^ 1) for z in range(4)])
        self.far = both([(z, z ^ 2) for z in range(4)])
        self.middle = both([(1, 2), (2, 1)])
        self.outward = both([(1, 0), (2, 3)])
        self.inward = both([(0, 1), (3, 2)])
        self.cores = [(i, i ^ 1) for i in range(8)]
        self.sides = [(0, 1), (1, 0)]

    def line(self, array, pairs):
        with jax.named_scope(self.label + "_line"):
            return lax.ppermute(array, "expert", pairs)

    def sibling(self, array):
        with jax.named_scope(self.label + "_cores"):
            return lax.ppermute(array, "expert", self.cores)

    def across(self, array):
        with jax.named_scope(self.label + "_across"):
            return lax.ppermute(array, "helper", self.sides)

    def first_hops(self, own):
        near = self.line(own, self.near)
        far = self.line(own, self.far)
        middle = self.line(own, self.middle)
        return near, far, middle

    def chunk(self, *pieces):
        return [*pieces, *(self.sibling(p) for p in pieces)]

    def send(self, own, received):
        return call(
            send_kernel,
            self.label + "_send",
            (own, received),
            jax.ShapeDtypeStruct(own.shape[1:], own.dtype),
        )

    def slots(self, own, received, arrived):
        rows, columns = arrived.shape
        slot = jax.ShapeDtypeStruct((rows // 2, columns), arrived.dtype)
        return call(slots_kernel, self.label + "_slots", (own, received, arrived), (slot, slot))


def load_kernel(*refs):
    sources, targets, sems = refs[:3], refs[3:6], refs[6]
    copies = [
        pltpu.make_async_copy(source, target, sems.at[i])
        for i, (source, target) in enumerate(zip(sources, targets))
    ]
    for copy in copies:
        copy.start()
    for copy in copies:
        copy.wait()


def load(*mats):
    return pl.pallas_call(
        load_kernel,
        out_shape=tuple(jax.ShapeDtypeStruct(mat.shape, mat.dtype) for mat in mats),
        in_specs=[pl.BlockSpec(memory_space=pltpu.HBM)] * len(mats),
        out_specs=(VMEM,) * len(mats),
        scratch_shapes=[pltpu.SemaphoreType.DMA((len(mats),))],
        compiler_params=pltpu.CompilerParams(vmem_limit_bytes=2**20),
        name="load",
    )(*mats)


def space(clock):
    return pl.pallas_call(
        lambda old, new: None,
        out_shape=jax.ShapeDtypeStruct(clock.shape, clock.dtype),
        in_specs=[pl.BlockSpec(memory_space=pl.ANY)],
        out_specs=pl.BlockSpec(memory_space=pl.ANY),
        input_output_aliases={0: 0},
        compiler_params=pltpu.CompilerParams(vmem_limit_bytes=2**20),
        cost_estimate=pl.CostEstimate(flops=12 * 10**9, bytes_accessed=0, transcendentals=0),
        name="space",
    )(clock)


class Order:
    def __init__(self):
        self.token = None

    def __call__(self, function, *operands, also=()):
        if self.token is not None:
            operands, _ = lax.optimization_barrier((operands, (self.token, also)))
        result = function(*operands)
        self.token = result
        return result


def lined_up(tokens, expert_ids, pick_counts, gate_scores, gate_local, up_local, down_local, grad_out):
    experts = lax.axis_size("expert")
    width = tokens.shape[1]
    picks = (expert_ids.T, pick_counts[None, :], gate_scores.T)
    rows, grads, outs, ins = (FourChips(label) for label in ("rows", "grads", "out", "in"))
    order = Order()

    own, other, clock = order(lambda r: prepare_rows(*picks, r, experts), tokens)
    near, far, middle = rows.first_hops(own)
    mats = order(load, gate_local, up_local, down_local)
    near_across = rows.across(near)
    near_rows = rows.chunk(own, other, near, near_across)
    relay = rows.line(far, rows.outward)
    far_across = rows.across(far)
    own, other = order(prepare_grads, grad_out, also=(far, middle, near))
    near, far_grad, middle_grad = grads.first_hops(own)
    near_grads = grads.chunk(own, other, near, grads.across(near))
    last = order(jnp.add, middle, relay)
    far_rows = rows.chunk(far, far_across, last, rows.across(last))

    near_gate, near_up, near_act, near_out, sent = order(
        lambda *r: forward(r, *mats, experts), *near_rows, also=far_across
    )
    near_received = outs.sibling(sent)
    relay = grads.line(far_grad, grads.outward)
    far_gate, far_up, far_act, far_out, sent = order(
        lambda *r: forward(r, *mats, experts), *far_rows, also=(near, far_grad, middle_grad)
    )
    far_received = outs.sibling(sent)
    far_across = grads.across(far_grad)
    last = order(jnp.add, middle_grad, relay)
    far_grads = grads.chunk(far_grad, far_across, last, grads.across(last))
    clock = order(space, clock, also=(far_across, near_grads))
    sent = order(outs.send, far_out, far_received)
    far_arrived = outs.across(sent)
    step = lambda g, r, *pre: backward(g, r, *pre, *mats, experts)
    near_d_gate, near_d_up, near_in, sent = order(
        step, near_grads, near_rows, near_gate, near_up
    )
    near_in_received = ins.sibling(sent)
    clock = order(space, clock, also=far_grads)
    sent = order(outs.send, near_out, near_received)
    near_arrived = outs.across(sent)
    far_d_gate, far_d_up, far_in, sent = order(step, far_grads, far_rows, far_gate, far_up)
    far_in_received = ins.sibling(sent)
    far_slot, last_slot = order(outs.slots, far_out, far_received, far_arrived)
    relay = outs.line(last_slot, outs.inward)
    middle = outs.line(last_slot, outs.middle)
    clock = order(space, clock)
    sent = order(ins.send, far_in, far_in_received)
    far_in_arrived = ins.across(sent)
    sent = order(ins.send, near_in, near_in_received)
    near_in_arrived = ins.across(sent)
    product_of = lambda name, by_hidden: lambda r, *acts: weights(name, r, acts, width, by_hidden)
    grad_down = order(
        product_of("grad_down", True), near_grads + far_grads, near_act, far_act
    )
    own_slot, near_slot = order(outs.slots, near_out, near_received, near_arrived)
    near = outs.line(near_slot, outs.near)
    far = outs.line(order(jnp.add, far_slot, relay), outs.far)
    out_sums = (own_slot, far, near, middle)
    all_rows = near_rows + far_rows
    grad_gate = order(product_of("grad_gate", False), all_rows, near_d_gate, far_d_gate)
    far_slot, last_slot = order(ins.slots, far_in, far_in_received, far_in_arrived)
    relay = ins.line(last_slot, ins.inward)
    middle = ins.line(last_slot, ins.middle)
    grad_up = order(product_of("grad_up", False), all_rows, near_d_up, far_d_up)
    far = ins.line(order(jnp.add, far_slot, relay), ins.far)
    own_slot, near_slot = order(ins.slots, near_in, near_in_received, near_in_arrived)
    near = ins.line(near_slot, ins.near)
    in_sums = (own_slot, far, near, middle)

    columns = jax.ShapeDtypeStruct((tokens.shape[0], width // 2), jnp.bfloat16)
    output_cols = order(
        lambda *sums: call(finish_outputs_kernel, "finish_outputs", sums, columns), *out_sums
    )
    input_cols, d_scores = order(
        lambda *sums: call(
            functools.partial(finish_inputs_kernel, experts),
            "finish_inputs",
            (*picks, clock, *sums),
            (columns, jax.ShapeDtypeStruct(picks[2].shape, jnp.float32)),
        ),
        *in_sums,
    )
    return output_cols, input_cols, d_scores.T, grad_gate[None], grad_up[None], grad_down[None]


def any_mesh(tokens, expert_ids, pick_counts, gate_scores, gate_local, up_local, down_local, grad_out):
    tok_rows = tokens.shape[0]
    pick_width = expert_ids.shape[1]
    experts = lax.axis_size("expert")
    active_mask = lax.broadcasted_iota(jnp.int32, (tok_rows, pick_width), 1) < pick_counts[:, None]
    active_float = active_mask.astype(jnp.float32)
    weighted = gate_scores * active_float
    score_sum = jnp.sum(weighted, axis=1, keepdims=True)
    gate_weights = weighted / score_sum
    picked = (expert_ids[:, :, None] == lax.broadcasted_iota(jnp.int32, (1, 1, experts), 2)).astype(
        jnp.float32
    )
    gate_table = jnp.sum(gate_weights[:, :, None] * picked, axis=1)

    def combine(partial):
        summed = lax.psum_scatter(partial, "expert", scatter_dimension=0, tiled=True)
        return lax.psum_scatter(summed, "helper", scatter_dimension=1, tiled=True)

    rows = lax.all_gather(tokens, "expert", tiled=True)
    tables = lax.all_gather(gate_table.T, "expert", tiled=False)
    gates = jnp.take(tables, lax.axis_index("expert"), axis=1).reshape(-1, 1)
    grads = lax.all_gather(grad_out, "expert", tiled=True)

    pre_gate = product(rows, gate_local)
    pre_up = product(rows, up_local)
    silu_value, silu_slope = silu_parts(pre_gate)
    hidden_act = silu_value * pre_up
    gated_act = (gates * hidden_act).astype(jnp.bfloat16)
    output_cols = combine(product(gated_act, down_local).astype(jnp.bfloat16))

    raw_act = right_transposed(grads, down_local)
    gate_part = jnp.sum(raw_act * hidden_act, axis=1)
    d_act = gates * raw_act
    d_pre_gate = (d_act * pre_up * silu_slope).astype(jnp.bfloat16)
    d_pre_up = (d_act * silu_value).astype(jnp.bfloat16)
    input_cols = combine(
        (right_transposed(d_pre_gate, gate_local) + right_transposed(d_pre_up, up_local)).astype(
            jnp.bfloat16
        )
    )

    gate_parts = lax.all_gather(
        gate_part.reshape(-1, tok_rows), ("expert", "helper"), tiled=False
    )
    own_parts = jnp.take(gate_parts, lax.axis_index("expert"), axis=1)
    by_expert = jnp.sum(own_parts.reshape(experts, -1, tok_rows), axis=1).T
    d_gates = jnp.sum(by_expert[:, None, :] * picked, axis=2)
    d_scores = (
        active_float
        * (d_gates - jnp.sum(gate_weights * d_gates, axis=1, keepdims=True))
        / score_sum
    )

    def over_dp(whole, dimension):
        return lax.psum_scatter(
            whole.astype(jnp.bfloat16), "dp", scatter_dimension=dimension, tiled=True
        )[None]

    grad_w_gate = over_dp(transposed_product(rows, d_pre_gate), 0)
    grad_w_up = over_dp(transposed_product(rows, d_pre_up), 0)
    grad_w_down = over_dp(transposed_product(gated_act, grads), 1)
    return output_cols, input_cols, d_scores, grad_w_gate, grad_w_up, grad_w_down


def on_device(tokens, expert_ids, pick_counts, gate_scores, w_gate, w_up, w_down, grad_out):
    sizes = tuple(lax.axis_size(axis) for axis in ("expert", "helper", "dp"))
    layer = lined_up if sizes == (8, 2, 1) else any_mesh
    return layer(
        tokens, expert_ids, pick_counts, gate_scores, w_gate[0], w_up[0], w_down[0], grad_out
    )


def solution(mesh):
    in_specs = (
        P(("groups", "expert", "dp"), None),
        P(("groups", "expert", "dp"), None),
        P(("groups", "expert", "dp")),
        P(("groups", "expert", "dp"), None),
        P("expert", None, "helper"),
        P("expert", None, "helper"),
        P("expert", "helper", None),
        P(("groups", "expert", "dp"), None),
    )
    out_specs = (
        P(("groups", "expert", "dp"), "helper"),
        P(("groups", "expert", "dp"), "helper"),
        P(("groups", "expert", "dp"), None),
        P(("groups", "expert"), "dp", "helper"),
        P(("groups", "expert"), "dp", "helper"),
        P(("groups", "expert"), "helper", "dp"),
    )
    return jax.shard_map(
        on_device, mesh=mesh, in_specs=in_specs, out_specs=out_specs, check_vma=False
    )
```

```python
import functools

import jax
import jax.numpy as jnp
from jax import lax
from jax.experimental import pallas as pl
from jax.experimental.pallas import tpu as pltpu
from jax.sharding import PartitionSpec as P

LANES = 128
VMEM = pl.BlockSpec(memory_space=pltpu.VMEM)


def product(first_mat, second_mat):
    return jnp.dot(first_mat, second_mat, preferred_element_type=jnp.float32)


def transposed_product(first_mat, second_mat):
    return lax.dot_general(
        first_mat, second_mat, (((0,), (0,)), ((), ())), preferred_element_type=jnp.float32
    )


def right_transposed(first_mat, second_mat):
    return lax.dot_general(
        first_mat, second_mat, (((1,), (1,)), ((), ())), preferred_element_type=jnp.float32
    )


def silu_parts(argument):
    sigmoid_part = jax.nn.sigmoid(argument)
    return argument * sigmoid_part, sigmoid_part * (1.0 + argument * (1.0 - sigmoid_part))


def total_of(terms):
    return functools.reduce(jnp.add, terms)


def call(kernel, name, operands, out_shape, scratch=(), flops=0, moved=0, mebibytes=16):
    return pl.pallas_call(
        kernel,
        out_shape=out_shape,
        in_specs=[VMEM] * len(operands),
        out_specs=jax.tree.map(lambda _: VMEM, out_shape),
        scratch_shapes=scratch,
        compiler_params=pltpu.CompilerParams(vmem_limit_bytes=mebibytes * 2**20),
        cost_estimate=pl.CostEstimate(
            flops=flops, bytes_accessed=moved, transcendentals=0
        ),
        name=name,
    )(*operands)


def half_at(array, which):
    rows = array.shape[0] // 2
    return array[which * rows : (which + 1) * rows]


def swap_halves(array):
    return jnp.concatenate([half_at(array, 1), half_at(array, 0)], axis=0)


def hi_lo(values, is_high):
    high = values.astype(jnp.bfloat16).astype(jnp.float32)
    return jnp.where(is_high, high, values - high).astype(jnp.bfloat16)


def gate_rows(counts, scores):
    used = [(counts > k).astype(jnp.float32) for k in range(scores.shape[0])]
    weighted = [scores[k : k + 1] * used[k] for k in range(scores.shape[0])]
    score_sum = total_of(weighted)
    return [w / score_sum for w in weighted], used, score_sum


def prepare_rows_kernel(experts, *refs):
    sources, (own, other, clock), targets, sems = refs[:4], refs[4:7], refs[7:11], refs[11]
    ids, counts, scores, rows = targets
    copies = [
        pltpu.make_async_copy(source, target, sems.at[i])
        for i, (source, target) in enumerate(zip(sources, targets))
    ]
    for copy in copies:
        copy.start()
    for copy in copies:
        copy.wait()
    total, width = rows.shape
    clock[...] = jnp.zeros_like(clock)
    lane = lax.broadcasted_iota(jnp.int32, (LANES, total), 0)
    gates, _, _ = gate_rows(counts[...], scores[...])
    table = jnp.zeros((LANES, total), jnp.float32)
    for k, gate in enumerate(gates):
        named = ids[k : k + 1, :]
        table = table + jnp.where((lane == named) | (lane == named + experts), gate, 0.0)
    table = table.T
    table = hi_lo(table, lax.broadcasted_iota(jnp.int32, table.shape, 1) < experts)
    for side in range(2):

        @pl.when(lax.axis_index("helper") == side)
        def _(side=side):
            for target, which in ((own, side), (other, 1 - side)):
                target[:, :width] = half_at(rows, which)
                target[:, width:] = half_at(table, which)


def prepare_rows(ids, counts, scores, rows, experts):
    total, width = rows.shape
    piece = jax.ShapeDtypeStruct((total // 2, width + LANES), jnp.bfloat16)
    operands = (ids, counts, scores, rows)
    return pl.pallas_call(
        functools.partial(prepare_rows_kernel, experts),
        out_shape=(piece, piece, jax.ShapeDtypeStruct((8, LANES), jnp.float32)),
        in_specs=[pl.BlockSpec(memory_space=pltpu.HBM)] * len(operands),
        out_specs=(VMEM,) * 3,
        scratch_shapes=[
            *(pltpu.VMEM(operand.shape, operand.dtype) for operand in operands),
            pltpu.SemaphoreType.DMA((len(operands),)),
        ],
        compiler_params=pltpu.CompilerParams(vmem_limit_bytes=8 * 2**20),
        name="prepare_rows",
    )(*(pltpu.with_memory_space_constraint(operand, pltpu.HBM) for operand in operands))


def prepare_grads_kernel(rows, own, other):
    for side in range(2):

        @pl.when(lax.axis_index("helper") == side)
        def _(side=side):
            own[...] = half_at(rows, side)
            other[...] = half_at(rows, 1 - side)


def prepare_grads(rows):
    total, width = rows.shape
    piece = jax.ShapeDtypeStruct((total // 2, width), jnp.bfloat16)
    return call(prepare_grads_kernel, "prepare_grads", (rows,), (piece, piece))


def lay_out(pieces, target, columns):
    rows = pieces[0].shape[0]
    for i, piece in enumerate(pieces):
        target[i * rows : (i + 1) * rows, :] = piece[:, columns]


def gate_column(experts, pieces, width):
    table = jnp.concatenate([piece[:, width:] for piece in pieces], axis=0)
    lane = lax.broadcasted_iota(jnp.int32, table.shape, 1)
    expert = lax.axis_index("expert")
    mine = (lane == expert) | (lane == expert + experts)
    return jnp.sum(jnp.where(mine, table.astype(jnp.float32), 0.0), axis=1, keepdims=True)


def forward_kernel(experts, tile, *refs):
    pieces, refs = refs[:8], refs[8:]
    gate_mat, up_mat, down_mat, pre_gate, pre_up, gated, own, other, rows = refs
    width = rows.shape[1]
    half = width // 2
    lay_out(pieces, rows, slice(0, width))
    gate = gate_column(experts, pieces, width)
    for start in range(0, gated.shape[1], tile):
        columns = slice(start, start + tile)
        gate_part = product(rows[...], gate_mat[:, columns])
        up_part = product(rows[...], up_mat[:, columns])
        silu_value, _ = silu_parts(gate_part)
        pre_gate[:, columns] = gate_part
        pre_up[:, columns] = up_part
        gated[:, columns] = (gate * silu_value * up_part).astype(jnp.bfloat16)
    for which in range(2):
        stays = (lax.axis_index("helper") == which).astype(jnp.int32)
        for start in range(0, half, tile):
            columns = slice(start, start + tile)
            first = which * half + start
            out = product(gated[...], down_mat[:, first : first + tile]).astype(jnp.bfloat16)
            own[stays, :, columns] = half_at(out, 0)
            other[stays, :, columns] = half_at(out, 1)


def forward(pieces, gate_mat, up_mat, down_mat, experts, estimate):
    width, hidden = gate_mat.shape
    total = 8 * pieces[0].shape[0]
    pre = jax.ShapeDtypeStruct((total, hidden), jnp.float32)
    act = jax.ShapeDtypeStruct((total, hidden), jnp.bfloat16)
    sums = jax.ShapeDtypeStruct((2, total // 2, width // 2), jnp.bfloat16)
    return call(
        functools.partial(forward_kernel, experts, 256),
        "forward",
        (*pieces, gate_mat, up_mat, down_mat),
        (pre, pre, act, sums, sums),
        [pltpu.VMEM((total, width), jnp.bfloat16)],
        flops=estimate,
    )


def backward_kernel(experts, tile, *refs):
    pieces, gate_pieces, refs = refs[:8], refs[8:16], refs[16:]
    down_mat, pre_gate, pre_up, gate_mat, up_mat = refs[:5]
    d_gate, d_up, own, other, grads = refs[5:]
    total, width = grads.shape
    half = width // 2
    lay_out(pieces, grads, slice(0, width))
    gate = gate_column(experts, gate_pieces, width)
    shares = []
    for start in range(0, d_gate.shape[1], tile):
        columns = slice(start, start + tile)
        raw = right_transposed(grads[...], down_mat[columns, :])
        up_part = pre_up[:, columns]
        silu_value, silu_slope = silu_parts(pre_gate[:, columns])
        share = raw * silu_value * up_part
        shares = shares + [share[:, c : c + LANES] for c in range(0, tile, LANES)]
        d_act = gate * raw
        d_gate[:, columns] = (d_act * up_part * silu_slope).astype(jnp.bfloat16)
        d_up[:, columns] = (d_act * silu_value).astype(jnp.bfloat16)
    value = jnp.sum(total_of(shares), axis=1, keepdims=True)
    lane = lax.broadcasted_iota(jnp.int32, (total, LANES), 1)
    high = 2 * lax.axis_index("expert") + lax.axis_index("helper")
    value = jnp.where((lane == high) | (lane == high + 2 * experts), value, 0.0)
    value = hi_lo(value, lane < 2 * experts)
    for which in range(2):
        own[which, :, half:] = half_at(value, 0)
        other[which, :, half:] = half_at(value, 1)
    for which in range(2):
        stays = (lax.axis_index("helper") == which).astype(jnp.int32)
        for start in range(0, half, tile):
            columns = slice(start, start + tile)
            first = which * half + start
            back = right_transposed(d_gate[...], gate_mat[first : first + tile, :])
            back = back + right_transposed(d_up[...], up_mat[first : first + tile, :])
            back = back.astype(jnp.bfloat16)
            own[stays, :, columns] = half_at(back, 0)
            other[stays, :, columns] = half_at(back, 1)


def backward(pieces, gate_pieces, pre_gate, pre_up, gate_mat, up_mat, down_mat, experts):
    width, hidden = gate_mat.shape
    total = pre_gate.shape[0]
    act = jax.ShapeDtypeStruct((total, hidden), jnp.bfloat16)
    sums = jax.ShapeDtypeStruct((2, total // 2, width // 2 + LANES), jnp.bfloat16)
    return call(
        functools.partial(backward_kernel, experts, 256),
        "backward",
        (*pieces, *gate_pieces, down_mat, pre_gate, pre_up, gate_mat, up_mat),
        (act, act, sums, sums),
        [pltpu.VMEM((total, width), jnp.bfloat16)],
        flops=6 * total * width * hidden,
    )


def weights_kernel(width, hidden, tile, *refs):
    pieces, refs = refs[:16], refs[16:]
    first, second, grad, rows, acts = refs
    lay_out(pieces, rows, slice(0, width))
    lay_out((first, second), acts, slice(0, hidden))
    left, right = (acts, rows) if grad.shape[0] == hidden else (rows, acts)
    for start in range(0, grad.shape[0], tile):
        columns = slice(start, start + tile)
        grad[columns, :] = transposed_product(left[:, columns], right[...]).astype(jnp.bfloat16)


def weights(name, pieces, acts, width, by_hidden):
    rows, hidden = acts[0].shape
    shape = (hidden, width) if by_hidden else (width, hidden)
    return call(
        functools.partial(weights_kernel, width, hidden, 256),
        name,
        (*pieces, *acts),
        jax.ShapeDtypeStruct(shape, jnp.bfloat16),
        [
            pltpu.VMEM((2 * rows, width), jnp.bfloat16),
            pltpu.VMEM((2 * rows, hidden), jnp.bfloat16),
        ],
        flops=4 * rows * width * hidden,
    )


def send_kernel(own, received, *sent):
    rows = sent[0].shape[0]
    for i, target in enumerate(sent):
        here = slice(i * rows, (i + 1) * rows)
        target[...] = own[0, here, :] + received[0, here, :]


def slot_sum(own, received, arrived, slot, offset):
    rows = LANES
    half = rows // 2
    here = slice(slot * rows, (slot + 1) * rows)
    other = arrived[offset : offset + rows, :].astype(jnp.float32)
    kept = own[1, here, :].astype(jnp.float32) + received[1, here, :].astype(jnp.float32)
    return kept + jnp.concatenate([other[half:], other[:half]], axis=0)


def slots_kernel(own, received, arrived, first, second):
    for slot, target in enumerate((first, second)):
        target[...] = slot_sum(own, received, arrived, slot, slot * LANES).astype(target.dtype)


def slot_kernel(slot, own, received, arrived, *refs):
    whole = slot_sum(own, received, arrived, slot, 0)
    if len(refs) > 1:
        whole = whole + refs[0][...].astype(jnp.float32)
    refs[-1][...] = whole.astype(refs[-1].dtype)


def finish_outputs_kernel(*refs):
    columns = refs[-1]
    whole = total_of([ref[...].astype(jnp.float32) for ref in refs[:-1]])
    whole = jnp.where(lax.axis_index("helper") == 0, whole, swap_halves(whole))
    columns[...] = whole.astype(jnp.bfloat16)


def finish_inputs_kernel(experts, ids, counts, scores, clock, own, received, arrived, *refs):
    columns, d_scores = refs[-2:]
    width = columns.shape[1]
    whole = slot_sum(own, received, arrived, 0, 0)
    whole = total_of([whole] + [ref[...].astype(jnp.float32) for ref in refs[:-2]])
    whole = jnp.where(lax.axis_index("helper") == 0, whole, swap_halves(whole))
    columns[...] = whole[:, :width].astype(jnp.bfloat16)
    table = whole[:, width:].T
    lane = lax.broadcasted_iota(jnp.int32, table.shape, 0)
    named_by = (lane % (2 * experts)) // 2
    gates, used, score_sum = gate_rows(counts[...], scores[...])
    d_gates = []
    for k in range(len(gates)):
        hit = (named_by == ids[k : k + 1, :]) & (lane < 4 * experts)
        d_gates.append(jnp.sum(jnp.where(hit, table, 0.0), axis=0, keepdims=True))
    mean = total_of([gate * d_gate for gate, d_gate in zip(gates, d_gates)])
    for k, d_gate in enumerate(d_gates):
        d_scores[k : k + 1, :] = used[k] * (d_gate - mean) / score_sum


class FourChips:
    def __init__(self, label):
        self.label = label
        both = lambda pairs: [(2 * a + c, 2 * b + c) for a, b in pairs for c in (0, 1)]
        self.near = both([(z, z ^ 1) for z in range(4)])
        self.far = both([(z, z ^ 2) for z in range(4)])
        self.last = both([(z, z ^ 3) for z in range(4)])
        self.middle = both([(1, 2), (2, 1)])
        self.outward = both([(1, 0), (2, 3)])
        self.inward = both([(0, 1), (3, 2)])
        self.cores = [(i, i ^ 1) for i in range(8)]
        self.sides = [(0, 1), (1, 0)]

    def line(self, array, pairs):
        with jax.named_scope(self.label + "_line"):
            return lax.ppermute(array, "expert", pairs)

    def sibling(self, array):
        with jax.named_scope(self.label + "_cores"):
            return lax.ppermute(array, "expert", self.cores)

    def across(self, array):
        with jax.named_scope(self.label + "_across"):
            return lax.ppermute(array, "helper", self.sides)

    def chunk(self, *pieces):
        return [*pieces, *(self.sibling(p) for p in pieces)]

    def send(self, own, received, parts=1):
        _, rows, columns = own.shape
        part = jax.ShapeDtypeStruct((rows // parts, columns), own.dtype)
        return call(send_kernel, self.label + "_send", (own, received), (part,) * parts)

    def slots(self, own, received, arrived):
        rows, columns = arrived.shape
        slot = jax.ShapeDtypeStruct((rows // 2, columns), arrived.dtype)
        return call(slots_kernel, self.label + "_slots", (own, received, arrived), (slot, slot))

    def slot(self, which, own, received, arrived, *others):
        return call(
            functools.partial(slot_kernel, which),
            self.label + "_slot",
            (own, received, arrived, *others),
            jax.ShapeDtypeStruct(arrived.shape, arrived.dtype),
        )


def load_kernel(*refs):
    sources, targets, sems = refs[:3], refs[3:6], refs[6]
    copies = [
        pltpu.make_async_copy(source, target, sems.at[i])
        for i, (source, target) in enumerate(zip(sources, targets))
    ]
    for copy in copies:
        copy.start()
    for copy in copies:
        copy.wait()


def load(*mats):
    return pl.pallas_call(
        load_kernel,
        out_shape=tuple(jax.ShapeDtypeStruct(mat.shape, mat.dtype) for mat in mats),
        in_specs=[pl.BlockSpec(memory_space=pltpu.HBM)] * len(mats),
        out_specs=(VMEM,) * len(mats),
        scratch_shapes=[pltpu.SemaphoreType.DMA((len(mats),))],
        compiler_params=pltpu.CompilerParams(vmem_limit_bytes=2**20),
        name="load",
    )(*(pltpu.with_memory_space_constraint(mat, pltpu.HBM) for mat in mats))


def space(clock, flops=12 * 10**9):
    return pl.pallas_call(
        lambda old, new: None,
        out_shape=jax.ShapeDtypeStruct(clock.shape, clock.dtype),
        in_specs=[pl.BlockSpec(memory_space=pl.ANY)],
        out_specs=pl.BlockSpec(memory_space=pl.ANY),
        input_output_aliases={0: 0},
        compiler_params=pltpu.CompilerParams(vmem_limit_bytes=2**20),
        cost_estimate=pl.CostEstimate(flops=flops, bytes_accessed=0, transcendentals=0),
        name="space",
    )(clock)


def tick(clock):
    return space(clock, 2 * 10**9)


class Order:
    def __init__(self):
        self.token = None

    def __call__(self, function, *operands, also=()):
        if self.token is not None:
            operands, _ = lax.optimization_barrier((operands, (self.token, also)))
        result = function(*operands)
        self.token = result
        return result


def lined_up(tokens, expert_ids, pick_counts, gate_scores, gate_local, up_local, down_local, grad_out):
    experts = lax.axis_size("expert")
    width = tokens.shape[1]
    picks = (expert_ids.T, pick_counts[None, :], gate_scores.T)
    rows, grads, outs, ins = (FourChips(label) for label in ("rows", "grads", "out", "in"))
    order = Order()
    hold = lambda value, *tokens: lax.optimization_barrier((value, tokens))[0]

    own, other, clock = order(lambda r: prepare_rows(*picks, r, experts), tokens)
    near = rows.line(own, rows.near)
    middle = rows.line(own, rows.middle)
    mats = order(load, gate_local, up_local, down_local)
    clock = order(space, clock)
    near, middle = hold((near, middle), clock)
    far = rows.line(hold(own, near), rows.far)
    near_across = rows.across(near)
    clock = order(space, clock, also=(near, middle))
    near_rows = rows.chunk(own, other, near, hold(near_across, clock))
    near_gate, near_up, near_act, near_out, sent = order(
        lambda *r: forward(r, *mats, experts, 0), *near_rows
    )
    near_received = outs.sibling(sent)
    far = hold(far, near_act)
    far_across = rows.across(far)
    relay = rows.line(far, rows.outward)
    own, other = order(prepare_grads, grad_out, also=far)
    far_grad = grads.line(own, grads.far)
    clock = order(space, clock)
    far_across, relay = hold((far_across, relay), clock)
    last = order(jnp.add, middle, relay, also=far_across)
    last_across = rows.across(last)
    near = grads.line(hold(own, last), grads.near)
    middle_grad = grads.line(hold(own, last), grads.middle)
    clock = order(tick, clock, also=far_grad)
    last_across, near, middle_grad = hold((last_across, near, middle_grad), clock)
    far_rows = rows.chunk(far, far_across, last, last_across)
    far_across = grads.across(far_grad)
    near_across = grads.across(near)
    relay = grads.line(far_grad, grads.outward)
    clock = order(space, clock, also=(last_across, near, middle_grad, far_grad))

    far_gate, far_up, far_act, far_out, sent = order(
        lambda *r: forward(r, *mats, experts, 6 * far.size * 8 * gate_local.shape[1]), *far_rows
    )
    far_received = outs.sibling(sent)
    relay, far_across, near_across = hold((relay, far_across, near_across), far_act)
    near_grads = grads.chunk(own, other, near, near_across)
    last = order(jnp.add, middle_grad, relay)
    last_across = grads.across(last)
    far_grads = grads.chunk(far_grad, far_across, last, last_across)
    clock = order(space, clock, also=(far_across, near_grads))
    (sent,) = order(outs.send, far_out, far_received)
    far_arrived = outs.across(sent)
    clock = order(space, clock)
    step = lambda g, r, *pre: backward(g, r, *pre, *mats, experts)
    near_d_gate, near_d_up, near_in, sent = order(
        step, near_grads, near_rows, near_gate, near_up
    )
    near_in_received = ins.sibling(sent)
    (sent,) = order(outs.send, near_out, near_received, also=last_across)
    near_arrived = outs.across(sent)
    clock = order(space, clock, also=far_grads)
    far_d_gate, far_d_up, far_in, sent = order(step, far_grads, far_rows, far_gate, far_up)
    far_in_received = ins.sibling(sent)
    far_slot, last_slot = order(outs.slots, far_out, far_received, far_arrived)
    far_sum = outs.line(far_slot, outs.far)
    last_sum = outs.line(last_slot, outs.last)
    clock = order(space, clock)
    far_sent, last_sent = order(lambda *s: ins.send(*s, parts=2), far_in, far_in_received)
    last_arrived = ins.across(last_sent)
    far_in_arrived = ins.across(far_sent)
    own_sent, near_sent = order(lambda *s: ins.send(*s, parts=2), near_in, near_in_received)
    near_in_arrived = ins.across(near_sent)
    clock = order(space, clock)
    product_of = lambda name, by_hidden: lambda r, *acts: weights(name, r, acts, width, by_hidden)
    grad_down = order(
        product_of("grad_down", True), near_grads + far_grads, near_act, far_act
    )
    own_slot, near_slot = order(outs.slots, near_out, near_received, near_arrived)
    near_sum = outs.line(near_slot, outs.near)
    all_rows = near_rows + far_rows
    grad_gate = order(product_of("grad_gate", False), all_rows, near_d_gate, far_d_gate)
    slot = order(lambda *s: ins.slot(1, *s), far_in, far_in_received, last_arrived)
    relay = ins.line(slot, ins.inward)
    middle = ins.line(slot, ins.middle)
    clock = order(space, clock)
    grad_up = order(
        product_of("grad_up", False), all_rows, near_d_up, far_d_up
    )
    slot = order(lambda *s: ins.slot(0, *s), far_in, far_in_received, far_in_arrived, relay)
    far = ins.line(slot, ins.far)
    own_in_arrived = ins.across(hold(own_sent, slot))
    clock = order(space, clock)

    slot = order(
        lambda *s: ins.slot(1, *s), near_in, near_in_received, near_in_arrived, also=middle
    )
    near = ins.line(slot, ins.near)
    clock = order(space, clock)
    columns = jax.ShapeDtypeStruct((tokens.shape[0], width // 2), jnp.bfloat16)
    output_cols = order(
        lambda *sums: call(finish_outputs_kernel, "finish_outputs", sums, columns),
        own_slot,
        near_sum,
        far_sum,
        last_sum,
    )
    near, far, own_in_arrived = hold((near, far, own_in_arrived), output_cols)
    input_cols, d_scores = order(
        lambda *sums: call(
            functools.partial(finish_inputs_kernel, experts),
            "finish_inputs",
            (*picks, clock, *sums),
            (columns, jax.ShapeDtypeStruct(picks[2].shape, jnp.float32)),
        ),
        near_in,
        near_in_received,
        own_in_arrived,
        far,
        near,
        middle,
    )
    return output_cols, input_cols, d_scores.T, grad_gate[None], grad_up[None], grad_down[None]


def any_mesh(tokens, expert_ids, pick_counts, gate_scores, gate_local, up_local, down_local, grad_out):
    tok_rows = tokens.shape[0]
    pick_width = expert_ids.shape[1]
    experts = lax.axis_size("expert")
    active_mask = lax.broadcasted_iota(jnp.int32, (tok_rows, pick_width), 1) < pick_counts[:, None]
    active_float = active_mask.astype(jnp.float32)
    weighted = gate_scores * active_float
    score_sum = jnp.sum(weighted, axis=1, keepdims=True)
    gate_weights = weighted / score_sum
    picked = (expert_ids[:, :, None] == lax.broadcasted_iota(jnp.int32, (1, 1, experts), 2)).astype(
        jnp.float32
    )
    gate_table = jnp.sum(gate_weights[:, :, None] * picked, axis=1)

    def combine(partial):
        summed = lax.psum_scatter(partial, "expert", scatter_dimension=0, tiled=True)
        return lax.psum_scatter(summed, "helper", scatter_dimension=1, tiled=True)

    rows = lax.all_gather(tokens, "expert", tiled=True)
    tables = lax.all_gather(gate_table.T, "expert", tiled=False)
    gates = jnp.take(tables, lax.axis_index("expert"), axis=1).reshape(-1, 1)
    grads = lax.all_gather(grad_out, "expert", tiled=True)

    pre_gate = product(rows, gate_local)
    pre_up = product(rows, up_local)
    silu_value, silu_slope = silu_parts(pre_gate)
    hidden_act = silu_value * pre_up
    gated_act = (gates * hidden_act).astype(jnp.bfloat16)
    output_cols = combine(product(gated_act, down_local).astype(jnp.bfloat16))

    raw_act = right_transposed(grads, down_local)
    gate_part = jnp.sum(raw_act * hidden_act, axis=1)
    d_act = gates * raw_act
    d_pre_gate = (d_act * pre_up * silu_slope).astype(jnp.bfloat16)
    d_pre_up = (d_act * silu_value).astype(jnp.bfloat16)
    input_cols = combine(
        (right_transposed(d_pre_gate, gate_local) + right_transposed(d_pre_up, up_local)).astype(
            jnp.bfloat16
        )
    )

    gate_parts = lax.all_gather(
        gate_part.reshape(-1, tok_rows), ("expert", "helper"), tiled=False
    )
    own_parts = jnp.take(gate_parts, lax.axis_index("expert"), axis=1)
    by_expert = jnp.sum(own_parts.reshape(experts, -1, tok_rows), axis=1).T
    d_gates = jnp.sum(by_expert[:, None, :] * picked, axis=2)
    d_scores = (
        active_float
        * (d_gates - jnp.sum(gate_weights * d_gates, axis=1, keepdims=True))
        / score_sum
    )

    def over_dp(whole, dimension):
        return lax.psum_scatter(
            whole.astype(jnp.bfloat16), "dp", scatter_dimension=dimension, tiled=True
        )[None]

    grad_w_gate = over_dp(transposed_product(rows, d_pre_gate), 0)
    grad_w_up = over_dp(transposed_product(rows, d_pre_up), 0)
    grad_w_down = over_dp(transposed_product(gated_act, grads), 1)
    return output_cols, input_cols, d_scores, grad_w_gate, grad_w_up, grad_w_down


def on_device(tokens, expert_ids, pick_counts, gate_scores, w_gate, w_up, w_down, grad_out):
    sizes = tuple(lax.axis_size(axis) for axis in ("expert", "helper", "dp"))
    layer = lined_up if sizes == (8, 2, 1) else any_mesh
    return layer(
        tokens, expert_ids, pick_counts, gate_scores, w_gate[0], w_up[0], w_down[0], grad_out
    )


def solution(mesh):
    in_specs = (
        P(("groups", "expert", "dp"), None),
        P(("groups", "expert", "dp"), None),
        P(("groups", "expert", "dp")),
        P(("groups", "expert", "dp"), None),
        P("expert", None, "helper"),
        P("expert", None, "helper"),
        P("expert", "helper", None),
        P(("groups", "expert", "dp"), None),
    )
    out_specs = (
        P(("groups", "expert", "dp"), "helper"),
        P(("groups", "expert", "dp"), "helper"),
        P(("groups", "expert", "dp"), None),
        P(("groups", "expert"), "dp", "helper"),
        P(("groups", "expert"), "dp", "helper"),
        P(("groups", "expert"), "helper", "dp"),
    )
    return jax.shard_map(
        on_device, mesh=mesh, in_specs=in_specs, out_specs=out_specs, check_vma=False
    )
```

```python
import functools

import jax
import jax.numpy as jnp
from jax import lax
from jax.experimental import pallas as pl
from jax.experimental.pallas import tpu as pltpu
from jax.sharding import PartitionSpec as P

LANES = 128
VMEM = pl.BlockSpec(memory_space=pltpu.VMEM)


def product(first_mat, second_mat):
    return jnp.dot(first_mat, second_mat, preferred_element_type=jnp.float32)


def transposed_product(first_mat, second_mat):
    return lax.dot_general(
        first_mat, second_mat, (((0,), (0,)), ((), ())), preferred_element_type=jnp.float32
    )


def right_transposed(first_mat, second_mat):
    return lax.dot_general(
        first_mat, second_mat, (((1,), (1,)), ((), ())), preferred_element_type=jnp.float32
    )


def silu_parts(argument):
    sigmoid_part = jax.nn.sigmoid(argument)
    return argument * sigmoid_part, sigmoid_part * (1.0 + argument * (1.0 - sigmoid_part))


def total_of(terms):
    return functools.reduce(jnp.add, terms)


def call(kernel, name, operands, out_shape, scratch=(), flops=0, moved=0, mebibytes=16):
    return pl.pallas_call(
        kernel,
        out_shape=out_shape,
        in_specs=[VMEM] * len(operands),
        out_specs=jax.tree.map(lambda _: VMEM, out_shape),
        scratch_shapes=scratch,
        compiler_params=pltpu.CompilerParams(vmem_limit_bytes=mebibytes * 2**20),
        cost_estimate=pl.CostEstimate(
            flops=flops, bytes_accessed=moved, transcendentals=0
        ),
        name=name,
    )(*operands)


def half_at(array, which):
    rows = array.shape[0] // 2
    return array[which * rows : (which + 1) * rows]


def swap_halves(array):
    return jnp.concatenate([half_at(array, 1), half_at(array, 0)], axis=0)


def hi_lo(values, is_high):
    high = values.astype(jnp.bfloat16).astype(jnp.float32)
    return jnp.where(is_high, high, values - high).astype(jnp.bfloat16)


def gate_rows(counts, scores):
    used = [(counts > k).astype(jnp.float32) for k in range(scores.shape[0])]
    weighted = [scores[k : k + 1] * used[k] for k in range(scores.shape[0])]
    score_sum = total_of(weighted)
    return [w / score_sum for w in weighted], used, score_sum


def prepare_rows_kernel(experts, *refs):
    sources, (own, pair, clock), targets, sems = refs[:4], refs[4:7], refs[7:11], refs[11]
    ids, counts, scores, rows = targets
    copies = [
        pltpu.make_async_copy(source, target, sems.at[i])
        for i, (source, target) in enumerate(zip(sources, targets))
    ]
    for copy in copies:
        copy.start()
    for copy in copies:
        copy.wait()
    total, width = rows.shape
    clock[...] = jnp.zeros_like(clock)
    lane = lax.broadcasted_iota(jnp.int32, (LANES, total), 0)
    gates, _, _ = gate_rows(counts[...], scores[...])
    table = jnp.zeros((LANES, total), jnp.float32)
    for k, gate in enumerate(gates):
        named = ids[k : k + 1, :]
        table = table + jnp.where((lane == named) | (lane == named + experts), gate, 0.0)
    table = table.T
    table = hi_lo(table, lax.broadcasted_iota(jnp.int32, table.shape, 1) < experts)
    for side in range(2):

        @pl.when(lax.axis_index("helper") == side)
        def _(side=side):
            own[:, :width] = half_at(rows, side)
            own[:, width:] = half_at(table, side)
            for i, which in enumerate((side, 1 - side)):
                here = slice(i * total // 2, (i + 1) * total // 2)
                pair[here, :width] = half_at(rows, which)
                pair[here, width:] = half_at(table, which)


def prepare_rows(ids, counts, scores, rows, experts):
    total, width = rows.shape
    piece = jax.ShapeDtypeStruct((total // 2, width + LANES), jnp.bfloat16)
    operands = (ids, counts, scores, rows)
    return pl.pallas_call(
        functools.partial(prepare_rows_kernel, experts),
        out_shape=(
            piece,
            jax.ShapeDtypeStruct((total, width + LANES), jnp.bfloat16),
            jax.ShapeDtypeStruct((8, LANES), jnp.float32),
        ),
        in_specs=[pl.BlockSpec(memory_space=pltpu.HBM)] * len(operands),
        out_specs=(VMEM,) * 3,
        scratch_shapes=[
            *(pltpu.VMEM(operand.shape, operand.dtype) for operand in operands),
            pltpu.SemaphoreType.DMA((len(operands),)),
        ],
        compiler_params=pltpu.CompilerParams(vmem_limit_bytes=8 * 2**20),
        name="prepare_rows",
    )(*(pltpu.with_memory_space_constraint(operand, pltpu.HBM) for operand in operands))


def prepare_grads_kernel(rows, own, pair):
    half = rows.shape[0] // 2
    for side in range(2):

        @pl.when(lax.axis_index("helper") == side)
        def _(side=side):
            own[...] = half_at(rows, side)
            pair[:half, :] = half_at(rows, side)
            pair[half:, :] = half_at(rows, 1 - side)


def prepare_grads(rows):
    total, width = rows.shape
    piece = jax.ShapeDtypeStruct((total // 2, width), jnp.bfloat16)
    return call(
        prepare_grads_kernel,
        "prepare_grads",
        (rows,),
        (piece, jax.ShapeDtypeStruct(rows.shape, jnp.bfloat16)),
    )


def pair_kernel(first, second, pair):
    half = first.shape[0]
    pair[:half, :] = first[...]
    pair[half:, :] = second[...]


def pair_up(first, second):
    rows, width = first.shape
    shape = jax.ShapeDtypeStruct((2 * rows, width), first.dtype)
    return call(pair_kernel, "pair", (first, second), shape)


def lay_out(pieces, target, columns):
    rows = pieces[0].shape[0]
    for i, piece in enumerate(pieces):
        target[i * rows : (i + 1) * rows, :] = piece[:, columns]


def gate_column(experts, pieces, width):
    table = jnp.concatenate([piece[:, width:] for piece in pieces], axis=0)
    lane = lax.broadcasted_iota(jnp.int32, table.shape, 1)
    expert = lax.axis_index("expert")
    mine = (lane == expert) | (lane == expert + experts)
    return jnp.sum(jnp.where(mine, table.astype(jnp.float32), 0.0), axis=1, keepdims=True)


def forward_kernel(experts, tile, *refs):
    pieces, refs = refs[:4], refs[4:]
    gate_mat, up_mat, down_mat, pre_gate, pre_up, gated, own, other, rows = refs
    width = rows.shape[1]
    half = width // 2
    lay_out(pieces, rows, slice(0, width))
    gate = gate_column(experts, pieces, width)
    for start in range(0, gated.shape[1], tile):
        columns = slice(start, start + tile)
        gate_part = product(rows[...], gate_mat[:, columns])
        up_part = product(rows[...], up_mat[:, columns])
        silu_value, _ = silu_parts(gate_part)
        pre_gate[:, columns] = gate_part
        pre_up[:, columns] = up_part
        gated[:, columns] = (gate * silu_value * up_part).astype(jnp.bfloat16)
    for which in range(2):
        stays = (lax.axis_index("helper") == which).astype(jnp.int32)
        for start in range(0, half, tile):
            columns = slice(start, start + tile)
            first = which * half + start
            out = product(gated[...], down_mat[:, first : first + tile]).astype(jnp.bfloat16)
            own[stays, :, columns] = half_at(out, 0)
            other[stays, :, columns] = half_at(out, 1)


def forward(pieces, gate_mat, up_mat, down_mat, experts, estimate):
    width, hidden = gate_mat.shape
    total = 4 * pieces[0].shape[0]
    pre = jax.ShapeDtypeStruct((total, hidden), jnp.float32)
    act = jax.ShapeDtypeStruct((total, hidden), jnp.bfloat16)
    sums = jax.ShapeDtypeStruct((2, total // 2, width // 2), jnp.bfloat16)
    return call(
        functools.partial(forward_kernel, experts, 256),
        "forward",
        (*pieces, gate_mat, up_mat, down_mat),
        (pre, pre, act, sums, sums),
        [pltpu.VMEM((total, width), jnp.bfloat16)],
        flops=estimate,
    )


def backward_kernel(experts, tile, *refs):
    pieces, gate_pieces, refs = refs[:4], refs[4:8], refs[8:]
    down_mat, pre_gate, pre_up, gate_mat, up_mat = refs[:5]
    d_gate, d_up, own, other, grads = refs[5:]
    total, width = grads.shape
    half = width // 2
    lay_out(pieces, grads, slice(0, width))
    gate = gate_column(experts, gate_pieces, width)
    shares = []
    for start in range(0, d_gate.shape[1], tile):
        columns = slice(start, start + tile)
        raw = right_transposed(grads[...], down_mat[columns, :])
        up_part = pre_up[:, columns]
        silu_value, silu_slope = silu_parts(pre_gate[:, columns])
        share = raw * silu_value * up_part
        shares = shares + [share[:, c : c + LANES] for c in range(0, tile, LANES)]
        d_act = gate * raw
        d_gate[:, columns] = (d_act * up_part * silu_slope).astype(jnp.bfloat16)
        d_up[:, columns] = (d_act * silu_value).astype(jnp.bfloat16)
    value = jnp.sum(total_of(shares), axis=1, keepdims=True)
    lane = lax.broadcasted_iota(jnp.int32, (total, LANES), 1)
    high = 2 * lax.axis_index("expert") + lax.axis_index("helper")
    value = jnp.where((lane == high) | (lane == high + 2 * experts), value, 0.0)
    value = hi_lo(value, lane < 2 * experts)
    for which in range(2):
        own[which, :, half:] = half_at(value, 0)
        other[which, :, half:] = half_at(value, 1)
    for which in range(2):
        stays = (lax.axis_index("helper") == which).astype(jnp.int32)
        for start in range(0, half, tile):
            columns = slice(start, start + tile)
            first = which * half + start
            back = right_transposed(d_gate[...], gate_mat[first : first + tile, :])
            back = back + right_transposed(d_up[...], up_mat[first : first + tile, :])
            back = back.astype(jnp.bfloat16)
            own[stays, :, columns] = half_at(back, 0)
            other[stays, :, columns] = half_at(back, 1)


def backward(pieces, gate_pieces, pre_gate, pre_up, gate_mat, up_mat, down_mat, experts):
    width, hidden = gate_mat.shape
    total = pre_gate.shape[0]
    act = jax.ShapeDtypeStruct((total, hidden), jnp.bfloat16)
    sums = jax.ShapeDtypeStruct((2, total // 2, width // 2 + LANES), jnp.bfloat16)
    return call(
        functools.partial(backward_kernel, experts, 256),
        "backward",
        (*pieces, *gate_pieces, down_mat, pre_gate, pre_up, gate_mat, up_mat),
        (act, act, sums, sums),
        [pltpu.VMEM((total, width), jnp.bfloat16)],
        flops=6 * total * width * hidden,
    )


def weights_kernel(width, hidden, tile, *refs):
    pieces, refs = refs[:8], refs[8:]
    first, second, grad, rows, acts = refs
    lay_out(pieces, rows, slice(0, width))
    lay_out((first, second), acts, slice(0, hidden))
    left, right = (acts, rows) if grad.shape[0] == hidden else (rows, acts)
    for start in range(0, grad.shape[0], tile):
        columns = slice(start, start + tile)
        grad[columns, :] = transposed_product(left[:, columns], right[...]).astype(jnp.bfloat16)


def weights(name, pieces, acts, width, by_hidden):
    rows, hidden = acts[0].shape
    shape = (hidden, width) if by_hidden else (width, hidden)
    return call(
        functools.partial(weights_kernel, width, hidden, 256),
        name,
        (*pieces, *acts),
        jax.ShapeDtypeStruct(shape, jnp.bfloat16),
        [
            pltpu.VMEM((2 * rows, width), jnp.bfloat16),
            pltpu.VMEM((2 * rows, hidden), jnp.bfloat16),
        ],
        flops=4 * rows * width * hidden,
    )


def send_kernel(own, received, *sent):
    rows = sent[0].shape[0]
    for i, target in enumerate(sent):
        here = slice(i * rows, (i + 1) * rows)
        target[...] = own[0, here, :] + received[0, here, :]


def slot_sum(own, received, arrived, slot, offset):
    rows = LANES
    half = rows // 2
    here = slice(slot * rows, (slot + 1) * rows)
    other = arrived[offset : offset + rows, :].astype(jnp.float32)
    kept = own[1, here, :].astype(jnp.float32) + received[1, here, :].astype(jnp.float32)
    return kept + jnp.concatenate([other[half:], other[:half]], axis=0)


def slots_kernel(own, received, arrived, first, second):
    for slot, target in enumerate((first, second)):
        target[...] = slot_sum(own, received, arrived, slot, slot * LANES).astype(target.dtype)


def slot_kernel(slot, own, received, arrived, *refs):
    whole = slot_sum(own, received, arrived, slot, 0)
    if len(refs) > 1:
        whole = whole + refs[0][...].astype(jnp.float32)
    refs[-1][...] = whole.astype(refs[-1].dtype)


def finish_outputs_kernel(*refs):
    columns = refs[-1]
    whole = total_of([ref[...].astype(jnp.float32) for ref in refs[:-1]])
    whole = jnp.where(lax.axis_index("helper") == 0, whole, swap_halves(whole))
    columns[...] = whole.astype(jnp.bfloat16)


def finish_inputs_kernel(experts, ids, counts, scores, clock, own, received, arrived, *refs):
    columns, d_scores = refs[-2:]
    width = columns.shape[1]
    whole = slot_sum(own, received, arrived, 0, 0)
    whole = total_of([whole] + [ref[...].astype(jnp.float32) for ref in refs[:-2]])
    whole = jnp.where(lax.axis_index("helper") == 0, whole, swap_halves(whole))
    columns[...] = whole[:, :width].astype(jnp.bfloat16)
    table = whole[:, width:].T
    lane = lax.broadcasted_iota(jnp.int32, table.shape, 0)
    named_by = (lane % (2 * experts)) // 2
    gates, used, score_sum = gate_rows(counts[...], scores[...])
    d_gates = []
    for k in range(len(gates)):
        hit = (named_by == ids[k : k + 1, :]) & (lane < 4 * experts)
        d_gates.append(jnp.sum(jnp.where(hit, table, 0.0), axis=0, keepdims=True))
    mean = total_of([gate * d_gate for gate, d_gate in zip(gates, d_gates)])
    for k, d_gate in enumerate(d_gates):
        d_scores[k : k + 1, :] = used[k] * (d_gate - mean) / score_sum


class FourChips:
    def __init__(self, label):
        self.label = label
        both = lambda pairs: [(2 * a + c, 2 * b + c) for a, b in pairs for c in (0, 1)]
        self.near = both([(z, z ^ 1) for z in range(4)])
        self.far = both([(z, z ^ 2) for z in range(4)])
        self.last = both([(z, z ^ 3) for z in range(4)])
        self.middle = both([(1, 2), (2, 1)])
        self.outward = both([(1, 0), (2, 3)])
        self.inward = both([(0, 1), (3, 2)])
        self.cores = [(i, i ^ 1) for i in range(8)]
        self.sides = [(0, 1), (1, 0)]

    def line(self, array, pairs):
        with jax.named_scope(self.label + "_line"):
            return lax.ppermute(array, "expert", pairs)

    def sibling(self, array):
        with jax.named_scope(self.label + "_cores"):
            return lax.ppermute(array, "expert", self.cores)

    def across(self, array):
        with jax.named_scope(self.label + "_across"):
            return lax.ppermute(array, "helper", self.sides)

    def send(self, own, received, parts=1):
        _, rows, columns = own.shape
        part = jax.ShapeDtypeStruct((rows // parts, columns), own.dtype)
        return call(send_kernel, self.label + "_send", (own, received), (part,) * parts)

    def slots(self, own, received, arrived):
        rows, columns = arrived.shape
        slot = jax.ShapeDtypeStruct((rows // 2, columns), arrived.dtype)
        return call(slots_kernel, self.label + "_slots", (own, received, arrived), (slot, slot))

    def slot(self, which, own, received, arrived, *others):
        return call(
            functools.partial(slot_kernel, which),
            self.label + "_slot",
            (own, received, arrived, *others),
            jax.ShapeDtypeStruct(arrived.shape, arrived.dtype),
        )


def load_kernel(*refs):
    sources, targets, sems = refs[:3], refs[3:6], refs[6]
    copies = [
        pltpu.make_async_copy(source, target, sems.at[i])
        for i, (source, target) in enumerate(zip(sources, targets))
    ]
    for copy in copies:
        copy.start()
    for copy in copies:
        copy.wait()


def load(*mats):
    return pl.pallas_call(
        load_kernel,
        out_shape=tuple(jax.ShapeDtypeStruct(mat.shape, mat.dtype) for mat in mats),
        in_specs=[pl.BlockSpec(memory_space=pltpu.HBM)] * len(mats),
        out_specs=(VMEM,) * len(mats),
        scratch_shapes=[pltpu.SemaphoreType.DMA((len(mats),))],
        compiler_params=pltpu.CompilerParams(vmem_limit_bytes=2**20),
        name="load",
    )(*(pltpu.with_memory_space_constraint(mat, pltpu.HBM) for mat in mats))


def space(clock):
    return pl.pallas_call(
        lambda old, new: None,
        out_shape=jax.ShapeDtypeStruct(clock.shape, clock.dtype),
        in_specs=[pl.BlockSpec(memory_space=pl.ANY)],
        out_specs=pl.BlockSpec(memory_space=pl.ANY),
        input_output_aliases={0: 0},
        compiler_params=pltpu.CompilerParams(vmem_limit_bytes=2**20),
        cost_estimate=pl.CostEstimate(flops=12 * 10**9, bytes_accessed=0, transcendentals=0),
        name="space",
    )(clock)


class Order:
    def __init__(self):
        self.token = None

    def __call__(self, function, *operands, also=()):
        if self.token is not None:
            operands, _ = lax.optimization_barrier((operands, (self.token, also)))
        result = function(*operands)
        self.token = result
        return result


def lined_up(tokens, expert_ids, pick_counts, gate_scores, gate_local, up_local, down_local, grad_out):
    experts = lax.axis_size("expert")
    width, hidden = gate_local.shape
    picks = (expert_ids.T, pick_counts[None, :], gate_scores.T)
    rows, grads, outs, ins = (FourChips(label) for label in ("rows", "grads", "out", "in"))
    order = Order()
    hold = lambda value, *tokens: lax.optimization_barrier((value, tokens))[0]
    ahead = lambda *pieces: forward(pieces, *mats, experts, 24 * tokens.size * hidden)
    back = lambda g, r, *pre: backward(g, r, *pre, *mats, experts)
    product_of = lambda name, by_hidden: lambda r, *acts: weights(name, r, acts, width, by_hidden)

    own, pair, clock = order(lambda r: prepare_rows(*picks, r, experts), tokens)
    near = rows.line(own, rows.near)
    middle = rows.line(own, rows.middle)
    sibling_pair = rows.sibling(pair)
    mats = order(load, gate_local, up_local, down_local)
    near, sibling_pair = hold((near, sibling_pair), mats)
    near_across = rows.across(near)
    far = rows.line(hold(own, near), rows.far)
    near_first = pair
    near_sibling = sibling_pair

    own, pair = order(prepare_grads, grad_out, also=(far, middle))
    far_across = rows.across(far)
    relay = rows.line(far, rows.outward)
    far_grad = grads.line(own, grads.far)
    sibling_pair = grads.sibling(pair)
    near_pair = order(pair_up, near, near_across)
    near_rows = [near_first, near_pair, near_sibling, rows.sibling(near_pair)]
    near_gate, near_up, near_act, near_out, sent = order(ahead, *near_rows)
    near_received = outs.sibling(sent)

    relay, far_across = hold((relay, far_across), near_act)
    last = order(jnp.add, middle, relay)
    last_across = rows.across(last)
    near = grads.line(hold(own, last), grads.near)
    middle_grad = grads.line(hold(own, last), grads.middle)
    far_pair = order(pair_up, far, far_across, also=sibling_pair)
    far_sibling = rows.sibling(far_pair)
    clock = order(space, clock, also=far_grad)
    last_across, near, middle_grad, far_sibling = hold(
        (last_across, near, middle_grad, far_sibling), clock
    )
    far_across = grads.across(far_grad)
    relay = grads.line(far_grad, grads.outward)
    last_pair = order(pair_up, last, last_across, also=(far_grad, far_sibling))
    far_rows = [far_pair, last_pair, far_sibling, rows.sibling(last_pair)]
    near_across = grads.across(near)
    far_gate, far_up, far_act, far_out, sent = order(ahead, *far_rows, also=(near, middle_grad))
    far_received = outs.sibling(sent)

    relay, far_across, near_across = hold((relay, far_across, near_across), far_act)
    last = order(jnp.add, middle_grad, relay)
    last_across = grads.across(last)
    near_pair = order(pair_up, near, near_across)
    near_grads = [pair, near_pair, sibling_pair, grads.sibling(near_pair)]
    far_pair = order(pair_up, far_grad, far_across)
    far_sibling = grads.sibling(far_pair)
    clock = order(space, clock)
    far_received, near_received = hold((far_received, near_received), clock)
    (sent,) = order(outs.send, far_out, far_received, also=(far_sibling, near_grads))
    far_arrived = outs.across(sent)
    (near_sent,) = order(outs.send, near_out, near_received)
    near_d_gate, near_d_up, near_in, sent = order(
        back, near_grads, near_rows, near_gate, near_up
    )
    near_in_received = ins.sibling(sent)
    near_arrived = outs.across(hold(near_sent, near_d_gate))
    far_slot, last_slot = order(outs.slots, far_out, far_received, far_arrived)
    far_sum = outs.line(far_slot, outs.far)
    last_sum = outs.line(last_slot, outs.last)
    last_across = hold(last_across, near_d_gate)
    last_pair = order(pair_up, last, last_across)
    far_grads = [far_pair, last_pair, far_sibling, grads.sibling(last_pair)]
    far_d_gate, far_d_up, far_in, sent = order(
        back, far_grads, far_rows, far_gate, far_up
    )
    far_in_received = ins.sibling(sent)
    near_arrived = hold(near_arrived, far_d_gate)
    own_slot, near_slot = order(outs.slots, near_out, near_received, near_arrived)
    near_sum = outs.line(near_slot, outs.near)
    clock = order(space, clock)
    far_in_received = hold(far_in_received, clock)
    far_sent, last_sent = order(lambda *s: ins.send(*s, parts=2), far_in, far_in_received)
    last_arrived = ins.across(last_sent)
    far_in_arrived = ins.across(far_sent)
    own_sent, near_sent = order(lambda *s: ins.send(*s, parts=2), near_in, near_in_received)
    grad_down = order(
        product_of("grad_down", True), near_grads + far_grads, near_act, far_act
    )
    all_rows = near_rows + far_rows
    slot = order(lambda *s: ins.slot(1, *s), far_in, far_in_received, last_arrived)
    near_in_arrived = ins.across(hold(near_sent, slot))
    relay = ins.line(slot, ins.inward)
    middle = ins.line(slot, ins.middle)
    grad_gate = order(product_of("grad_gate", False), all_rows, near_d_gate, far_d_gate)
    columns = jax.ShapeDtypeStruct((tokens.shape[0], width // 2), jnp.bfloat16)
    output_cols = order(
        lambda *sums: call(finish_outputs_kernel, "finish_outputs", sums, columns),
        own_slot,
        near_sum,
        far_sum,
        last_sum,
    )
    slot = order(lambda *s: ins.slot(0, *s), far_in, far_in_received, far_in_arrived, relay)
    far = ins.line(slot, ins.far)
    own_in_arrived = ins.across(hold(own_sent, slot))
    grad_up = order(product_of("grad_up", False), all_rows, near_d_up, far_d_up)
    slot = order(
        lambda *s: ins.slot(1, *s), near_in, near_in_received, near_in_arrived, also=middle
    )
    near = ins.line(slot, ins.near)
    input_cols, d_scores = order(
        lambda *sums: call(
            functools.partial(finish_inputs_kernel, experts),
            "finish_inputs",
            (*picks, clock, *sums),
            (columns, jax.ShapeDtypeStruct(picks[2].shape, jnp.float32)),
        ),
        near_in,
        near_in_received,
        own_in_arrived,
        far,
        near,
        middle,
    )
    return output_cols, input_cols, d_scores.T, grad_gate[None], grad_up[None], grad_down[None]


def any_mesh(tokens, expert_ids, pick_counts, gate_scores, gate_local, up_local, down_local, grad_out):
    tok_rows = tokens.shape[0]
    pick_width = expert_ids.shape[1]
    experts = lax.axis_size("expert")
    active_mask = lax.broadcasted_iota(jnp.int32, (tok_rows, pick_width), 1) < pick_counts[:, None]
    active_float = active_mask.astype(jnp.float32)
    weighted = gate_scores * active_float
    score_sum = jnp.sum(weighted, axis=1, keepdims=True)
    gate_weights = weighted / score_sum
    picked = (expert_ids[:, :, None] == lax.broadcasted_iota(jnp.int32, (1, 1, experts), 2)).astype(
        jnp.float32
    )
    gate_table = jnp.sum(gate_weights[:, :, None] * picked, axis=1)

    def combine(partial):
        summed = lax.psum_scatter(partial, "expert", scatter_dimension=0, tiled=True)
        return lax.psum_scatter(summed, "helper", scatter_dimension=1, tiled=True)

    rows = lax.all_gather(tokens, "expert", tiled=True)
    tables = lax.all_gather(gate_table.T, "expert", tiled=False)
    gates = jnp.take(tables, lax.axis_index("expert"), axis=1).reshape(-1, 1)
    grads = lax.all_gather(grad_out, "expert", tiled=True)

    pre_gate = product(rows, gate_local)
    pre_up = product(rows, up_local)
    silu_value, silu_slope = silu_parts(pre_gate)
    hidden_act = silu_value * pre_up
    gated_act = (gates * hidden_act).astype(jnp.bfloat16)
    output_cols = combine(product(gated_act, down_local).astype(jnp.bfloat16))

    raw_act = right_transposed(grads, down_local)
    gate_part = jnp.sum(raw_act * hidden_act, axis=1)
    d_act = gates * raw_act
    d_pre_gate = (d_act * pre_up * silu_slope).astype(jnp.bfloat16)
    d_pre_up = (d_act * silu_value).astype(jnp.bfloat16)
    input_cols = combine(
        (right_transposed(d_pre_gate, gate_local) + right_transposed(d_pre_up, up_local)).astype(
            jnp.bfloat16
        )
    )

    gate_parts = lax.all_gather(
        gate_part.reshape(-1, tok_rows), ("expert", "helper"), tiled=False
    )
    own_parts = jnp.take(gate_parts, lax.axis_index("expert"), axis=1)
    by_expert = jnp.sum(own_parts.reshape(experts, -1, tok_rows), axis=1).T
    d_gates = jnp.sum(by_expert[:, None, :] * picked, axis=2)
    d_scores = (
        active_float
        * (d_gates - jnp.sum(gate_weights * d_gates, axis=1, keepdims=True))
        / score_sum
    )

    def over_dp(whole, dimension):
        return lax.psum_scatter(
            whole.astype(jnp.bfloat16), "dp", scatter_dimension=dimension, tiled=True
        )[None]

    grad_w_gate = over_dp(transposed_product(rows, d_pre_gate), 0)
    grad_w_up = over_dp(transposed_product(rows, d_pre_up), 0)
    grad_w_down = over_dp(transposed_product(gated_act, grads), 1)
    return output_cols, input_cols, d_scores, grad_w_gate, grad_w_up, grad_w_down


def on_device(tokens, expert_ids, pick_counts, gate_scores, w_gate, w_up, w_down, grad_out):
    sizes = tuple(lax.axis_size(axis) for axis in ("expert", "helper", "dp"))
    layer = lined_up if sizes == (8, 2, 1) else any_mesh
    return layer(
        tokens, expert_ids, pick_counts, gate_scores, w_gate[0], w_up[0], w_down[0], grad_out
    )


def solution(mesh):
    in_specs = (
        P(("groups", "expert", "dp"), None),
        P(("groups", "expert", "dp"), None),
        P(("groups", "expert", "dp")),
        P(("groups", "expert", "dp"), None),
        P("expert", None, "helper"),
        P("expert", None, "helper"),
        P("expert", "helper", None),
        P(("groups", "expert", "dp"), None),
    )
    out_specs = (
        P(("groups", "expert", "dp"), "helper"),
        P(("groups", "expert", "dp"), "helper"),
        P(("groups", "expert", "dp"), None),
        P(("groups", "expert"), "dp", "helper"),
        P(("groups", "expert"), "dp", "helper"),
        P(("groups", "expert"), "helper", "dp"),
    )
    return jax.shard_map(
        on_device, mesh=mesh, in_specs=in_specs, out_specs=out_specs, check_vma=False
    )
```

```python
import functools

import jax
import jax.numpy as jnp
from jax import lax
from jax.experimental import pallas as pl
from jax.experimental.pallas import tpu as pltpu
from jax.sharding import PartitionSpec as P

LANES = 128
VMEM = pl.BlockSpec(memory_space=pltpu.VMEM)


def product(first_mat, second_mat):
    return jnp.dot(first_mat, second_mat, preferred_element_type=jnp.float32)


def transposed_product(first_mat, second_mat):
    return lax.dot_general(
        first_mat, second_mat, (((0,), (0,)), ((), ())), preferred_element_type=jnp.float32
    )


def right_transposed(first_mat, second_mat):
    return lax.dot_general(
        first_mat, second_mat, (((1,), (1,)), ((), ())), preferred_element_type=jnp.float32
    )


def silu_parts(argument):
    sigmoid_part = jax.nn.sigmoid(argument)
    return argument * sigmoid_part, sigmoid_part * (1.0 + argument * (1.0 - sigmoid_part))


def total_of(terms):
    return functools.reduce(jnp.add, terms)


def call(kernel, name, operands, out_shape, scratch=(), flops=0, moved=0, mebibytes=16):
    return pl.pallas_call(
        kernel,
        out_shape=out_shape,
        in_specs=[VMEM] * len(operands),
        out_specs=jax.tree.map(lambda _: VMEM, out_shape),
        scratch_shapes=scratch,
        compiler_params=pltpu.CompilerParams(vmem_limit_bytes=mebibytes * 2**20),
        cost_estimate=pl.CostEstimate(
            flops=flops, bytes_accessed=moved, transcendentals=0
        ),
        name=name,
    )(*operands)


def half_at(array, which):
    rows = array.shape[0] // 2
    return array[which * rows : (which + 1) * rows]


def swap_halves(array):
    return jnp.concatenate([half_at(array, 1), half_at(array, 0)], axis=0)


def hi_lo(values, is_high):
    high = values.astype(jnp.bfloat16).astype(jnp.float32)
    return jnp.where(is_high, high, values - high).astype(jnp.bfloat16)


def gate_rows(counts, scores):
    used = [(counts > k).astype(jnp.float32) for k in range(scores.shape[0])]
    weighted = [scores[k : k + 1] * used[k] for k in range(scores.shape[0])]
    score_sum = total_of(weighted)
    return [w / score_sum for w in weighted], used, score_sum


def prepare_rows_kernel(experts, *refs):
    sources, (own, pair, clock), targets, sems = refs[:4], refs[4:7], refs[7:11], refs[11]
    ids, counts, scores, rows = targets
    copies = [
        pltpu.make_async_copy(source, target, sems.at[i])
        for i, (source, target) in enumerate(zip(sources, targets))
    ]
    for copy in copies:
        copy.start()
    for copy in copies:
        copy.wait()
    total, width = rows.shape
    clock[...] = jnp.zeros_like(clock)
    lane = lax.broadcasted_iota(jnp.int32, (LANES, total), 0)
    gates, _, _ = gate_rows(counts[...], scores[...])
    table = jnp.zeros((LANES, total), jnp.float32)
    for k, gate in enumerate(gates):
        named = ids[k : k + 1, :]
        table = table + jnp.where((lane == named) | (lane == named + experts), gate, 0.0)
    table = table.T
    table = hi_lo(table, lax.broadcasted_iota(jnp.int32, table.shape, 1) < experts)
    for side in range(2):

        @pl.when(lax.axis_index("helper") == side)
        def _(side=side):
            own[:, :width] = half_at(rows, side)
            own[:, width:] = half_at(table, side)
            for i, which in enumerate((side, 1 - side)):
                here = slice(i * total // 2, (i + 1) * total // 2)
                pair[here, :width] = half_at(rows, which)
                pair[here, width:] = half_at(table, which)


def prepare_rows(ids, counts, scores, rows, experts):
    total, width = rows.shape
    piece = jax.ShapeDtypeStruct((total // 2, width + LANES), jnp.bfloat16)
    operands = (ids, counts, scores, rows)
    return pl.pallas_call(
        functools.partial(prepare_rows_kernel, experts),
        out_shape=(
            piece,
            jax.ShapeDtypeStruct((total, width + LANES), jnp.bfloat16),
            jax.ShapeDtypeStruct((8, LANES), jnp.float32),
        ),
        in_specs=[pl.BlockSpec(memory_space=pltpu.HBM)] * len(operands),
        out_specs=(VMEM,) * 3,
        scratch_shapes=[
            *(pltpu.VMEM(operand.shape, operand.dtype) for operand in operands),
            pltpu.SemaphoreType.DMA((len(operands),)),
        ],
        compiler_params=pltpu.CompilerParams(vmem_limit_bytes=8 * 2**20),
        name="prepare_rows",
    )(*(pltpu.with_memory_space_constraint(operand, pltpu.HBM) for operand in operands))


def prepare_grads_kernel(rows, own, pair):
    half = rows.shape[0] // 2
    for side in range(2):

        @pl.when(lax.axis_index("helper") == side)
        def _(side=side):
            own[...] = half_at(rows, side)
            pair[:half, :] = half_at(rows, side)
            pair[half:, :] = half_at(rows, 1 - side)


def prepare_grads(rows):
    total, width = rows.shape
    piece = jax.ShapeDtypeStruct((total // 2, width), jnp.bfloat16)
    return call(
        prepare_grads_kernel,
        "prepare_grads",
        (rows,),
        (piece, jax.ShapeDtypeStruct(rows.shape, jnp.bfloat16)),
    )


def pair_kernel(first, second, pair):
    half = first.shape[0]
    pair[:half, :] = first[...]
    pair[half:, :] = second[...]


def pair_up(first, second):
    rows, width = first.shape
    shape = jax.ShapeDtypeStruct((2 * rows, width), first.dtype)
    return call(pair_kernel, "pair", (first, second), shape)


def lay_out(pieces, target, columns):
    rows = pieces[0].shape[0]
    for i, piece in enumerate(pieces):
        target[i * rows : (i + 1) * rows, :] = piece[:, columns]


def gate_column(experts, pieces, width):
    table = jnp.concatenate([piece[:, width:] for piece in pieces], axis=0)
    lane = lax.broadcasted_iota(jnp.int32, table.shape, 1)
    expert = lax.axis_index("expert")
    mine = (lane == expert) | (lane == expert + experts)
    return jnp.sum(jnp.where(mine, table.astype(jnp.float32), 0.0), axis=1, keepdims=True)


def forward_kernel(experts, tile, *refs):
    pieces, refs = refs[:4], refs[4:]
    gate_mat, up_mat, down_mat, pre_gate, pre_up, gated, own, other, rows = refs
    width = rows.shape[1]
    half = width // 2
    lay_out(pieces, rows, slice(0, width))
    gate = gate_column(experts, pieces, width)
    for start in range(0, gated.shape[1], tile):
        columns = slice(start, start + tile)
        gate_part = product(rows[...], gate_mat[:, columns])
        up_part = product(rows[...], up_mat[:, columns])
        silu_value, _ = silu_parts(gate_part)
        pre_gate[:, columns] = gate_part
        pre_up[:, columns] = up_part
        gated[:, columns] = (gate * silu_value * up_part).astype(jnp.bfloat16)
    for which in range(2):
        stays = (lax.axis_index("helper") == which).astype(jnp.int32)
        for start in range(0, half, tile):
            columns = slice(start, start + tile)
            first = which * half + start
            out = product(gated[...], down_mat[:, first : first + tile]).astype(jnp.bfloat16)
            own[stays, :, columns] = half_at(out, 0)
            other[stays, :, columns] = half_at(out, 1)


def forward(pieces, gate_mat, up_mat, down_mat, experts, estimate):
    width, hidden = gate_mat.shape
    total = 4 * pieces[0].shape[0]
    pre = jax.ShapeDtypeStruct((total, hidden), jnp.float32)
    act = jax.ShapeDtypeStruct((total, hidden), jnp.bfloat16)
    sums = jax.ShapeDtypeStruct((2, total // 2, width // 2), jnp.bfloat16)
    return call(
        functools.partial(forward_kernel, experts, 256),
        "forward",
        (*pieces, gate_mat, up_mat, down_mat),
        (pre, pre, act, sums, sums),
        [pltpu.VMEM((total, width), jnp.bfloat16)],
        flops=estimate,
    )


def backward_kernel(experts, tile, *refs):
    pieces, gate_pieces, refs = refs[:4], refs[4:8], refs[8:]
    down_mat, pre_gate, pre_up, gate_mat, up_mat = refs[:5]
    d_gate, d_up, own, other, grads = refs[5:]
    total, width = grads.shape
    half = width // 2
    lay_out(pieces, grads, slice(0, width))
    gate = gate_column(experts, gate_pieces, width)
    shares = []
    for start in range(0, d_gate.shape[1], tile):
        columns = slice(start, start + tile)
        raw = right_transposed(grads[...], down_mat[columns, :])
        up_part = pre_up[:, columns]
        silu_value, silu_slope = silu_parts(pre_gate[:, columns])
        share = raw * silu_value * up_part
        shares = shares + [share[:, c : c + LANES] for c in range(0, tile, LANES)]
        d_act = gate * raw
        d_gate[:, columns] = (d_act * up_part * silu_slope).astype(jnp.bfloat16)
        d_up[:, columns] = (d_act * silu_value).astype(jnp.bfloat16)
    value = jnp.sum(total_of(shares), axis=1, keepdims=True)
    lane = lax.broadcasted_iota(jnp.int32, (total, LANES), 1)
    high = 2 * lax.axis_index("expert") + lax.axis_index("helper")
    value = jnp.where((lane == high) | (lane == high + 2 * experts), value, 0.0)
    value = hi_lo(value, lane < 2 * experts)
    for which in range(2):
        own[which, :, half:] = half_at(value, 0)
        other[which, :, half:] = half_at(value, 1)
    for which in range(2):
        stays = (lax.axis_index("helper") == which).astype(jnp.int32)
        for start in range(0, half, tile):
            columns = slice(start, start + tile)
            first = which * half + start
            back = right_transposed(d_gate[...], gate_mat[first : first + tile, :])
            back = back + right_transposed(d_up[...], up_mat[first : first + tile, :])
            back = back.astype(jnp.bfloat16)
            own[stays, :, columns] = half_at(back, 0)
            other[stays, :, columns] = half_at(back, 1)


def backward(pieces, gate_pieces, pre_gate, pre_up, gate_mat, up_mat, down_mat, experts):
    width, hidden = gate_mat.shape
    total = pre_gate.shape[0]
    act = jax.ShapeDtypeStruct((total, hidden), jnp.bfloat16)
    sums = jax.ShapeDtypeStruct((2, total // 2, width // 2 + LANES), jnp.bfloat16)
    return call(
        functools.partial(backward_kernel, experts, 256),
        "backward",
        (*pieces, *gate_pieces, down_mat, pre_gate, pre_up, gate_mat, up_mat),
        (act, act, sums, sums),
        [pltpu.VMEM((total, width), jnp.bfloat16)],
        flops=6 * total * width * hidden,
    )


def weights_kernel(width, hidden, tile, *refs):
    pieces, refs = refs[:8], refs[8:]
    first, second, grad, rows, acts = refs
    lay_out(pieces, rows, slice(0, width))
    lay_out((first, second), acts, slice(0, hidden))
    left, right = (acts, rows) if grad.shape[0] == hidden else (rows, acts)
    for start in range(0, grad.shape[0], tile):
        columns = slice(start, start + tile)
        grad[columns, :] = transposed_product(left[:, columns], right[...]).astype(jnp.bfloat16)


def weights(name, pieces, acts, width, by_hidden):
    rows, hidden = acts[0].shape
    shape = (hidden, width) if by_hidden else (width, hidden)
    return call(
        functools.partial(weights_kernel, width, hidden, 256),
        name,
        (*pieces, *acts),
        jax.ShapeDtypeStruct(shape, jnp.bfloat16),
        [
            pltpu.VMEM((2 * rows, width), jnp.bfloat16),
            pltpu.VMEM((2 * rows, hidden), jnp.bfloat16),
        ],
        flops=4 * rows * width * hidden,
    )


def send_kernel(own, received, *sent):
    rows = sent[0].shape[0]
    for i, target in enumerate(sent):
        here = slice(i * rows, (i + 1) * rows)
        target[...] = own[0, here, :] + received[0, here, :]


def slot_sum(own, received, arrived, slot, offset):
    rows = LANES
    half = rows // 2
    here = slice(slot * rows, (slot + 1) * rows)
    other = arrived[offset : offset + rows, :].astype(jnp.float32)
    kept = own[1, here, :].astype(jnp.float32) + received[1, here, :].astype(jnp.float32)
    return kept + jnp.concatenate([other[half:], other[:half]], axis=0)


def slots_kernel(own, received, arrived, first, second):
    for slot, target in enumerate((first, second)):
        target[...] = slot_sum(own, received, arrived, slot, slot * LANES).astype(target.dtype)


def slot_kernel(slot, own, received, arrived, *refs):
    whole = slot_sum(own, received, arrived, slot, 0)
    if len(refs) > 1:
        whole = whole + refs[0][...].astype(jnp.float32)
    refs[-1][...] = whole.astype(refs[-1].dtype)


def finish_outputs_kernel(*refs):
    columns = refs[-1]
    whole = total_of([ref[...].astype(jnp.float32) for ref in refs[:-1]])
    whole = jnp.where(lax.axis_index("helper") == 0, whole, swap_halves(whole))
    columns[...] = whole.astype(jnp.bfloat16)


def finish_inputs_kernel(experts, ids, counts, scores, clock, own, received, arrived, *refs):
    columns, d_scores = refs[-2:]
    width = columns.shape[1]
    whole = slot_sum(own, received, arrived, 0, 0)
    whole = total_of([whole] + [ref[...].astype(jnp.float32) for ref in refs[:-2]])
    whole = jnp.where(lax.axis_index("helper") == 0, whole, swap_halves(whole))
    columns[...] = whole[:, :width].astype(jnp.bfloat16)
    table = whole[:, width:].T
    lane = lax.broadcasted_iota(jnp.int32, table.shape, 0)
    named_by = (lane % (2 * experts)) // 2
    gates, used, score_sum = gate_rows(counts[...], scores[...])
    d_gates = []
    for k in range(len(gates)):
        hit = (named_by == ids[k : k + 1, :]) & (lane < 4 * experts)
        d_gates.append(jnp.sum(jnp.where(hit, table, 0.0), axis=0, keepdims=True))
    mean = total_of([gate * d_gate for gate, d_gate in zip(gates, d_gates)])
    for k, d_gate in enumerate(d_gates):
        d_scores[k : k + 1, :] = used[k] * (d_gate - mean) / score_sum


class FourChips:
    def __init__(self, label):
        self.label = label
        both = lambda pairs: [(2 * a + c, 2 * b + c) for a, b in pairs for c in (0, 1)]
        self.near = both([(z, z ^ 1) for z in range(4)])
        self.far = both([(z, z ^ 2) for z in range(4)])
        self.cores = [(i, i ^ 1) for i in range(8)]
        self.sides = [(0, 1), (1, 0)]

    def line(self, array, pairs):
        with jax.named_scope(self.label + "_line"):
            return lax.ppermute(array, "expert", pairs)

    def sibling(self, array):
        with jax.named_scope(self.label + "_cores"):
            return lax.ppermute(array, "expert", self.cores)

    def across(self, array):
        with jax.named_scope(self.label + "_across"):
            return lax.ppermute(array, "helper", self.sides)

    def send(self, own, received, parts=1):
        _, rows, columns = own.shape
        part = jax.ShapeDtypeStruct((rows // parts, columns), own.dtype)
        return call(send_kernel, self.label + "_send", (own, received), (part,) * parts)

    def slots(self, own, received, arrived):
        rows, columns = arrived.shape
        slot = jax.ShapeDtypeStruct((rows // 2, columns), arrived.dtype)
        return call(slots_kernel, self.label + "_slots", (own, received, arrived), (slot, slot))

    def slot(self, which, own, received, arrived, *others):
        return call(
            functools.partial(slot_kernel, which),
            self.label + "_slot",
            (own, received, arrived, *others),
            jax.ShapeDtypeStruct(arrived.shape, arrived.dtype),
        )


def load_kernel(*refs):
    sources, targets, sems = refs[:3], refs[3:6], refs[6]
    copies = [
        pltpu.make_async_copy(source, target, sems.at[i])
        for i, (source, target) in enumerate(zip(sources, targets))
    ]
    for copy in copies:
        copy.start()
    for copy in copies:
        copy.wait()


def load(*mats):
    return pl.pallas_call(
        load_kernel,
        out_shape=tuple(jax.ShapeDtypeStruct(mat.shape, mat.dtype) for mat in mats),
        in_specs=[pl.BlockSpec(memory_space=pltpu.HBM)] * len(mats),
        out_specs=(VMEM,) * len(mats),
        scratch_shapes=[pltpu.SemaphoreType.DMA((len(mats),))],
        compiler_params=pltpu.CompilerParams(vmem_limit_bytes=2**20),
        name="load",
    )(*(pltpu.with_memory_space_constraint(mat, pltpu.HBM) for mat in mats))


def space(clock, flops=12 * 10**9):
    return pl.pallas_call(
        lambda old, new: None,
        out_shape=jax.ShapeDtypeStruct(clock.shape, clock.dtype),
        in_specs=[pl.BlockSpec(memory_space=pl.ANY)],
        out_specs=pl.BlockSpec(memory_space=pl.ANY),
        input_output_aliases={0: 0},
        compiler_params=pltpu.CompilerParams(vmem_limit_bytes=2**20),
        cost_estimate=pl.CostEstimate(flops=flops, bytes_accessed=0, transcendentals=0),
        name="space",
    )(clock)


class Order:
    def __init__(self):
        self.token = None

    def __call__(self, function, *operands, also=()):
        if self.token is not None:
            operands, _ = lax.optimization_barrier((operands, (self.token, also)))
        result = function(*operands)
        self.token = result
        return result


def lined_up(tokens, expert_ids, pick_counts, gate_scores, gate_local, up_local, down_local, grad_out):
    experts = lax.axis_size("expert")
    width, hidden = gate_local.shape
    picks = (expert_ids.T, pick_counts[None, :], gate_scores.T)
    rows, grads, outs, ins = (FourChips(label) for label in ("rows", "grads", "out", "in"))
    order = Order()
    hold = lambda value, *tokens: lax.optimization_barrier((value, tokens))[0]
    ahead = lambda *pieces: forward(pieces, *mats, experts, 24 * tokens.size * hidden)
    back = lambda g, r, *pre: backward(g, r, *pre, *mats, experts)
    product_of = lambda name, by_hidden: lambda r, *acts: weights(name, r, acts, width, by_hidden)

    own, pair, clock = order(lambda r: prepare_rows(*picks, r, experts), tokens)
    near = rows.line(own, rows.near)
    far = rows.line(own, rows.far)
    sibling_pair = rows.sibling(pair)
    mats = order(load, gate_local, up_local, down_local)
    near, sibling_pair = hold((near, sibling_pair), mats)
    near_across = rows.across(near)
    far = hold(far, near)
    far_across = rows.across(far)
    last = rows.line(far, rows.near)
    near_first, near_sibling = pair, sibling_pair
    own, pair = order(prepare_grads, grad_out, also=far)
    sibling_pair = grads.sibling(pair)
    near_pair = order(pair_up, near, near_across)
    near_rows = [near_first, near_pair, near_sibling, rows.sibling(near_pair)]
    last_across = rows.across(last)
    near = grads.line(hold(own, last), grads.near)
    far_grad = grads.line(hold(own, last), grads.far)
    near_gate, near_up, near_act, near_out, sent = order(
        ahead, *near_rows, also=(last, sibling_pair)
    )
    near_received = outs.sibling(sent)

    near = hold(near, near_act)
    far_grad = hold(far_grad, near)
    far_across, last_across = hold((far_across, last_across), far_grad)
    far_pair = order(pair_up, far, far_across)
    far_sibling = rows.sibling(far_pair)
    last_pair = order(pair_up, last, last_across, also=far_sibling)
    far_rows = [far_pair, last_pair, far_sibling, rows.sibling(last_pair)]
    near_across = grads.across(near)
    far_across = grads.across(far_grad)
    last = grads.line(far_grad, grads.near)
    far_gate, far_up, far_act, far_out, sent = order(ahead, *far_rows, also=(near, far_grad))
    far_received = outs.sibling(sent)

    last, near_across = hold((last, near_across), far_act)
    far_across = hold(far_across, near_across)
    last_across = grads.across(last)
    near_pair = order(pair_up, near, near_across)
    near_grads = [pair, near_pair, sibling_pair, grads.sibling(near_pair)]
    far_pair = order(pair_up, far_grad, far_across)
    far_sibling = grads.sibling(far_pair)
    clock = order(space, clock)
    far_received, near_received = hold((far_received, near_received), clock)
    (sent,) = order(outs.send, far_out, far_received, also=(far_sibling, near_grads))
    far_arrived = outs.across(sent)
    (near_sent,) = order(outs.send, near_out, near_received)
    near_d_gate, near_d_up, near_in, sent = order(
        back, near_grads, near_rows, near_gate, near_up
    )
    near_in_received = ins.sibling(sent)
    near_arrived = outs.across(hold(near_sent, near_d_gate))
    far_slot, last_slot = order(outs.slots, far_out, far_received, far_arrived)
    last_sum = outs.line(last_slot, outs.near)
    last_across = hold(last_across, near_d_gate)
    last_pair = order(pair_up, last, last_across)
    far_grads = [far_pair, last_pair, far_sibling, grads.sibling(last_pair)]
    far_d_gate, far_d_up, far_in, sent = order(
        back, far_grads, far_rows, far_gate, far_up
    )
    far_in_received = ins.sibling(sent)
    near_arrived = hold(near_arrived, far_d_gate)
    clock = order(space, clock, also=near_arrived)
    far_in_received = hold(far_in_received, clock)
    far_sent, last_sent = order(lambda *s: ins.send(*s, parts=2), far_in, far_in_received)
    last_arrived = ins.across(last_sent)
    far_in_arrived = ins.across(far_sent)
    own_sent, near_sent = order(lambda *s: ins.send(*s, parts=2), near_in, near_in_received)
    far_sum = outs.line(order(jnp.add, far_slot, last_sum), outs.far)
    own_slot, near_slot = order(outs.slots, near_out, near_received, near_arrived)
    near_sum = outs.line(near_slot, outs.near)
    near_in_arrived = ins.across(hold(near_sent, own_slot))
    grad_down = order(
        product_of("grad_down", True), near_grads + far_grads, near_act, far_act
    )
    all_rows = near_rows + far_rows
    slot = order(lambda *s: ins.slot(1, *s), far_in, far_in_received, last_arrived)
    last_sum = ins.line(slot, ins.near)
    own_in_arrived = ins.across(hold(own_sent, slot))
    grad_gate = order(product_of("grad_gate", False), all_rows, near_d_gate, far_d_gate)
    slot = order(lambda *s: ins.slot(0, *s), far_in, far_in_received, far_in_arrived, last_sum)
    far = ins.line(slot, ins.far)
    columns = jax.ShapeDtypeStruct((tokens.shape[0], width // 2), jnp.bfloat16)
    output_cols = order(
        lambda *sums: call(finish_outputs_kernel, "finish_outputs", sums, columns),
        own_slot,
        near_sum,
        far_sum,
    )
    grad_up = order(product_of("grad_up", False), all_rows, near_d_up, far_d_up)
    slot = order(lambda *s: ins.slot(1, *s), near_in, near_in_received, near_in_arrived)
    near = ins.line(slot, ins.near)
    clock = order(lambda c: space(c, 2 * 10**9), clock, also=far)
    near, own_in_arrived = hold((near, own_in_arrived), clock)
    input_cols, d_scores = order(
        lambda *sums: call(
            functools.partial(finish_inputs_kernel, experts),
            "finish_inputs",
            (*picks, clock, *sums),
            (columns, jax.ShapeDtypeStruct(picks[2].shape, jnp.float32)),
        ),
        near_in,
        near_in_received,
        own_in_arrived,
        far,
        near,
    )
    return output_cols, input_cols, d_scores.T, grad_gate[None], grad_up[None], grad_down[None]


def any_mesh(tokens, expert_ids, pick_counts, gate_scores, gate_local, up_local, down_local, grad_out):
    tok_rows = tokens.shape[0]
    pick_width = expert_ids.shape[1]
    experts = lax.axis_size("expert")
    active_mask = lax.broadcasted_iota(jnp.int32, (tok_rows, pick_width), 1) < pick_counts[:, None]
    active_float = active_mask.astype(jnp.float32)
    weighted = gate_scores * active_float
    score_sum = jnp.sum(weighted, axis=1, keepdims=True)
    gate_weights = weighted / score_sum
    picked = (expert_ids[:, :, None] == lax.broadcasted_iota(jnp.int32, (1, 1, experts), 2)).astype(
        jnp.float32
    )
    gate_table = jnp.sum(gate_weights[:, :, None] * picked, axis=1)

    def combine(partial):
        summed = lax.psum_scatter(partial, "expert", scatter_dimension=0, tiled=True)
        return lax.psum_scatter(summed, "helper", scatter_dimension=1, tiled=True)

    rows = lax.all_gather(tokens, "expert", tiled=True)
    tables = lax.all_gather(gate_table.T, "expert", tiled=False)
    gates = jnp.take(tables, lax.axis_index("expert"), axis=1).reshape(-1, 1)
    grads = lax.all_gather(grad_out, "expert", tiled=True)

    pre_gate = product(rows, gate_local)
    pre_up = product(rows, up_local)
    silu_value, silu_slope = silu_parts(pre_gate)
    hidden_act = silu_value * pre_up
    gated_act = (gates * hidden_act).astype(jnp.bfloat16)
    output_cols = combine(product(gated_act, down_local).astype(jnp.bfloat16))

    raw_act = right_transposed(grads, down_local)
    gate_part = jnp.sum(raw_act * hidden_act, axis=1)
    d_act = gates * raw_act
    d_pre_gate = (d_act * pre_up * silu_slope).astype(jnp.bfloat16)
    d_pre_up = (d_act * silu_value).astype(jnp.bfloat16)
    input_cols = combine(
        (right_transposed(d_pre_gate, gate_local) + right_transposed(d_pre_up, up_local)).astype(
            jnp.bfloat16
        )
    )

    gate_parts = lax.all_gather(
        gate_part.reshape(-1, tok_rows), ("expert", "helper"), tiled=False
    )
    own_parts = jnp.take(gate_parts, lax.axis_index("expert"), axis=1)
    by_expert = jnp.sum(own_parts.reshape(experts, -1, tok_rows), axis=1).T
    d_gates = jnp.sum(by_expert[:, None, :] * picked, axis=2)
    d_scores = (
        active_float
        * (d_gates - jnp.sum(gate_weights * d_gates, axis=1, keepdims=True))
        / score_sum
    )

    def over_dp(whole, dimension):
        return lax.psum_scatter(
            whole.astype(jnp.bfloat16), "dp", scatter_dimension=dimension, tiled=True
        )[None]

    grad_w_gate = over_dp(transposed_product(rows, d_pre_gate), 0)
    grad_w_up = over_dp(transposed_product(rows, d_pre_up), 0)
    grad_w_down = over_dp(transposed_product(gated_act, grads), 1)
    return output_cols, input_cols, d_scores, grad_w_gate, grad_w_up, grad_w_down


def on_device(tokens, expert_ids, pick_counts, gate_scores, w_gate, w_up, w_down, grad_out):
    sizes = tuple(lax.axis_size(axis) for axis in ("expert", "helper", "dp"))
    layer = lined_up if sizes == (8, 2, 1) else any_mesh
    return layer(
        tokens, expert_ids, pick_counts, gate_scores, w_gate[0], w_up[0], w_down[0], grad_out
    )


def solution(mesh):
    in_specs = (
        P(("groups", "expert", "dp"), None),
        P(("groups", "expert", "dp"), None),
        P(("groups", "expert", "dp")),
        P(("groups", "expert", "dp"), None),
        P("expert", None, "helper"),
        P("expert", None, "helper"),
        P("expert", "helper", None),
        P(("groups", "expert", "dp"), None),
    )
    out_specs = (
        P(("groups", "expert", "dp"), "helper"),
        P(("groups", "expert", "dp"), "helper"),
        P(("groups", "expert", "dp"), None),
        P(("groups", "expert"), "dp", "helper"),
        P(("groups", "expert"), "dp", "helper"),
        P(("groups", "expert"), "helper", "dp"),
    )
    return jax.shard_map(
        on_device, mesh=mesh, in_specs=in_specs, out_specs=out_specs, check_vma=False
    )
```

```python
import functools

import jax
import jax.numpy as jnp
from jax import lax
from jax.experimental import pallas as pl
from jax.experimental.pallas import tpu as pltpu
from jax.sharding import PartitionSpec as P

LANES = 128
VMEM = pl.BlockSpec(memory_space=pltpu.VMEM)


def product(first_mat, second_mat):
    return jnp.dot(first_mat, second_mat, preferred_element_type=jnp.float32)


def transposed_product(first_mat, second_mat):
    return lax.dot_general(
        first_mat, second_mat, (((0,), (0,)), ((), ())), preferred_element_type=jnp.float32
    )


def right_transposed(first_mat, second_mat):
    return lax.dot_general(
        first_mat, second_mat, (((1,), (1,)), ((), ())), preferred_element_type=jnp.float32
    )


def silu_parts(argument):
    sigmoid_part = jax.nn.sigmoid(argument)
    return argument * sigmoid_part, sigmoid_part * (1.0 + argument * (1.0 - sigmoid_part))


def total_of(terms):
    return functools.reduce(jnp.add, terms)


def call(kernel, name, operands, out_shape, scratch=(), flops=0, moved=0, mebibytes=12):
    return pl.pallas_call(
        kernel,
        out_shape=out_shape,
        in_specs=[VMEM] * len(operands),
        out_specs=jax.tree.map(lambda _: VMEM, out_shape),
        scratch_shapes=scratch,
        compiler_params=pltpu.CompilerParams(vmem_limit_bytes=mebibytes * 2**20),
        cost_estimate=pl.CostEstimate(
            flops=flops, bytes_accessed=moved, transcendentals=0
        ),
        name=name,
    )(*operands)


def half_at(array, which):
    rows = array.shape[0] // 2
    return array[which * rows : (which + 1) * rows]


def swap_halves(array):
    return jnp.concatenate([half_at(array, 1), half_at(array, 0)], axis=0)


def hi_lo(values, is_high):
    high = values.astype(jnp.bfloat16).astype(jnp.float32)
    return jnp.where(is_high, high, values - high).astype(jnp.bfloat16)


def gate_rows(counts, scores):
    used = [(counts > k).astype(jnp.float32) for k in range(scores.shape[0])]
    weighted = [scores[k : k + 1] * used[k] for k in range(scores.shape[0])]
    score_sum = total_of(weighted)
    return [w / score_sum for w in weighted], used, score_sum


def prepare_rows_kernel(experts, *refs):
    sources, (own, pair, clock), targets, sems = refs[:4], refs[4:7], refs[7:11], refs[11]
    ids, counts, scores, rows = targets
    copies = [
        pltpu.make_async_copy(source, target, sems.at[i])
        for i, (source, target) in enumerate(zip(sources, targets))
    ]
    for copy in copies:
        copy.start()
    for copy in copies:
        copy.wait()
    total, width = rows.shape
    clock[...] = jnp.zeros_like(clock)
    lane = lax.broadcasted_iota(jnp.int32, (LANES, total), 0)
    gates, _, _ = gate_rows(counts[...], scores[...])
    table = jnp.zeros((LANES, total), jnp.float32)
    for k, gate in enumerate(gates):
        named = ids[k : k + 1, :]
        table = table + jnp.where((lane == named) | (lane == named + experts), gate, 0.0)
    table = table.T
    table = hi_lo(table, lax.broadcasted_iota(jnp.int32, table.shape, 1) < experts)
    for side in range(2):

        @pl.when(lax.axis_index("helper") == side)
        def _(side=side):
            own[:, :width] = half_at(rows, side)
            own[:, width:] = half_at(table, side)
            for i, which in enumerate((side, 1 - side)):
                here = slice(i * total // 2, (i + 1) * total // 2)
                pair[here, :width] = half_at(rows, which)
                pair[here, width:] = half_at(table, which)


def prepare_rows(ids, counts, scores, rows, experts):
    total, width = rows.shape
    piece = jax.ShapeDtypeStruct((total // 2, width + LANES), jnp.bfloat16)
    operands = (ids, counts, scores, rows)
    return pl.pallas_call(
        functools.partial(prepare_rows_kernel, experts),
        out_shape=(
            piece,
            jax.ShapeDtypeStruct((total, width + LANES), jnp.bfloat16),
            jax.ShapeDtypeStruct((8, LANES), jnp.float32),
        ),
        in_specs=[pl.BlockSpec(memory_space=pltpu.HBM)] * len(operands),
        out_specs=(VMEM,) * 3,
        scratch_shapes=[
            *(pltpu.VMEM(operand.shape, operand.dtype) for operand in operands),
            pltpu.SemaphoreType.DMA((len(operands),)),
        ],
        compiler_params=pltpu.CompilerParams(vmem_limit_bytes=8 * 2**20),
        name="prepare_rows",
    )(*(pltpu.with_memory_space_constraint(operand, pltpu.HBM) for operand in operands))


def prepare_grads_kernel(rows, own, pair):
    half = rows.shape[0] // 2
    for side in range(2):

        @pl.when(lax.axis_index("helper") == side)
        def _(side=side):
            own[...] = half_at(rows, side)
            pair[:half, :] = half_at(rows, side)
            pair[half:, :] = half_at(rows, 1 - side)


def prepare_grads(rows):
    total, width = rows.shape
    piece = jax.ShapeDtypeStruct((total // 2, width), jnp.bfloat16)
    return call(
        prepare_grads_kernel,
        "prepare_grads",
        (rows,),
        (piece, jax.ShapeDtypeStruct(rows.shape, jnp.bfloat16)),
    )


def pair_kernel(first, second, pair):
    half = first.shape[0]
    pair[:half, :] = first[...]
    pair[half:, :] = second[...]


def pair_up(first, second):
    rows, width = first.shape
    shape = jax.ShapeDtypeStruct((2 * rows, width), first.dtype)
    return call(pair_kernel, "pair", (first, second), shape)


def parts_of(pieces):
    pair, line_pair, across_pair, last_pair = pieces
    rows = pair.shape[0]
    half = rows // 2
    parts = [(pair, 0, rows)]
    for slot in range(2):
        parts = parts + [(line_pair, slot * half, half), (across_pair, slot * half, half)]
    return parts + [(last_pair, 0, rows)]


def lay_out(pieces, target, columns):
    at = 0
    for piece, start, rows in parts_of(pieces[:4]) + parts_of(pieces[4:]):
        target[at : at + rows, :] = piece[start : start + rows, columns]
        at = at + rows


def gate_column(experts, pieces, width):
    parts = parts_of(pieces[:4]) + parts_of(pieces[4:])
    table = jnp.concatenate(
        [piece[start : start + rows, width:] for piece, start, rows in parts], axis=0
    )
    lane = lax.broadcasted_iota(jnp.int32, table.shape, 1)
    expert = lax.axis_index("expert")
    mine = (lane == expert) | (lane == expert + experts)
    return jnp.sum(jnp.where(mine, table.astype(jnp.float32), 0.0), axis=1, keepdims=True)


def hidden_kernel(experts, tile, *refs):
    pieces, refs = refs[:8], refs[8:]
    gate_mat, up_mat, pre_gate, pre_up, gated, rows = refs
    width = rows.shape[1]
    lay_out(pieces, rows, slice(0, width))
    gate = gate_column(experts, pieces, width)
    for start in range(0, gated.shape[1], tile):
        columns = slice(start, start + tile)
        gate_part = product(rows[...], gate_mat[:, columns])
        up_part = product(rows[...], up_mat[:, columns])
        silu_value, _ = silu_parts(gate_part)
        pre_gate[:, columns] = gate_part
        pre_up[:, columns] = up_part
        gated[:, columns] = (gate * silu_value * up_part).astype(jnp.bfloat16)


def hidden_units(pieces, gate_mat, up_mat, experts):
    width, hidden = gate_mat.shape
    total = 8 * pieces[0].shape[0]
    pre = jax.ShapeDtypeStruct((total, hidden), jnp.float32)
    act = jax.ShapeDtypeStruct((total, hidden), jnp.bfloat16)
    return call(
        functools.partial(hidden_kernel, experts, 256),
        "hidden_units",
        (*pieces, gate_mat, up_mat),
        (pre, pre, act),
        [pltpu.VMEM((total, width), jnp.bfloat16)],
        flops=4 * total * width * hidden,
        mebibytes=12,
    )


def outputs_kernel(tile, gated, down_mat, own, other):
    half = own.shape[2]
    for which in range(2):
        stays = (lax.axis_index("helper") == which).astype(jnp.int32)
        for start in range(0, half, tile):
            columns = slice(start, start + tile)
            first = which * half + start
            out = product(gated[...], down_mat[:, first : first + tile]).astype(jnp.bfloat16)
            own[stays, :, columns] = half_at(out, 0)
            other[stays, :, columns] = half_at(out, 1)


def outputs_of(gated, down_mat):
    total, hidden = gated.shape
    width = down_mat.shape[1]
    sums = jax.ShapeDtypeStruct((2, total // 2, width // 2), jnp.bfloat16)
    return call(
        functools.partial(outputs_kernel, 256),
        "outputs",
        (gated, down_mat),
        (sums, sums),
        flops=2 * total * width * hidden,
    )


def hidden_grads_kernel(experts, tile, *refs):
    pieces, gate_pieces, refs = refs[:8], refs[8:16], refs[16:]
    down_mat, pre_gate, pre_up, d_gate, d_up, shares_out, grads = refs
    total, width = grads.shape
    lay_out(pieces, grads, slice(0, width))
    gate = gate_column(experts, gate_pieces, width)
    shares = []
    for start in range(0, d_gate.shape[1], tile):
        columns = slice(start, start + tile)
        raw = right_transposed(grads[...], down_mat[columns, :])
        up_part = pre_up[:, columns]
        silu_value, silu_slope = silu_parts(pre_gate[:, columns])
        share = raw * silu_value * up_part
        shares = shares + [share[:, c : c + LANES] for c in range(0, tile, LANES)]
        d_act = gate * raw
        d_gate[:, columns] = (d_act * up_part * silu_slope).astype(jnp.bfloat16)
        d_up[:, columns] = (d_act * silu_value).astype(jnp.bfloat16)
    value = jnp.sum(total_of(shares), axis=1, keepdims=True)
    lane = lax.broadcasted_iota(jnp.int32, (total, LANES), 1)
    high = 2 * lax.axis_index("expert") + lax.axis_index("helper")
    value = jnp.where((lane == high) | (lane == high + 2 * experts), value, 0.0)
    shares_out[...] = hi_lo(value, lane < 2 * experts)


def hidden_grads(pieces, gate_pieces, pre_gate, pre_up, down_mat, experts):
    hidden, width = down_mat.shape
    total = pre_gate.shape[0]
    act = jax.ShapeDtypeStruct((total, hidden), jnp.bfloat16)
    return call(
        functools.partial(hidden_grads_kernel, experts, 256),
        "hidden_grads",
        (*pieces, *gate_pieces, down_mat, pre_gate, pre_up),
        (act, act, jax.ShapeDtypeStruct((total, LANES), jnp.bfloat16)),
        [pltpu.VMEM((total, width), jnp.bfloat16)],
        flops=2 * total * width * hidden,
        mebibytes=12,
    )


def input_grads_kernel(tile, d_gate, d_up, shares, gate_mat, up_mat, own, other):
    half = own.shape[2] - LANES
    for which in range(2):
        own[which, :, half:] = half_at(shares, 0)
        other[which, :, half:] = half_at(shares, 1)
    for which in range(2):
        stays = (lax.axis_index("helper") == which).astype(jnp.int32)
        for start in range(0, half, tile):
            columns = slice(start, start + tile)
            first = which * half + start
            back = right_transposed(d_gate[...], gate_mat[first : first + tile, :])
            back = back + right_transposed(d_up[...], up_mat[first : first + tile, :])
            back = back.astype(jnp.bfloat16)
            own[stays, :, columns] = half_at(back, 0)
            other[stays, :, columns] = half_at(back, 1)


def input_grads_of(d_gate, d_up, shares, gate_mat, up_mat):
    width, hidden = gate_mat.shape
    total = d_gate.shape[0]
    sums = jax.ShapeDtypeStruct((2, total // 2, width // 2 + LANES), jnp.bfloat16)
    return call(
        functools.partial(input_grads_kernel, 256),
        "input_grads",
        (d_gate, d_up, shares, gate_mat, up_mat),
        (sums, sums),
        flops=0,
        mebibytes=12,
    )


def weights_kernel(width, tile, *refs):
    pieces, (acts, grad, rows) = refs[:8], refs[8:]
    lay_out(pieces, rows, slice(0, width))
    left, right = (acts, rows) if grad.shape[1] == width else (rows, acts)
    for start in range(0, grad.shape[0], tile):
        columns = slice(start, start + tile)
        grad[columns, :] = transposed_product(left[:, columns], right[...]).astype(jnp.bfloat16)


def weights(name, pieces, acts, width, by_hidden):
    rows, hidden = acts.shape
    shape = (hidden, width) if by_hidden else (width, hidden)
    return call(
        functools.partial(weights_kernel, width, 256),
        name,
        (*pieces, acts),
        jax.ShapeDtypeStruct(shape, jnp.bfloat16),
        [pltpu.VMEM((rows, width), jnp.bfloat16)],
        flops=2 * rows * width * hidden,
    )


def send_kernel(own, received, *sent):
    rows = sent[0].shape[0]
    for i, target in enumerate(sent):
        here = slice(i * rows, (i + 1) * rows)
        target[...] = own[0, here, :] + received[0, here, :]


def slot_sum(own, received, arrived, slot, offset):
    rows = LANES
    half = rows // 2
    here = slice(slot * rows, (slot + 1) * rows)
    other = arrived[offset : offset + rows, :].astype(jnp.float32)
    kept = own[1, here, :].astype(jnp.float32) + received[1, here, :].astype(jnp.float32)
    return kept + jnp.concatenate([other[half:], other[:half]], axis=0)


def slots_kernel(own, received, arrived, own_slot, near_and_last, far_slot):
    rows = own_slot.shape[0]
    targets = (own_slot, near_and_last.at[:rows], far_slot, near_and_last.at[rows:])
    for slot, target in enumerate(targets):
        target[...] = slot_sum(own, received, arrived, slot, slot * rows).astype(target.dtype)


def add_last_kernel(far_slot, arrived, total):
    rows = far_slot.shape[0]
    total[...] = far_slot[...] + arrived[rows:, :]


def slot_kernel(slot, own, received, arrived, *refs):
    whole = slot_sum(own, received, arrived, slot, 0)
    if len(refs) > 1:
        whole = whole + refs[0][...].astype(jnp.float32)
    refs[-1][...] = whole.astype(refs[-1].dtype)


def finish_outputs_kernel(own, near_and_last, far, columns):
    near = near_and_last[: own.shape[0], :]
    whole = total_of([term.astype(jnp.float32) for term in (own[...], near, far[...])])
    whole = jnp.where(lax.axis_index("helper") == 0, whole, swap_halves(whole))
    columns[...] = whole.astype(jnp.bfloat16)


def finish_inputs_kernel(experts, ids, counts, scores, clock, own, received, arrived, *refs):
    columns, d_scores = refs[-2:]
    width = columns.shape[1]
    whole = slot_sum(own, received, arrived, 0, 0)
    whole = total_of([whole] + [ref[...].astype(jnp.float32) for ref in refs[:-2]])
    whole = jnp.where(lax.axis_index("helper") == 0, whole, swap_halves(whole))
    columns[...] = whole[:, :width].astype(jnp.bfloat16)
    table = whole[:, width:].T
    lane = lax.broadcasted_iota(jnp.int32, table.shape, 0)
    named_by = (lane % (2 * experts)) // 2
    gates, used, score_sum = gate_rows(counts[...], scores[...])
    d_gates = []
    for k in range(len(gates)):
        hit = (named_by == ids[k : k + 1, :]) & (lane < 4 * experts)
        d_gates.append(jnp.sum(jnp.where(hit, table, 0.0), axis=0, keepdims=True))
    mean = total_of([gate * d_gate for gate, d_gate in zip(gates, d_gates)])
    for k, d_gate in enumerate(d_gates):
        d_scores[k : k + 1, :] = used[k] * (d_gate - mean) / score_sum


class FourChips:
    def __init__(self, label):
        self.label = label
        both = lambda pairs: [(2 * a + c, 2 * b + c) for a, b in pairs for c in (0, 1)]
        self.near = both([(z, z ^ 1) for z in range(4)])
        self.far = both([(z, z ^ 2) for z in range(4)])
        self.cores = [(i, i ^ 1) for i in range(8)]
        self.sides = [(0, 1), (1, 0)]

    def line(self, array, pairs):
        with jax.named_scope(self.label + "_line"):
            return lax.ppermute(array, "expert", pairs)

    def sibling(self, array):
        with jax.named_scope(self.label + "_cores"):
            return lax.ppermute(array, "expert", self.cores)

    def across(self, array):
        with jax.named_scope(self.label + "_across"):
            return lax.ppermute(array, "helper", self.sides)

    def send(self, own, received, parts=1):
        _, rows, columns = own.shape
        part = jax.ShapeDtypeStruct((rows // parts, columns), own.dtype)
        return call(send_kernel, self.label + "_send", (own, received), (part,) * parts)

    def slots(self, own, received, arrived):
        rows, columns = arrived.shape
        shape = lambda slots: jax.ShapeDtypeStruct((slots * rows // 4, columns), arrived.dtype)
        return call(
            slots_kernel,
            self.label + "_slots",
            (own, received, arrived),
            (shape(1), shape(2), shape(1)),
        )

    def slot(self, which, own, received, arrived, *others):
        return call(
            functools.partial(slot_kernel, which),
            self.label + "_slot",
            (own, received, arrived, *others),
            jax.ShapeDtypeStruct(arrived.shape, arrived.dtype),
        )


def load_kernel(*refs):
    sources, targets, sems = refs[:3], refs[3:6], refs[6]
    copies = [
        pltpu.make_async_copy(source, target, sems.at[i])
        for i, (source, target) in enumerate(zip(sources, targets))
    ]
    for copy in copies:
        copy.start()
    for copy in copies:
        copy.wait()


def load(*mats):
    return pl.pallas_call(
        load_kernel,
        out_shape=tuple(jax.ShapeDtypeStruct(mat.shape, mat.dtype) for mat in mats),
        in_specs=[pl.BlockSpec(memory_space=pltpu.HBM)] * len(mats),
        out_specs=(VMEM,) * len(mats),
        scratch_shapes=[pltpu.SemaphoreType.DMA((len(mats),))],
        compiler_params=pltpu.CompilerParams(vmem_limit_bytes=2**20),
        name="load",
    )(*(pltpu.with_memory_space_constraint(mat, pltpu.HBM) for mat in mats))


def space(clock, flops=36 * 10**9):
    return pl.pallas_call(
        lambda old, new: None,
        out_shape=jax.ShapeDtypeStruct(clock.shape, clock.dtype),
        in_specs=[pl.BlockSpec(memory_space=pl.ANY)],
        out_specs=pl.BlockSpec(memory_space=pl.ANY),
        input_output_aliases={0: 0},
        compiler_params=pltpu.CompilerParams(vmem_limit_bytes=2**20),
        cost_estimate=pl.CostEstimate(flops=flops, bytes_accessed=0, transcendentals=0),
        name="space",
    )(clock)


class Order:
    def __init__(self):
        self.token = None

    def __call__(self, function, *operands, also=()):
        if self.token is not None:
            operands, _ = lax.optimization_barrier((operands, (self.token, also)))
        result = function(*operands)
        self.token = result
        return result


def lined_up(tokens, expert_ids, pick_counts, gate_scores, gate_local, up_local, down_local, grad_out):
    experts = lax.axis_size("expert")
    width = gate_local.shape[0]
    picks = (expert_ids.T, pick_counts[None, :], gate_scores.T)
    rows, grads, outs, ins = (FourChips(label) for label in ("rows", "grads", "out", "in"))
    order = Order()
    hold = lambda value, *tokens: lax.optimization_barrier((value, tokens))[0]
    product_of = lambda name, by_hidden: lambda r, acts: weights(name, r, acts, width, by_hidden)

    own, pair, clock = order(lambda r: prepare_rows(*picks, r, experts), tokens)
    near = rows.line(own, rows.near)
    far = rows.line(own, rows.far)
    sibling_pair = rows.sibling(pair)
    gate_mat, up_mat, down_mat = order(load, gate_local, up_local, down_local)
    sibling_pair = hold(sibling_pair, down_mat)
    line_pair = order(pair_up, near, far, also=sibling_pair)
    across_pair = rows.across(line_pair)
    last = rows.line(hold(far, line_pair), rows.near)
    sibling_line = rows.sibling(line_pair)
    all_rows = [pair, line_pair]
    sibling_rows = [sibling_pair, sibling_line]
    own, pair = order(prepare_grads, grad_out)
    far = grads.line(own, grads.far)
    last_across = rows.across(last)
    near = grads.line(hold(own, last), grads.near)
    clock = order(space, clock, also=last)
    across_pair = hold(across_pair, clock)
    sibling_across = rows.sibling(across_pair)
    far = hold(far, across_pair)
    grads_last = grads.line(far, grads.near)
    clock = order(lambda c: space(c, 2 * 10**9), clock, also=far)
    line_pair = order(pair_up, near, far, also=sibling_across)
    sibling_pair, sibling_line = grads.sibling(pair), grads.sibling(line_pair)
    grads_across = grads.across(line_pair)
    last_pair = order(pair_up, last, last_across, also=line_pair)
    all_rows = all_rows + [across_pair, last_pair]
    all_rows = all_rows + sibling_rows + [sibling_across, rows.sibling(last_pair)]
    pre_gate, pre_up, gated = order(
        lambda *r: hidden_units(r, gate_mat, up_mat, experts), *all_rows
    )
    grads_last, grads_across = hold((grads_last, grads_across), gated)
    last_across = grads.across(grads_last)
    sibling_across = grads.sibling(grads_across)
    near_out, sent = order(
        outputs_of, gated, down_mat, also=(grads_across, sibling_pair, sibling_line)
    )
    received = outs.sibling(sent)
    last_pair = order(pair_up, grads_last, last_across)
    clock = order(space, clock, also=sibling_across)
    received = hold(received, clock)
    (sent,) = order(outs.send, near_out, received)
    arrived = outs.across(sent)
    all_grads = [pair, line_pair, grads_across, last_pair]
    all_grads = all_grads + [sibling_pair, sibling_line, sibling_across, grads.sibling(last_pair)]
    d_gate, d_up, shares = order(
        lambda g, r, *pre: hidden_grads(g, r, *pre, down_mat, experts),
        all_grads,
        all_rows,
        pre_gate,
        pre_up,
    )
    in_own, sent = order(
        lambda *d: input_grads_of(*d, gate_mat, up_mat), d_gate, d_up, shares
    )
    in_received = ins.sibling(sent)
    arrived = hold(arrived, in_own)
    own_slot, near_slots, far_slot = order(outs.slots, near_out, received, arrived)
    clock = order(space, clock)
    in_received = hold(in_received, clock)
    sent = order(lambda *s: ins.send(*s, parts=4), in_own, in_received)
    own_sent, near_sent, far_sent, last_sent = sent
    last_arrived = ins.across(last_sent)
    near_sums = outs.line(near_slots, outs.near)
    grad_down = order(product_of("grad_down", True), all_grads, gated)
    slot = order(lambda *s: ins.slot(3, *s), in_own, in_received, last_arrived)
    last_sum = ins.line(slot, ins.near)
    far_arrived = ins.across(hold(far_sent, slot))
    far_slot = order(
        lambda *s: call(add_last_kernel, "add_last", s, jax.ShapeDtypeStruct(s[0].shape, s[0].dtype)),
        far_slot,
        near_sums,
    )
    far_sum = outs.line(far_slot, outs.far)
    grad_gate = order(product_of("grad_gate", False), all_rows, d_gate)
    slot = order(lambda *s: ins.slot(2, *s), in_own, in_received, far_arrived, last_sum)
    far = ins.line(slot, ins.far)
    near_arrived = ins.across(hold(near_sent, slot))
    grad_up = order(product_of("grad_up", False), all_rows, d_up)
    slot = order(lambda *s: ins.slot(1, *s), in_own, in_received, near_arrived)
    near = ins.line(slot, ins.near)
    own_arrived = ins.across(hold(own_sent, slot))
    columns = jax.ShapeDtypeStruct((tokens.shape[0], width // 2), jnp.bfloat16)
    output_cols = order(
        lambda *sums: call(finish_outputs_kernel, "finish_outputs", sums, columns),
        own_slot,
        near_sums,
        far_sum,
    )
    clock = order(lambda c: space(c, 2 * 10**9), clock, also=far)
    near, own_arrived = hold((near, own_arrived), clock)
    input_cols, d_scores = order(
        lambda *sums: call(
            functools.partial(finish_inputs_kernel, experts),
            "finish_inputs",
            (*picks, clock, *sums),
            (columns, jax.ShapeDtypeStruct(picks[2].shape, jnp.float32)),
        ),
        in_own,
        in_received,
        own_arrived,
        far,
        near,
    )
    return output_cols, input_cols, d_scores.T, grad_gate[None], grad_up[None], grad_down[None]


def any_mesh(tokens, expert_ids, pick_counts, gate_scores, gate_local, up_local, down_local, grad_out):
    tok_rows = tokens.shape[0]
    pick_width = expert_ids.shape[1]
    experts = lax.axis_size("expert")
    active_mask = lax.broadcasted_iota(jnp.int32, (tok_rows, pick_width), 1) < pick_counts[:, None]
    active_float = active_mask.astype(jnp.float32)
    weighted = gate_scores * active_float
    score_sum = jnp.sum(weighted, axis=1, keepdims=True)
    gate_weights = weighted / score_sum
    picked = (expert_ids[:, :, None] == lax.broadcasted_iota(jnp.int32, (1, 1, experts), 2)).astype(
        jnp.float32
    )
    gate_table = jnp.sum(gate_weights[:, :, None] * picked, axis=1)

    def combine(partial):
        summed = lax.psum_scatter(partial, "expert", scatter_dimension=0, tiled=True)
        return lax.psum_scatter(summed, "helper", scatter_dimension=1, tiled=True)

    rows = lax.all_gather(tokens, "expert", tiled=True)
    tables = lax.all_gather(gate_table.T, "expert", tiled=False)
    gates = jnp.take(tables, lax.axis_index("expert"), axis=1).reshape(-1, 1)
    grads = lax.all_gather(grad_out, "expert", tiled=True)

    pre_gate = product(rows, gate_local)
    pre_up = product(rows, up_local)
    silu_value, silu_slope = silu_parts(pre_gate)
    hidden_act = silu_value * pre_up
    gated_act = (gates * hidden_act).astype(jnp.bfloat16)
    output_cols = combine(product(gated_act, down_local).astype(jnp.bfloat16))

    raw_act = right_transposed(grads, down_local)
    gate_part = jnp.sum(raw_act * hidden_act, axis=1)
    d_act = gates * raw_act
    d_pre_gate = (d_act * pre_up * silu_slope).astype(jnp.bfloat16)
    d_pre_up = (d_act * silu_value).astype(jnp.bfloat16)
    input_cols = combine(
        (right_transposed(d_pre_gate, gate_local) + right_transposed(d_pre_up, up_local)).astype(
            jnp.bfloat16
        )
    )

    gate_parts = lax.all_gather(
        gate_part.reshape(-1, tok_rows), ("expert", "helper"), tiled=False
    )
    own_parts = jnp.take(gate_parts, lax.axis_index("expert"), axis=1)
    by_expert = jnp.sum(own_parts.reshape(experts, -1, tok_rows), axis=1).T
    d_gates = jnp.sum(by_expert[:, None, :] * picked, axis=2)
    d_scores = (
        active_float
        * (d_gates - jnp.sum(gate_weights * d_gates, axis=1, keepdims=True))
        / score_sum
    )

    def over_dp(whole, dimension):
        return lax.psum_scatter(
            whole.astype(jnp.bfloat16), "dp", scatter_dimension=dimension, tiled=True
        )[None]

    grad_w_gate = over_dp(transposed_product(rows, d_pre_gate), 0)
    grad_w_up = over_dp(transposed_product(rows, d_pre_up), 0)
    grad_w_down = over_dp(transposed_product(gated_act, grads), 1)
    return output_cols, input_cols, d_scores, grad_w_gate, grad_w_up, grad_w_down


def on_device(tokens, expert_ids, pick_counts, gate_scores, w_gate, w_up, w_down, grad_out):
    sizes = tuple(lax.axis_size(axis) for axis in ("expert", "helper", "dp"))
    layer = lined_up if sizes == (8, 2, 1) else any_mesh
    return layer(
        tokens, expert_ids, pick_counts, gate_scores, w_gate[0], w_up[0], w_down[0], grad_out
    )


def solution(mesh):
    in_specs = (
        P(("groups", "expert", "dp"), None),
        P(("groups", "expert", "dp"), None),
        P(("groups", "expert", "dp")),
        P(("groups", "expert", "dp"), None),
        P("expert", None, "helper"),
        P("expert", None, "helper"),
        P("expert", "helper", None),
        P(("groups", "expert", "dp"), None),
    )
    out_specs = (
        P(("groups", "expert", "dp"), "helper"),
        P(("groups", "expert", "dp"), "helper"),
        P(("groups", "expert", "dp"), None),
        P(("groups", "expert"), "dp", "helper"),
        P(("groups", "expert"), "dp", "helper"),
        P(("groups", "expert"), "helper", "dp"),
    )
    return jax.shard_map(
        on_device, mesh=mesh, in_specs=in_specs, out_specs=out_specs, check_vma=False
    )
```

```python
import functools

import jax
import jax.numpy as jnp
from jax import lax
from jax.experimental import pallas as pl
from jax.experimental.pallas import tpu as pltpu
from jax.sharding import PartitionSpec as P

LANES = 128
VMEM = pl.BlockSpec(memory_space=pltpu.VMEM)


def product(first_mat, second_mat):
    return jnp.dot(first_mat, second_mat, preferred_element_type=jnp.float32)


def transposed_product(first_mat, second_mat):
    return lax.dot_general(
        first_mat, second_mat, (((0,), (0,)), ((), ())), preferred_element_type=jnp.float32
    )


def right_transposed(first_mat, second_mat):
    return lax.dot_general(
        first_mat, second_mat, (((1,), (1,)), ((), ())), preferred_element_type=jnp.float32
    )


def silu_parts(argument):
    sigmoid_part = jax.nn.sigmoid(argument)
    return argument * sigmoid_part, sigmoid_part * (1.0 + argument * (1.0 - sigmoid_part))


def total_of(terms):
    return functools.reduce(jnp.add, terms)


def call(kernel, name, operands, out_shape, scratch=(), flops=0, moved=0, mebibytes=12):
    return pl.pallas_call(
        kernel,
        out_shape=out_shape,
        in_specs=[VMEM] * len(operands),
        out_specs=jax.tree.map(lambda _: VMEM, out_shape),
        scratch_shapes=scratch,
        compiler_params=pltpu.CompilerParams(vmem_limit_bytes=mebibytes * 2**20),
        cost_estimate=pl.CostEstimate(
            flops=flops, bytes_accessed=moved, transcendentals=0
        ),
        name=name,
    )(*operands)


def half_at(array, which):
    rows = array.shape[0] // 2
    return array[which * rows : (which + 1) * rows]


def swap_halves(array):
    return jnp.concatenate([half_at(array, 1), half_at(array, 0)], axis=0)


def hi_lo(values, is_high):
    high = values.astype(jnp.bfloat16).astype(jnp.float32)
    return jnp.where(is_high, high, values - high).astype(jnp.bfloat16)


def gate_rows(counts, scores):
    used = [(counts > k).astype(jnp.float32) for k in range(scores.shape[0])]
    weighted = [scores[k : k + 1] * used[k] for k in range(scores.shape[0])]
    score_sum = total_of(weighted)
    return [w / score_sum for w in weighted], used, score_sum


def prepare_rows_kernel(experts, *refs):
    sources, (own, pair, clock), targets, sems = refs[:4], refs[4:7], refs[7:11], refs[11]
    ids, counts, scores, rows = targets
    copies = [
        pltpu.make_async_copy(source, target, sems.at[i])
        for i, (source, target) in enumerate(zip(sources, targets))
    ]
    for copy in copies:
        copy.start()
    for copy in copies:
        copy.wait()
    total, width = rows.shape
    clock[...] = jnp.zeros_like(clock)
    lane = lax.broadcasted_iota(jnp.int32, (LANES, total), 0)
    gates, _, _ = gate_rows(counts[...], scores[...])
    table = jnp.zeros((LANES, total), jnp.float32)
    for k, gate in enumerate(gates):
        named = ids[k : k + 1, :]
        table = table + jnp.where((lane == named) | (lane == named + experts), gate, 0.0)
    table = table.T
    table = hi_lo(table, lax.broadcasted_iota(jnp.int32, table.shape, 1) < experts)
    for side in range(2):

        @pl.when(lax.axis_index("helper") == side)
        def _(side=side):
            own[:, :width] = half_at(rows, side)
            own[:, width:] = half_at(table, side)
            for i, which in enumerate((side, 1 - side)):
                here = slice(i * total // 2, (i + 1) * total // 2)
                pair[here, :width] = half_at(rows, which)
                pair[here, width:] = half_at(table, which)


def prepare_rows(ids, counts, scores, rows, experts):
    total, width = rows.shape
    piece = jax.ShapeDtypeStruct((total // 2, width + LANES), jnp.bfloat16)
    operands = (ids, counts, scores, rows)
    return pl.pallas_call(
        functools.partial(prepare_rows_kernel, experts),
        out_shape=(
            piece,
            jax.ShapeDtypeStruct((total, width + LANES), jnp.bfloat16),
            jax.ShapeDtypeStruct((8, LANES), jnp.float32),
        ),
        in_specs=[pl.BlockSpec(memory_space=pltpu.HBM)] * len(operands),
        out_specs=(VMEM,) * 3,
        scratch_shapes=[
            *(pltpu.VMEM(operand.shape, operand.dtype) for operand in operands),
            pltpu.SemaphoreType.DMA((len(operands),)),
        ],
        compiler_params=pltpu.CompilerParams(vmem_limit_bytes=8 * 2**20),
        name="prepare_rows",
    )(*(pltpu.with_memory_space_constraint(operand, pltpu.HBM) for operand in operands))


def prepare_grads_kernel(rows, own, pair):
    half = rows.shape[0] // 2
    for side in range(2):

        @pl.when(lax.axis_index("helper") == side)
        def _(side=side):
            own[...] = half_at(rows, side)
            pair[:half, :] = half_at(rows, side)
            pair[half:, :] = half_at(rows, 1 - side)


def prepare_grads(rows):
    total, width = rows.shape
    piece = jax.ShapeDtypeStruct((total // 2, width), jnp.bfloat16)
    return call(
        prepare_grads_kernel,
        "prepare_grads",
        (rows,),
        (piece, jax.ShapeDtypeStruct(rows.shape, jnp.bfloat16)),
    )


def join_kernel(*refs):
    at = 0
    for piece in refs[:-1]:
        refs[-1][at : at + piece.shape[0], :] = piece[...]
        at = at + piece.shape[0]


def join(*pieces):
    total = sum(piece.shape[0] for piece in pieces)
    shape = jax.ShapeDtypeStruct((total, pieces[0].shape[1]), pieces[0].dtype)
    return call(join_kernel, "join", pieces, shape)


def parts_of(pair, rest):
    rows = pair.shape[0]
    half = rows // 2
    parts = [(pair, 0, rows)]
    for slot in range(2):
        parts = parts + [(rest, slot * half, half), (rest, rows + slot * half, half)]
    return parts + [(rest, 2 * rows, rows)]


def lay_out(pieces, target, columns):
    at = 0
    for piece, start, rows in parts_of(*pieces[:2]) + parts_of(*pieces[2:]):
        target[at : at + rows, :] = piece[start : start + rows, columns]
        at = at + rows


def gate_column(experts, pieces, width):
    parts = parts_of(*pieces[:2]) + parts_of(*pieces[2:])
    table = jnp.concatenate(
        [piece[start : start + rows, width:] for piece, start, rows in parts], axis=0
    )
    lane = lax.broadcasted_iota(jnp.int32, table.shape, 1)
    expert = lax.axis_index("expert")
    mine = (lane == expert) | (lane == expert + experts)
    return jnp.sum(jnp.where(mine, table.astype(jnp.float32), 0.0), axis=1, keepdims=True)


def hidden_kernel(experts, tile, *refs):
    pieces, refs = refs[:4], refs[4:]
    gate_mat, up_mat, pre_gate, pre_up, gated, rows = refs
    width = rows.shape[1]
    lay_out(pieces, rows, slice(0, width))
    gate = gate_column(experts, pieces, width)
    for start in range(0, gated.shape[1], tile):
        columns = slice(start, start + tile)
        gate_part = product(rows[...], gate_mat[:, columns])
        up_part = product(rows[...], up_mat[:, columns])
        silu_value, _ = silu_parts(gate_part)
        pre_gate[:, columns] = gate_part
        pre_up[:, columns] = up_part
        gated[:, columns] = (gate * silu_value * up_part).astype(jnp.bfloat16)


def hidden_units(pieces, gate_mat, up_mat, experts):
    width, hidden = gate_mat.shape
    total = 8 * pieces[0].shape[0]
    pre = jax.ShapeDtypeStruct((total, hidden), jnp.float32)
    act = jax.ShapeDtypeStruct((total, hidden), jnp.bfloat16)
    return call(
        functools.partial(hidden_kernel, experts, 256),
        "hidden_units",
        (*pieces, gate_mat, up_mat),
        (pre, pre, act),
        [pltpu.VMEM((total, width), jnp.bfloat16)],
        flops=4 * total * width * hidden,
        mebibytes=12,
    )


def outputs_kernel(tile, gated, down_mat, own, other):
    half = own.shape[2]
    for which in range(2):
        stays = (lax.axis_index("helper") == which).astype(jnp.int32)
        for start in range(0, half, tile):
            columns = slice(start, start + tile)
            first = which * half + start
            out = product(gated[...], down_mat[:, first : first + tile]).astype(jnp.bfloat16)
            own[stays, :, columns] = half_at(out, 0)
            other[stays, :, columns] = half_at(out, 1)


def outputs_of(gated, down_mat):
    total, hidden = gated.shape
    width = down_mat.shape[1]
    sums = jax.ShapeDtypeStruct((2, total // 2, width // 2), jnp.bfloat16)
    return call(
        functools.partial(outputs_kernel, 256),
        "outputs",
        (gated, down_mat),
        (sums, sums),
        flops=2 * total * width * hidden,
    )


def hidden_grads_kernel(experts, tile, *refs):
    pieces, gate_pieces, refs = refs[:4], refs[4:8], refs[8:]
    down_mat, pre_gate, pre_up, d_gate, d_up, shares_out, grads = refs
    total, width = grads.shape
    lay_out(pieces, grads, slice(0, width))
    gate = gate_column(experts, gate_pieces, width)
    shares = []
    for start in range(0, d_gate.shape[1], tile):
        columns = slice(start, start + tile)
        raw = right_transposed(grads[...], down_mat[columns, :])
        up_part = pre_up[:, columns]
        silu_value, silu_slope = silu_parts(pre_gate[:, columns])
        share = raw * silu_value * up_part
        shares = shares + [share[:, c : c + LANES] for c in range(0, tile, LANES)]
        d_act = gate * raw
        d_gate[:, columns] = (d_act * up_part * silu_slope).astype(jnp.bfloat16)
        d_up[:, columns] = (d_act * silu_value).astype(jnp.bfloat16)
    value = jnp.sum(total_of(shares), axis=1, keepdims=True)
    lane = lax.broadcasted_iota(jnp.int32, (total, LANES), 1)
    high = 2 * lax.axis_index("expert") + lax.axis_index("helper")
    value = jnp.where((lane == high) | (lane == high + 2 * experts), value, 0.0)
    shares_out[...] = hi_lo(value, lane < 2 * experts)


def hidden_grads(pieces, gate_pieces, pre_gate, pre_up, down_mat, experts):
    hidden, width = down_mat.shape
    total = pre_gate.shape[0]
    act = jax.ShapeDtypeStruct((total, hidden), jnp.bfloat16)
    return call(
        functools.partial(hidden_grads_kernel, experts, 256),
        "hidden_grads",
        (*pieces, *gate_pieces, down_mat, pre_gate, pre_up),
        (act, act, jax.ShapeDtypeStruct((total, LANES), jnp.bfloat16)),
        [pltpu.VMEM((total, width), jnp.bfloat16)],
        flops=2 * total * width * hidden,
        mebibytes=12,
    )


def input_grads_kernel(tile, d_gate, d_up, shares, gate_mat, up_mat, own, other):
    half = own.shape[2] - LANES
    for which in range(2):
        own[which, :, half:] = half_at(shares, 0)
        other[which, :, half:] = half_at(shares, 1)
    for which in range(2):
        stays = (lax.axis_index("helper") == which).astype(jnp.int32)
        for start in range(0, half, tile):
            columns = slice(start, start + tile)
            first = which * half + start
            back = right_transposed(d_gate[...], gate_mat[first : first + tile, :])
            back = back + right_transposed(d_up[...], up_mat[first : first + tile, :])
            back = back.astype(jnp.bfloat16)
            own[stays, :, columns] = half_at(back, 0)
            other[stays, :, columns] = half_at(back, 1)


def input_grads_of(d_gate, d_up, shares, gate_mat, up_mat):
    width, hidden = gate_mat.shape
    total = d_gate.shape[0]
    sums = jax.ShapeDtypeStruct((2, total // 2, width // 2 + LANES), jnp.bfloat16)
    return call(
        functools.partial(input_grads_kernel, 256),
        "input_grads",
        (d_gate, d_up, shares, gate_mat, up_mat),
        (sums, sums),
        flops=0,
        mebibytes=12,
    )


def weights_kernel(width, tile, *refs):
    pieces, (acts, grad, rows) = refs[:4], refs[4:]
    lay_out(pieces, rows, slice(0, width))
    left, right = (acts, rows) if grad.shape[1] == width else (rows, acts)
    for start in range(0, grad.shape[0], tile):
        columns = slice(start, start + tile)
        grad[columns, :] = transposed_product(left[:, columns], right[...]).astype(jnp.bfloat16)


def weights(name, pieces, acts, width, by_hidden):
    rows, hidden = acts.shape
    shape = (hidden, width) if by_hidden else (width, hidden)
    return call(
        functools.partial(weights_kernel, width, 256),
        name,
        (*pieces, acts),
        jax.ShapeDtypeStruct(shape, jnp.bfloat16),
        [pltpu.VMEM((rows, width), jnp.bfloat16)],
        flops=2 * rows * width * hidden,
    )


def send_kernel(own, received, *sent):
    rows = sent[0].shape[0]
    for i, target in enumerate(sent):
        here = slice(i * rows, (i + 1) * rows)
        target[...] = own[0, here, :] + received[0, here, :]


def slot_sum(own, received, arrived, slot, offset):
    rows = LANES
    half = rows // 2
    here = slice(slot * rows, (slot + 1) * rows)
    other = arrived[offset : offset + rows, :].astype(jnp.float32)
    kept = own[1, here, :].astype(jnp.float32) + received[1, here, :].astype(jnp.float32)
    return kept + jnp.concatenate([other[half:], other[:half]], axis=0)


def slots_kernel(own, received, arrived, own_slot, near_and_last, far_slot):
    rows = own_slot.shape[0]
    targets = (own_slot, near_and_last.at[:rows], far_slot, near_and_last.at[rows:])
    for slot, target in enumerate(targets):
        target[...] = slot_sum(own, received, arrived, slot, slot * rows).astype(target.dtype)


def add_last_kernel(far_slot, arrived, total):
    rows = far_slot.shape[0]
    total[...] = far_slot[...] + arrived[rows:, :]


def slot_kernel(slot, own, received, arrived, *refs):
    whole = slot_sum(own, received, arrived, slot, 0)
    if len(refs) > 1:
        whole = whole + refs[0][...].astype(jnp.float32)
    refs[-1][...] = whole.astype(refs[-1].dtype)


def finish_outputs_kernel(own, near_and_last, far, columns):
    near = near_and_last[: own.shape[0], :]
    whole = total_of([term.astype(jnp.float32) for term in (own[...], near, far[...])])
    whole = jnp.where(lax.axis_index("helper") == 0, whole, swap_halves(whole))
    columns[...] = whole.astype(jnp.bfloat16)


def finish_inputs_kernel(experts, ids, counts, scores, clock, own, received, arrived, *refs):
    columns, d_scores = refs[-2:]
    width = columns.shape[1]
    whole = slot_sum(own, received, arrived, 0, 0)
    whole = total_of([whole] + [ref[...].astype(jnp.float32) for ref in refs[:-2]])
    whole = jnp.where(lax.axis_index("helper") == 0, whole, swap_halves(whole))
    columns[...] = whole[:, :width].astype(jnp.bfloat16)
    table = whole[:, width:].T
    lane = lax.broadcasted_iota(jnp.int32, table.shape, 0)
    named_by = (lane % (2 * experts)) // 2
    gates, used, score_sum = gate_rows(counts[...], scores[...])
    d_gates = []
    for k in range(len(gates)):
        hit = (named_by == ids[k : k + 1, :]) & (lane < 4 * experts)
        d_gates.append(jnp.sum(jnp.where(hit, table, 0.0), axis=0, keepdims=True))
    mean = total_of([gate * d_gate for gate, d_gate in zip(gates, d_gates)])
    for k, d_gate in enumerate(d_gates):
        d_scores[k : k + 1, :] = used[k] * (d_gate - mean) / score_sum


class FourChips:
    def __init__(self, label):
        self.label = label
        both = lambda pairs: [(2 * a + c, 2 * b + c) for a, b in pairs for c in (0, 1)]
        self.near = both([(z, z ^ 1) for z in range(4)])
        self.far = both([(z, z ^ 2) for z in range(4)])
        self.cores = [(i, i ^ 1) for i in range(8)]
        self.sides = [(0, 1), (1, 0)]

    def line(self, array, pairs):
        with jax.named_scope(self.label + "_line"):
            return lax.ppermute(array, "expert", pairs)

    def sibling(self, array):
        with jax.named_scope(self.label + "_cores"):
            return lax.ppermute(array, "expert", self.cores)

    def across(self, array):
        with jax.named_scope(self.label + "_across"):
            return lax.ppermute(array, "helper", self.sides)

    def send(self, own, received, parts=1):
        _, rows, columns = own.shape
        part = jax.ShapeDtypeStruct((rows // parts, columns), own.dtype)
        return call(send_kernel, self.label + "_send", (own, received), (part,) * parts)

    def slots(self, own, received, arrived):
        rows, columns = arrived.shape
        shape = lambda slots: jax.ShapeDtypeStruct((slots * rows // 4, columns), arrived.dtype)
        return call(
            slots_kernel,
            self.label + "_slots",
            (own, received, arrived),
            (shape(1), shape(2), shape(1)),
        )

    def slot(self, which, own, received, arrived, *others):
        return call(
            functools.partial(slot_kernel, which),
            self.label + "_slot",
            (own, received, arrived, *others),
            jax.ShapeDtypeStruct(arrived.shape, arrived.dtype),
        )


def load_kernel(*refs):
    sources, targets, sems = refs[:3], refs[3:6], refs[6]
    copies = [
        pltpu.make_async_copy(source, target, sems.at[i])
        for i, (source, target) in enumerate(zip(sources, targets))
    ]
    for copy in copies:
        copy.start()
    for copy in copies:
        copy.wait()


def load(*mats):
    return pl.pallas_call(
        load_kernel,
        out_shape=tuple(jax.ShapeDtypeStruct(mat.shape, mat.dtype) for mat in mats),
        in_specs=[pl.BlockSpec(memory_space=pltpu.HBM)] * len(mats),
        out_specs=(VMEM,) * len(mats),
        scratch_shapes=[pltpu.SemaphoreType.DMA((len(mats),))],
        compiler_params=pltpu.CompilerParams(vmem_limit_bytes=2**20),
        name="load",
    )(*(pltpu.with_memory_space_constraint(mat, pltpu.HBM) for mat in mats))


def space(clock, flops=36 * 10**9):
    return pl.pallas_call(
        lambda old, new: None,
        out_shape=jax.ShapeDtypeStruct(clock.shape, clock.dtype),
        in_specs=[pl.BlockSpec(memory_space=pl.ANY)],
        out_specs=pl.BlockSpec(memory_space=pl.ANY),
        input_output_aliases={0: 0},
        compiler_params=pltpu.CompilerParams(vmem_limit_bytes=2**20),
        cost_estimate=pl.CostEstimate(flops=flops, bytes_accessed=0, transcendentals=0),
        name="space",
    )(clock)


class Order:
    def __init__(self):
        self.token = None

    def __call__(self, function, *operands, also=()):
        if self.token is not None:
            operands, _ = lax.optimization_barrier((operands, (self.token, also)))
        result = function(*operands)
        self.token = result
        return result


def lined_up(tokens, expert_ids, pick_counts, gate_scores, gate_local, up_local, down_local, grad_out):
    experts = lax.axis_size("expert")
    width = gate_local.shape[0]
    picks = (expert_ids.T, pick_counts[None, :], gate_scores.T)
    rows, grads, outs, ins = (FourChips(label) for label in ("rows", "grads", "out", "in"))
    order = Order()
    hold = lambda value, *tokens: lax.optimization_barrier((value, tokens))[0]
    product_of = lambda name, by_hidden: lambda r, acts: weights(name, r, acts, width, by_hidden)

    own, pair, clock = order(lambda r: prepare_rows(*picks, r, experts), tokens)
    near = rows.line(own, rows.near)
    far = rows.line(own, rows.far)
    sibling_pair = rows.sibling(pair)
    gate_mat, up_mat, down_mat = order(load, gate_local, up_local, down_local)
    sibling_pair = hold(sibling_pair, down_mat)
    line_pair = order(join, near, far, also=sibling_pair)
    last = rows.line(hold(far, line_pair), rows.near)
    across_pair = rows.across(line_pair)
    own, grads_pair = order(prepare_grads, grad_out)
    far = grads.line(own, grads.far)
    last_across = rows.across(last)
    near = grads.line(hold(own, last), grads.near)
    far = hold(far, last)
    grads_last = grads.line(far, grads.near)
    clock = order(lambda c: space(c, 2 * 10**9), clock, also=far)
    grads_line = order(join, near, far)
    grads_across = grads.across(grads_line)
    grads_sibling = grads.sibling(grads_pair)
    rest = order(join, line_pair, across_pair, last, last_across)
    all_rows = [pair, rest, sibling_pair, rows.sibling(rest)]
    pre_gate, pre_up, gated = order(
        lambda *r: hidden_units(r, gate_mat, up_mat, experts), *all_rows
    )
    grads_last = hold(grads_last, gated)
    last_across = grads.across(grads_last)
    near_out, sent = order(outputs_of, gated, down_mat, also=(grads_last, grads_sibling))
    received = outs.sibling(sent)
    clock = order(space, clock, also=(grads_across, last_across))
    received = hold(received, clock)
    (sent,) = order(outs.send, near_out, received)
    arrived = outs.across(sent)
    rest = order(join, grads_line, grads_across, grads_last, last_across)
    all_grads = [grads_pair, rest, grads_sibling, grads.sibling(rest)]
    d_gate, d_up, shares = order(
        lambda g, r, *pre: hidden_grads(g, r, *pre, down_mat, experts),
        all_grads,
        all_rows,
        pre_gate,
        pre_up,
    )
    in_own, sent = order(
        lambda *d: input_grads_of(*d, gate_mat, up_mat), d_gate, d_up, shares
    )
    in_received = ins.sibling(sent)
    arrived = hold(arrived, in_own)
    own_slot, near_slots, far_slot = order(outs.slots, near_out, received, arrived)
    clock = order(space, clock)
    in_received = hold(in_received, clock)
    sent = order(lambda *s: ins.send(*s, parts=4), in_own, in_received)
    own_sent, near_sent, far_sent, last_sent = sent
    last_arrived = ins.across(last_sent)
    near_sums = outs.line(near_slots, outs.near)
    grad_down = order(product_of("grad_down", True), all_grads, gated)
    slot = order(lambda *s: ins.slot(3, *s), in_own, in_received, last_arrived)
    last_sum = ins.line(slot, ins.near)
    far_arrived = ins.across(hold(far_sent, slot))
    grad_gate = order(product_of("grad_gate", False), all_rows, d_gate)
    far_slot = order(
        lambda *s: call(add_last_kernel, "add_last", s, jax.ShapeDtypeStruct(s[0].shape, s[0].dtype)),
        far_slot,
        near_sums,
    )
    far_sum = outs.line(far_slot, outs.far)
    slot = order(lambda *s: ins.slot(2, *s), in_own, in_received, far_arrived, last_sum)
    far = ins.line(slot, ins.far)
    near_arrived = ins.across(hold(near_sent, slot))
    grad_up = order(product_of("grad_up", False), all_rows, d_up)
    slot = order(lambda *s: ins.slot(1, *s), in_own, in_received, near_arrived)
    near = ins.line(slot, ins.near)
    own_arrived = ins.across(hold(own_sent, slot))
    columns = jax.ShapeDtypeStruct((tokens.shape[0], width // 2), jnp.bfloat16)
    output_cols = order(
        lambda *sums: call(finish_outputs_kernel, "finish_outputs", sums, columns),
        own_slot,
        near_sums,
        far_sum,
    )
    clock = order(lambda c: space(c, 2 * 10**9), clock, also=far)
    near, own_arrived = hold((near, own_arrived), clock)
    input_cols, d_scores = order(
        lambda *sums: call(
            functools.partial(finish_inputs_kernel, experts),
            "finish_inputs",
            (*picks, clock, *sums),
            (columns, jax.ShapeDtypeStruct(picks[2].shape, jnp.float32)),
        ),
        in_own,
        in_received,
        own_arrived,
        far,
        near,
    )
    return output_cols, input_cols, d_scores.T, grad_gate[None], grad_up[None], grad_down[None]


def any_mesh(tokens, expert_ids, pick_counts, gate_scores, gate_local, up_local, down_local, grad_out):
    tok_rows = tokens.shape[0]
    pick_width = expert_ids.shape[1]
    experts = lax.axis_size("expert")
    active_mask = lax.broadcasted_iota(jnp.int32, (tok_rows, pick_width), 1) < pick_counts[:, None]
    active_float = active_mask.astype(jnp.float32)
    weighted = gate_scores * active_float
    score_sum = jnp.sum(weighted, axis=1, keepdims=True)
    gate_weights = weighted / score_sum
    picked = (expert_ids[:, :, None] == lax.broadcasted_iota(jnp.int32, (1, 1, experts), 2)).astype(
        jnp.float32
    )
    gate_table = jnp.sum(gate_weights[:, :, None] * picked, axis=1)

    def combine(partial):
        summed = lax.psum_scatter(partial, "expert", scatter_dimension=0, tiled=True)
        return lax.psum_scatter(summed, "helper", scatter_dimension=1, tiled=True)

    rows = lax.all_gather(tokens, "expert", tiled=True)
    tables = lax.all_gather(gate_table.T, "expert", tiled=False)
    gates = jnp.take(tables, lax.axis_index("expert"), axis=1).reshape(-1, 1)
    grads = lax.all_gather(grad_out, "expert", tiled=True)

    pre_gate = product(rows, gate_local)
    pre_up = product(rows, up_local)
    silu_value, silu_slope = silu_parts(pre_gate)
    hidden_act = silu_value * pre_up
    gated_act = (gates * hidden_act).astype(jnp.bfloat16)
    output_cols = combine(product(gated_act, down_local).astype(jnp.bfloat16))

    raw_act = right_transposed(grads, down_local)
    gate_part = jnp.sum(raw_act * hidden_act, axis=1)
    d_act = gates * raw_act
    d_pre_gate = (d_act * pre_up * silu_slope).astype(jnp.bfloat16)
    d_pre_up = (d_act * silu_value).astype(jnp.bfloat16)
    input_cols = combine(
        (right_transposed(d_pre_gate, gate_local) + right_transposed(d_pre_up, up_local)).astype(
            jnp.bfloat16
        )
    )

    gate_parts = lax.all_gather(
        gate_part.reshape(-1, tok_rows), ("expert", "helper"), tiled=False
    )
    own_parts = jnp.take(gate_parts, lax.axis_index("expert"), axis=1)
    by_expert = jnp.sum(own_parts.reshape(experts, -1, tok_rows), axis=1).T
    d_gates = jnp.sum(by_expert[:, None, :] * picked, axis=2)
    d_scores = (
        active_float
        * (d_gates - jnp.sum(gate_weights * d_gates, axis=1, keepdims=True))
        / score_sum
    )

    def over_dp(whole, dimension):
        return lax.psum_scatter(
            whole.astype(jnp.bfloat16), "dp", scatter_dimension=dimension, tiled=True
        )[None]

    grad_w_gate = over_dp(transposed_product(rows, d_pre_gate), 0)
    grad_w_up = over_dp(transposed_product(rows, d_pre_up), 0)
    grad_w_down = over_dp(transposed_product(gated_act, grads), 1)
    return output_cols, input_cols, d_scores, grad_w_gate, grad_w_up, grad_w_down


def on_device(tokens, expert_ids, pick_counts, gate_scores, w_gate, w_up, w_down, grad_out):
    sizes = tuple(lax.axis_size(axis) for axis in ("expert", "helper", "dp"))
    layer = lined_up if sizes == (8, 2, 1) else any_mesh
    return layer(
        tokens, expert_ids, pick_counts, gate_scores, w_gate[0], w_up[0], w_down[0], grad_out
    )


def solution(mesh):
    in_specs = (
        P(("groups", "expert", "dp"), None),
        P(("groups", "expert", "dp"), None),
        P(("groups", "expert", "dp")),
        P(("groups", "expert", "dp"), None),
        P("expert", None, "helper"),
        P("expert", None, "helper"),
        P("expert", "helper", None),
        P(("groups", "expert", "dp"), None),
    )
    out_specs = (
        P(("groups", "expert", "dp"), "helper"),
        P(("groups", "expert", "dp"), "helper"),
        P(("groups", "expert", "dp"), None),
        P(("groups", "expert"), "dp", "helper"),
        P(("groups", "expert"), "dp", "helper"),
        P(("groups", "expert"), "helper", "dp"),
    )
    return jax.shard_map(
        on_device, mesh=mesh, in_specs=in_specs, out_specs=out_specs, check_vma=False
    )
```

```python
import functools

import jax
import jax.numpy as jnp
from jax import lax
from jax.experimental import pallas as pl
from jax.experimental.pallas import tpu as pltpu
from jax.sharding import PartitionSpec as P

LANES = 128
VMEM = pl.BlockSpec(memory_space=pltpu.VMEM)


def product(first_mat, second_mat):
    return jnp.dot(first_mat, second_mat, preferred_element_type=jnp.float32)


def transposed_product(first_mat, second_mat):
    return lax.dot_general(
        first_mat, second_mat, (((0,), (0,)), ((), ())), preferred_element_type=jnp.float32
    )


def right_transposed(first_mat, second_mat):
    return lax.dot_general(
        first_mat, second_mat, (((1,), (1,)), ((), ())), preferred_element_type=jnp.float32
    )


def silu_parts(argument):
    sigmoid_part = jax.nn.sigmoid(argument)
    return argument * sigmoid_part, sigmoid_part * (1.0 + argument * (1.0 - sigmoid_part))


def total_of(terms):
    return functools.reduce(jnp.add, terms)


def call(kernel, name, operands, out_shape, scratch=(), flops=0, moved=0, mebibytes=12):
    return pl.pallas_call(
        kernel,
        out_shape=out_shape,
        in_specs=[VMEM] * len(operands),
        out_specs=jax.tree.map(lambda _: VMEM, out_shape),
        scratch_shapes=scratch,
        compiler_params=pltpu.CompilerParams(vmem_limit_bytes=mebibytes * 2**20),
        cost_estimate=pl.CostEstimate(
            flops=flops, bytes_accessed=moved, transcendentals=0
        ),
        name=name,
    )(*operands)


def half_at(array, which):
    rows = array.shape[0] // 2
    return array[which * rows : (which + 1) * rows]


def swap_halves(array):
    return jnp.concatenate([half_at(array, 1), half_at(array, 0)], axis=0)


def hi_lo(values, is_high):
    high = values.astype(jnp.bfloat16).astype(jnp.float32)
    return jnp.where(is_high, high, values - high).astype(jnp.bfloat16)


def gate_rows(counts, scores):
    used = [(counts > k).astype(jnp.float32) for k in range(scores.shape[0])]
    weighted = [scores[k : k + 1] * used[k] for k in range(scores.shape[0])]
    score_sum = total_of(weighted)
    return [w / score_sum for w in weighted], used, score_sum


def prepare_rows_kernel(experts, *refs):
    sources, (own, pair, clock), targets, sems = refs[:4], refs[4:7], refs[7:11], refs[11]
    ids, counts, scores, rows = targets
    copies = [
        pltpu.make_async_copy(source, target, sems.at[i])
        for i, (source, target) in enumerate(zip(sources, targets))
    ]
    for copy in copies:
        copy.start()
    for copy in copies:
        copy.wait()
    total, width = rows.shape
    clock[...] = jnp.zeros_like(clock)
    lane = lax.broadcasted_iota(jnp.int32, (LANES, total), 0)
    gates, _, _ = gate_rows(counts[...], scores[...])
    table = jnp.zeros((LANES, total), jnp.float32)
    for k, gate in enumerate(gates):
        named = ids[k : k + 1, :]
        table = table + jnp.where((lane == named) | (lane == named + experts), gate, 0.0)
    table = table.T
    table = hi_lo(table, lax.broadcasted_iota(jnp.int32, table.shape, 1) < experts)
    for side in range(2):

        @pl.when(lax.axis_index("helper") == side)
        def _(side=side):
            own[:, :width] = half_at(rows, side)
            own[:, width:] = half_at(table, side)
            for i, which in enumerate((side, 1 - side)):
                here = slice(i * total // 2, (i + 1) * total // 2)
                pair[here, :width] = half_at(rows, which)
                pair[here, width:] = half_at(table, which)


def prepare_rows(ids, counts, scores, rows, experts):
    total, width = rows.shape
    piece = jax.ShapeDtypeStruct((total // 2, width + LANES), jnp.bfloat16)
    operands = (ids, counts, scores, rows)
    return pl.pallas_call(
        functools.partial(prepare_rows_kernel, experts),
        out_shape=(
            piece,
            jax.ShapeDtypeStruct((total, width + LANES), jnp.bfloat16),
            jax.ShapeDtypeStruct((8, LANES), jnp.float32),
        ),
        in_specs=[pl.BlockSpec(memory_space=pltpu.HBM)] * len(operands),
        out_specs=(VMEM,) * 3,
        scratch_shapes=[
            *(pltpu.VMEM(operand.shape, operand.dtype) for operand in operands),
            pltpu.SemaphoreType.DMA((len(operands),)),
        ],
        compiler_params=pltpu.CompilerParams(vmem_limit_bytes=8 * 2**20),
        name="prepare_rows",
    )(*(pltpu.with_memory_space_constraint(operand, pltpu.HBM) for operand in operands))


def prepare_grads_kernel(rows, own, pair):
    half = rows.shape[0] // 2
    for side in range(2):

        @pl.when(lax.axis_index("helper") == side)
        def _(side=side):
            own[...] = half_at(rows, side)
            pair[:half, :] = half_at(rows, side)
            pair[half:, :] = half_at(rows, 1 - side)


def prepare_grads(rows):
    total, width = rows.shape
    piece = jax.ShapeDtypeStruct((total // 2, width), jnp.bfloat16)
    return call(
        prepare_grads_kernel,
        "prepare_grads",
        (rows,),
        (piece, jax.ShapeDtypeStruct(rows.shape, jnp.bfloat16)),
    )


def join_kernel(*refs):
    at = 0
    for piece in refs[:-1]:
        refs[-1][at : at + piece.shape[0], :] = piece[...]
        at = at + piece.shape[0]


def join(*pieces):
    total = sum(piece.shape[0] for piece in pieces)
    shape = jax.ShapeDtypeStruct((total, pieces[0].shape[1]), pieces[0].dtype)
    return call(join_kernel, "join", pieces, shape)


def parts_of(pair, rest):
    rows = pair.shape[0]
    half = rows // 2
    parts = [(pair, 0, rows)]
    for slot in range(2):
        parts = parts + [(rest, slot * half, half), (rest, rows + slot * half, half)]
    return parts + [(rest, 2 * rows, rows)]


def lay_out(pieces, target, columns):
    at = 0
    for piece, start, rows in parts_of(*pieces[:2]) + parts_of(*pieces[2:]):
        target[at : at + rows, :] = piece[start : start + rows, columns]
        at = at + rows


def gate_column(experts, pieces, width):
    parts = parts_of(*pieces[:2]) + parts_of(*pieces[2:])
    table = jnp.concatenate(
        [piece[start : start + rows, width:] for piece, start, rows in parts], axis=0
    )
    lane = lax.broadcasted_iota(jnp.int32, table.shape, 1)
    expert = lax.axis_index("expert")
    mine = (lane == expert) | (lane == expert + experts)
    return jnp.sum(jnp.where(mine, table.astype(jnp.float32), 0.0), axis=1, keepdims=True)


def hidden_kernel(experts, tile, *refs):
    pieces, refs = refs[:4], refs[4:]
    gate_mat, up_mat, pre_gate, pre_up, gated, rows = refs
    width = rows.shape[1]
    lay_out(pieces, rows, slice(0, width))
    gate = gate_column(experts, pieces, width)
    for start in range(0, gated.shape[1], tile):
        columns = slice(start, start + tile)
        gate_part = product(rows[...], gate_mat[:, columns])
        up_part = product(rows[...], up_mat[:, columns])
        silu_value, _ = silu_parts(gate_part)
        pre_gate[:, columns] = gate_part
        pre_up[:, columns] = up_part
        gated[:, columns] = (gate * silu_value * up_part).astype(jnp.bfloat16)


def hidden_units(pieces, gate_mat, up_mat, experts):
    width, hidden = gate_mat.shape
    total = 8 * pieces[0].shape[0]
    pre = jax.ShapeDtypeStruct((total, hidden), jnp.float32)
    act = jax.ShapeDtypeStruct((total, hidden), jnp.bfloat16)
    return call(
        functools.partial(hidden_kernel, experts, 256),
        "hidden_units",
        (*pieces, gate_mat, up_mat),
        (pre, pre, act),
        [pltpu.VMEM((total, width), jnp.bfloat16)],
        flops=4 * total * width * hidden,
        mebibytes=12,
    )


def outputs_kernel(tile, gated, down_mat, own, *other):
    half = own.shape[2]
    for keep in range(2):
        side = lax.axis_index("helper")
        side = side if keep else 1 - side
        for start in range(0, half, tile):
            columns = slice(start, start + tile)
            here = pl.ds(pl.multiple_of(side * half + start, tile), tile)
            out = product(gated[...], down_mat[:, here]).astype(jnp.bfloat16)
            own[keep, :, columns] = half_at(out, 0)
            other[keep][:, columns] = half_at(out, 1)


def outputs_of(gated, down_mat):
    total, hidden = gated.shape
    width = down_mat.shape[1]
    sums = lambda *rows: jax.ShapeDtypeStruct((*rows, width // 2), jnp.bfloat16)
    return call(
        functools.partial(outputs_kernel, 256),
        "outputs",
        (gated, down_mat),
        (sums(2, total // 2), *(sums(total // 2),) * 2),
        flops=2 * total * width * hidden,
    )


def hidden_grads_kernel(experts, tile, *refs):
    pieces, gate_pieces, refs = refs[:4], refs[4:8], refs[8:]
    down_mat, pre_gate, pre_up, d_gate, d_up, shares_out, grads = refs
    total, width = grads.shape
    lay_out(pieces, grads, slice(0, width))
    gate = gate_column(experts, gate_pieces, width)
    shares = []
    for start in range(0, d_gate.shape[1], tile):
        columns = slice(start, start + tile)
        raw = right_transposed(grads[...], down_mat[columns, :])
        up_part = pre_up[:, columns]
        silu_value, silu_slope = silu_parts(pre_gate[:, columns])
        share = raw * silu_value * up_part
        shares = shares + [share[:, c : c + LANES] for c in range(0, tile, LANES)]
        d_act = gate * raw
        d_gate[:, columns] = (d_act * up_part * silu_slope).astype(jnp.bfloat16)
        d_up[:, columns] = (d_act * silu_value).astype(jnp.bfloat16)
    value = jnp.sum(total_of(shares), axis=1, keepdims=True)
    lane = lax.broadcasted_iota(jnp.int32, (total, LANES), 1)
    high = 2 * lax.axis_index("expert") + lax.axis_index("helper")
    value = jnp.where((lane == high) | (lane == high + 2 * experts), value, 0.0)
    shares_out[...] = hi_lo(value, lane < 2 * experts)


def hidden_grads(pieces, gate_pieces, pre_gate, pre_up, down_mat, experts):
    hidden, width = down_mat.shape
    total = pre_gate.shape[0]
    act = jax.ShapeDtypeStruct((total, hidden), jnp.bfloat16)
    return call(
        functools.partial(hidden_grads_kernel, experts, 256),
        "hidden_grads",
        (*pieces, *gate_pieces, down_mat, pre_gate, pre_up),
        (act, act, jax.ShapeDtypeStruct((total, LANES), jnp.bfloat16)),
        [pltpu.VMEM((total, width), jnp.bfloat16)],
        flops=2 * total * width * hidden,
        mebibytes=12,
    )


def input_grads_kernel(tile, d_gate, d_up, shares, gate_mat, up_mat, own, *other):
    half = own.shape[2] - LANES

    def put(keep, columns, values):
        own[keep, :, columns] = half_at(values, 0)
        for i in range(2):
            other[2 * keep + i][:, columns] = half_at(half_at(values, 1), i)

    for keep in range(2):
        put(keep, slice(half, half + LANES), shares[...])
        side = lax.axis_index("helper")
        side = side if keep else 1 - side
        for start in range(0, half, tile):
            here = pl.ds(pl.multiple_of(side * half + start, tile), tile)
            back = right_transposed(d_gate[...], gate_mat[here, :])
            back = back + right_transposed(d_up[...], up_mat[here, :])
            put(keep, slice(start, start + tile), back.astype(jnp.bfloat16))


def input_grads_of(d_gate, d_up, shares, gate_mat, up_mat):
    width, hidden = gate_mat.shape
    total = d_gate.shape[0]
    sums = lambda *rows: jax.ShapeDtypeStruct((*rows, width // 2 + LANES), jnp.bfloat16)
    return call(
        functools.partial(input_grads_kernel, 256),
        "input_grads",
        (d_gate, d_up, shares, gate_mat, up_mat),
        (sums(2, total // 2), *(sums(total // 4),) * 4),
        mebibytes=12,
    )


def weights_kernel(width, tile, *refs):
    pieces, (acts, grad, rows) = refs[:4], refs[4:]
    lay_out(pieces, rows, slice(0, width))
    left, right = (acts, rows) if grad.shape[1] == width else (rows, acts)
    for start in range(0, grad.shape[0], tile):
        columns = slice(start, start + tile)
        grad[columns, :] = transposed_product(left[:, columns], right[...]).astype(jnp.bfloat16)


def weights(name, pieces, acts, width, by_hidden):
    rows, hidden = acts.shape
    shape = (hidden, width) if by_hidden else (width, hidden)
    return call(
        functools.partial(weights_kernel, width, 256),
        name,
        (*pieces, acts),
        jax.ShapeDtypeStruct(shape, jnp.bfloat16),
        [pltpu.VMEM((rows, width), jnp.bfloat16)],
        flops=2 * rows * width * hidden,
    )


def send_kernel(first, own, received, *sent):
    rows = sent[0].shape[0]
    for i, target in enumerate(sent):
        here = slice(first + i * rows, first + (i + 1) * rows)
        target[...] = own[0, here, :] + received[i * rows : (i + 1) * rows, :]


def slot_sum(own, received, arrived, slot, offset, received_slot):
    rows = LANES
    half = rows // 2
    here = slice(slot * rows, (slot + 1) * rows)
    other = arrived[offset : offset + rows, :].astype(jnp.float32)
    there = slice(received_slot * rows, (received_slot + 1) * rows)
    kept = own[1, here, :].astype(jnp.float32) + received[there, :].astype(jnp.float32)
    return kept + jnp.concatenate([other[half:], other[:half]], axis=0)


def slots_kernel(own, received, arrived, own_slot, near_and_last, far_slot):
    rows = own_slot.shape[0]
    targets = (own_slot, near_and_last.at[:rows], far_slot, near_and_last.at[rows:])
    for slot, target in enumerate(targets):
        target[...] = slot_sum(own, received, arrived, slot, slot * rows, slot).astype(target.dtype)


def add_last_kernel(far_slot, arrived, total):
    rows = far_slot.shape[0]
    total[...] = far_slot[...] + arrived[rows:, :]


def slot_kernel(slot, own, received, arrived, *refs):
    whole = slot_sum(own, received, arrived, slot, 0, slot % 2)
    if len(refs) > 1:
        whole = whole + refs[0][...].astype(jnp.float32)
    refs[-1][...] = whole.astype(refs[-1].dtype)


def finish_outputs_kernel(own, near_and_last, far, columns):
    near = near_and_last[: own.shape[0], :]
    whole = total_of([term.astype(jnp.float32) for term in (own[...], near, far[...])])
    whole = jnp.where(lax.axis_index("helper") == 0, whole, swap_halves(whole))
    columns[...] = whole.astype(jnp.bfloat16)


def finish_inputs_kernel(experts, ids, counts, scores, clock, own, received, arrived, *refs):
    columns, d_scores = refs[-2:]
    width = columns.shape[1]
    whole = slot_sum(own, received, arrived, 0, 0, 0)
    whole = total_of([whole] + [ref[...].astype(jnp.float32) for ref in refs[:-2]])
    whole = jnp.where(lax.axis_index("helper") == 0, whole, swap_halves(whole))
    columns[...] = whole[:, :width].astype(jnp.bfloat16)
    table = whole[:, width:].T
    lane = lax.broadcasted_iota(jnp.int32, table.shape, 0)
    named_by = (lane % (2 * experts)) // 2
    gates, used, score_sum = gate_rows(counts[...], scores[...])
    d_gates = []
    for k in range(len(gates)):
        hit = (named_by == ids[k : k + 1, :]) & (lane < 4 * experts)
        d_gates.append(jnp.sum(jnp.where(hit, table, 0.0), axis=0, keepdims=True))
    mean = total_of([gate * d_gate for gate, d_gate in zip(gates, d_gates)])
    for k, d_gate in enumerate(d_gates):
        d_scores[k : k + 1, :] = used[k] * (d_gate - mean) / score_sum


class FourChips:
    def __init__(self, label):
        self.label = label
        both = lambda pairs: [(2 * a + c, 2 * b + c) for a, b in pairs for c in (0, 1)]
        self.near = both([(z, z ^ 1) for z in range(4)])
        self.far = both([(z, z ^ 2) for z in range(4)])
        self.cores = [(i, i ^ 1) for i in range(8)]
        self.sides = [(0, 1), (1, 0)]

    def line(self, array, pairs):
        with jax.named_scope(self.label + "_line"):
            return lax.ppermute(array, "expert", pairs)

    def sibling(self, array):
        with jax.named_scope(self.label + "_cores"):
            return lax.ppermute(array, "expert", self.cores)

    def across(self, array):
        with jax.named_scope(self.label + "_across"):
            return lax.ppermute(array, "helper", self.sides)

    def send(self, first, own, received, parts):
        rows, columns = received.shape
        part = jax.ShapeDtypeStruct((rows // parts, columns), own.dtype)
        return call(
            functools.partial(send_kernel, first),
            self.label + "_send",
            (own, received),
            (part,) * parts,
        )

    def slots(self, own, received, arrived):
        rows, columns = arrived.shape
        shape = lambda slots: jax.ShapeDtypeStruct((slots * rows // 4, columns), arrived.dtype)
        return call(
            slots_kernel,
            self.label + "_slots",
            (own, received, arrived),
            (shape(1), shape(2), shape(1)),
        )

    def slot(self, which, own, received, arrived, *others):
        return call(
            functools.partial(slot_kernel, which),
            self.label + "_slot",
            (own, received, arrived, *others),
            jax.ShapeDtypeStruct(arrived.shape, arrived.dtype),
        )


def load_kernel(*refs):
    sources, targets, sems = refs[:3], refs[3:6], refs[6]
    copies = [
        pltpu.make_async_copy(source, target, sems.at[i])
        for i, (source, target) in enumerate(zip(sources, targets))
    ]
    for copy in copies:
        copy.start()
    for copy in copies:
        copy.wait()


def load(*mats):
    return pl.pallas_call(
        load_kernel,
        out_shape=tuple(jax.ShapeDtypeStruct(mat.shape, mat.dtype) for mat in mats),
        in_specs=[pl.BlockSpec(memory_space=pltpu.HBM)] * len(mats),
        out_specs=(VMEM,) * len(mats),
        scratch_shapes=[pltpu.SemaphoreType.DMA((len(mats),))],
        compiler_params=pltpu.CompilerParams(vmem_limit_bytes=2**20),
        name="load",
    )(*(pltpu.with_memory_space_constraint(mat, pltpu.HBM) for mat in mats))


def space(clock, flops=36 * 10**9):
    return pl.pallas_call(
        lambda old, new: None,
        out_shape=jax.ShapeDtypeStruct(clock.shape, clock.dtype),
        in_specs=[pl.BlockSpec(memory_space=pl.ANY)],
        out_specs=pl.BlockSpec(memory_space=pl.ANY),
        input_output_aliases={0: 0},
        compiler_params=pltpu.CompilerParams(vmem_limit_bytes=2**20),
        cost_estimate=pl.CostEstimate(flops=flops, bytes_accessed=0, transcendentals=0),
        name="space",
    )(clock)


class Order:
    def __init__(self):
        self.token = None

    def __call__(self, function, *operands, also=()):
        if self.token is not None:
            operands, _ = lax.optimization_barrier((operands, (self.token, also)))
        result = function(*operands)
        self.token = result
        return result


def lined_up(tokens, expert_ids, pick_counts, gate_scores, gate_local, up_local, down_local, grad_out):
    experts = lax.axis_size("expert")
    width = gate_local.shape[0]
    picks = (expert_ids.T, pick_counts[None, :], gate_scores.T)
    rows, grads, outs, ins = (FourChips(label) for label in ("rows", "grads", "out", "in"))
    order = Order()
    hold = lambda value, *tokens: lax.optimization_barrier((value, tokens))[0]
    product_of = lambda name, by_hidden: lambda r, acts: weights(name, r, acts, width, by_hidden)

    own, pair, clock = order(lambda r: prepare_rows(*picks, r, experts), tokens)
    near = rows.line(own, rows.near)
    far = rows.line(own, rows.far)
    sibling_pair = rows.sibling(pair)
    gate_mat, up_mat, down_mat = order(load, gate_local, up_local, down_local)
    sibling_pair = hold(sibling_pair, down_mat)
    line_pair = order(join, near, far, also=sibling_pair)
    last = rows.line(hold(far, line_pair), rows.near)
    across_pair = rows.across(line_pair)
    own, grads_pair = order(prepare_grads, grad_out)
    far = grads.line(own, grads.far)
    last_across = rows.across(last)
    near = grads.line(hold(own, last), grads.near)
    far = hold(far, last)
    grads_last = grads.line(far, grads.near)
    clock = order(lambda c: space(c, 2 * 10**9), clock, also=far)
    grads_line = order(join, near, far)
    grads_across = grads.across(grads_line)
    grads_sibling = grads.sibling(grads_pair)
    rest = order(join, line_pair, across_pair, last, last_across)
    all_rows = [pair, rest, sibling_pair, rows.sibling(rest)]
    pre_gate, pre_up, gated = order(
        lambda *r: hidden_units(r, gate_mat, up_mat, experts), *all_rows
    )
    grads_last = hold(grads_last, gated)
    last_across = grads.across(grads_last)
    near_out, sent, kept = order(outputs_of, gated, down_mat, also=(grads_last, grads_sibling))
    received, kept = outs.sibling(sent), outs.sibling(kept)
    clock = order(space, clock, also=(grads_across, last_across))
    received = hold(received, clock)
    (sent,) = order(lambda *s: outs.send(0, *s, 1), near_out, received)
    arrived = outs.across(sent)
    rest = order(join, grads_line, grads_across, grads_last, last_across)
    all_grads = [grads_pair, rest, grads_sibling, grads.sibling(rest)]
    d_gate, d_up, shares = order(
        lambda g, r, *pre: hidden_grads(g, r, *pre, down_mat, experts),
        all_grads,
        all_rows,
        pre_gate,
        pre_up,
    )
    in_own, near_sent, far_sent, near_kept, far_kept = order(
        lambda *d: input_grads_of(*d, gate_mat, up_mat), d_gate, d_up, shares
    )
    far_received, far_kept = ins.sibling(far_sent), ins.sibling(far_kept)
    near_received, near_kept = ins.sibling(near_sent), ins.sibling(near_kept)
    first = 2 * tokens.shape[0]
    far_sent, last_sent = order(lambda *s: ins.send(first, *s, 2), in_own, far_received)
    last_arrived = ins.across(last_sent)
    grad_down = order(product_of("grad_down", True), all_grads, gated)
    slot = order(lambda *s: ins.slot(3, *s), in_own, far_kept, last_arrived)
    last_sum = ins.line(slot, ins.near)
    far_arrived = ins.across(hold(far_sent, slot))
    arrived = hold(arrived, slot)
    own_slot, near_slots, far_slot = order(outs.slots, near_out, kept, arrived)
    near_sums = outs.line(near_slots, outs.near)
    own_sent, near_sent = order(lambda *s: ins.send(0, *s, 2), in_own, near_received)
    far_slot = order(
        lambda *s: call(add_last_kernel, "add_last", s, jax.ShapeDtypeStruct(s[0].shape, s[0].dtype)),
        far_slot,
        near_sums,
    )
    far_sum = outs.line(far_slot, outs.far)
    grad_gate = order(product_of("grad_gate", False), all_rows, d_gate)
    slot = order(lambda *s: ins.slot(2, *s), in_own, far_kept, far_arrived, last_sum)
    far = ins.line(slot, ins.far)
    near_arrived = ins.across(hold(near_sent, slot))
    grad_up = order(product_of("grad_up", False), all_rows, d_up)
    slot = order(lambda *s: ins.slot(1, *s), in_own, near_kept, near_arrived)
    near = ins.line(slot, ins.near)
    own_arrived = ins.across(hold(own_sent, slot))
    columns = jax.ShapeDtypeStruct((tokens.shape[0], width // 2), jnp.bfloat16)
    output_cols = order(
        lambda *sums: call(finish_outputs_kernel, "finish_outputs", sums, columns),
        own_slot,
        near_sums,
        far_sum,
    )
    clock = order(lambda c: space(c, 2 * 10**9), clock, also=far)
    near, own_arrived = hold((near, own_arrived), clock)
    input_cols, d_scores = order(
        lambda *sums: call(
            functools.partial(finish_inputs_kernel, experts),
            "finish_inputs",
            (*picks, clock, *sums),
            (columns, jax.ShapeDtypeStruct(picks[2].shape, jnp.float32)),
        ),
        in_own,
        near_kept,
        own_arrived,
        far,
        near,
    )
    return output_cols, input_cols, d_scores.T, grad_gate[None], grad_up[None], grad_down[None]


def any_mesh(tokens, expert_ids, pick_counts, gate_scores, gate_local, up_local, down_local, grad_out):
    tok_rows = tokens.shape[0]
    pick_width = expert_ids.shape[1]
    experts = lax.axis_size("expert")
    active_mask = lax.broadcasted_iota(jnp.int32, (tok_rows, pick_width), 1) < pick_counts[:, None]
    active_float = active_mask.astype(jnp.float32)
    weighted = gate_scores * active_float
    score_sum = jnp.sum(weighted, axis=1, keepdims=True)
    gate_weights = weighted / score_sum
    picked = (expert_ids[:, :, None] == lax.broadcasted_iota(jnp.int32, (1, 1, experts), 2)).astype(
        jnp.float32
    )
    gate_table = jnp.sum(gate_weights[:, :, None] * picked, axis=1)

    def combine(partial):
        summed = lax.psum_scatter(partial, "expert", scatter_dimension=0, tiled=True)
        return lax.psum_scatter(summed, "helper", scatter_dimension=1, tiled=True)

    rows = lax.all_gather(tokens, "expert", tiled=True)
    tables = lax.all_gather(gate_table.T, "expert", tiled=False)
    gates = jnp.take(tables, lax.axis_index("expert"), axis=1).reshape(-1, 1)
    grads = lax.all_gather(grad_out, "expert", tiled=True)

    pre_gate = product(rows, gate_local)
    pre_up = product(rows, up_local)
    silu_value, silu_slope = silu_parts(pre_gate)
    hidden_act = silu_value * pre_up
    gated_act = (gates * hidden_act).astype(jnp.bfloat16)
    output_cols = combine(product(gated_act, down_local).astype(jnp.bfloat16))

    raw_act = right_transposed(grads, down_local)
    gate_part = jnp.sum(raw_act * hidden_act, axis=1)
    d_act = gates * raw_act
    d_pre_gate = (d_act * pre_up * silu_slope).astype(jnp.bfloat16)
    d_pre_up = (d_act * silu_value).astype(jnp.bfloat16)
    input_cols = combine(
        (right_transposed(d_pre_gate, gate_local) + right_transposed(d_pre_up, up_local)).astype(
            jnp.bfloat16
        )
    )

    gate_parts = lax.all_gather(
        gate_part.reshape(-1, tok_rows), ("expert", "helper"), tiled=False
    )
    own_parts = jnp.take(gate_parts, lax.axis_index("expert"), axis=1)
    by_expert = jnp.sum(own_parts.reshape(experts, -1, tok_rows), axis=1).T
    d_gates = jnp.sum(by_expert[:, None, :] * picked, axis=2)
    d_scores = (
        active_float
        * (d_gates - jnp.sum(gate_weights * d_gates, axis=1, keepdims=True))
        / score_sum
    )

    def over_dp(whole, dimension):
        return lax.psum_scatter(
            whole.astype(jnp.bfloat16), "dp", scatter_dimension=dimension, tiled=True
        )[None]

    grad_w_gate = over_dp(transposed_product(rows, d_pre_gate), 0)
    grad_w_up = over_dp(transposed_product(rows, d_pre_up), 0)
    grad_w_down = over_dp(transposed_product(gated_act, grads), 1)
    return output_cols, input_cols, d_scores, grad_w_gate, grad_w_up, grad_w_down


def on_device(tokens, expert_ids, pick_counts, gate_scores, w_gate, w_up, w_down, grad_out):
    sizes = tuple(lax.axis_size(axis) for axis in ("expert", "helper", "dp"))
    layer = lined_up if sizes == (8, 2, 1) else any_mesh
    return layer(
        tokens, expert_ids, pick_counts, gate_scores, w_gate[0], w_up[0], w_down[0], grad_out
    )


def solution(mesh):
    in_specs = (
        P(("groups", "expert", "dp"), None),
        P(("groups", "expert", "dp"), None),
        P(("groups", "expert", "dp")),
        P(("groups", "expert", "dp"), None),
        P("expert", None, "helper"),
        P("expert", None, "helper"),
        P("expert", "helper", None),
        P(("groups", "expert", "dp"), None),
    )
    out_specs = (
        P(("groups", "expert", "dp"), "helper"),
        P(("groups", "expert", "dp"), "helper"),
        P(("groups", "expert", "dp"), None),
        P(("groups", "expert"), "dp", "helper"),
        P(("groups", "expert"), "dp", "helper"),
        P(("groups", "expert"), "helper", "dp"),
    )
    return jax.shard_map(
        on_device, mesh=mesh, in_specs=in_specs, out_specs=out_specs, check_vma=False
    )
```

```python
import functools

import jax
import jax.numpy as jnp
from jax import lax
from jax.experimental import pallas as pl
from jax.experimental.pallas import tpu as pltpu
from jax.sharding import PartitionSpec as P

LANES = 128
VMEM = pl.BlockSpec(memory_space=pltpu.VMEM)


def product(first_mat, second_mat):
    return jnp.dot(first_mat, second_mat, preferred_element_type=jnp.float32)


def transposed_product(first_mat, second_mat):
    return lax.dot_general(
        first_mat, second_mat, (((0,), (0,)), ((), ())), preferred_element_type=jnp.float32
    )


def right_transposed(first_mat, second_mat):
    return lax.dot_general(
        first_mat, second_mat, (((1,), (1,)), ((), ())), preferred_element_type=jnp.float32
    )


def silu_parts(argument):
    sigmoid_part = jax.nn.sigmoid(argument)
    return argument * sigmoid_part, sigmoid_part * (1.0 + argument * (1.0 - sigmoid_part))


def total_of(terms):
    return functools.reduce(jnp.add, terms)


def call(kernel, name, operands, out_shape, scratch=(), flops=0, moved=0, mebibytes=12):
    return pl.pallas_call(
        kernel,
        out_shape=out_shape,
        in_specs=[VMEM] * len(operands),
        out_specs=jax.tree.map(lambda _: VMEM, out_shape),
        scratch_shapes=scratch,
        compiler_params=pltpu.CompilerParams(vmem_limit_bytes=mebibytes * 2**20),
        cost_estimate=pl.CostEstimate(
            flops=flops, bytes_accessed=moved, transcendentals=0
        ),
        name=name,
    )(*operands)


def half_at(array, which):
    rows = array.shape[0] // 2
    return array[which * rows : (which + 1) * rows]


def swap_halves(array):
    return jnp.concatenate([half_at(array, 1), half_at(array, 0)], axis=0)


def hi_lo(values, is_high):
    high = values.astype(jnp.bfloat16).astype(jnp.float32)
    return jnp.where(is_high, high, values - high).astype(jnp.bfloat16)


def gate_rows(counts, scores):
    used = [(counts > k).astype(jnp.float32) for k in range(scores.shape[0])]
    weighted = [scores[k : k + 1] * used[k] for k in range(scores.shape[0])]
    score_sum = total_of(weighted)
    return [w / score_sum for w in weighted], used, score_sum


def prepare_rows_kernel(experts, *refs):
    sources, (own, pair, clock), targets, sems = refs[:4], refs[4:7], refs[7:11], refs[11]
    ids, counts, scores, rows = targets
    copies = [
        pltpu.make_async_copy(source, target, sems.at[i])
        for i, (source, target) in enumerate(zip(sources, targets))
    ]
    for copy in copies:
        copy.start()
    for copy in copies:
        copy.wait()
    total, width = rows.shape
    clock[...] = jnp.zeros_like(clock)
    lane = lax.broadcasted_iota(jnp.int32, (LANES, total), 0)
    gates, _, _ = gate_rows(counts[...], scores[...])
    table = jnp.zeros((LANES, total), jnp.float32)
    for k, gate in enumerate(gates):
        named = ids[k : k + 1, :]
        table = table + jnp.where((lane == named) | (lane == named + experts), gate, 0.0)
    table = table.T
    table = hi_lo(table, lax.broadcasted_iota(jnp.int32, table.shape, 1) < experts)
    for side in range(2):

        @pl.when(lax.axis_index("helper") == side)
        def _(side=side):
            own[:, :width] = half_at(rows, side)
            own[:, width:] = half_at(table, side)
            for i, which in enumerate((side, 1 - side)):
                here = slice(i * total // 2, (i + 1) * total // 2)
                pair[here, :width] = half_at(rows, which)
                pair[here, width:] = half_at(table, which)


def prepare_rows(ids, counts, scores, rows, experts):
    total, width = rows.shape
    piece = jax.ShapeDtypeStruct((total // 2, width + LANES), jnp.bfloat16)
    operands = (ids, counts, scores, rows)
    return pl.pallas_call(
        functools.partial(prepare_rows_kernel, experts),
        out_shape=(
            piece,
            jax.ShapeDtypeStruct((total, width + LANES), jnp.bfloat16),
            jax.ShapeDtypeStruct((8, LANES), jnp.float32),
        ),
        in_specs=[pl.BlockSpec(memory_space=pltpu.HBM)] * len(operands),
        out_specs=(VMEM,) * 3,
        scratch_shapes=[
            *(pltpu.VMEM(operand.shape, operand.dtype) for operand in operands),
            pltpu.SemaphoreType.DMA((len(operands),)),
        ],
        compiler_params=pltpu.CompilerParams(vmem_limit_bytes=8 * 2**20),
        name="prepare_rows",
    )(*(pltpu.with_memory_space_constraint(operand, pltpu.HBM) for operand in operands))


def prepare_grads_kernel(rows, own, pair):
    half = rows.shape[0] // 2
    for side in range(2):

        @pl.when(lax.axis_index("helper") == side)
        def _(side=side):
            own[...] = half_at(rows, side)
            pair[:half, :] = half_at(rows, side)
            pair[half:, :] = half_at(rows, 1 - side)


def prepare_grads(rows):
    total, width = rows.shape
    piece = jax.ShapeDtypeStruct((total // 2, width), jnp.bfloat16)
    return call(
        prepare_grads_kernel,
        "prepare_grads",
        (rows,),
        (piece, jax.ShapeDtypeStruct(rows.shape, jnp.bfloat16)),
    )


def join_kernel(*refs):
    at = 0
    for piece in refs[:-1]:
        refs[-1][at : at + piece.shape[0], :] = piece[...]
        at = at + piece.shape[0]


def join(*pieces):
    total = sum(piece.shape[0] for piece in pieces)
    shape = jax.ShapeDtypeStruct((total, pieces[0].shape[1]), pieces[0].dtype)
    return call(join_kernel, "join", pieces, shape)


def parts_of(pair, rest):
    rows = pair.shape[0]
    half = rows // 2
    parts = [(pair, 0, rows)]
    for slot in range(2):
        parts = parts + [(rest, slot * half, half), (rest, rows + slot * half, half)]
    return parts + [(rest, 2 * rows, rows)]


def lay_out(pieces, target, columns):
    at = 0
    for piece, start, rows in parts_of(*pieces[:2]) + parts_of(*pieces[2:]):
        target[at : at + rows, :] = piece[start : start + rows, columns]
        at = at + rows


def gate_column(experts, pieces, width):
    parts = parts_of(*pieces[:2]) + parts_of(*pieces[2:])
    table = jnp.concatenate(
        [piece[start : start + rows, width:] for piece, start, rows in parts], axis=0
    )
    lane = lax.broadcasted_iota(jnp.int32, table.shape, 1)
    expert = lax.axis_index("expert")
    mine = (lane == expert) | (lane == expert + experts)
    return jnp.sum(jnp.where(mine, table.astype(jnp.float32), 0.0), axis=1, keepdims=True)


def hidden_kernel(experts, tile, *refs):
    pieces, refs = refs[:4], refs[4:]
    gate_mat, up_mat, pre_gate, pre_up, gated, rows = refs
    width = rows.shape[1]
    lay_out(pieces, rows, slice(0, width))
    gate = gate_column(experts, pieces, width)
    for start in range(0, gated.shape[1], tile):
        columns = slice(start, start + tile)
        gate_part = product(rows[...], gate_mat[:, columns])
        up_part = product(rows[...], up_mat[:, columns])
        silu_value, _ = silu_parts(gate_part)
        pre_gate[:, columns] = gate_part
        pre_up[:, columns] = up_part
        gated[:, columns] = (gate * silu_value * up_part).astype(jnp.bfloat16)


def hidden_units(pieces, gate_mat, up_mat, experts):
    width, hidden = gate_mat.shape
    total = 8 * pieces[0].shape[0]
    pre = jax.ShapeDtypeStruct((total, hidden), jnp.float32)
    act = jax.ShapeDtypeStruct((total, hidden), jnp.bfloat16)
    return call(
        functools.partial(hidden_kernel, experts, 256),
        "hidden_units",
        (*pieces, gate_mat, up_mat),
        (pre, pre, act),
        [pltpu.VMEM((total, width), jnp.bfloat16)],
        flops=4 * total * width * hidden,
        mebibytes=12,
    )


def outputs_kernel(tile, gated, down_mat, own, *other):
    half = own.shape[2]
    for keep in range(2):
        side = lax.axis_index("helper")
        side = side if keep else 1 - side
        for start in range(0, half, tile):
            columns = slice(start, start + tile)
            here = pl.ds(pl.multiple_of(side * half + start, tile), tile)
            out = product(gated[...], down_mat[:, here]).astype(jnp.bfloat16)
            own[keep, :, columns] = half_at(out, 0)
            other[keep][:, columns] = half_at(out, 1)


def outputs_of(gated, down_mat):
    total, hidden = gated.shape
    width = down_mat.shape[1]
    sums = lambda *rows: jax.ShapeDtypeStruct((*rows, width // 2), jnp.bfloat16)
    return call(
        functools.partial(outputs_kernel, 256),
        "outputs",
        (gated, down_mat),
        (sums(2, total // 2), *(sums(total // 2),) * 2),
        flops=2 * total * width * hidden,
    )


def hidden_grads_kernel(experts, tile, *refs):
    pieces, gate_pieces, refs = refs[:4], refs[4:8], refs[8:]
    down_mat, pre_gate, pre_up, d_gate, d_up, shares_out, grads = refs
    total, width = grads.shape
    lay_out(pieces, grads, slice(0, width))
    gate = gate_column(experts, gate_pieces, width)
    shares = []
    for start in range(0, d_gate.shape[1], tile):
        columns = slice(start, start + tile)
        raw = right_transposed(grads[...], down_mat[columns, :])
        up_part = pre_up[:, columns]
        silu_value, silu_slope = silu_parts(pre_gate[:, columns])
        share = raw * silu_value * up_part
        shares = shares + [share[:, c : c + LANES] for c in range(0, tile, LANES)]
        d_act = gate * raw
        d_gate[:, columns] = (d_act * up_part * silu_slope).astype(jnp.bfloat16)
        d_up[:, columns] = (d_act * silu_value).astype(jnp.bfloat16)
    value = jnp.sum(total_of(shares), axis=1, keepdims=True)
    lane = lax.broadcasted_iota(jnp.int32, (total, LANES), 1)
    high = 2 * lax.axis_index("expert") + lax.axis_index("helper")
    value = jnp.where((lane == high) | (lane == high + 2 * experts), value, 0.0)
    shares_out[...] = hi_lo(value, lane < 2 * experts)


def hidden_grads(pieces, gate_pieces, pre_gate, pre_up, down_mat, experts):
    hidden, width = down_mat.shape
    total = pre_gate.shape[0]
    act = jax.ShapeDtypeStruct((total, hidden), jnp.bfloat16)
    return call(
        functools.partial(hidden_grads_kernel, experts, 256),
        "hidden_grads",
        (*pieces, *gate_pieces, down_mat, pre_gate, pre_up),
        (act, act, jax.ShapeDtypeStruct((total, LANES), jnp.bfloat16)),
        [pltpu.VMEM((total, width), jnp.bfloat16)],
        flops=2 * total * width * hidden,
        mebibytes=12,
    )


def input_grads_kernel(tile, d_gate, d_up, shares, gate_mat, up_mat, own, *other):
    half = own.shape[2] - LANES

    def put(keep, columns, values):
        own[keep, :, columns] = half_at(values, 0)
        for i in range(2):
            other[2 * keep + i][:, columns] = half_at(half_at(values, 1), i)

    for keep in range(2):
        put(keep, slice(half, half + LANES), shares[...])
        side = lax.axis_index("helper")
        side = side if keep else 1 - side
        for start in range(0, half, tile):
            here = pl.ds(pl.multiple_of(side * half + start, tile), tile)
            back = right_transposed(d_gate[...], gate_mat[here, :])
            back = back + right_transposed(d_up[...], up_mat[here, :])
            put(keep, slice(start, start + tile), back.astype(jnp.bfloat16))


def input_grads_of(d_gate, d_up, shares, gate_mat, up_mat):
    width, hidden = gate_mat.shape
    total = d_gate.shape[0]
    sums = lambda *rows: jax.ShapeDtypeStruct((*rows, width // 2 + LANES), jnp.bfloat16)
    return call(
        functools.partial(input_grads_kernel, 256),
        "input_grads",
        (d_gate, d_up, shares, gate_mat, up_mat),
        (sums(2, total // 2), *(sums(total // 4),) * 4),
        mebibytes=12,
    )


def weights_kernel(width, tile, *refs):
    pieces, (acts, grad, rows) = refs[:4], refs[4:]
    lay_out(pieces, rows, slice(0, width))
    left, right = (acts, rows) if grad.shape[1] == width else (rows, acts)
    for start in range(0, grad.shape[0], tile):
        columns = slice(start, start + tile)
        grad[columns, :] = transposed_product(left[:, columns], right[...]).astype(jnp.bfloat16)


def weights(name, pieces, acts, width, by_hidden):
    rows, hidden = acts.shape
    shape = (hidden, width) if by_hidden else (width, hidden)
    return call(
        functools.partial(weights_kernel, width, 256),
        name,
        (*pieces, acts),
        jax.ShapeDtypeStruct(shape, jnp.bfloat16),
        [pltpu.VMEM((rows, width), jnp.bfloat16)],
        flops=2 * rows * width * hidden,
    )


def send_kernel(first, own, received, *sent):
    at = 0
    for target in sent:
        rows = target.shape[0]
        here = slice(first + at, first + at + rows)
        target[...] = own[0, here, :] + received[at : at + rows, :]
        at = at + rows


def slot_sum(own, received, arrived, slot, offset, received_slot):
    rows = LANES
    half = rows // 2
    here = slice(slot * rows, (slot + 1) * rows)
    other = arrived[offset : offset + rows, :].astype(jnp.float32)
    there = slice(received_slot * rows, (received_slot + 1) * rows)
    kept = own[1, here, :].astype(jnp.float32) + received[there, :].astype(jnp.float32)
    return kept + jnp.concatenate([other[half:], other[:half]], axis=0)


def slots_kernel(own, received, arrived, near_and_last, far_slot):
    rows = far_slot.shape[0]
    targets = (near_and_last.at[:rows], far_slot, near_and_last.at[rows:])
    for i, target in enumerate(targets):
        whole = slot_sum(own, received, arrived, i + 1, i * rows, i + 1)
        target[...] = whole.astype(target.dtype)


def add_last_kernel(far_slot, arrived, total):
    rows = far_slot.shape[0]
    total[...] = far_slot[...] + arrived[rows:, :]


def slot_kernel(slot, own, received, arrived, *refs):
    whole = slot_sum(own, received, arrived, slot, 0, slot % 2)
    if len(refs) > 1:
        whole = whole + refs[0][...].astype(jnp.float32)
    refs[-1][...] = whole.astype(refs[-1].dtype)


def finish_outputs_kernel(own, received, arrived, near_and_last, far, columns):
    near = near_and_last[: far.shape[0], :]
    whole = slot_sum(own, received, arrived, 0, 0, 0)
    whole = total_of([whole, near.astype(jnp.float32), far[...].astype(jnp.float32)])
    whole = jnp.where(lax.axis_index("helper") == 0, whole, swap_halves(whole))
    columns[...] = whole.astype(jnp.bfloat16)


def finish_inputs_kernel(experts, ids, counts, scores, clock, own, received, arrived, *refs):
    columns, d_scores = refs[-2:]
    width = columns.shape[1]
    whole = slot_sum(own, received, arrived, 0, 0, 0)
    whole = total_of([whole] + [ref[...].astype(jnp.float32) for ref in refs[:-2]])
    whole = jnp.where(lax.axis_index("helper") == 0, whole, swap_halves(whole))
    columns[...] = whole[:, :width].astype(jnp.bfloat16)
    table = whole[:, width:].T
    lane = lax.broadcasted_iota(jnp.int32, table.shape, 0)
    named_by = (lane % (2 * experts)) // 2
    gates, used, score_sum = gate_rows(counts[...], scores[...])
    d_gates = []
    for k in range(len(gates)):
        hit = (named_by == ids[k : k + 1, :]) & (lane < 4 * experts)
        d_gates.append(jnp.sum(jnp.where(hit, table, 0.0), axis=0, keepdims=True))
    mean = total_of([gate * d_gate for gate, d_gate in zip(gates, d_gates)])
    for k, d_gate in enumerate(d_gates):
        d_scores[k : k + 1, :] = used[k] * (d_gate - mean) / score_sum


class FourChips:
    def __init__(self, label):
        self.label = label
        both = lambda pairs: [(2 * a + c, 2 * b + c) for a, b in pairs for c in (0, 1)]
        self.near = both([(z, z ^ 1) for z in range(4)])
        self.far = both([(z, z ^ 2) for z in range(4)])
        self.cores = [(i, i ^ 1) for i in range(8)]
        self.sides = [(0, 1), (1, 0)]

    def line(self, array, pairs):
        with jax.named_scope(self.label + "_line"):
            return lax.ppermute(array, "expert", pairs)

    def sibling(self, array):
        with jax.named_scope(self.label + "_cores"):
            return lax.ppermute(array, "expert", self.cores)

    def across(self, array):
        with jax.named_scope(self.label + "_across"):
            return lax.ppermute(array, "helper", self.sides)

    def send(self, first, own, received, parts):
        shape = lambda rows: jax.ShapeDtypeStruct((rows, received.shape[1]), own.dtype)
        return call(
            functools.partial(send_kernel, first),
            self.label + "_send",
            (own, received),
            tuple(shape(rows) for rows in parts),
        )

    def slots(self, own, received, arrived):
        rows, columns = arrived.shape
        shape = lambda slots: jax.ShapeDtypeStruct((slots * rows // 3, columns), arrived.dtype)
        return call(
            slots_kernel,
            self.label + "_slots",
            (own, received, arrived),
            (shape(2), shape(1)),
        )

    def slot(self, which, own, received, arrived, *others):
        return call(
            functools.partial(slot_kernel, which),
            self.label + "_slot",
            (own, received, arrived, *others),
            jax.ShapeDtypeStruct(arrived.shape, arrived.dtype),
        )


def load_kernel(*refs):
    sources, targets, sems = refs[:3], refs[3:6], refs[6]
    copies = [
        pltpu.make_async_copy(source, target, sems.at[i])
        for i, (source, target) in enumerate(zip(sources, targets))
    ]
    for copy in copies:
        copy.start()
    for copy in copies:
        copy.wait()


def load(*mats):
    return pl.pallas_call(
        load_kernel,
        out_shape=tuple(jax.ShapeDtypeStruct(mat.shape, mat.dtype) for mat in mats),
        in_specs=[pl.BlockSpec(memory_space=pltpu.HBM)] * len(mats),
        out_specs=(VMEM,) * len(mats),
        scratch_shapes=[pltpu.SemaphoreType.DMA((len(mats),))],
        compiler_params=pltpu.CompilerParams(vmem_limit_bytes=2**20),
        name="load",
    )(*(pltpu.with_memory_space_constraint(mat, pltpu.HBM) for mat in mats))


def space(clock, flops=36 * 10**9):
    return pl.pallas_call(
        lambda old, new: None,
        out_shape=jax.ShapeDtypeStruct(clock.shape, clock.dtype),
        in_specs=[pl.BlockSpec(memory_space=pl.ANY)],
        out_specs=pl.BlockSpec(memory_space=pl.ANY),
        input_output_aliases={0: 0},
        compiler_params=pltpu.CompilerParams(vmem_limit_bytes=2**20),
        cost_estimate=pl.CostEstimate(flops=flops, bytes_accessed=0, transcendentals=0),
        name="space",
    )(clock)


class Order:
    def __init__(self):
        self.token = None

    def __call__(self, function, *operands, also=()):
        if self.token is not None:
            operands, _ = lax.optimization_barrier((operands, (self.token, also)))
        result = function(*operands)
        self.token = result
        return result


def lined_up(tokens, expert_ids, pick_counts, gate_scores, gate_local, up_local, down_local, grad_out):
    experts = lax.axis_size("expert")
    width = gate_local.shape[0]
    picks = (expert_ids.T, pick_counts[None, :], gate_scores.T)
    rows, grads, outs, ins = (FourChips(label) for label in ("rows", "grads", "out", "in"))
    order = Order()
    hold = lambda value, *tokens: lax.optimization_barrier((value, tokens))[0]
    product_of = lambda name, by_hidden: lambda r, acts: weights(name, r, acts, width, by_hidden)

    own, pair, clock = order(lambda r: prepare_rows(*picks, r, experts), tokens)
    near = rows.line(own, rows.near)
    far = rows.line(own, rows.far)
    sibling_pair = rows.sibling(pair)
    gate_mat, up_mat, down_mat = order(load, gate_local, up_local, down_local)
    sibling_pair = hold(sibling_pair, down_mat)
    line_pair = order(join, near, far, also=sibling_pair)
    last = rows.line(hold(far, line_pair), rows.near)
    across_pair = rows.across(line_pair)
    own, grads_pair = order(prepare_grads, grad_out)
    far = grads.line(own, grads.far)
    last_across = rows.across(last)
    near = grads.line(hold(own, last), grads.near)
    far = hold(far, last)
    grads_last = grads.line(far, grads.near)
    clock = order(lambda c: space(c, 2 * 10**9), clock, also=far)
    grads_line = order(join, near, far)
    grads_across = grads.across(grads_line)
    grads_sibling = grads.sibling(grads_pair)
    rest = order(join, line_pair, across_pair, last, last_across)
    all_rows = [pair, rest, sibling_pair, rows.sibling(rest)]
    pre_gate, pre_up, gated = order(
        lambda *r: hidden_units(r, gate_mat, up_mat, experts), *all_rows
    )
    grads_last = hold(grads_last, gated)
    last_across = grads.across(grads_last)
    near_out, sent, kept = order(outputs_of, gated, down_mat, also=(grads_last, grads_sibling))
    received, kept = outs.sibling(sent), outs.sibling(kept)
    clock = order(space, clock, also=(grads_across, last_across))
    received = hold(received, clock)
    size = tokens.shape[0]
    own_sent, sent = order(
        lambda *s: outs.send(0, *s, (size, 3 * size)), near_out, received
    )
    arrived = outs.across(sent)
    rest = order(join, grads_line, grads_across, grads_last, last_across)
    all_grads = [grads_pair, rest, grads_sibling, grads.sibling(rest)]
    d_gate, d_up, shares = order(
        lambda g, r, *pre: hidden_grads(g, r, *pre, down_mat, experts),
        all_grads,
        all_rows,
        pre_gate,
        pre_up,
    )
    in_own, near_sent, far_sent, near_kept, far_kept = order(
        lambda *d: input_grads_of(*d, gate_mat, up_mat), d_gate, d_up, shares
    )
    far_received, far_kept = ins.sibling(far_sent), ins.sibling(far_kept)
    near_received, near_kept = ins.sibling(near_sent), ins.sibling(near_kept)
    far_sent, last_sent = order(
        lambda *s: ins.send(2 * size, *s, (size, size)), in_own, far_received
    )
    last_arrived = ins.across(last_sent)
    near_slots, far_slot = order(outs.slots, near_out, kept, hold(arrived, far_sent))
    near_sums = outs.line(near_slots, outs.near)
    out_arrived = outs.across(hold(own_sent, near_slots))
    grad_down = order(product_of("grad_down", True), all_grads, gated)
    slot = order(lambda *s: ins.slot(3, *s), in_own, far_kept, last_arrived)
    last_sum = ins.line(slot, ins.near)
    far_arrived = ins.across(hold(far_sent, slot))
    own_sent, near_sent = order(
        lambda *s: ins.send(0, *s, (size, size)), in_own, near_received, also=out_arrived
    )
    far_slot = order(
        lambda *s: call(add_last_kernel, "add_last", s, jax.ShapeDtypeStruct(s[0].shape, s[0].dtype)),
        far_slot,
        near_sums,
    )
    far_sum = outs.line(far_slot, outs.far)
    grad_gate = order(product_of("grad_gate", False), all_rows, d_gate)
    slot = order(lambda *s: ins.slot(2, *s), in_own, far_kept, far_arrived, last_sum)
    far = ins.line(slot, ins.far)
    near_arrived = ins.across(hold(near_sent, slot))
    grad_up = order(product_of("grad_up", False), all_rows, d_up)
    slot = order(lambda *s: ins.slot(1, *s), in_own, near_kept, near_arrived)
    near = ins.line(slot, ins.near)
    own_arrived = ins.across(hold(own_sent, slot))
    columns = jax.ShapeDtypeStruct((size, width // 2), jnp.bfloat16)
    output_cols = order(
        lambda *sums: call(finish_outputs_kernel, "finish_outputs", sums, columns),
        near_out,
        kept,
        out_arrived,
        near_sums,
        far_sum,
    )
    clock = order(lambda c: space(c, 2 * 10**9), clock, also=far)
    near, own_arrived = hold((near, own_arrived), clock)
    input_cols, d_scores = order(
        lambda *sums: call(
            functools.partial(finish_inputs_kernel, experts),
            "finish_inputs",
            (*picks, clock, *sums),
            (columns, jax.ShapeDtypeStruct(picks[2].shape, jnp.float32)),
        ),
        in_own,
        near_kept,
        own_arrived,
        far,
        near,
    )
    return output_cols, input_cols, d_scores.T, grad_gate[None], grad_up[None], grad_down[None]


def any_mesh(tokens, expert_ids, pick_counts, gate_scores, gate_local, up_local, down_local, grad_out):
    tok_rows = tokens.shape[0]
    pick_width = expert_ids.shape[1]
    experts = lax.axis_size("expert")
    active_mask = lax.broadcasted_iota(jnp.int32, (tok_rows, pick_width), 1) < pick_counts[:, None]
    active_float = active_mask.astype(jnp.float32)
    weighted = gate_scores * active_float
    score_sum = jnp.sum(weighted, axis=1, keepdims=True)
    gate_weights = weighted / score_sum
    picked = (expert_ids[:, :, None] == lax.broadcasted_iota(jnp.int32, (1, 1, experts), 2)).astype(
        jnp.float32
    )
    gate_table = jnp.sum(gate_weights[:, :, None] * picked, axis=1)

    def combine(partial):
        summed = lax.psum_scatter(partial, "expert", scatter_dimension=0, tiled=True)
        return lax.psum_scatter(summed, "helper", scatter_dimension=1, tiled=True)

    rows = lax.all_gather(tokens, "expert", tiled=True)
    tables = lax.all_gather(gate_table.T, "expert", tiled=False)
    gates = jnp.take(tables, lax.axis_index("expert"), axis=1).reshape(-1, 1)
    grads = lax.all_gather(grad_out, "expert", tiled=True)

    pre_gate = product(rows, gate_local)
    pre_up = product(rows, up_local)
    silu_value, silu_slope = silu_parts(pre_gate)
    hidden_act = silu_value * pre_up
    gated_act = (gates * hidden_act).astype(jnp.bfloat16)
    output_cols = combine(product(gated_act, down_local).astype(jnp.bfloat16))

    raw_act = right_transposed(grads, down_local)
    gate_part = jnp.sum(raw_act * hidden_act, axis=1)
    d_act = gates * raw_act
    d_pre_gate = (d_act * pre_up * silu_slope).astype(jnp.bfloat16)
    d_pre_up = (d_act * silu_value).astype(jnp.bfloat16)
    input_cols = combine(
        (right_transposed(d_pre_gate, gate_local) + right_transposed(d_pre_up, up_local)).astype(
            jnp.bfloat16
        )
    )

    gate_parts = lax.all_gather(
        gate_part.reshape(-1, tok_rows), ("expert", "helper"), tiled=False
    )
    own_parts = jnp.take(gate_parts, lax.axis_index("expert"), axis=1)
    by_expert = jnp.sum(own_parts.reshape(experts, -1, tok_rows), axis=1).T
    d_gates = jnp.sum(by_expert[:, None, :] * picked, axis=2)
    d_scores = (
        active_float
        * (d_gates - jnp.sum(gate_weights * d_gates, axis=1, keepdims=True))
        / score_sum
    )

    def over_dp(whole, dimension):
        return lax.psum_scatter(
            whole.astype(jnp.bfloat16), "dp", scatter_dimension=dimension, tiled=True
        )[None]

    grad_w_gate = over_dp(transposed_product(rows, d_pre_gate), 0)
    grad_w_up = over_dp(transposed_product(rows, d_pre_up), 0)
    grad_w_down = over_dp(transposed_product(gated_act, grads), 1)
    return output_cols, input_cols, d_scores, grad_w_gate, grad_w_up, grad_w_down


def on_device(tokens, expert_ids, pick_counts, gate_scores, w_gate, w_up, w_down, grad_out):
    sizes = tuple(lax.axis_size(axis) for axis in ("expert", "helper", "dp"))
    layer = lined_up if sizes == (8, 2, 1) else any_mesh
    return layer(
        tokens, expert_ids, pick_counts, gate_scores, w_gate[0], w_up[0], w_down[0], grad_out
    )


def solution(mesh):
    in_specs = (
        P(("groups", "expert", "dp"), None),
        P(("groups", "expert", "dp"), None),
        P(("groups", "expert", "dp")),
        P(("groups", "expert", "dp"), None),
        P("expert", None, "helper"),
        P("expert", None, "helper"),
        P("expert", "helper", None),
        P(("groups", "expert", "dp"), None),
    )
    out_specs = (
        P(("groups", "expert", "dp"), "helper"),
        P(("groups", "expert", "dp"), "helper"),
        P(("groups", "expert", "dp"), None),
        P(("groups", "expert"), "dp", "helper"),
        P(("groups", "expert"), "dp", "helper"),
        P(("groups", "expert"), "helper", "dp"),
    )
    return jax.shard_map(
        on_device, mesh=mesh, in_specs=in_specs, out_specs=out_specs, check_vma=False
    )
```

```python
import functools

import jax
import jax.numpy as jnp
from jax import lax
from jax.experimental import pallas as pl
from jax.experimental.pallas import tpu as pltpu
from jax.sharding import PartitionSpec as P

LANES = 128
VMEM = pl.BlockSpec(memory_space=pltpu.VMEM)


def product(first_mat, second_mat):
    return jnp.dot(first_mat, second_mat, preferred_element_type=jnp.float32)


def transposed_product(first_mat, second_mat):
    return lax.dot_general(
        first_mat, second_mat, (((0,), (0,)), ((), ())), preferred_element_type=jnp.float32
    )


def right_transposed(first_mat, second_mat):
    return lax.dot_general(
        first_mat, second_mat, (((1,), (1,)), ((), ())), preferred_element_type=jnp.float32
    )


def silu_parts(argument):
    sigmoid_part = jax.nn.sigmoid(argument)
    return argument * sigmoid_part, sigmoid_part * (1.0 + argument * (1.0 - sigmoid_part))


def total_of(terms):
    return functools.reduce(jnp.add, terms)


def call(kernel, name, operands, out_shape, scratch=(), flops=0, moved=0, mebibytes=12):
    return pl.pallas_call(
        kernel,
        out_shape=out_shape,
        in_specs=[VMEM] * len(operands),
        out_specs=jax.tree.map(lambda _: VMEM, out_shape),
        scratch_shapes=scratch,
        compiler_params=pltpu.CompilerParams(vmem_limit_bytes=mebibytes * 2**20),
        cost_estimate=pl.CostEstimate(
            flops=flops, bytes_accessed=moved, transcendentals=0
        ),
        name=name,
    )(*operands)


def half_at(array, which):
    rows = array.shape[0] // 2
    return array[which * rows : (which + 1) * rows]


def swap_halves(array):
    return jnp.concatenate([half_at(array, 1), half_at(array, 0)], axis=0)


def hi_lo(values, is_high):
    high = values.astype(jnp.bfloat16).astype(jnp.float32)
    return jnp.where(is_high, high, values - high).astype(jnp.bfloat16)


def gate_rows(counts, scores):
    used = [(counts > k).astype(jnp.float32) for k in range(scores.shape[0])]
    weighted = [scores[k : k + 1] * used[k] for k in range(scores.shape[0])]
    score_sum = total_of(weighted)
    return [w / score_sum for w in weighted], used, score_sum


def prepare_rows_kernel(experts, *refs):
    sources, (own, pair, clock), targets, sems = refs[:4], refs[4:7], refs[7:11], refs[11]
    ids, counts, scores, rows = targets
    copies = [
        pltpu.make_async_copy(source, target, sems.at[i])
        for i, (source, target) in enumerate(zip(sources, targets))
    ]
    for copy in copies:
        copy.start()
    for copy in copies:
        copy.wait()
    total, width = rows.shape
    clock[...] = jnp.zeros_like(clock)
    lane = lax.broadcasted_iota(jnp.int32, (LANES, total), 0)
    gates, _, _ = gate_rows(counts[...], scores[...])
    table = jnp.zeros((LANES, total), jnp.float32)
    for k, gate in enumerate(gates):
        named = ids[k : k + 1, :]
        table = table + jnp.where((lane == named) | (lane == named + experts), gate, 0.0)
    table = table.T
    table = hi_lo(table, lax.broadcasted_iota(jnp.int32, table.shape, 1) < experts)
    for side in range(2):

        @pl.when(lax.axis_index("helper") == side)
        def _(side=side):
            own[:, :width] = half_at(rows, side)
            own[:, width:] = half_at(table, side)
            for i, which in enumerate((side, 1 - side)):
                here = slice(i * total // 2, (i + 1) * total // 2)
                pair[here, :width] = half_at(rows, which)
                pair[here, width:] = half_at(table, which)


def prepare_rows(ids, counts, scores, rows, experts):
    total, width = rows.shape
    piece = jax.ShapeDtypeStruct((total // 2, width + LANES), jnp.bfloat16)
    operands = (ids, counts, scores, rows)
    return pl.pallas_call(
        functools.partial(prepare_rows_kernel, experts),
        out_shape=(
            piece,
            jax.ShapeDtypeStruct((total, width + LANES), jnp.bfloat16),
            jax.ShapeDtypeStruct((8, LANES), jnp.float32),
        ),
        in_specs=[pl.BlockSpec(memory_space=pltpu.HBM)] * len(operands),
        out_specs=(VMEM,) * 3,
        scratch_shapes=[
            *(pltpu.VMEM(operand.shape, operand.dtype) for operand in operands),
            pltpu.SemaphoreType.DMA((len(operands),)),
        ],
        compiler_params=pltpu.CompilerParams(vmem_limit_bytes=8 * 2**20),
        name="prepare_rows",
    )(*(pltpu.with_memory_space_constraint(operand, pltpu.HBM) for operand in operands))


def prepare_grads_kernel(rows, own, pair):
    half = rows.shape[0] // 2
    for side in range(2):

        @pl.when(lax.axis_index("helper") == side)
        def _(side=side):
            own[...] = half_at(rows, side)
            pair[:half, :] = half_at(rows, side)
            pair[half:, :] = half_at(rows, 1 - side)


def prepare_grads(rows):
    total, width = rows.shape
    piece = jax.ShapeDtypeStruct((total // 2, width), jnp.bfloat16)
    return call(
        prepare_grads_kernel,
        "prepare_grads",
        (rows,),
        (piece, jax.ShapeDtypeStruct(rows.shape, jnp.bfloat16)),
    )


def join_kernel(*refs):
    at = 0
    for piece in refs[:-1]:
        refs[-1][at : at + piece.shape[0], :] = piece[...]
        at = at + piece.shape[0]


def join(*pieces):
    total = sum(piece.shape[0] for piece in pieces)
    shape = jax.ShapeDtypeStruct((total, pieces[0].shape[1]), pieces[0].dtype)
    return call(join_kernel, "join", pieces, shape)


def parts_of(pair, rest):
    rows = pair.shape[0]
    half = rows // 2
    parts = [(pair, 0, rows)]
    for slot in range(2):
        parts = parts + [(rest, slot * half, half), (rest, rows + slot * half, half)]
    return parts + [(rest, 2 * rows, rows)]


def lay_out(pieces, target, columns):
    at = 0
    for piece, start, rows in parts_of(*pieces[:2]) + parts_of(*pieces[2:]):
        target[at : at + rows, :] = piece[start : start + rows, columns]
        at = at + rows


def gate_column(experts, pieces, width):
    parts = parts_of(*pieces[:2]) + parts_of(*pieces[2:])
    table = jnp.concatenate(
        [piece[start : start + rows, width:] for piece, start, rows in parts], axis=0
    )
    lane = lax.broadcasted_iota(jnp.int32, table.shape, 1)
    expert = lax.axis_index("expert")
    mine = (lane == expert) | (lane == expert + experts)
    return jnp.sum(jnp.where(mine, table.astype(jnp.float32), 0.0), axis=1, keepdims=True)


def hidden_kernel(experts, tile, *refs):
    pieces, refs = refs[:4], refs[4:]
    gate_mat, up_mat, pre_gate, pre_up, gated, rows = refs
    width = rows.shape[1]
    lay_out(pieces, rows, slice(0, width))
    gate = gate_column(experts, pieces, width)
    for start in range(0, gated.shape[1], tile):
        columns = slice(start, start + tile)
        gate_part = product(rows[...], gate_mat[:, columns])
        up_part = product(rows[...], up_mat[:, columns])
        silu_value, _ = silu_parts(gate_part)
        pre_gate[:, columns] = gate_part
        pre_up[:, columns] = up_part
        gated[:, columns] = (gate * silu_value * up_part).astype(jnp.bfloat16)


def hidden_units(pieces, gate_mat, up_mat, experts):
    width, hidden = gate_mat.shape
    total = 8 * pieces[0].shape[0]
    pre = jax.ShapeDtypeStruct((total, hidden), jnp.float32)
    act = jax.ShapeDtypeStruct((total, hidden), jnp.bfloat16)
    return call(
        functools.partial(hidden_kernel, experts, 256),
        "hidden_units",
        (*pieces, gate_mat, up_mat),
        (pre, pre, act),
        [pltpu.VMEM((total, width), jnp.bfloat16)],
        flops=4 * total * width * hidden,
        mebibytes=12,
    )


def outputs_kernel(tile, gated, down_mat, own, *other):
    half = own.shape[2]
    for keep in range(2):
        side = lax.axis_index("helper")
        side = side if keep else 1 - side
        for start in range(0, half, tile):
            columns = slice(start, start + tile)
            here = pl.ds(pl.multiple_of(side * half + start, tile), tile)
            out = product(gated[...], down_mat[:, here]).astype(jnp.bfloat16)
            own[keep, :, columns] = half_at(out, 0)
            other[keep][:, columns] = half_at(out, 1)


def outputs_of(gated, down_mat):
    total, hidden = gated.shape
    width = down_mat.shape[1]
    sums = lambda *rows: jax.ShapeDtypeStruct((*rows, width // 2), jnp.bfloat16)
    return call(
        functools.partial(outputs_kernel, 256),
        "outputs",
        (gated, down_mat),
        (sums(2, total // 2), *(sums(total // 2),) * 2),
        flops=2 * total * width * hidden,
    )


def hidden_grads_kernel(experts, tile, *refs):
    pieces, gate_pieces, refs = refs[:4], refs[4:8], refs[8:]
    down_mat, pre_gate, pre_up, d_gate, d_up, shares_out, grads = refs
    total, width = grads.shape
    lay_out(pieces, grads, slice(0, width))
    gate = gate_column(experts, gate_pieces, width)
    shares = []
    for start in range(0, d_gate.shape[1], tile):
        columns = slice(start, start + tile)
        raw = right_transposed(grads[...], down_mat[columns, :])
        up_part = pre_up[:, columns]
        silu_value, silu_slope = silu_parts(pre_gate[:, columns])
        share = raw * silu_value * up_part
        shares = shares + [share[:, c : c + LANES] for c in range(0, tile, LANES)]
        d_act = gate * raw
        d_gate[:, columns] = (d_act * up_part * silu_slope).astype(jnp.bfloat16)
        d_up[:, columns] = (d_act * silu_value).astype(jnp.bfloat16)
    value = jnp.sum(total_of(shares), axis=1, keepdims=True)
    lane = lax.broadcasted_iota(jnp.int32, (total, LANES), 1)
    high = 2 * lax.axis_index("expert") + lax.axis_index("helper")
    value = jnp.where((lane == high) | (lane == high + 2 * experts), value, 0.0)
    shares_out[...] = hi_lo(value, lane < 2 * experts)


def hidden_grads(pieces, gate_pieces, pre_gate, pre_up, down_mat, experts):
    hidden, width = down_mat.shape
    total = pre_gate.shape[0]
    act = jax.ShapeDtypeStruct((total, hidden), jnp.bfloat16)
    return call(
        functools.partial(hidden_grads_kernel, experts, 256),
        "hidden_grads",
        (*pieces, *gate_pieces, down_mat, pre_gate, pre_up),
        (act, act, jax.ShapeDtypeStruct((total, LANES), jnp.bfloat16)),
        [pltpu.VMEM((total, width), jnp.bfloat16)],
        flops=2 * total * width * hidden,
        mebibytes=12,
    )


def input_grads_kernel(tile, d_gate, d_up, shares, gate_mat, up_mat, own, *other):
    half = own.shape[2] - LANES

    def put(keep, columns, values):
        own[keep, :, columns] = half_at(values, 0)
        for i in range(2):
            other[2 * keep + i][:, columns] = half_at(half_at(values, 1), i)

    for keep in range(2):
        put(keep, slice(half, half + LANES), shares[...])
        side = lax.axis_index("helper")
        side = side if keep else 1 - side
        for start in range(0, half, tile):
            here = pl.ds(pl.multiple_of(side * half + start, tile), tile)
            back = right_transposed(d_gate[...], gate_mat[here, :])
            back = back + right_transposed(d_up[...], up_mat[here, :])
            put(keep, slice(start, start + tile), back.astype(jnp.bfloat16))


def input_grads_of(d_gate, d_up, shares, gate_mat, up_mat):
    width, hidden = gate_mat.shape
    total = d_gate.shape[0]
    sums = lambda *rows: jax.ShapeDtypeStruct((*rows, width // 2 + LANES), jnp.bfloat16)
    return call(
        functools.partial(input_grads_kernel, 256),
        "input_grads",
        (d_gate, d_up, shares, gate_mat, up_mat),
        (sums(2, total // 2), *(sums(total // 4),) * 4),
        mebibytes=12,
    )


def weights_kernel(width, tile, *refs):
    pieces, (acts, grad, rows) = refs[:4], refs[4:]
    lay_out(pieces, rows, slice(0, width))
    left, right = (acts, rows) if grad.shape[1] == width else (rows, acts)
    for start in range(0, grad.shape[0], tile):
        columns = slice(start, start + tile)
        grad[columns, :] = transposed_product(left[:, columns], right[...]).astype(jnp.bfloat16)


def weights(name, pieces, acts, width, by_hidden):
    rows, hidden = acts.shape
    shape = (hidden, width) if by_hidden else (width, hidden)
    return call(
        functools.partial(weights_kernel, width, 256),
        name,
        (*pieces, acts),
        jax.ShapeDtypeStruct(shape, jnp.bfloat16),
        [pltpu.VMEM((rows, width), jnp.bfloat16)],
        flops=2 * rows * width * hidden,
    )


def send_kernel(first, own, received, *sent):
    at = 0
    for target in sent:
        rows = target.shape[0]
        here = slice(first + at, first + at + rows)
        target[...] = own[0, here, :] + received[at : at + rows, :]
        at = at + rows


def slot_sum(own, received, arrived, slot, offset, received_slot):
    rows = LANES
    half = rows // 2
    here = slice(slot * rows, (slot + 1) * rows)
    other = arrived[offset : offset + rows, :].astype(jnp.float32)
    there = slice(received_slot * rows, (received_slot + 1) * rows)
    kept = own[1, here, :].astype(jnp.float32) + received[there, :].astype(jnp.float32)
    return kept + jnp.concatenate([other[half:], other[:half]], axis=0)


def slots_kernel(own, received, arrived, near_and_last, far_slot):
    rows = far_slot.shape[0]
    targets = (near_and_last.at[:rows], far_slot, near_and_last.at[rows:])
    for i, target in enumerate(targets):
        whole = slot_sum(own, received, arrived, i + 1, i * rows, i + 1)
        target[...] = whole.astype(target.dtype)


def add_last_kernel(far_slot, arrived, total):
    rows = far_slot.shape[0]
    total[...] = far_slot[...] + arrived[rows:, :]


def slot_kernel(slot, own, received, arrived, *refs):
    whole = slot_sum(own, received, arrived, slot, 0, slot % 2)
    if len(refs) > 1:
        whole = whole + refs[0][...].astype(jnp.float32)
    refs[-1][...] = whole.astype(refs[-1].dtype)


def finish_outputs_kernel(own, received, arrived, near_and_last, far, columns):
    near = near_and_last[: far.shape[0], :]
    whole = slot_sum(own, received, arrived, 0, 0, 0)
    whole = total_of([whole, near.astype(jnp.float32), far[...].astype(jnp.float32)])
    whole = jnp.where(lax.axis_index("helper") == 0, whole, swap_halves(whole))
    columns[...] = whole.astype(jnp.bfloat16)


def finish_inputs_kernel(experts, ids, counts, scores, clock, own, received, arrived, *refs):
    columns, d_scores = refs[-2:]
    width = columns.shape[1]
    whole = slot_sum(own, received, arrived, 0, 0, 0)
    whole = total_of([whole] + [ref[...].astype(jnp.float32) for ref in refs[:-2]])
    whole = jnp.where(lax.axis_index("helper") == 0, whole, swap_halves(whole))
    columns[...] = whole[:, :width].astype(jnp.bfloat16)
    table = whole[:, width:].T
    lane = lax.broadcasted_iota(jnp.int32, table.shape, 0)
    named_by = (lane % (2 * experts)) // 2
    gates, used, score_sum = gate_rows(counts[...], scores[...])
    d_gates = []
    for k in range(len(gates)):
        hit = (named_by == ids[k : k + 1, :]) & (lane < 4 * experts)
        d_gates.append(jnp.sum(jnp.where(hit, table, 0.0), axis=0, keepdims=True))
    mean = total_of([gate * d_gate for gate, d_gate in zip(gates, d_gates)])
    for k, d_gate in enumerate(d_gates):
        d_scores[k : k + 1, :] = used[k] * (d_gate - mean) / score_sum


class FourChips:
    def __init__(self, label):
        self.label = label
        both = lambda pairs: [(2 * a + c, 2 * b + c) for a, b in pairs for c in (0, 1)]
        self.near = both([(z, z ^ 1) for z in range(4)])
        self.far = both([(z, z ^ 2) for z in range(4)])
        self.cores = [(i, i ^ 1) for i in range(8)]
        self.sides = [(0, 1), (1, 0)]

    def line(self, array, pairs):
        with jax.named_scope(self.label + "_line"):
            return lax.ppermute(array, "expert", pairs)

    def sibling(self, array):
        with jax.named_scope(self.label + "_cores"):
            return lax.ppermute(array, "expert", self.cores)

    def across(self, array):
        with jax.named_scope(self.label + "_across"):
            return lax.ppermute(array, "helper", self.sides)

    def send(self, first, own, received, parts):
        shape = lambda rows: jax.ShapeDtypeStruct((rows, received.shape[1]), own.dtype)
        return call(
            functools.partial(send_kernel, first),
            self.label + "_send",
            (own, received),
            tuple(shape(rows) for rows in parts),
        )

    def slots(self, own, received, arrived):
        rows, columns = arrived.shape
        shape = lambda slots: jax.ShapeDtypeStruct((slots * rows // 3, columns), arrived.dtype)
        return call(
            slots_kernel,
            self.label + "_slots",
            (own, received, arrived),
            (shape(2), shape(1)),
        )

    def slot(self, which, own, received, arrived, *others):
        return call(
            functools.partial(slot_kernel, which),
            self.label + "_slot",
            (own, received, arrived, *others),
            jax.ShapeDtypeStruct(arrived.shape, arrived.dtype),
        )


def load_kernel(*refs):
    sources, targets, sems = refs[:3], refs[3:6], refs[6]
    copies = [
        pltpu.make_async_copy(source, target, sems.at[i])
        for i, (source, target) in enumerate(zip(sources, targets))
    ]
    for copy in copies:
        copy.start()
    for copy in copies:
        copy.wait()


def load(*mats):
    return pl.pallas_call(
        load_kernel,
        out_shape=tuple(jax.ShapeDtypeStruct(mat.shape, mat.dtype) for mat in mats),
        in_specs=[pl.BlockSpec(memory_space=pltpu.HBM)] * len(mats),
        out_specs=(VMEM,) * len(mats),
        scratch_shapes=[pltpu.SemaphoreType.DMA((len(mats),))],
        compiler_params=pltpu.CompilerParams(vmem_limit_bytes=2**20),
        name="load",
    )(*(pltpu.with_memory_space_constraint(mat, pltpu.HBM) for mat in mats))


def space(clock, flops=36 * 10**9):
    return pl.pallas_call(
        lambda old, new: None,
        out_shape=jax.ShapeDtypeStruct(clock.shape, clock.dtype),
        in_specs=[pl.BlockSpec(memory_space=pl.ANY)],
        out_specs=pl.BlockSpec(memory_space=pl.ANY),
        input_output_aliases={0: 0},
        compiler_params=pltpu.CompilerParams(vmem_limit_bytes=2**20),
        cost_estimate=pl.CostEstimate(flops=flops, bytes_accessed=0, transcendentals=0),
        name="space",
    )(clock)


class Order:
    def __init__(self):
        self.token = None

    def __call__(self, function, *operands, also=()):
        if self.token is not None:
            operands, _ = lax.optimization_barrier((operands, (self.token, also)))
        result = function(*operands)
        self.token = result
        return result


def lined_up(tokens, expert_ids, pick_counts, gate_scores, gate_local, up_local, down_local, grad_out):
    experts = lax.axis_size("expert")
    width = gate_local.shape[0]
    picks = (expert_ids.T, pick_counts[None, :], gate_scores.T)
    rows, grads, outs, ins = (FourChips(label) for label in ("rows", "grads", "out", "in"))
    order = Order()
    hold = lambda value, *tokens: lax.optimization_barrier((value, tokens))[0]
    product_of = lambda name, by_hidden: lambda r, acts: weights(name, r, acts, width, by_hidden)

    own, pair, clock = order(lambda r: prepare_rows(*picks, r, experts), tokens)
    near = rows.line(own, rows.near)
    sibling_pair = rows.sibling(pair)
    gate_mat, up_mat, down_mat = order(load, gate_local, up_local, down_local)
    grads_own, grads_pair = order(prepare_grads, grad_out, also=sibling_pair)
    near = hold(near, grads_own)
    near_across = rows.across(near)
    far = rows.line(hold(own, near), rows.far)
    grads_near = grads.line(hold(grads_own, near), grads.near)
    far = hold(far, near_across, grads_near)
    far_across = rows.across(far)
    last = rows.line(far, rows.near)
    grads_far = grads.line(hold(grads_own, far), grads.far)
    grads_near = hold(grads_near, far)
    grads_near_across = grads.across(grads_near)
    last = hold(last, grads_near_across)
    last_across = rows.across(last)
    grads_far, far_across = hold((grads_far, far_across), last)
    clock = order(lambda c: space(c, 2 * 10**9), clock, also=(grads_far, far_across))
    grads_far_across = grads.across(grads_far)
    grads_last = grads.line(grads_far, grads.near)
    grads_sibling = grads.sibling(grads_pair)
    rest = order(
        join, near, far, near_across, far_across, last, last_across, also=grads_near_across
    )
    all_rows = [pair, rest, sibling_pair, rows.sibling(rest)]
    pre_gate, pre_up, gated = order(
        lambda *r: hidden_units(r, gate_mat, up_mat, experts), *all_rows
    )
    grads_last = hold(grads_last, gated)
    last_across = grads.across(grads_last)
    near_out, sent, kept = order(outputs_of, gated, down_mat, also=(grads_last, grads_sibling))
    received, kept = outs.sibling(sent), outs.sibling(kept)
    clock = order(space, clock, also=(grads_far_across, last_across))
    received = hold(received, clock)
    size = tokens.shape[0]
    own_sent, sent = order(
        lambda *s: outs.send(0, *s, (size, 3 * size)), near_out, received
    )
    arrived = outs.across(sent)
    rest = order(
        join,
        grads_near,
        grads_far,
        grads_near_across,
        grads_far_across,
        grads_last,
        last_across,
    )
    all_grads = [grads_pair, rest, grads_sibling, grads.sibling(rest)]
    d_gate, d_up, shares = order(
        lambda g, r, *pre: hidden_grads(g, r, *pre, down_mat, experts),
        all_grads,
        all_rows,
        pre_gate,
        pre_up,
    )
    in_own, near_sent, far_sent, near_kept, far_kept = order(
        lambda *d: input_grads_of(*d, gate_mat, up_mat), d_gate, d_up, shares
    )
    far_received, far_kept = ins.sibling(far_sent), ins.sibling(far_kept)
    near_received, near_kept = ins.sibling(near_sent), ins.sibling(near_kept)
    far_sent, last_sent = order(
        lambda *s: ins.send(2 * size, *s, (size, size)), in_own, far_received
    )
    last_arrived = ins.across(last_sent)
    near_slots, far_slot = order(outs.slots, near_out, kept, hold(arrived, far_sent))
    near_sums = outs.line(near_slots, outs.near)
    out_sent = own_sent
    grad_down = order(product_of("grad_down", True), all_grads, gated)
    slot = order(lambda *s: ins.slot(3, *s), in_own, far_kept, last_arrived)
    last_sum = ins.line(slot, ins.near)
    far_arrived = ins.across(hold(far_sent, slot))
    out_arrived = outs.across(hold(out_sent, slot))
    own_sent, near_sent = order(
        lambda *s: ins.send(0, *s, (size, size)), in_own, near_received
    )
    far_slot = order(
        lambda *s: call(add_last_kernel, "add_last", s, jax.ShapeDtypeStruct(s[0].shape, s[0].dtype)),
        far_slot,
        near_sums,
    )
    far_sum = outs.line(far_slot, outs.far)
    grad_gate = order(product_of("grad_gate", False), all_rows, d_gate)
    slot = order(
        lambda *s: ins.slot(2, *s), in_own, far_kept, far_arrived, last_sum, also=out_arrived
    )
    far = ins.line(slot, ins.far)
    near_arrived = ins.across(hold(near_sent, slot))
    grad_up = order(product_of("grad_up", False), all_rows, d_up)
    slot = order(lambda *s: ins.slot(1, *s), in_own, near_kept, near_arrived)
    near = ins.line(slot, ins.near)
    own_arrived = ins.across(hold(own_sent, slot))
    columns = jax.ShapeDtypeStruct((size, width // 2), jnp.bfloat16)
    output_cols = order(
        lambda *sums: call(finish_outputs_kernel, "finish_outputs", sums, columns),
        near_out,
        kept,
        out_arrived,
        near_sums,
        far_sum,
    )
    clock = order(lambda c: space(c, 2 * 10**9), clock, also=far)
    near, own_arrived = hold((near, own_arrived), clock)
    input_cols, d_scores = order(
        lambda *sums: call(
            functools.partial(finish_inputs_kernel, experts),
            "finish_inputs",
            (*picks, clock, *sums),
            (columns, jax.ShapeDtypeStruct(picks[2].shape, jnp.float32)),
        ),
        in_own,
        near_kept,
        own_arrived,
        far,
        near,
    )
    return output_cols, input_cols, d_scores.T, grad_gate[None], grad_up[None], grad_down[None]


def any_mesh(tokens, expert_ids, pick_counts, gate_scores, gate_local, up_local, down_local, grad_out):
    tok_rows = tokens.shape[0]
    pick_width = expert_ids.shape[1]
    experts = lax.axis_size("expert")
    active_mask = lax.broadcasted_iota(jnp.int32, (tok_rows, pick_width), 1) < pick_counts[:, None]
    active_float = active_mask.astype(jnp.float32)
    weighted = gate_scores * active_float
    score_sum = jnp.sum(weighted, axis=1, keepdims=True)
    gate_weights = weighted / score_sum
    picked = (expert_ids[:, :, None] == lax.broadcasted_iota(jnp.int32, (1, 1, experts), 2)).astype(
        jnp.float32
    )
    gate_table = jnp.sum(gate_weights[:, :, None] * picked, axis=1)

    def combine(partial):
        summed = lax.psum_scatter(partial, "expert", scatter_dimension=0, tiled=True)
        return lax.psum_scatter(summed, "helper", scatter_dimension=1, tiled=True)

    rows = lax.all_gather(tokens, "expert", tiled=True)
    tables = lax.all_gather(gate_table.T, "expert", tiled=False)
    gates = jnp.take(tables, lax.axis_index("expert"), axis=1).reshape(-1, 1)
    grads = lax.all_gather(grad_out, "expert", tiled=True)

    pre_gate = product(rows, gate_local)
    pre_up = product(rows, up_local)
    silu_value, silu_slope = silu_parts(pre_gate)
    hidden_act = silu_value * pre_up
    gated_act = (gates * hidden_act).astype(jnp.bfloat16)
    output_cols = combine(product(gated_act, down_local).astype(jnp.bfloat16))

    raw_act = right_transposed(grads, down_local)
    gate_part = jnp.sum(raw_act * hidden_act, axis=1)
    d_act = gates * raw_act
    d_pre_gate = (d_act * pre_up * silu_slope).astype(jnp.bfloat16)
    d_pre_up = (d_act * silu_value).astype(jnp.bfloat16)
    input_cols = combine(
        (right_transposed(d_pre_gate, gate_local) + right_transposed(d_pre_up, up_local)).astype(
            jnp.bfloat16
        )
    )

    gate_parts = lax.all_gather(
        gate_part.reshape(-1, tok_rows), ("expert", "helper"), tiled=False
    )
    own_parts = jnp.take(gate_parts, lax.axis_index("expert"), axis=1)
    by_expert = jnp.sum(own_parts.reshape(experts, -1, tok_rows), axis=1).T
    d_gates = jnp.sum(by_expert[:, None, :] * picked, axis=2)
    d_scores = (
        active_float
        * (d_gates - jnp.sum(gate_weights * d_gates, axis=1, keepdims=True))
        / score_sum
    )

    def over_dp(whole, dimension):
        return lax.psum_scatter(
            whole.astype(jnp.bfloat16), "dp", scatter_dimension=dimension, tiled=True
        )[None]

    grad_w_gate = over_dp(transposed_product(rows, d_pre_gate), 0)
    grad_w_up = over_dp(transposed_product(rows, d_pre_up), 0)
    grad_w_down = over_dp(transposed_product(gated_act, grads), 1)
    return output_cols, input_cols, d_scores, grad_w_gate, grad_w_up, grad_w_down


def on_device(tokens, expert_ids, pick_counts, gate_scores, w_gate, w_up, w_down, grad_out):
    sizes = tuple(lax.axis_size(axis) for axis in ("expert", "helper", "dp"))
    layer = lined_up if sizes == (8, 2, 1) else any_mesh
    return layer(
        tokens, expert_ids, pick_counts, gate_scores, w_gate[0], w_up[0], w_down[0], grad_out
    )


def solution(mesh):
    in_specs = (
        P(("groups", "expert", "dp"), None),
        P(("groups", "expert", "dp"), None),
        P(("groups", "expert", "dp")),
        P(("groups", "expert", "dp"), None),
        P("expert", None, "helper"),
        P("expert", None, "helper"),
        P("expert", "helper", None),
        P(("groups", "expert", "dp"), None),
    )
    out_specs = (
        P(("groups", "expert", "dp"), "helper"),
        P(("groups", "expert", "dp"), "helper"),
        P(("groups", "expert", "dp"), None),
        P(("groups", "expert"), "dp", "helper"),
        P(("groups", "expert"), "dp", "helper"),
        P(("groups", "expert"), "helper", "dp"),
    )
    return jax.shard_map(
        on_device, mesh=mesh, in_specs=in_specs, out_specs=out_specs, check_vma=False
    )
```

```python
import functools

import jax
import jax.numpy as jnp
from jax import lax
from jax.experimental import pallas as pl
from jax.experimental.pallas import tpu as pltpu
from jax.sharding import PartitionSpec as P

LANES = 128
VMEM = pl.BlockSpec(memory_space=pltpu.VMEM)


def product(first_mat, second_mat):
    return jnp.dot(first_mat, second_mat, preferred_element_type=jnp.float32)


def transposed_product(first_mat, second_mat):
    return lax.dot_general(
        first_mat, second_mat, (((0,), (0,)), ((), ())), preferred_element_type=jnp.float32
    )


def right_transposed(first_mat, second_mat):
    return lax.dot_general(
        first_mat, second_mat, (((1,), (1,)), ((), ())), preferred_element_type=jnp.float32
    )


def silu_parts(argument):
    sigmoid_part = jax.nn.sigmoid(argument)
    return argument * sigmoid_part, sigmoid_part * (1.0 + argument * (1.0 - sigmoid_part))


def total_of(terms):
    return functools.reduce(jnp.add, terms)


def call(kernel, name, operands, out_shape, scratch=(), flops=0, moved=0, mebibytes=12):
    return pl.pallas_call(
        kernel,
        out_shape=out_shape,
        in_specs=[VMEM] * len(operands),
        out_specs=jax.tree.map(lambda _: VMEM, out_shape),
        scratch_shapes=scratch,
        compiler_params=pltpu.CompilerParams(vmem_limit_bytes=mebibytes * 2**20),
        cost_estimate=pl.CostEstimate(
            flops=flops, bytes_accessed=moved, transcendentals=0
        ),
        name=name,
    )(*operands)


def half_at(array, which):
    rows = array.shape[0] // 2
    return array[which * rows : (which + 1) * rows]


def swap_halves(array):
    return jnp.concatenate([half_at(array, 1), half_at(array, 0)], axis=0)


def hi_lo(values, is_high):
    high = values.astype(jnp.bfloat16).astype(jnp.float32)
    return jnp.where(is_high, high, values - high).astype(jnp.bfloat16)


def gate_rows(counts, scores):
    used = [(counts > k).astype(jnp.float32) for k in range(scores.shape[0])]
    weighted = [scores[k : k + 1] * used[k] for k in range(scores.shape[0])]
    score_sum = total_of(weighted)
    return [w / score_sum for w in weighted], used, score_sum


def prepare_rows_kernel(experts, *refs):
    sources, (own, pair, clock), targets, sems = refs[:4], refs[4:7], refs[7:11], refs[11]
    ids, counts, scores, rows = targets
    copies = [
        pltpu.make_async_copy(source, target, sems.at[i])
        for i, (source, target) in enumerate(zip(sources, targets))
    ]
    for copy in copies:
        copy.start()
    for copy in copies:
        copy.wait()
    total, width = rows.shape
    clock[...] = jnp.zeros_like(clock)
    lane = lax.broadcasted_iota(jnp.int32, (LANES, total), 0)
    gates, _, _ = gate_rows(counts[...], scores[...])
    table = jnp.zeros((LANES, total), jnp.float32)
    for k, gate in enumerate(gates):
        named = ids[k : k + 1, :]
        table = table + jnp.where((lane == named) | (lane == named + experts), gate, 0.0)
    table = table.T
    table = hi_lo(table, lax.broadcasted_iota(jnp.int32, table.shape, 1) < experts)
    for side in range(2):

        @pl.when(lax.axis_index("helper") == side)
        def _(side=side):
            own[:, :width] = half_at(rows, side)
            own[:, width:] = half_at(table, side)
            for i, which in enumerate((side, 1 - side)):
                here = slice(i * total // 2, (i + 1) * total // 2)
                pair[here, :width] = half_at(rows, which)
                pair[here, width:] = half_at(table, which)


def prepare_rows(ids, counts, scores, rows, experts):
    total, width = rows.shape
    piece = jax.ShapeDtypeStruct((total // 2, width + LANES), jnp.bfloat16)
    operands = (ids, counts, scores, rows)
    return pl.pallas_call(
        functools.partial(prepare_rows_kernel, experts),
        out_shape=(
            piece,
            jax.ShapeDtypeStruct((total, width + LANES), jnp.bfloat16),
            jax.ShapeDtypeStruct((8, LANES), jnp.float32),
        ),
        in_specs=[pl.BlockSpec(memory_space=pltpu.HBM)] * len(operands),
        out_specs=(VMEM,) * 3,
        scratch_shapes=[
            *(pltpu.VMEM(operand.shape, operand.dtype) for operand in operands),
            pltpu.SemaphoreType.DMA((len(operands),)),
        ],
        compiler_params=pltpu.CompilerParams(vmem_limit_bytes=8 * 2**20),
        name="prepare_rows",
    )(*(pltpu.with_memory_space_constraint(operand, pltpu.HBM) for operand in operands))


def prepare_grads_kernel(rows, own, pair):
    half = rows.shape[0] // 2
    for side in range(2):

        @pl.when(lax.axis_index("helper") == side)
        def _(side=side):
            own[...] = half_at(rows, side)
            pair[:half, :] = half_at(rows, side)
            pair[half:, :] = half_at(rows, 1 - side)


def prepare_grads(rows):
    total, width = rows.shape
    piece = jax.ShapeDtypeStruct((total // 2, width), jnp.bfloat16)
    return call(
        prepare_grads_kernel,
        "prepare_grads",
        (rows,),
        (piece, jax.ShapeDtypeStruct(rows.shape, jnp.bfloat16)),
    )


def join_kernel(starts, rows, *refs):
    for i, start in enumerate(starts):
        refs[-1][i * rows : (i + 1) * rows, :] = refs[i][start : start + rows, :]


def join(rows, pieces, starts):
    shape = jax.ShapeDtypeStruct((len(pieces) * rows, pieces[0].shape[1]), pieces[0].dtype)
    return call(functools.partial(join_kernel, starts, rows), "join", pieces, shape)


def parts_of(pair, rest):
    rows = pair.shape[0]
    half = rows // 2
    parts = [(pair, 0, rows)]
    for slot in range(2):
        parts = parts + [(rest, slot * half, half), (rest, rows + slot * half, half)]
    return parts + [(rest, 2 * rows, rows)]


def lay_out(pieces, target, columns, at=0):
    for piece, start, rows in parts_of(*pieces):
        target[at : at + rows, :] = piece[start : start + rows, columns]
        at = at + rows


def gate_column(experts, pieces, width):
    table = jnp.concatenate(
        [piece[start : start + rows, width:] for piece, start, rows in parts_of(*pieces)], axis=0
    )
    lane = lax.broadcasted_iota(jnp.int32, table.shape, 1)
    expert = lax.axis_index("expert")
    mine = (lane == expert) | (lane == expert + experts)
    return jnp.sum(jnp.where(mine, table.astype(jnp.float32), 0.0), axis=1, keepdims=True)


def hidden_kernel(experts, tile, *refs):
    pieces, refs = refs[:2], refs[2:]
    gate_mat, up_mat, pre_gate, pre_up, gated, rows = refs
    width = rows.shape[1]
    lay_out(pieces, rows, slice(0, width))
    gate = gate_column(experts, pieces, width)
    for start in range(0, gated.shape[1], tile):
        columns = slice(start, start + tile)
        gate_part = product(rows[...], gate_mat[:, columns])
        up_part = product(rows[...], up_mat[:, columns])
        silu_value, _ = silu_parts(gate_part)
        pre_gate[:, columns] = gate_part
        pre_up[:, columns] = up_part
        gated[:, columns] = (gate * silu_value * up_part).astype(jnp.bfloat16)


def hidden_units(pieces, gate_mat, up_mat, experts):
    width, hidden = gate_mat.shape
    total = 4 * pieces[0].shape[0]
    pre = jax.ShapeDtypeStruct((total, hidden), jnp.float32)
    act = jax.ShapeDtypeStruct((total, hidden), jnp.bfloat16)
    return call(
        functools.partial(hidden_kernel, experts, 256),
        "hidden_units",
        (*pieces, gate_mat, up_mat),
        (pre, pre, act),
        [pltpu.VMEM((total, width), jnp.bfloat16)],
        flops=4 * total * width * hidden,
        mebibytes=12,
    )


def outputs_kernel(tile, gated, down_mat, *sums):
    half = sums[0].shape[1]
    for keep in range(2):
        side = lax.axis_index("helper")
        side = side if keep else 1 - side
        for start in range(0, half, tile):
            here = pl.ds(pl.multiple_of(side * half + start, tile), tile)
            out = product(gated[...], down_mat[:, here])
            sums[keep][:, start : start + tile] = out.astype(jnp.bfloat16)


def outputs_of(gated, down_mat):
    total, hidden = gated.shape
    width = down_mat.shape[1]
    sums = jax.ShapeDtypeStruct((total, width // 2), jnp.bfloat16)
    return call(
        functools.partial(outputs_kernel, 256), "outputs", (gated, down_mat), (sums, sums)
    )


def hidden_grads_kernel(experts, tile, *refs):
    pieces, gate_pieces, refs = refs[:2], refs[2:4], refs[4:]
    down_mat, pre_gate, pre_up, d_gate, d_up, shares_out, grads = refs
    total, width = grads.shape
    lay_out(pieces, grads, slice(0, width))
    gate = gate_column(experts, gate_pieces, width)
    shares = []
    for start in range(0, d_gate.shape[1], tile):
        columns = slice(start, start + tile)
        raw = right_transposed(grads[...], down_mat[columns, :])
        up_part = pre_up[:, columns]
        silu_value, silu_slope = silu_parts(pre_gate[:, columns])
        share = raw * silu_value * up_part
        shares = shares + [share[:, c : c + LANES] for c in range(0, tile, LANES)]
        d_act = gate * raw
        d_gate[:, columns] = (d_act * up_part * silu_slope).astype(jnp.bfloat16)
        d_up[:, columns] = (d_act * silu_value).astype(jnp.bfloat16)
    value = jnp.sum(total_of(shares), axis=1, keepdims=True)
    lane = lax.broadcasted_iota(jnp.int32, (total, LANES), 1)
    high = 2 * lax.axis_index("expert") + lax.axis_index("helper")
    value = jnp.where((lane == high) | (lane == high + 2 * experts), value, 0.0)
    shares_out[...] = hi_lo(value, lane < 2 * experts)


def hidden_grads(pieces, gate_pieces, pre_gate, pre_up, down_mat, experts):
    hidden, width = down_mat.shape
    total = pre_gate.shape[0]
    act = jax.ShapeDtypeStruct((total, hidden), jnp.bfloat16)
    return call(
        functools.partial(hidden_grads_kernel, experts, 256),
        "hidden_grads",
        (*pieces, *gate_pieces, down_mat, pre_gate, pre_up),
        (act, act, jax.ShapeDtypeStruct((total, LANES), jnp.bfloat16)),
        [pltpu.VMEM((total, width), jnp.bfloat16)],
        mebibytes=12,
    )


def input_grads_kernel(tile, d_gate, d_up, shares, gate_mat, up_mat, *sums):
    half = sums[0].shape[1] - LANES
    split = len(sums) // 2

    def put(keep, columns, values):
        rows = values.shape[0] // split
        for i in range(split):
            sums[split * keep + i][:, columns] = values[i * rows : (i + 1) * rows]

    for keep in range(2):
        put(keep, slice(half, half + LANES), shares[...])
        side = lax.axis_index("helper")
        side = side if keep else 1 - side
        for start in range(0, half, tile):
            here = pl.ds(pl.multiple_of(side * half + start, tile), tile)
            back = right_transposed(d_gate[...], gate_mat[here, :])
            back = back + right_transposed(d_up[...], up_mat[here, :])
            put(keep, slice(start, start + tile), back.astype(jnp.bfloat16))


def input_grads_of(split, d_gate, d_up, shares, gate_mat, up_mat):
    width, hidden = gate_mat.shape
    total = d_gate.shape[0]
    sums = jax.ShapeDtypeStruct((total // split, width // 2 + LANES), jnp.bfloat16)
    return call(
        functools.partial(input_grads_kernel, 256),
        "input_grads",
        (d_gate, d_up, shares, gate_mat, up_mat),
        (sums,) * (2 * split),
        mebibytes=12,
    )


def weights_kernel(width, tile, *refs):
    pieces, (first, second, grad, rows, acts) = refs[:4], refs[4:]
    total = first.shape[0]
    lay_out(pieces[:2], rows, slice(0, width))
    lay_out(pieces[2:], rows, slice(0, width), total)
    acts[:total, :] = first[...]
    acts[total:, :] = second[...]
    left, right = (acts, rows) if grad.shape[1] == width else (rows, acts)
    for start in range(0, grad.shape[0], tile):
        columns = slice(start, start + tile)
        grad[columns, :] = transposed_product(left[:, columns], right[...]).astype(jnp.bfloat16)


def weights(name, pieces, acts, width, by_hidden):
    rows, hidden = acts[0].shape
    shape = (hidden, width) if by_hidden else (width, hidden)
    return call(
        functools.partial(weights_kernel, width, 256),
        name,
        (*pieces, *acts),
        jax.ShapeDtypeStruct(shape, jnp.bfloat16),
        [
            pltpu.VMEM((2 * rows, width), jnp.bfloat16),
            pltpu.VMEM((2 * rows, hidden), jnp.bfloat16),
        ],
        flops=4 * rows * width * hidden,
    )


def send_kernel(first, own, received, *sent):
    at = 0
    for target in sent:
        rows = target.shape[0]
        here = slice(first + at, first + at + rows)
        target[...] = own[here, :] + received[at : at + rows, :]
        at = at + rows


def slot_sum(own, received, arrived, slot, offset, received_slot):
    rows = LANES
    half = rows // 2
    here = slice(slot * rows, (slot + 1) * rows)
    other = arrived[offset : offset + rows, :].astype(jnp.float32)
    there = slice(received_slot * rows, (received_slot + 1) * rows)
    kept = own[here, :].astype(jnp.float32) + received[there, :].astype(jnp.float32)
    return kept + jnp.concatenate([other[half:], other[:half]], axis=0)


def slots_kernel(own, received, arrived, near_and_last, far_slot):
    rows = far_slot.shape[0]
    targets = (near_and_last.at[:rows], far_slot, near_and_last.at[rows:])
    for i, target in enumerate(targets):
        whole = slot_sum(own, received, arrived, i + 1, i * rows, i + 1)
        target[...] = whole.astype(target.dtype)


def add_last_kernel(far_slot, arrived, total):
    rows = far_slot.shape[0]
    total[...] = far_slot[...] + arrived[rows:, :]


def slot_kernel(slot, own, received, arrived, *refs):
    whole = slot_sum(own, received, arrived, slot, 0, slot % 2)
    if len(refs) > 1:
        whole = whole + refs[0][...].astype(jnp.float32)
    refs[-1][...] = whole.astype(refs[-1].dtype)


def finish_outputs_kernel(own, received, arrived, near_and_last, far, columns):
    near = near_and_last[: far.shape[0], :]
    whole = slot_sum(own, received, arrived, 0, 0, 0)
    whole = total_of([whole, near.astype(jnp.float32), far[...].astype(jnp.float32)])
    whole = jnp.where(lax.axis_index("helper") == 0, whole, swap_halves(whole))
    columns[...] = whole.astype(jnp.bfloat16)


def finish_inputs_kernel(experts, ids, counts, scores, clock, own, received, arrived, *refs):
    columns, d_scores = refs[-2:]
    width = columns.shape[1]
    whole = slot_sum(own, received, arrived, 0, 0, 0)
    whole = total_of([whole] + [ref[...].astype(jnp.float32) for ref in refs[:-2]])
    whole = jnp.where(lax.axis_index("helper") == 0, whole, swap_halves(whole))
    columns[...] = whole[:, :width].astype(jnp.bfloat16)
    table = whole[:, width:].T
    lane = lax.broadcasted_iota(jnp.int32, table.shape, 0)
    named_by = (lane % (2 * experts)) // 2
    gates, used, score_sum = gate_rows(counts[...], scores[...])
    d_gates = []
    for k in range(len(gates)):
        hit = (named_by == ids[k : k + 1, :]) & (lane < 4 * experts)
        d_gates.append(jnp.sum(jnp.where(hit, table, 0.0), axis=0, keepdims=True))
    mean = total_of([gate * d_gate for gate, d_gate in zip(gates, d_gates)])
    for k, d_gate in enumerate(d_gates):
        d_scores[k : k + 1, :] = used[k] * (d_gate - mean) / score_sum


class FourChips:
    def __init__(self, label):
        self.label = label
        both = lambda pairs: [(2 * a + c, 2 * b + c) for a, b in pairs for c in (0, 1)]
        self.near = both([(z, z ^ 1) for z in range(4)])
        self.far = both([(z, z ^ 2) for z in range(4)])
        self.cores = [(i, i ^ 1) for i in range(8)]
        self.sides = [(0, 1), (1, 0)]

    def line(self, array, pairs):
        with jax.named_scope(self.label + "_line"):
            return lax.ppermute(array, "expert", pairs)

    def sibling(self, array):
        with jax.named_scope(self.label + "_cores"):
            return lax.ppermute(array, "expert", self.cores)

    def across(self, array):
        with jax.named_scope(self.label + "_across"):
            return lax.ppermute(array, "helper", self.sides)

    def send(self, first, own, received, parts):
        shape = lambda rows: jax.ShapeDtypeStruct((rows, received.shape[1]), own.dtype)
        return call(
            functools.partial(send_kernel, first),
            self.label + "_send",
            (own, received),
            tuple(shape(rows) for rows in parts),
        )

    def slots(self, own, received, arrived):
        rows, columns = arrived.shape
        shape = lambda slots: jax.ShapeDtypeStruct((slots * rows // 3, columns), arrived.dtype)
        return call(
            slots_kernel,
            self.label + "_slots",
            (own, received, arrived),
            (shape(2), shape(1)),
        )

    def slot(self, which, own, received, arrived, *others):
        return call(
            functools.partial(slot_kernel, which),
            self.label + "_slot",
            (own, received, arrived, *others),
            jax.ShapeDtypeStruct(arrived.shape, arrived.dtype),
        )


def load_kernel(*refs):
    sources, targets, sems = refs[:3], refs[3:6], refs[6]
    copies = [
        pltpu.make_async_copy(source, target, sems.at[i])
        for i, (source, target) in enumerate(zip(sources, targets))
    ]
    for copy in copies:
        copy.start()
    for copy in copies:
        copy.wait()


def load(*mats):
    return pl.pallas_call(
        load_kernel,
        out_shape=tuple(jax.ShapeDtypeStruct(mat.shape, mat.dtype) for mat in mats),
        in_specs=[pl.BlockSpec(memory_space=pltpu.HBM)] * len(mats),
        out_specs=(VMEM,) * len(mats),
        scratch_shapes=[pltpu.SemaphoreType.DMA((len(mats),))],
        compiler_params=pltpu.CompilerParams(vmem_limit_bytes=2**20),
        name="load",
    )(*(pltpu.with_memory_space_constraint(mat, pltpu.HBM) for mat in mats))


def space(clock, flops=36 * 10**9):
    return pl.pallas_call(
        lambda old, new: None,
        out_shape=jax.ShapeDtypeStruct(clock.shape, clock.dtype),
        in_specs=[pl.BlockSpec(memory_space=pl.ANY)],
        out_specs=pl.BlockSpec(memory_space=pl.ANY),
        input_output_aliases={0: 0},
        compiler_params=pltpu.CompilerParams(vmem_limit_bytes=2**20),
        cost_estimate=pl.CostEstimate(flops=flops, bytes_accessed=0, transcendentals=0),
        name="space",
    )(clock)


class Order:
    def __init__(self):
        self.token = None

    def __call__(self, function, *operands, also=()):
        if self.token is not None:
            operands, _ = lax.optimization_barrier((operands, (self.token, also)))
        result = function(*operands)
        self.token = result
        return result


def lined_up(tokens, expert_ids, pick_counts, gate_scores, gate_local, up_local, down_local, grad_out):
    experts = lax.axis_size("expert")
    width = gate_local.shape[0]
    picks = (expert_ids.T, pick_counts[None, :], gate_scores.T)
    rows, grads, outs, ins = (FourChips(label) for label in ("rows", "grads", "out", "in"))
    order = Order()
    hold = lambda value, *tokens: lax.optimization_barrier((value, tokens))[0]
    product_of = lambda name, by_hidden: lambda r, acts: weights(name, r, acts, width, by_hidden)

    size = tokens.shape[0]
    half = size // 2
    zeros = (0,) * 6
    own, pair, clock = order(lambda r: prepare_rows(*picks, r, experts), tokens)
    near = rows.line(own, rows.near)
    far = rows.line(own, rows.far)
    sibling_pair = rows.sibling(pair)
    gate_mat, up_mat, down_mat = order(load, gate_local, up_local, down_local)
    sibling_pair = hold(sibling_pair, down_mat)
    line_pair = order(lambda *p: join(half, p, zeros[:2]), near, far, also=sibling_pair)
    last = rows.line(hold(far, line_pair), rows.near)
    across_pair = rows.across(line_pair)
    own, grads_pair = order(prepare_grads, grad_out)
    far = grads.line(own, grads.far)
    last_across = rows.across(last)
    far = hold(far, last)
    grads_last = grads.line(far, grads.near)
    far_across = grads.across(far)
    near = grads.line(hold(grads_pair, last), grads.near)
    clock = order(lambda c: space(c, 2 * 10**9), clock, also=far)
    across_pair, last_across = hold((across_pair, last_across), clock)
    rest = order(
        lambda *p: join(half, p, (0, half, 0, half, 0, 0)),
        line_pair,
        line_pair,
        across_pair,
        across_pair,
        last,
        last_across,
    )
    own_rows = (pair, rest)
    sibling_rest = rows.sibling(rest)
    clock = order(space, clock)
    other_rows = (sibling_pair, hold(sibling_rest, clock))
    hidden = lambda *r: hidden_units(r, gate_mat, up_mat, experts)
    own_gate, own_up, own_act = order(hidden, *own_rows)
    grads_last, far_across = hold((grads_last, far_across), own_act)
    last_across = grads.across(grads_last)
    grads_sibling = grads.sibling(hold(grads_pair, own_act))
    other_gate, other_up, other_act = order(hidden, *other_rows, also=(grads_last, far_across))
    sent, kept = order(outputs_of, other_act, down_mat)
    received, kept = outs.sibling(sent), outs.sibling(kept)
    out_send, out_keep = order(outputs_of, own_act, down_mat)
    clock = order(space, clock, also=(near, last_across, grads_sibling))
    received = hold(received, clock)
    out_sent, sent = order(
        lambda *s: outs.send(0, *s, (size, 3 * size)), out_send, received
    )
    arrived = outs.across(sent)
    rest = order(
        lambda *p: join(half, p, (0, 0, half, 0, 0, 0)),
        near,
        far,
        near,
        far_across,
        grads_last,
        last_across,
    )
    own_grads = (grads_pair, rest)
    other_grads = (grads_sibling, grads.sibling(rest))
    back = lambda g, r, *pre: hidden_grads(g, r, *pre, down_mat, experts)
    own_d_gate, own_d_up, own_shares = order(back, own_grads, own_rows, own_gate, own_up)
    other_d_gate, other_d_up, other_shares = order(
        back, other_grads, other_rows, other_gate, other_up
    )
    near_sent, far_sent, near_kept, far_kept = order(
        lambda *d: input_grads_of(2, *d, gate_mat, up_mat), other_d_gate, other_d_up, other_shares
    )
    far_received, far_kept = ins.sibling(far_sent), ins.sibling(far_kept)
    near_received, near_kept = ins.sibling(near_sent), ins.sibling(near_kept)
    in_send, in_keep = order(
        lambda *d: input_grads_of(1, *d, gate_mat, up_mat), own_d_gate, own_d_up, own_shares
    )
    far_sent, last_sent = order(
        lambda *s: ins.send(2 * size, *s, (size, size)), in_send, far_received
    )
    last_arrived = ins.across(last_sent)
    near_slots, far_slot = order(outs.slots, out_keep, kept, hold(arrived, far_sent))
    near_sums = outs.line(near_slots, outs.near)
    grad_down = order(product_of("grad_down", True), own_grads + other_grads, (own_act, other_act))
    slot = order(lambda *s: ins.slot(3, *s), in_keep, far_kept, last_arrived)
    last_sum = ins.line(slot, ins.near)
    far_arrived = ins.across(hold(far_sent, slot))
    out_arrived = outs.across(hold(out_sent, slot))
    own_sent, near_sent = order(
        lambda *s: ins.send(0, *s, (size, size)), in_send, near_received
    )
    far_slot = order(
        lambda *s: call(add_last_kernel, "add_last", s, jax.ShapeDtypeStruct(s[0].shape, s[0].dtype)),
        far_slot,
        near_sums,
    )
    far_sum = outs.line(far_slot, outs.far)
    grad_gate = order(product_of("grad_gate", False), own_rows + other_rows, (own_d_gate, other_d_gate))
    slot = order(
        lambda *s: ins.slot(2, *s), in_keep, far_kept, far_arrived, last_sum, also=out_arrived
    )
    far = ins.line(slot, ins.far)
    near_arrived = ins.across(hold(near_sent, slot))
    grad_up = order(product_of("grad_up", False), own_rows + other_rows, (own_d_up, other_d_up))
    slot = order(lambda *s: ins.slot(1, *s), in_keep, near_kept, near_arrived)
    near = ins.line(slot, ins.near)
    own_arrived = ins.across(hold(own_sent, slot))
    columns = jax.ShapeDtypeStruct((size, width // 2), jnp.bfloat16)
    output_cols = order(
        lambda *sums: call(finish_outputs_kernel, "finish_outputs", sums, columns),
        out_keep,
        kept,
        out_arrived,
        near_sums,
        far_sum,
    )
    clock = order(lambda c: space(c, 2 * 10**9), clock, also=far)
    near, own_arrived = hold((near, own_arrived), clock)
    input_cols, d_scores = order(
        lambda *sums: call(
            functools.partial(finish_inputs_kernel, experts),
            "finish_inputs",
            (*picks, clock, *sums),
            (columns, jax.ShapeDtypeStruct(picks[2].shape, jnp.float32)),
        ),
        in_keep,
        near_kept,
        own_arrived,
        far,
        near,
    )
    return output_cols, input_cols, d_scores.T, grad_gate[None], grad_up[None], grad_down[None]


def any_mesh(tokens, expert_ids, pick_counts, gate_scores, gate_local, up_local, down_local, grad_out):
    tok_rows = tokens.shape[0]
    pick_width = expert_ids.shape[1]
    experts = lax.axis_size("expert")
    active_mask = lax.broadcasted_iota(jnp.int32, (tok_rows, pick_width), 1) < pick_counts[:, None]
    active_float = active_mask.astype(jnp.float32)
    weighted = gate_scores * active_float
    score_sum = jnp.sum(weighted, axis=1, keepdims=True)
    gate_weights = weighted / score_sum
    picked = (expert_ids[:, :, None] == lax.broadcasted_iota(jnp.int32, (1, 1, experts), 2)).astype(
        jnp.float32
    )
    gate_table = jnp.sum(gate_weights[:, :, None] * picked, axis=1)

    def combine(partial):
        summed = lax.psum_scatter(partial, "expert", scatter_dimension=0, tiled=True)
        return lax.psum_scatter(summed, "helper", scatter_dimension=1, tiled=True)

    rows = lax.all_gather(tokens, "expert", tiled=True)
    tables = lax.all_gather(gate_table.T, "expert", tiled=False)
    gates = jnp.take(tables, lax.axis_index("expert"), axis=1).reshape(-1, 1)
    grads = lax.all_gather(grad_out, "expert", tiled=True)

    pre_gate = product(rows, gate_local)
    pre_up = product(rows, up_local)
    silu_value, silu_slope = silu_parts(pre_gate)
    hidden_act = silu_value * pre_up
    gated_act = (gates * hidden_act).astype(jnp.bfloat16)
    output_cols = combine(product(gated_act, down_local).astype(jnp.bfloat16))

    raw_act = right_transposed(grads, down_local)
    gate_part = jnp.sum(raw_act * hidden_act, axis=1)
    d_act = gates * raw_act
    d_pre_gate = (d_act * pre_up * silu_slope).astype(jnp.bfloat16)
    d_pre_up = (d_act * silu_value).astype(jnp.bfloat16)
    input_cols = combine(
        (right_transposed(d_pre_gate, gate_local) + right_transposed(d_pre_up, up_local)).astype(
            jnp.bfloat16
        )
    )

    gate_parts = lax.all_gather(
        gate_part.reshape(-1, tok_rows), ("expert", "helper"), tiled=False
    )
    own_parts = jnp.take(gate_parts, lax.axis_index("expert"), axis=1)
    by_expert = jnp.sum(own_parts.reshape(experts, -1, tok_rows), axis=1).T
    d_gates = jnp.sum(by_expert[:, None, :] * picked, axis=2)
    d_scores = (
        active_float
        * (d_gates - jnp.sum(gate_weights * d_gates, axis=1, keepdims=True))
        / score_sum
    )

    def over_dp(whole, dimension):
        return lax.psum_scatter(
            whole.astype(jnp.bfloat16), "dp", scatter_dimension=dimension, tiled=True
        )[None]

    grad_w_gate = over_dp(transposed_product(rows, d_pre_gate), 0)
    grad_w_up = over_dp(transposed_product(rows, d_pre_up), 0)
    grad_w_down = over_dp(transposed_product(gated_act, grads), 1)
    return output_cols, input_cols, d_scores, grad_w_gate, grad_w_up, grad_w_down


def on_device(tokens, expert_ids, pick_counts, gate_scores, w_gate, w_up, w_down, grad_out):
    sizes = tuple(lax.axis_size(axis) for axis in ("expert", "helper", "dp"))
    layer = lined_up if sizes == (8, 2, 1) else any_mesh
    return layer(
        tokens, expert_ids, pick_counts, gate_scores, w_gate[0], w_up[0], w_down[0], grad_out
    )


def solution(mesh):
    in_specs = (
        P(("groups", "expert", "dp"), None),
        P(("groups", "expert", "dp"), None),
        P(("groups", "expert", "dp")),
        P(("groups", "expert", "dp"), None),
        P("expert", None, "helper"),
        P("expert", None, "helper"),
        P("expert", "helper", None),
        P(("groups", "expert", "dp"), None),
    )
    out_specs = (
        P(("groups", "expert", "dp"), "helper"),
        P(("groups", "expert", "dp"), "helper"),
        P(("groups", "expert", "dp"), None),
        P(("groups", "expert"), "dp", "helper"),
        P(("groups", "expert"), "dp", "helper"),
        P(("groups", "expert"), "helper", "dp"),
    )
    return jax.shard_map(
        on_device, mesh=mesh, in_specs=in_specs, out_specs=out_specs, check_vma=False
    )
```

```python
import functools

import jax
import jax.numpy as jnp
from jax import lax
from jax.experimental import pallas as pl
from jax.experimental.pallas import tpu as pltpu
from jax.sharding import PartitionSpec as P

LANES = 128
VMEM = pl.BlockSpec(memory_space=pltpu.VMEM)


def product(first_mat, second_mat):
    return jnp.dot(first_mat, second_mat, preferred_element_type=jnp.float32)


def transposed_product(first_mat, second_mat):
    return lax.dot_general(
        first_mat, second_mat, (((0,), (0,)), ((), ())), preferred_element_type=jnp.float32
    )


def right_transposed(first_mat, second_mat):
    return lax.dot_general(
        first_mat, second_mat, (((1,), (1,)), ((), ())), preferred_element_type=jnp.float32
    )


def silu_parts(argument):
    sigmoid_part = jax.nn.sigmoid(argument)
    return argument * sigmoid_part, sigmoid_part * (1.0 + argument * (1.0 - sigmoid_part))


def total_of(terms):
    return functools.reduce(jnp.add, terms)


def call(kernel, name, operands, out_shape, scratch=(), flops=0, moved=0, mebibytes=12):
    return pl.pallas_call(
        kernel,
        out_shape=out_shape,
        in_specs=[VMEM] * len(operands),
        out_specs=jax.tree.map(lambda _: VMEM, out_shape),
        scratch_shapes=scratch,
        compiler_params=pltpu.CompilerParams(vmem_limit_bytes=mebibytes * 2**20),
        cost_estimate=pl.CostEstimate(
            flops=flops, bytes_accessed=moved, transcendentals=0
        ),
        name=name,
    )(*operands)


def half_at(array, which):
    rows = array.shape[0] // 2
    return array[which * rows : (which + 1) * rows]


def swap_halves(array):
    return jnp.concatenate([half_at(array, 1), half_at(array, 0)], axis=0)


def hi_lo(values, is_high):
    high = values.astype(jnp.bfloat16).astype(jnp.float32)
    return jnp.where(is_high, high, values - high).astype(jnp.bfloat16)


def gate_rows(counts, scores):
    used = [(counts > k).astype(jnp.float32) for k in range(scores.shape[0])]
    weighted = [scores[k : k + 1] * used[k] for k in range(scores.shape[0])]
    score_sum = total_of(weighted)
    return [w / score_sum for w in weighted], used, score_sum


def prepare_rows_kernel(experts, *refs):
    sources, (own, pair, clock), targets, sems = refs[:4], refs[4:7], refs[7:11], refs[11]
    ids, counts, scores, rows = targets
    copies = [
        pltpu.make_async_copy(source, target, sems.at[i])
        for i, (source, target) in enumerate(zip(sources, targets))
    ]
    for copy in copies:
        copy.start()
    for copy in copies:
        copy.wait()
    total, width = rows.shape
    clock[...] = jnp.zeros_like(clock)
    lane = lax.broadcasted_iota(jnp.int32, (LANES, total), 0)
    gates, _, _ = gate_rows(counts[...], scores[...])
    table = jnp.zeros((LANES, total), jnp.float32)
    for k, gate in enumerate(gates):
        named = ids[k : k + 1, :]
        table = table + jnp.where((lane == named) | (lane == named + experts), gate, 0.0)
    table = table.T
    table = hi_lo(table, lax.broadcasted_iota(jnp.int32, table.shape, 1) < experts)
    for side in range(2):

        @pl.when(lax.axis_index("helper") == side)
        def _(side=side):
            own[:, :width] = half_at(rows, side)
            own[:, width:] = half_at(table, side)
            for i, which in enumerate((side, 1 - side)):
                here = slice(i * total // 2, (i + 1) * total // 2)
                pair[here, :width] = half_at(rows, which)
                pair[here, width:] = half_at(table, which)


def prepare_rows(ids, counts, scores, rows, experts):
    total, width = rows.shape
    piece = jax.ShapeDtypeStruct((total // 2, width + LANES), jnp.bfloat16)
    operands = (ids, counts, scores, rows)
    return pl.pallas_call(
        functools.partial(prepare_rows_kernel, experts),
        out_shape=(
            piece,
            jax.ShapeDtypeStruct((total, width + LANES), jnp.bfloat16),
            jax.ShapeDtypeStruct((8, LANES), jnp.float32),
        ),
        in_specs=[pl.BlockSpec(memory_space=pltpu.HBM)] * len(operands),
        out_specs=(VMEM,) * 3,
        scratch_shapes=[
            *(pltpu.VMEM(operand.shape, operand.dtype) for operand in operands),
            pltpu.SemaphoreType.DMA((len(operands),)),
        ],
        compiler_params=pltpu.CompilerParams(vmem_limit_bytes=8 * 2**20),
        name="prepare_rows",
    )(*(pltpu.with_memory_space_constraint(operand, pltpu.HBM) for operand in operands))


def prepare_grads_kernel(rows, own, pair):
    half = rows.shape[0] // 2
    for side in range(2):

        @pl.when(lax.axis_index("helper") == side)
        def _(side=side):
            own[...] = half_at(rows, side)
            pair[:half, :] = half_at(rows, side)
            pair[half:, :] = half_at(rows, 1 - side)


def prepare_grads(rows):
    total, width = rows.shape
    piece = jax.ShapeDtypeStruct((total // 2, width), jnp.bfloat16)
    return call(
        prepare_grads_kernel,
        "prepare_grads",
        (rows,),
        (piece, jax.ShapeDtypeStruct(rows.shape, jnp.bfloat16)),
    )


def join_kernel(starts, rows, *refs):
    for i, start in enumerate(starts):
        refs[-1][i * rows : (i + 1) * rows, :] = refs[i][start : start + rows, :]


def join(rows, pieces, starts):
    shape = jax.ShapeDtypeStruct((len(pieces) * rows, pieces[0].shape[1]), pieces[0].dtype)
    return call(functools.partial(join_kernel, starts, rows), "join", pieces, shape)


def parts_of(pair, rest):
    rows = pair.shape[0]
    half = rows // 2
    parts = [(pair, 0, rows)]
    for slot in range(2):
        parts = parts + [(rest, slot * half, half), (rest, rows + slot * half, half)]
    return parts + [(rest, 2 * rows, rows)]


def lay_out(pieces, target, columns, at=0):
    for piece, start, rows in parts_of(*pieces):
        target[at : at + rows, :] = piece[start : start + rows, columns]
        at = at + rows


def gate_column(experts, pieces, width):
    table = jnp.concatenate(
        [piece[start : start + rows, width:] for piece, start, rows in parts_of(*pieces)], axis=0
    )
    lane = lax.broadcasted_iota(jnp.int32, table.shape, 1)
    expert = lax.axis_index("expert")
    mine = (lane == expert) | (lane == expert + experts)
    return jnp.sum(jnp.where(mine, table.astype(jnp.float32), 0.0), axis=1, keepdims=True)


def hidden_kernel(experts, tile, *refs):
    pieces, refs = refs[:2], refs[2:]
    gate_mat, up_mat, pre_gate, pre_up, gated, rows = refs
    width = rows.shape[1]
    lay_out(pieces, rows, slice(0, width))
    gate = gate_column(experts, pieces, width)
    for start in range(0, gated.shape[1], tile):
        columns = slice(start, start + tile)
        gate_part = product(rows[...], gate_mat[:, columns])
        up_part = product(rows[...], up_mat[:, columns])
        silu_value, _ = silu_parts(gate_part)
        pre_gate[:, columns] = gate_part
        pre_up[:, columns] = up_part
        gated[:, columns] = (gate * silu_value * up_part).astype(jnp.bfloat16)


def hidden_units(pieces, gate_mat, up_mat, experts):
    width, hidden = gate_mat.shape
    total = 4 * pieces[0].shape[0]
    pre = jax.ShapeDtypeStruct((total, hidden), jnp.float32)
    act = jax.ShapeDtypeStruct((total, hidden), jnp.bfloat16)
    return call(
        functools.partial(hidden_kernel, experts, 256),
        "hidden_units",
        (*pieces, gate_mat, up_mat),
        (pre, pre, act),
        [pltpu.VMEM((total, width), jnp.bfloat16)],
        flops=4 * total * width * hidden,
        mebibytes=12,
    )


def outputs_kernel(tile, gated, down_mat, *sums):
    half = sums[0].shape[1]
    for keep in range(2):
        side = lax.axis_index("helper")
        side = side if keep else 1 - side
        for start in range(0, half, tile):
            here = pl.ds(pl.multiple_of(side * half + start, tile), tile)
            out = product(gated[...], down_mat[:, here])
            sums[keep][:, start : start + tile] = out.astype(jnp.bfloat16)


def outputs_of(gated, down_mat):
    total, hidden = gated.shape
    width = down_mat.shape[1]
    sums = jax.ShapeDtypeStruct((total, width // 2), jnp.bfloat16)
    return call(
        functools.partial(outputs_kernel, 256), "outputs", (gated, down_mat), (sums, sums)
    )


def hidden_grads_kernel(experts, tile, *refs):
    pieces, gate_pieces, refs = refs[:2], refs[2:4], refs[4:]
    down_mat, pre_gate, pre_up, d_gate, d_up, shares_out, grads = refs
    total, width = grads.shape
    lay_out(pieces, grads, slice(0, width))
    gate = gate_column(experts, gate_pieces, width)
    shares = []
    for start in range(0, d_gate.shape[1], tile):
        columns = slice(start, start + tile)
        raw = right_transposed(grads[...], down_mat[columns, :])
        up_part = pre_up[:, columns]
        silu_value, silu_slope = silu_parts(pre_gate[:, columns])
        share = raw * silu_value * up_part
        shares = shares + [share[:, c : c + LANES] for c in range(0, tile, LANES)]
        d_act = gate * raw
        d_gate[:, columns] = (d_act * up_part * silu_slope).astype(jnp.bfloat16)
        d_up[:, columns] = (d_act * silu_value).astype(jnp.bfloat16)
    value = jnp.sum(total_of(shares), axis=1, keepdims=True)
    lane = lax.broadcasted_iota(jnp.int32, (total, LANES), 1)
    high = 2 * lax.axis_index("expert") + lax.axis_index("helper")
    value = jnp.where((lane == high) | (lane == high + 2 * experts), value, 0.0)
    shares_out[...] = hi_lo(value, lane < 2 * experts)


def hidden_grads(pieces, gate_pieces, pre_gate, pre_up, down_mat, experts):
    hidden, width = down_mat.shape
    total = pre_gate.shape[0]
    act = jax.ShapeDtypeStruct((total, hidden), jnp.bfloat16)
    return call(
        functools.partial(hidden_grads_kernel, experts, 256),
        "hidden_grads",
        (*pieces, *gate_pieces, down_mat, pre_gate, pre_up),
        (act, act, jax.ShapeDtypeStruct((total, LANES), jnp.bfloat16)),
        [pltpu.VMEM((total, width), jnp.bfloat16)],
        mebibytes=12,
    )


def input_grads_kernel(tile, d_gate, d_up, shares, gate_mat, up_mat, *sums):
    half = sums[0].shape[1] - LANES
    split = len(sums) // 2

    def put(keep, columns, values):
        rows = values.shape[0] // split
        for i in range(split):
            sums[split * keep + i][:, columns] = values[i * rows : (i + 1) * rows]

    for keep in range(2):
        put(keep, slice(half, half + LANES), shares[...])
        side = lax.axis_index("helper")
        side = side if keep else 1 - side
        for start in range(0, half, tile):
            here = pl.ds(pl.multiple_of(side * half + start, tile), tile)
            back = right_transposed(d_gate[...], gate_mat[here, :])
            back = back + right_transposed(d_up[...], up_mat[here, :])
            put(keep, slice(start, start + tile), back.astype(jnp.bfloat16))


def input_grads_of(split, d_gate, d_up, shares, gate_mat, up_mat):
    width, hidden = gate_mat.shape
    total = d_gate.shape[0]
    sums = jax.ShapeDtypeStruct((total // split, width // 2 + LANES), jnp.bfloat16)
    return call(
        functools.partial(input_grads_kernel, 256),
        "input_grads",
        (d_gate, d_up, shares, gate_mat, up_mat),
        (sums,) * (2 * split),
        mebibytes=12,
    )


def weights_kernel(width, tile, *refs):
    pieces, (first, second, grad, rows, acts, made, sems) = refs[:4], refs[4:]
    total = first.shape[0]
    lay_out(pieces[:2], rows, slice(0, width))
    lay_out(pieces[2:], rows, slice(0, width), total)
    acts[:total, :] = first[...]
    acts[total:, :] = second[...]
    left, right = (acts, rows) if grad.shape[1] == width else (rows, acts)

    def copy(step):
        here = pl.ds(pl.multiple_of(step * tile, tile), tile)
        return pltpu.make_async_copy(made.at[here, :], grad.at[here, :], sems.at[step])

    steps = grad.shape[0] // tile

    @pl.loop(0, steps, unroll=2)
    def _(step):
        here = pl.ds(pl.multiple_of(step * tile, tile), tile)
        made[here, :] = transposed_product(left[:, here], right[...]).astype(jnp.bfloat16)
        copy(step).start()

    @pl.loop(0, steps)
    def _(step):
        copy(step).wait()


def weights(name, pieces, acts, width, by_hidden):
    rows, hidden = acts[0].shape
    shape = (hidden, width) if by_hidden else (width, hidden)
    operands = (*pieces, *acts)
    return pl.pallas_call(
        functools.partial(weights_kernel, width, 512),
        out_shape=jax.ShapeDtypeStruct(shape, jnp.bfloat16),
        in_specs=[VMEM] * len(operands),
        out_specs=pl.BlockSpec(memory_space=pl.ANY),
        scratch_shapes=[
            pltpu.VMEM((2 * rows, width), jnp.bfloat16),
            pltpu.VMEM((2 * rows, hidden), jnp.bfloat16),
            pltpu.VMEM(shape, jnp.bfloat16),
            pltpu.SemaphoreType.DMA((shape[0] // 512,)),
        ],
        compiler_params=pltpu.CompilerParams(vmem_limit_bytes=16 * 2**20),
        cost_estimate=pl.CostEstimate(
            flops=4 * rows * width * hidden, bytes_accessed=0, transcendentals=0
        ),
        name=name,
    )(*operands)


def send_kernel(first, own, received, *sent):
    at = 0
    for target in sent:
        rows = target.shape[0]
        here = slice(first + at, first + at + rows)
        target[...] = own[here, :] + received[at : at + rows, :]
        at = at + rows


def slot_sum(own, received, arrived, slot, offset, received_slot):
    rows = LANES
    half = rows // 2
    here = slice(slot * rows, (slot + 1) * rows)
    other = arrived[offset : offset + rows, :].astype(jnp.float32)
    there = slice(received_slot * rows, (received_slot + 1) * rows)
    kept = own[here, :].astype(jnp.float32) + received[there, :].astype(jnp.float32)
    return kept + jnp.concatenate([other[half:], other[:half]], axis=0)


def slots_kernel(own, received, arrived, near_and_last, far_slot):
    rows = far_slot.shape[0]
    targets = (near_and_last.at[:rows], far_slot, near_and_last.at[rows:])
    for i, target in enumerate(targets):
        whole = slot_sum(own, received, arrived, i + 1, i * rows, i + 1)
        target[...] = whole.astype(target.dtype)


def add_last_kernel(far_slot, arrived, total):
    rows = far_slot.shape[0]
    total[...] = far_slot[...] + arrived[rows:, :]


def slot_kernel(slot, own, received, arrived, *refs):
    whole = slot_sum(own, received, arrived, slot, 0, slot % 2)
    if len(refs) > 1:
        whole = whole + refs[0][...].astype(jnp.float32)
    refs[-1][...] = whole.astype(refs[-1].dtype)


def finish_outputs_kernel(own, received, arrived, near_and_last, far, columns):
    near = near_and_last[: far.shape[0], :]
    whole = slot_sum(own, received, arrived, 0, 0, 0)
    whole = total_of([whole, near.astype(jnp.float32), far[...].astype(jnp.float32)])
    whole = jnp.where(lax.axis_index("helper") == 0, whole, swap_halves(whole))
    columns[...] = whole.astype(jnp.bfloat16)


def finish_inputs_kernel(experts, ids, counts, scores, clock, own, received, arrived, *refs):
    columns, d_scores = refs[-2:]
    width = columns.shape[1]
    whole = slot_sum(own, received, arrived, 0, 0, 0)
    whole = total_of([whole] + [ref[...].astype(jnp.float32) for ref in refs[:-2]])
    whole = jnp.where(lax.axis_index("helper") == 0, whole, swap_halves(whole))
    columns[...] = whole[:, :width].astype(jnp.bfloat16)
    table = whole[:, width:].T
    lane = lax.broadcasted_iota(jnp.int32, table.shape, 0)
    named_by = (lane % (2 * experts)) // 2
    gates, used, score_sum = gate_rows(counts[...], scores[...])
    d_gates = []
    for k in range(len(gates)):
        hit = (named_by == ids[k : k + 1, :]) & (lane < 4 * experts)
        d_gates.append(jnp.sum(jnp.where(hit, table, 0.0), axis=0, keepdims=True))
    mean = total_of([gate * d_gate for gate, d_gate in zip(gates, d_gates)])
    for k, d_gate in enumerate(d_gates):
        d_scores[k : k + 1, :] = used[k] * (d_gate - mean) / score_sum


class FourChips:
    def __init__(self, label):
        self.label = label
        both = lambda pairs: [(2 * a + c, 2 * b + c) for a, b in pairs for c in (0, 1)]
        self.near = both([(z, z ^ 1) for z in range(4)])
        self.far = both([(z, z ^ 2) for z in range(4)])
        self.cores = [(i, i ^ 1) for i in range(8)]
        self.sides = [(0, 1), (1, 0)]

    def line(self, array, pairs):
        with jax.named_scope(self.label + "_line"):
            return lax.ppermute(array, "expert", pairs)

    def sibling(self, array):
        with jax.named_scope(self.label + "_cores"):
            return lax.ppermute(array, "expert", self.cores)

    def across(self, array):
        with jax.named_scope(self.label + "_across"):
            return lax.ppermute(array, "helper", self.sides)

    def send(self, first, own, received, parts):
        shape = lambda rows: jax.ShapeDtypeStruct((rows, received.shape[1]), own.dtype)
        return call(
            functools.partial(send_kernel, first),
            self.label + "_send",
            (own, received),
            tuple(shape(rows) for rows in parts),
        )

    def slots(self, own, received, arrived):
        rows, columns = arrived.shape
        shape = lambda slots: jax.ShapeDtypeStruct((slots * rows // 3, columns), arrived.dtype)
        return call(
            slots_kernel,
            self.label + "_slots",
            (own, received, arrived),
            (shape(2), shape(1)),
        )

    def slot(self, which, own, received, arrived, *others):
        return call(
            functools.partial(slot_kernel, which),
            self.label + "_slot",
            (own, received, arrived, *others),
            jax.ShapeDtypeStruct(arrived.shape, arrived.dtype),
        )


def load_kernel(*refs):
    sources, targets, sems = refs[:3], refs[3:6], refs[6]
    copies = [
        pltpu.make_async_copy(source, target, sems.at[i])
        for i, (source, target) in enumerate(zip(sources, targets))
    ]
    for copy in copies:
        copy.start()
    for copy in copies:
        copy.wait()


def load(*mats):
    return pl.pallas_call(
        load_kernel,
        out_shape=tuple(jax.ShapeDtypeStruct(mat.shape, mat.dtype) for mat in mats),
        in_specs=[pl.BlockSpec(memory_space=pltpu.HBM)] * len(mats),
        out_specs=(VMEM,) * len(mats),
        scratch_shapes=[pltpu.SemaphoreType.DMA((len(mats),))],
        compiler_params=pltpu.CompilerParams(vmem_limit_bytes=2**20),
        name="load",
    )(*(pltpu.with_memory_space_constraint(mat, pltpu.HBM) for mat in mats))


def space(clock, flops=36 * 10**9):
    return pl.pallas_call(
        lambda old, new: None,
        out_shape=jax.ShapeDtypeStruct(clock.shape, clock.dtype),
        in_specs=[pl.BlockSpec(memory_space=pl.ANY)],
        out_specs=pl.BlockSpec(memory_space=pl.ANY),
        input_output_aliases={0: 0},
        compiler_params=pltpu.CompilerParams(vmem_limit_bytes=2**20),
        cost_estimate=pl.CostEstimate(flops=flops, bytes_accessed=0, transcendentals=0),
        name="space",
    )(clock)


class Order:
    def __init__(self):
        self.token = None

    def __call__(self, function, *operands, also=()):
        if self.token is not None:
            operands, _ = lax.optimization_barrier((operands, (self.token, also)))
        result = function(*operands)
        self.token = result
        return result


def lined_up(tokens, expert_ids, pick_counts, gate_scores, gate_local, up_local, down_local, grad_out):
    experts = lax.axis_size("expert")
    width = gate_local.shape[0]
    picks = (expert_ids.T, pick_counts[None, :], gate_scores.T)
    rows, grads, outs, ins = (FourChips(label) for label in ("rows", "grads", "out", "in"))
    order = Order()
    hold = lambda value, *tokens: lax.optimization_barrier((value, tokens))[0]
    product_of = lambda name, by_hidden: lambda r, acts: weights(name, r, acts, width, by_hidden)

    size = tokens.shape[0]
    half = size // 2
    zeros = (0,) * 6
    own, pair, clock = order(lambda r: prepare_rows(*picks, r, experts), tokens)
    near = rows.line(own, rows.near)
    far = rows.line(own, rows.far)
    sibling_pair = rows.sibling(pair)
    gate_mat, up_mat, down_mat = order(load, gate_local, up_local, down_local)
    sibling_pair = hold(sibling_pair, down_mat)
    line_pair = order(lambda *p: join(half, p, zeros[:2]), near, far, also=sibling_pair)
    last = rows.line(hold(far, line_pair), rows.near)
    across_pair = rows.across(line_pair)
    own, grads_pair = order(prepare_grads, grad_out)
    far = grads.line(own, grads.far)
    last_across = rows.across(last)
    far = hold(far, last)
    grads_last = grads.line(far, grads.near)
    far_across = grads.across(far)
    near = grads.line(hold(grads_pair, last), grads.near)
    clock = order(lambda c: space(c, 2 * 10**9), clock, also=far)
    across_pair, last_across = hold((across_pair, last_across), clock)
    rest = order(
        lambda *p: join(half, p, (0, half, 0, half, 0, 0)),
        line_pair,
        line_pair,
        across_pair,
        across_pair,
        last,
        last_across,
    )
    own_rows = (pair, rest)
    sibling_rest = rows.sibling(rest)
    clock = order(space, clock)
    other_rows = (sibling_pair, hold(sibling_rest, clock))
    hidden = lambda *r: hidden_units(r, gate_mat, up_mat, experts)
    own_gate, own_up, own_act = order(hidden, *own_rows)
    grads_last, far_across = hold((grads_last, far_across), own_act)
    last_across = grads.across(grads_last)
    grads_sibling = grads.sibling(hold(grads_pair, own_act))
    other_gate, other_up, other_act = order(hidden, *other_rows, also=(grads_last, far_across))
    sent, kept = order(outputs_of, other_act, down_mat)
    received, kept = outs.sibling(sent), outs.sibling(kept)
    out_send, out_keep = order(outputs_of, own_act, down_mat)
    clock = order(space, clock, also=(near, last_across, grads_sibling))
    received = hold(received, clock)
    out_sent, sent = order(
        lambda *s: outs.send(0, *s, (size, 3 * size)), out_send, received
    )
    arrived = outs.across(sent)
    rest = order(
        lambda *p: join(half, p, (0, 0, half, 0, 0, 0)),
        near,
        far,
        near,
        far_across,
        grads_last,
        last_across,
    )
    own_grads = (grads_pair, rest)
    other_grads = (grads_sibling, grads.sibling(rest))
    back = lambda g, r, *pre: hidden_grads(g, r, *pre, down_mat, experts)
    own_d_gate, own_d_up, own_shares = order(back, own_grads, own_rows, own_gate, own_up)
    other_d_gate, other_d_up, other_shares = order(
        back, other_grads, other_rows, other_gate, other_up
    )
    near_sent, far_sent, near_kept, far_kept = order(
        lambda *d: input_grads_of(2, *d, gate_mat, up_mat), other_d_gate, other_d_up, other_shares
    )
    far_received, far_kept = ins.sibling(far_sent), ins.sibling(far_kept)
    near_received, near_kept = ins.sibling(near_sent), ins.sibling(near_kept)
    in_send, in_keep = order(
        lambda *d: input_grads_of(1, *d, gate_mat, up_mat), own_d_gate, own_d_up, own_shares
    )
    far_sent, last_sent = order(
        lambda *s: ins.send(2 * size, *s, (size, size)), in_send, far_received
    )
    last_arrived = ins.across(last_sent)
    near_slots, far_slot = order(outs.slots, out_keep, kept, hold(arrived, far_sent))
    near_sums = outs.line(near_slots, outs.near)
    grad_down = order(product_of("grad_down", True), own_grads + other_grads, (own_act, other_act))
    slot = order(lambda *s: ins.slot(3, *s), in_keep, far_kept, last_arrived)
    last_sum = ins.line(slot, ins.near)
    far_arrived = ins.across(hold(far_sent, slot))
    out_arrived = outs.across(hold(out_sent, slot))
    own_sent, near_sent = order(
        lambda *s: ins.send(0, *s, (size, size)), in_send, near_received
    )
    far_slot = order(
        lambda *s: call(add_last_kernel, "add_last", s, jax.ShapeDtypeStruct(s[0].shape, s[0].dtype)),
        far_slot,
        near_sums,
    )
    far_sum = outs.line(far_slot, outs.far)
    grad_gate = order(product_of("grad_gate", False), own_rows + other_rows, (own_d_gate, other_d_gate))
    slot = order(
        lambda *s: ins.slot(2, *s), in_keep, far_kept, far_arrived, last_sum, also=out_arrived
    )
    far = ins.line(slot, ins.far)
    near_arrived = ins.across(hold(near_sent, slot))
    grad_up = order(product_of("grad_up", False), own_rows + other_rows, (own_d_up, other_d_up))
    slot = order(lambda *s: ins.slot(1, *s), in_keep, near_kept, near_arrived)
    near = ins.line(slot, ins.near)
    own_arrived = ins.across(hold(own_sent, slot))
    columns = jax.ShapeDtypeStruct((size, width // 2), jnp.bfloat16)
    output_cols = order(
        lambda *sums: call(finish_outputs_kernel, "finish_outputs", sums, columns),
        out_keep,
        kept,
        out_arrived,
        near_sums,
        far_sum,
    )
    clock = order(lambda c: space(c, 2 * 10**9), clock, also=far)
    near, own_arrived = hold((near, own_arrived), clock)
    input_cols, d_scores = order(
        lambda *sums: call(
            functools.partial(finish_inputs_kernel, experts),
            "finish_inputs",
            (*picks, clock, *sums),
            (columns, jax.ShapeDtypeStruct(picks[2].shape, jnp.float32)),
        ),
        in_keep,
        near_kept,
        own_arrived,
        far,
        near,
    )
    return output_cols, input_cols, d_scores.T, grad_gate[None], grad_up[None], grad_down[None]


def any_mesh(tokens, expert_ids, pick_counts, gate_scores, gate_local, up_local, down_local, grad_out):
    tok_rows = tokens.shape[0]
    pick_width = expert_ids.shape[1]
    experts = lax.axis_size("expert")
    active_mask = lax.broadcasted_iota(jnp.int32, (tok_rows, pick_width), 1) < pick_counts[:, None]
    active_float = active_mask.astype(jnp.float32)
    weighted = gate_scores * active_float
    score_sum = jnp.sum(weighted, axis=1, keepdims=True)
    gate_weights = weighted / score_sum
    picked = (expert_ids[:, :, None] == lax.broadcasted_iota(jnp.int32, (1, 1, experts), 2)).astype(
        jnp.float32
    )
    gate_table = jnp.sum(gate_weights[:, :, None] * picked, axis=1)

    def combine(partial):
        summed = lax.psum_scatter(partial, "expert", scatter_dimension=0, tiled=True)
        return lax.psum_scatter(summed, "helper", scatter_dimension=1, tiled=True)

    rows = lax.all_gather(tokens, "expert", tiled=True)
    tables = lax.all_gather(gate_table.T, "expert", tiled=False)
    gates = jnp.take(tables, lax.axis_index("expert"), axis=1).reshape(-1, 1)
    grads = lax.all_gather(grad_out, "expert", tiled=True)

    pre_gate = product(rows, gate_local)
    pre_up = product(rows, up_local)
    silu_value, silu_slope = silu_parts(pre_gate)
    hidden_act = silu_value * pre_up
    gated_act = (gates * hidden_act).astype(jnp.bfloat16)
    output_cols = combine(product(gated_act, down_local).astype(jnp.bfloat16))

    raw_act = right_transposed(grads, down_local)
    gate_part = jnp.sum(raw_act * hidden_act, axis=1)
    d_act = gates * raw_act
    d_pre_gate = (d_act * pre_up * silu_slope).astype(jnp.bfloat16)
    d_pre_up = (d_act * silu_value).astype(jnp.bfloat16)
    input_cols = combine(
        (right_transposed(d_pre_gate, gate_local) + right_transposed(d_pre_up, up_local)).astype(
            jnp.bfloat16
        )
    )

    gate_parts = lax.all_gather(
        gate_part.reshape(-1, tok_rows), ("expert", "helper"), tiled=False
    )
    own_parts = jnp.take(gate_parts, lax.axis_index("expert"), axis=1)
    by_expert = jnp.sum(own_parts.reshape(experts, -1, tok_rows), axis=1).T
    d_gates = jnp.sum(by_expert[:, None, :] * picked, axis=2)
    d_scores = (
        active_float
        * (d_gates - jnp.sum(gate_weights * d_gates, axis=1, keepdims=True))
        / score_sum
    )

    def over_dp(whole, dimension):
        return lax.psum_scatter(
            whole.astype(jnp.bfloat16), "dp", scatter_dimension=dimension, tiled=True
        )[None]

    grad_w_gate = over_dp(transposed_product(rows, d_pre_gate), 0)
    grad_w_up = over_dp(transposed_product(rows, d_pre_up), 0)
    grad_w_down = over_dp(transposed_product(gated_act, grads), 1)
    return output_cols, input_cols, d_scores, grad_w_gate, grad_w_up, grad_w_down


def on_device(tokens, expert_ids, pick_counts, gate_scores, w_gate, w_up, w_down, grad_out):
    sizes = tuple(lax.axis_size(axis) for axis in ("expert", "helper", "dp"))
    layer = lined_up if sizes == (8, 2, 1) else any_mesh
    return layer(
        tokens, expert_ids, pick_counts, gate_scores, w_gate[0], w_up[0], w_down[0], grad_out
    )


def solution(mesh):
    in_specs = (
        P(("groups", "expert", "dp"), None),
        P(("groups", "expert", "dp"), None),
        P(("groups", "expert", "dp")),
        P(("groups", "expert", "dp"), None),
        P("expert", None, "helper"),
        P("expert", None, "helper"),
        P("expert", "helper", None),
        P(("groups", "expert", "dp"), None),
    )
    out_specs = (
        P(("groups", "expert", "dp"), "helper"),
        P(("groups", "expert", "dp"), "helper"),
        P(("groups", "expert", "dp"), None),
        P(("groups", "expert"), "dp", "helper"),
        P(("groups", "expert"), "dp", "helper"),
        P(("groups", "expert"), "helper", "dp"),
    )
    return jax.shard_map(
        on_device, mesh=mesh, in_specs=in_specs, out_specs=out_specs, check_vma=False
    )
```

```python
import functools

import jax
import jax.numpy as jnp
from jax import lax
from jax.experimental import pallas as pl
from jax.experimental.pallas import tpu as pltpu
from jax.sharding import PartitionSpec as P

LANES = 128
VMEM = pl.BlockSpec(memory_space=pltpu.VMEM)


def product(first_mat, second_mat):
    return jnp.dot(first_mat, second_mat, preferred_element_type=jnp.float32)


def transposed_product(first_mat, second_mat):
    return lax.dot_general(
        first_mat, second_mat, (((0,), (0,)), ((), ())), preferred_element_type=jnp.float32
    )


def right_transposed(first_mat, second_mat):
    return lax.dot_general(
        first_mat, second_mat, (((1,), (1,)), ((), ())), preferred_element_type=jnp.float32
    )


def silu_parts(argument):
    sigmoid_part = jax.nn.sigmoid(argument)
    return argument * sigmoid_part, sigmoid_part * (1.0 + argument * (1.0 - sigmoid_part))


def total_of(terms):
    return functools.reduce(jnp.add, terms)


def call(kernel, name, operands, out_shape, scratch=(), flops=0, moved=0, mebibytes=12):
    return pl.pallas_call(
        kernel,
        out_shape=out_shape,
        in_specs=[VMEM] * len(operands),
        out_specs=jax.tree.map(lambda _: VMEM, out_shape),
        scratch_shapes=scratch,
        compiler_params=pltpu.CompilerParams(vmem_limit_bytes=mebibytes * 2**20),
        cost_estimate=pl.CostEstimate(
            flops=flops, bytes_accessed=moved, transcendentals=0
        ),
        name=name,
    )(*operands)


def half_at(array, which):
    rows = array.shape[0] // 2
    return array[which * rows : (which + 1) * rows]


def swap_halves(array):
    return jnp.concatenate([half_at(array, 1), half_at(array, 0)], axis=0)


def hi_lo(values, is_high):
    high = values.astype(jnp.bfloat16).astype(jnp.float32)
    return jnp.where(is_high, high, values - high).astype(jnp.bfloat16)


def gate_rows(counts, scores):
    used = [(counts > k).astype(jnp.float32) for k in range(scores.shape[0])]
    weighted = [scores[k : k + 1] * used[k] for k in range(scores.shape[0])]
    score_sum = total_of(weighted)
    return [w / score_sum for w in weighted], used, score_sum


def prepare_rows_kernel(experts, *refs):
    sources, (own, pair, clock), targets, sems = refs[:4], refs[4:7], refs[7:11], refs[11]
    ids, counts, scores, rows = targets
    copies = [
        pltpu.make_async_copy(source, target, sems.at[i])
        for i, (source, target) in enumerate(zip(sources, targets))
    ]
    for copy in copies:
        copy.start()
    for copy in copies:
        copy.wait()
    total, width = rows.shape
    clock[...] = jnp.zeros_like(clock)
    lane = lax.broadcasted_iota(jnp.int32, (LANES, total), 0)
    gates, _, _ = gate_rows(counts[...], scores[...])
    table = jnp.zeros((LANES, total), jnp.float32)
    for k, gate in enumerate(gates):
        named = ids[k : k + 1, :]
        table = table + jnp.where((lane == named) | (lane == named + experts), gate, 0.0)
    table = table.T
    table = hi_lo(table, lax.broadcasted_iota(jnp.int32, table.shape, 1) < experts)
    for side in range(2):

        @pl.when(lax.axis_index("helper") == side)
        def _(side=side):
            own[:, :width] = half_at(rows, side)
            own[:, width:] = half_at(table, side)
            for i, which in enumerate((side, 1 - side)):
                here = slice(i * total // 2, (i + 1) * total // 2)
                pair[here, :width] = half_at(rows, which)
                pair[here, width:] = half_at(table, which)


def prepare_rows(ids, counts, scores, rows, experts):
    total, width = rows.shape
    piece = jax.ShapeDtypeStruct((total // 2, width + LANES), jnp.bfloat16)
    operands = (ids, counts, scores, rows)
    return pl.pallas_call(
        functools.partial(prepare_rows_kernel, experts),
        out_shape=(
            piece,
            jax.ShapeDtypeStruct((total, width + LANES), jnp.bfloat16),
            jax.ShapeDtypeStruct((8, LANES), jnp.float32),
        ),
        in_specs=[pl.BlockSpec(memory_space=pltpu.HBM)] * len(operands),
        out_specs=(VMEM,) * 3,
        scratch_shapes=[
            *(pltpu.VMEM(operand.shape, operand.dtype) for operand in operands),
            pltpu.SemaphoreType.DMA((len(operands),)),
        ],
        compiler_params=pltpu.CompilerParams(vmem_limit_bytes=8 * 2**20),
        name="prepare_rows",
    )(*(pltpu.with_memory_space_constraint(operand, pltpu.HBM) for operand in operands))


def prepare_grads_kernel(rows, own, pair):
    half = rows.shape[0] // 2
    for side in range(2):

        @pl.when(lax.axis_index("helper") == side)
        def _(side=side):
            own[...] = half_at(rows, side)
            pair[:half, :] = half_at(rows, side)
            pair[half:, :] = half_at(rows, 1 - side)


def prepare_grads(rows):
    total, width = rows.shape
    piece = jax.ShapeDtypeStruct((total // 2, width), jnp.bfloat16)
    return call(
        prepare_grads_kernel,
        "prepare_grads",
        (rows,),
        (piece, jax.ShapeDtypeStruct(rows.shape, jnp.bfloat16)),
    )


def join_kernel(starts, rows, *refs):
    for i, start in enumerate(starts):
        refs[-1][i * rows : (i + 1) * rows, :] = refs[i][start : start + rows, :]


def join(rows, pieces, starts):
    shape = jax.ShapeDtypeStruct((len(pieces) * rows, pieces[0].shape[1]), pieces[0].dtype)
    return call(functools.partial(join_kernel, starts, rows), "join", pieces, shape)


def parts_of(pair, rest):
    rows = pair.shape[0]
    half = rows // 2
    parts = [(pair, 0, rows)]
    for slot in range(2):
        parts = parts + [(rest, slot * half, half), (rest, rows + slot * half, half)]
    return parts + [(rest, 2 * rows, rows)]


def lay_out(pieces, target, columns, at=0):
    for piece, start, rows in parts_of(*pieces):
        target[at : at + rows, :] = piece[start : start + rows, columns]
        at = at + rows


def gate_column(experts, pieces, width):
    table = jnp.concatenate(
        [piece[start : start + rows, width:] for piece, start, rows in parts_of(*pieces)], axis=0
    )
    lane = lax.broadcasted_iota(jnp.int32, table.shape, 1)
    expert = lax.axis_index("expert")
    mine = (lane == expert) | (lane == expert + experts)
    return jnp.sum(jnp.where(mine, table.astype(jnp.float32), 0.0), axis=1, keepdims=True)


def hidden_kernel(experts, tile, *refs):
    pieces, refs = refs[:2], refs[2:]
    gate_mat, up_mat, pre_gate, pre_up, gated, rows = refs
    width = rows.shape[1]
    lay_out(pieces, rows, slice(0, width))
    gate = gate_column(experts, pieces, width)
    for start in range(0, gated.shape[1], tile):
        columns = slice(start, start + tile)
        gate_part = product(rows[...], gate_mat[:, columns])
        up_part = product(rows[...], up_mat[:, columns])
        silu_value, _ = silu_parts(gate_part)
        pre_gate[:, columns] = gate_part
        pre_up[:, columns] = up_part
        gated[:, columns] = (gate * silu_value * up_part).astype(jnp.bfloat16)


def hidden_units(pieces, gate_mat, up_mat, experts):
    width, hidden = gate_mat.shape
    total = 4 * pieces[0].shape[0]
    pre = jax.ShapeDtypeStruct((total, hidden), jnp.float32)
    act = jax.ShapeDtypeStruct((total, hidden), jnp.bfloat16)
    return call(
        functools.partial(hidden_kernel, experts, 256),
        "hidden_units",
        (*pieces, gate_mat, up_mat),
        (pre, pre, act),
        [pltpu.VMEM((total, width), jnp.bfloat16)],
        flops=4 * total * width * hidden,
        mebibytes=12,
    )


def outputs_kernel(tile, gated, down_mat, *sums):
    half = sums[0].shape[1]
    for keep in range(2):
        side = lax.axis_index("helper")
        side = side if keep else 1 - side
        for start in range(0, half, tile):
            here = pl.ds(pl.multiple_of(side * half + start, tile), tile)
            out = product(gated[...], down_mat[:, here])
            sums[keep][:, start : start + tile] = out.astype(jnp.bfloat16)


def outputs_of(gated, down_mat):
    total, hidden = gated.shape
    width = down_mat.shape[1]
    sums = jax.ShapeDtypeStruct((total, width // 2), jnp.bfloat16)
    return call(
        functools.partial(outputs_kernel, 256), "outputs", (gated, down_mat), (sums, sums)
    )


def hidden_grads_kernel(experts, tile, *refs):
    pieces, gate_pieces, refs = refs[:2], refs[2:4], refs[4:]
    down_mat, pre_gate, pre_up, d_gate, d_up, shares_out, grads = refs
    total, width = grads.shape
    lay_out(pieces, grads, slice(0, width))
    gate = gate_column(experts, gate_pieces, width)
    shares = []
    for start in range(0, d_gate.shape[1], tile):
        columns = slice(start, start + tile)
        raw = right_transposed(grads[...], down_mat[columns, :])
        up_part = pre_up[:, columns]
        silu_value, silu_slope = silu_parts(pre_gate[:, columns])
        share = raw * silu_value * up_part
        shares = shares + [share[:, c : c + LANES] for c in range(0, tile, LANES)]
        d_act = gate * raw
        d_gate[:, columns] = (d_act * up_part * silu_slope).astype(jnp.bfloat16)
        d_up[:, columns] = (d_act * silu_value).astype(jnp.bfloat16)
    value = jnp.sum(total_of(shares), axis=1, keepdims=True)
    lane = lax.broadcasted_iota(jnp.int32, (total, LANES), 1)
    high = 2 * lax.axis_index("expert") + lax.axis_index("helper")
    value = jnp.where((lane == high) | (lane == high + 2 * experts), value, 0.0)
    shares_out[...] = hi_lo(value, lane < 2 * experts)


def hidden_grads(pieces, gate_pieces, pre_gate, pre_up, down_mat, experts):
    hidden, width = down_mat.shape
    total = pre_gate.shape[0]
    act = jax.ShapeDtypeStruct((total, hidden), jnp.bfloat16)
    return call(
        functools.partial(hidden_grads_kernel, experts, 256),
        "hidden_grads",
        (*pieces, *gate_pieces, down_mat, pre_gate, pre_up),
        (act, act, jax.ShapeDtypeStruct((total, LANES), jnp.bfloat16)),
        [pltpu.VMEM((total, width), jnp.bfloat16)],
        mebibytes=12,
    )


def input_grads_kernel(tile, d_gate, d_up, shares, gate_mat, up_mat, *sums):
    half = sums[0].shape[1] - LANES
    split = len(sums) // 2

    def put(keep, columns, values):
        rows = values.shape[0] // split
        for i in range(split):
            sums[split * keep + i][:, columns] = values[i * rows : (i + 1) * rows]

    for keep in range(2):
        put(keep, slice(half, half + LANES), shares[...])
        side = lax.axis_index("helper")
        side = side if keep else 1 - side
        for start in range(0, half, tile):
            here = pl.ds(pl.multiple_of(side * half + start, tile), tile)
            back = right_transposed(d_gate[...], gate_mat[here, :])
            back = back + right_transposed(d_up[...], up_mat[here, :])
            put(keep, slice(start, start + tile), back.astype(jnp.bfloat16))


def input_grads_of(split, d_gate, d_up, shares, gate_mat, up_mat):
    width, hidden = gate_mat.shape
    total = d_gate.shape[0]
    sums = jax.ShapeDtypeStruct((total // split, width // 2 + LANES), jnp.bfloat16)
    return call(
        functools.partial(input_grads_kernel, 256),
        "input_grads",
        (d_gate, d_up, shares, gate_mat, up_mat),
        (sums,) * (2 * split),
        mebibytes=12,
    )


def weights_kernel(width, tile, *refs):
    pieces, (first, second, grad, rows, acts, made, sems) = refs[:4], refs[4:]
    total = first.shape[0]
    lay_out(pieces[:2], rows, slice(0, width))
    lay_out(pieces[2:], rows, slice(0, width), total)
    acts[:total, :] = first[...]
    acts[total:, :] = second[...]
    left, right = (acts, rows) if grad.shape[1] == width else (rows, acts)

    def copy(step):
        here = pl.ds(pl.multiple_of(step * tile, tile), tile)
        return pltpu.make_async_copy(made.at[here, :], grad.at[here, :], sems.at[step])

    steps = grad.shape[0] // tile

    @pl.loop(0, steps, unroll=2)
    def _(step):
        here = pl.ds(pl.multiple_of(step * tile, tile), tile)
        made[here, :] = transposed_product(left[:, here], right[...]).astype(jnp.bfloat16)
        copy(step).start()

    @pl.loop(0, steps)
    def _(step):
        copy(step).wait()


def weights(name, pieces, acts, width, by_hidden, flops=0):
    rows, hidden = acts[0].shape
    shape = (hidden, width) if by_hidden else (width, hidden)
    operands = (*pieces, *acts)
    return pl.pallas_call(
        functools.partial(weights_kernel, width, 512),
        out_shape=jax.ShapeDtypeStruct(shape, jnp.bfloat16),
        in_specs=[VMEM] * len(operands),
        out_specs=pl.BlockSpec(memory_space=pl.ANY),
        scratch_shapes=[
            pltpu.VMEM((2 * rows, width), jnp.bfloat16),
            pltpu.VMEM((2 * rows, hidden), jnp.bfloat16),
            pltpu.VMEM(shape, jnp.bfloat16),
            pltpu.SemaphoreType.DMA((shape[0] // 512,)),
        ],
        compiler_params=pltpu.CompilerParams(vmem_limit_bytes=16 * 2**20),
        cost_estimate=pl.CostEstimate(
            flops=flops, bytes_accessed=0, transcendentals=0
        ),
        name=name,
    )(*operands)


def send_kernel(first, own, received, *sent):
    at = 0
    for target in sent:
        rows = target.shape[0]
        here = slice(first + at, first + at + rows)
        target[...] = own[here, :] + received[at : at + rows, :]
        at = at + rows


def slot_sum(own, received, arrived, slot, offset, received_slot):
    rows = LANES
    half = rows // 2
    here = slice(slot * rows, (slot + 1) * rows)
    other = arrived[offset : offset + rows, :].astype(jnp.float32)
    there = slice(received_slot * rows, (received_slot + 1) * rows)
    kept = own[here, :].astype(jnp.float32) + received[there, :].astype(jnp.float32)
    return kept + jnp.concatenate([other[half:], other[:half]], axis=0)


def slots_kernel(own, received, arrived, near_and_last, far_slot):
    rows = far_slot.shape[0]
    targets = (near_and_last.at[:rows], far_slot, near_and_last.at[rows:])
    for i, target in enumerate(targets):
        whole = slot_sum(own, received, arrived, i + 1, i * rows, i + 1)
        target[...] = whole.astype(target.dtype)


def add_last_kernel(far_slot, arrived, total):
    rows = far_slot.shape[0]
    total[...] = far_slot[...] + arrived[rows:, :]


def slot_kernel(slot, offset, own, received, arrived, *refs):
    whole = slot_sum(own, received, arrived, slot, offset, slot % 2)
    if len(refs) > 1:
        whole = whole + refs[0][...].astype(jnp.float32)
    refs[-1][...] = whole.astype(refs[-1].dtype)


def finish_outputs_kernel(own, received, arrived, near_and_last, far, columns):
    near = near_and_last[: far.shape[0], :]
    whole = slot_sum(own, received, arrived, 0, 0, 0)
    whole = total_of([whole, near.astype(jnp.float32), far[...].astype(jnp.float32)])
    whole = jnp.where(lax.axis_index("helper") == 0, whole, swap_halves(whole))
    columns[...] = whole.astype(jnp.bfloat16)


def finish_inputs_kernel(experts, ids, counts, scores, clock, own, received, arrived, *refs):
    columns, d_scores = refs[-2:]
    width = columns.shape[1]
    whole = slot_sum(own, received, arrived, 0, 0, 0)
    whole = total_of([whole] + [ref[...].astype(jnp.float32) for ref in refs[:-2]])
    whole = jnp.where(lax.axis_index("helper") == 0, whole, swap_halves(whole))
    columns[...] = whole[:, :width].astype(jnp.bfloat16)
    table = whole[:, width:].T
    lane = lax.broadcasted_iota(jnp.int32, table.shape, 0)
    named_by = (lane % (2 * experts)) // 2
    gates, used, score_sum = gate_rows(counts[...], scores[...])
    d_gates = []
    for k in range(len(gates)):
        hit = (named_by == ids[k : k + 1, :]) & (lane < 4 * experts)
        d_gates.append(jnp.sum(jnp.where(hit, table, 0.0), axis=0, keepdims=True))
    mean = total_of([gate * d_gate for gate, d_gate in zip(gates, d_gates)])
    for k, d_gate in enumerate(d_gates):
        d_scores[k : k + 1, :] = used[k] * (d_gate - mean) / score_sum


class FourChips:
    def __init__(self, label):
        self.label = label
        both = lambda pairs: [(2 * a + c, 2 * b + c) for a, b in pairs for c in (0, 1)]
        self.near = both([(z, z ^ 1) for z in range(4)])
        self.far = both([(z, z ^ 2) for z in range(4)])
        self.cores = [(i, i ^ 1) for i in range(8)]
        self.sides = [(0, 1), (1, 0)]

    def line(self, array, pairs):
        with jax.named_scope(self.label + "_line"):
            return lax.ppermute(array, "expert", pairs)

    def sibling(self, array):
        with jax.named_scope(self.label + "_cores"):
            return lax.ppermute(array, "expert", self.cores)

    def across(self, array):
        with jax.named_scope(self.label + "_across"):
            return lax.ppermute(array, "helper", self.sides)

    def send(self, first, own, received, parts):
        shape = lambda rows: jax.ShapeDtypeStruct((rows, received.shape[1]), own.dtype)
        return call(
            functools.partial(send_kernel, first),
            self.label + "_send",
            (own, received),
            tuple(shape(rows) for rows in parts),
        )

    def slots(self, own, received, arrived):
        rows, columns = arrived.shape
        shape = lambda slots: jax.ShapeDtypeStruct((slots * rows // 3, columns), arrived.dtype)
        return call(
            slots_kernel,
            self.label + "_slots",
            (own, received, arrived),
            (shape(2), shape(1)),
        )

    def slot(self, which, offset, own, received, arrived, *others):
        return call(
            functools.partial(slot_kernel, which, offset),
            self.label + "_slot",
            (own, received, arrived, *others),
            jax.ShapeDtypeStruct((own.shape[0] // 4, own.shape[1]), own.dtype),
        )


def load_kernel(*refs):
    sources, targets, sems = refs[:3], refs[3:6], refs[6]
    copies = [
        pltpu.make_async_copy(source, target, sems.at[i])
        for i, (source, target) in enumerate(zip(sources, targets))
    ]
    for copy in copies:
        copy.start()
    for copy in copies:
        copy.wait()


def load(*mats):
    return pl.pallas_call(
        load_kernel,
        out_shape=tuple(jax.ShapeDtypeStruct(mat.shape, mat.dtype) for mat in mats),
        in_specs=[pl.BlockSpec(memory_space=pltpu.HBM)] * len(mats),
        out_specs=(VMEM,) * len(mats),
        scratch_shapes=[pltpu.SemaphoreType.DMA((len(mats),))],
        compiler_params=pltpu.CompilerParams(vmem_limit_bytes=2**20),
        name="load",
    )(*(pltpu.with_memory_space_constraint(mat, pltpu.HBM) for mat in mats))


def space(clock, flops=36 * 10**9):
    return pl.pallas_call(
        lambda old, new: None,
        out_shape=jax.ShapeDtypeStruct(clock.shape, clock.dtype),
        in_specs=[pl.BlockSpec(memory_space=pl.ANY)],
        out_specs=pl.BlockSpec(memory_space=pl.ANY),
        input_output_aliases={0: 0},
        compiler_params=pltpu.CompilerParams(vmem_limit_bytes=2**20),
        cost_estimate=pl.CostEstimate(flops=flops, bytes_accessed=0, transcendentals=0),
        name="space",
    )(clock)


class Order:
    def __init__(self):
        self.token = None

    def __call__(self, function, *operands, also=()):
        if self.token is not None:
            operands, _ = lax.optimization_barrier((operands, (self.token, also)))
        result = function(*operands)
        self.token = result
        return result


def lined_up(tokens, expert_ids, pick_counts, gate_scores, gate_local, up_local, down_local, grad_out):
    experts = lax.axis_size("expert")
    width = gate_local.shape[0]
    picks = (expert_ids.T, pick_counts[None, :], gate_scores.T)
    rows, grads, outs, ins = (FourChips(label) for label in ("rows", "grads", "out", "in"))
    order = Order()
    hold = lambda value, *tokens: lax.optimization_barrier((value, tokens))[0]
    product_of = lambda name, by_hidden, flops=0: lambda r, acts: weights(
        name, r, acts, width, by_hidden, flops
    )
    estimate = 16 * tokens.size * gate_local.shape[1]

    size = tokens.shape[0]
    half = size // 2
    zeros = (0,) * 6
    own, pair, clock = order(lambda r: prepare_rows(*picks, r, experts), tokens)
    near = rows.line(own, rows.near)
    far = rows.line(own, rows.far)
    sibling_pair = rows.sibling(pair)
    gate_mat, up_mat, down_mat = order(load, gate_local, up_local, down_local)
    sibling_pair = hold(sibling_pair, down_mat)
    line_pair = order(lambda *p: join(half, p, zeros[:2]), near, far, also=sibling_pair)
    last = rows.line(hold(far, line_pair), rows.near)
    across_pair = rows.across(line_pair)
    own, grads_pair = order(prepare_grads, grad_out)
    far = grads.line(own, grads.far)
    last_across = rows.across(last)
    far = hold(far, last)
    grads_last = grads.line(far, grads.near)
    far_across = grads.across(far)
    near = grads.line(hold(grads_pair, last), grads.near)
    clock = order(lambda c: space(c, 2 * 10**9), clock, also=far)
    across_pair, last_across = hold((across_pair, last_across), clock)
    rest = order(
        lambda *p: join(half, p, (0, half, 0, half, 0, 0)),
        line_pair,
        line_pair,
        across_pair,
        across_pair,
        last,
        last_across,
    )
    own_rows = (pair, rest)
    sibling_rest = rows.sibling(rest)
    clock = order(space, clock)
    other_rows = (sibling_pair, hold(sibling_rest, clock))
    hidden = lambda *r: hidden_units(r, gate_mat, up_mat, experts)
    own_gate, own_up, own_act = order(hidden, *own_rows)
    grads_last, far_across = hold((grads_last, far_across), own_act)
    last_across = grads.across(grads_last)
    grads_sibling = grads.sibling(hold(grads_pair, own_act))
    other_gate, other_up, other_act = order(hidden, *other_rows, also=(grads_last, far_across))
    sent, kept = order(outputs_of, other_act, down_mat)
    received, kept = outs.sibling(sent), outs.sibling(kept)
    out_send, out_keep = order(outputs_of, own_act, down_mat)
    clock = order(space, clock, also=(near, last_across, grads_sibling))
    received = hold(received, clock)
    out_sent, sent = order(
        lambda *s: outs.send(0, *s, (size, 3 * size)), out_send, received
    )
    arrived = outs.across(sent)
    rest = order(
        lambda *p: join(half, p, (0, 0, half, 0, 0, 0)),
        near,
        far,
        near,
        far_across,
        grads_last,
        last_across,
    )
    own_grads = (grads_pair, rest)
    other_grads = (grads_sibling, grads.sibling(rest))
    back = lambda g, r, *pre: hidden_grads(g, r, *pre, down_mat, experts)
    own_d_gate, own_d_up, own_shares = order(back, own_grads, own_rows, own_gate, own_up)
    other_d_gate, other_d_up, other_shares = order(
        back, other_grads, other_rows, other_gate, other_up
    )
    near_sent, far_sent, near_kept, far_kept = order(
        lambda *d: input_grads_of(2, *d, gate_mat, up_mat), other_d_gate, other_d_up, other_shares
    )
    far_received, far_kept = ins.sibling(far_sent), ins.sibling(far_kept)
    near_received, near_kept = ins.sibling(near_sent), ins.sibling(near_kept)
    in_send, in_keep = order(
        lambda *d: input_grads_of(1, *d, gate_mat, up_mat), own_d_gate, own_d_up, own_shares
    )
    (sent,) = order(lambda *s: ins.send(2 * size, *s, (2 * size,)), in_send, far_received)
    far_arrived = ins.across(sent)
    near_slots, far_slot = order(outs.slots, out_keep, kept, hold(arrived, sent))
    near_sums = outs.line(near_slots, outs.near)
    grad_down = order(product_of("grad_down", True, estimate), own_grads + other_grads, (own_act, other_act))
    far_slot = order(
        lambda *s: call(add_last_kernel, "add_last", s, jax.ShapeDtypeStruct(s[0].shape, s[0].dtype)),
        far_slot,
        near_sums,
    )
    far_sum = outs.line(far_slot, outs.far)
    slot = order(lambda *s: ins.slot(3, size, *s), in_keep, far_kept, far_arrived)
    last_sum = ins.line(slot, ins.near)
    own_sent, near_sent = order(
        lambda *s: ins.send(0, *s, (size, size)), in_send, near_received
    )
    near_arrived = ins.across(near_sent)
    out_arrived = outs.across(hold(out_sent, slot))
    grad_gate = order(
        product_of("grad_gate", False, estimate), own_rows + other_rows, (own_d_gate, other_d_gate)
    )
    slot = order(lambda *s: ins.slot(2, 0, *s), in_keep, far_kept, far_arrived, last_sum)
    far = ins.line(slot, ins.far)
    near_arrived = hold(near_arrived, slot)
    slot = order(
        lambda *s: ins.slot(1, 0, *s), in_keep, near_kept, near_arrived, also=out_arrived
    )
    near = ins.line(slot, ins.near)
    own_arrived = ins.across(hold(own_sent, slot))
    columns = jax.ShapeDtypeStruct((size, width // 2), jnp.bfloat16)
    output_cols = order(
        lambda *sums: call(finish_outputs_kernel, "finish_outputs", sums, columns),
        out_keep,
        kept,
        out_arrived,
        near_sums,
        far_sum,
    )
    clock = order(lambda c: space(c, 10**9), clock)
    grad_up = order(
        product_of("grad_up", False), own_rows + other_rows, (own_d_up, other_d_up)
    )
    clock = order(lambda c: space(c, 2 * 10**9), clock, also=far)
    near, own_arrived = hold((near, own_arrived), clock)
    input_cols, d_scores = order(
        lambda *sums: call(
            functools.partial(finish_inputs_kernel, experts),
            "finish_inputs",
            (*picks, clock, *sums),
            (columns, jax.ShapeDtypeStruct(picks[2].shape, jnp.float32)),
        ),
        in_keep,
        near_kept,
        own_arrived,
        far,
        near,
    )
    return output_cols, input_cols, d_scores.T, grad_gate[None], grad_up[None], grad_down[None]


def any_mesh(tokens, expert_ids, pick_counts, gate_scores, gate_local, up_local, down_local, grad_out):
    tok_rows = tokens.shape[0]
    pick_width = expert_ids.shape[1]
    experts = lax.axis_size("expert")
    active_mask = lax.broadcasted_iota(jnp.int32, (tok_rows, pick_width), 1) < pick_counts[:, None]
    active_float = active_mask.astype(jnp.float32)
    weighted = gate_scores * active_float
    score_sum = jnp.sum(weighted, axis=1, keepdims=True)
    gate_weights = weighted / score_sum
    picked = (expert_ids[:, :, None] == lax.broadcasted_iota(jnp.int32, (1, 1, experts), 2)).astype(
        jnp.float32
    )
    gate_table = jnp.sum(gate_weights[:, :, None] * picked, axis=1)

    def combine(partial):
        summed = lax.psum_scatter(partial, "expert", scatter_dimension=0, tiled=True)
        return lax.psum_scatter(summed, "helper", scatter_dimension=1, tiled=True)

    rows = lax.all_gather(tokens, "expert", tiled=True)
    tables = lax.all_gather(gate_table.T, "expert", tiled=False)
    gates = jnp.take(tables, lax.axis_index("expert"), axis=1).reshape(-1, 1)
    grads = lax.all_gather(grad_out, "expert", tiled=True)

    pre_gate = product(rows, gate_local)
    pre_up = product(rows, up_local)
    silu_value, silu_slope = silu_parts(pre_gate)
    hidden_act = silu_value * pre_up
    gated_act = (gates * hidden_act).astype(jnp.bfloat16)
    output_cols = combine(product(gated_act, down_local).astype(jnp.bfloat16))

    raw_act = right_transposed(grads, down_local)
    gate_part = jnp.sum(raw_act * hidden_act, axis=1)
    d_act = gates * raw_act
    d_pre_gate = (d_act * pre_up * silu_slope).astype(jnp.bfloat16)
    d_pre_up = (d_act * silu_value).astype(jnp.bfloat16)
    input_cols = combine(
        (right_transposed(d_pre_gate, gate_local) + right_transposed(d_pre_up, up_local)).astype(
            jnp.bfloat16
        )
    )

    gate_parts = lax.all_gather(
        gate_part.reshape(-1, tok_rows), ("expert", "helper"), tiled=False
    )
    own_parts = jnp.take(gate_parts, lax.axis_index("expert"), axis=1)
    by_expert = jnp.sum(own_parts.reshape(experts, -1, tok_rows), axis=1).T
    d_gates = jnp.sum(by_expert[:, None, :] * picked, axis=2)
    d_scores = (
        active_float
        * (d_gates - jnp.sum(gate_weights * d_gates, axis=1, keepdims=True))
        / score_sum
    )

    def over_dp(whole, dimension):
        return lax.psum_scatter(
            whole.astype(jnp.bfloat16), "dp", scatter_dimension=dimension, tiled=True
        )[None]

    grad_w_gate = over_dp(transposed_product(rows, d_pre_gate), 0)
    grad_w_up = over_dp(transposed_product(rows, d_pre_up), 0)
    grad_w_down = over_dp(transposed_product(gated_act, grads), 1)
    return output_cols, input_cols, d_scores, grad_w_gate, grad_w_up, grad_w_down


def on_device(tokens, expert_ids, pick_counts, gate_scores, w_gate, w_up, w_down, grad_out):
    sizes = tuple(lax.axis_size(axis) for axis in ("expert", "helper", "dp"))
    layer = lined_up if sizes == (8, 2, 1) else any_mesh
    return layer(
        tokens, expert_ids, pick_counts, gate_scores, w_gate[0], w_up[0], w_down[0], grad_out
    )


def solution(mesh):
    in_specs = (
        P(("groups", "expert", "dp"), None),
        P(("groups", "expert", "dp"), None),
        P(("groups", "expert", "dp")),
        P(("groups", "expert", "dp"), None),
        P("expert", None, "helper"),
        P("expert", None, "helper"),
        P("expert", "helper", None),
        P(("groups", "expert", "dp"), None),
    )
    out_specs = (
        P(("groups", "expert", "dp"), "helper"),
        P(("groups", "expert", "dp"), "helper"),
        P(("groups", "expert", "dp"), None),
        P(("groups", "expert"), "dp", "helper"),
        P(("groups", "expert"), "dp", "helper"),
        P(("groups", "expert"), "helper", "dp"),
    )
    return jax.shard_map(
        on_device, mesh=mesh, in_specs=in_specs, out_specs=out_specs, check_vma=False
    )
```

```python
import functools

import jax
import jax.numpy as jnp
from jax import lax
from jax.experimental import pallas as pl
from jax.experimental.pallas import tpu as pltpu
from jax.sharding import PartitionSpec as P

LANES = 128
VMEM = pl.BlockSpec(memory_space=pltpu.VMEM)


def product(first_mat, second_mat):
    return jnp.dot(first_mat, second_mat, preferred_element_type=jnp.float32)


def transposed_product(first_mat, second_mat):
    return lax.dot_general(
        first_mat, second_mat, (((0,), (0,)), ((), ())), preferred_element_type=jnp.float32
    )


def right_transposed(first_mat, second_mat):
    return lax.dot_general(
        first_mat, second_mat, (((1,), (1,)), ((), ())), preferred_element_type=jnp.float32
    )


def silu_parts(argument):
    sigmoid_part = jax.nn.sigmoid(argument)
    return argument * sigmoid_part, sigmoid_part * (1.0 + argument * (1.0 - sigmoid_part))


def total_of(terms):
    return functools.reduce(jnp.add, terms)


def call(kernel, name, operands, out_shape, scratch=(), flops=0, moved=0, mebibytes=12):
    return pl.pallas_call(
        kernel,
        out_shape=out_shape,
        in_specs=[VMEM] * len(operands),
        out_specs=jax.tree.map(lambda _: VMEM, out_shape),
        scratch_shapes=scratch,
        compiler_params=pltpu.CompilerParams(vmem_limit_bytes=mebibytes * 2**20),
        cost_estimate=pl.CostEstimate(
            flops=flops, bytes_accessed=moved, transcendentals=0
        ),
        name=name,
    )(*operands)


def half_at(array, which):
    rows = array.shape[0] // 2
    return array[which * rows : (which + 1) * rows]


def swap_halves(array):
    return jnp.concatenate([half_at(array, 1), half_at(array, 0)], axis=0)


def hi_lo(values, is_high):
    high = values.astype(jnp.bfloat16).astype(jnp.float32)
    return jnp.where(is_high, high, values - high).astype(jnp.bfloat16)


def gate_rows(counts, scores):
    used = [(counts > k).astype(jnp.float32) for k in range(scores.shape[0])]
    weighted = [scores[k : k + 1] * used[k] for k in range(scores.shape[0])]
    score_sum = total_of(weighted)
    return [w / score_sum for w in weighted], used, score_sum


def prepare_rows_kernel(experts, *refs):
    sources, (own, pair, clock), targets, sems = refs[:4], refs[4:7], refs[7:11], refs[11]
    ids, counts, scores, rows = targets
    copies = [
        pltpu.make_async_copy(source, target, sems.at[i])
        for i, (source, target) in enumerate(zip(sources, targets))
    ]
    for copy in copies:
        copy.start()
    for copy in copies:
        copy.wait()
    total, width = rows.shape
    clock[...] = jnp.zeros_like(clock)
    lane = lax.broadcasted_iota(jnp.int32, (LANES, total), 0)
    gates, _, _ = gate_rows(counts[...], scores[...])
    table = jnp.zeros((LANES, total), jnp.float32)
    for k, gate in enumerate(gates):
        named = ids[k : k + 1, :]
        table = table + jnp.where((lane == named) | (lane == named + experts), gate, 0.0)
    table = table.T
    table = hi_lo(table, lax.broadcasted_iota(jnp.int32, table.shape, 1) < experts)
    for side in range(2):

        @pl.when(lax.axis_index("helper") == side)
        def _(side=side):
            own[:, :width] = half_at(rows, side)
            own[:, width:] = half_at(table, side)
            for i, which in enumerate((side, 1 - side)):
                here = slice(i * total // 2, (i + 1) * total // 2)
                pair[here, :width] = half_at(rows, which)
                pair[here, width:] = half_at(table, which)


def prepare_rows(ids, counts, scores, rows, experts):
    total, width = rows.shape
    piece = jax.ShapeDtypeStruct((total // 2, width + LANES), jnp.bfloat16)
    operands = (ids, counts, scores, rows)
    return pl.pallas_call(
        functools.partial(prepare_rows_kernel, experts),
        out_shape=(
            piece,
            jax.ShapeDtypeStruct((total, width + LANES), jnp.bfloat16),
            jax.ShapeDtypeStruct((8, LANES), jnp.float32),
        ),
        in_specs=[pl.BlockSpec(memory_space=pltpu.HBM)] * len(operands),
        out_specs=(VMEM,) * 3,
        scratch_shapes=[
            *(pltpu.VMEM(operand.shape, operand.dtype) for operand in operands),
            pltpu.SemaphoreType.DMA((len(operands),)),
        ],
        compiler_params=pltpu.CompilerParams(vmem_limit_bytes=8 * 2**20),
        name="prepare_rows",
    )(*(pltpu.with_memory_space_constraint(operand, pltpu.HBM) for operand in operands))


def prepare_grads_kernel(rows, own, pair):
    half = rows.shape[0] // 2
    for side in range(2):

        @pl.when(lax.axis_index("helper") == side)
        def _(side=side):
            own[...] = half_at(rows, side)
            pair[:half, :] = half_at(rows, side)
            pair[half:, :] = half_at(rows, 1 - side)


def prepare_grads(rows):
    total, width = rows.shape
    piece = jax.ShapeDtypeStruct((total // 2, width), jnp.bfloat16)
    return call(
        prepare_grads_kernel,
        "prepare_grads",
        (rows,),
        (piece, jax.ShapeDtypeStruct(rows.shape, jnp.bfloat16)),
    )


def join_kernel(starts, rows, *refs):
    for i, start in enumerate(starts):
        refs[-1][i * rows : (i + 1) * rows, :] = refs[i][start : start + rows, :]


def join(rows, pieces, starts):
    shape = jax.ShapeDtypeStruct((len(pieces) * rows, pieces[0].shape[1]), pieces[0].dtype)
    return call(functools.partial(join_kernel, starts, rows), "join", pieces, shape)


def parts_of(pair, rest):
    rows = pair.shape[0]
    half = rows // 2
    parts = [(pair, 0, rows)]
    for slot in range(2):
        parts = parts + [(rest, slot * half, half), (rest, rows + slot * half, half)]
    return parts + [(rest, 2 * rows, rows)]


def lay_out(pieces, target, columns, at=0):
    for piece, start, rows in parts_of(*pieces):
        target[at : at + rows, :] = piece[start : start + rows, columns]
        at = at + rows


def gate_column(experts, pieces, width):
    table = jnp.concatenate(
        [piece[start : start + rows, width:] for piece, start, rows in parts_of(*pieces)], axis=0
    )
    lane = lax.broadcasted_iota(jnp.int32, table.shape, 1)
    expert = lax.axis_index("expert")
    mine = (lane == expert) | (lane == expert + experts)
    return jnp.sum(jnp.where(mine, table.astype(jnp.float32), 0.0), axis=1, keepdims=True)


def hidden_kernel(experts, tile, *refs):
    pieces, refs = refs[:2], refs[2:]
    gate_mat, up_mat, pre_gate, pre_up, gated, rows = refs
    width = rows.shape[1]
    lay_out(pieces, rows, slice(0, width))
    gate = gate_column(experts, pieces, width)
    for start in range(0, gated.shape[1], tile):
        columns = slice(start, start + tile)
        gate_part = product(rows[...], gate_mat[:, columns])
        up_part = product(rows[...], up_mat[:, columns])
        silu_value, _ = silu_parts(gate_part)
        pre_gate[:, columns] = gate_part
        pre_up[:, columns] = up_part
        gated[:, columns] = (gate * silu_value * up_part).astype(jnp.bfloat16)


def hidden_units(pieces, gate_mat, up_mat, experts):
    width, hidden = gate_mat.shape
    total = 4 * pieces[0].shape[0]
    pre = jax.ShapeDtypeStruct((total, hidden), jnp.float32)
    act = jax.ShapeDtypeStruct((total, hidden), jnp.bfloat16)
    return call(
        functools.partial(hidden_kernel, experts, 512),
        "hidden_units",
        (*pieces, gate_mat, up_mat),
        (pre, pre, act),
        [pltpu.VMEM((total, width), jnp.bfloat16)],
        flops=4 * total * width * hidden,
        mebibytes=12,
    )


def outputs_kernel(tile, gated, down_mat, *sums):
    half = sums[0].shape[1]
    for keep in range(2):
        side = lax.axis_index("helper")
        side = side if keep else 1 - side
        for start in range(0, half, tile):
            here = pl.ds(pl.multiple_of(side * half + start, tile), tile)
            out = product(gated[...], down_mat[:, here])
            sums[keep][:, start : start + tile] = out.astype(jnp.bfloat16)


def outputs_of(gated, down_mat):
    total, hidden = gated.shape
    width = down_mat.shape[1]
    sums = jax.ShapeDtypeStruct((total, width // 2), jnp.bfloat16)
    return call(
        functools.partial(outputs_kernel, 512), "outputs", (gated, down_mat), (sums, sums)
    )


def hidden_grads_kernel(experts, tile, *refs):
    pieces, gate_pieces, refs = refs[:2], refs[2:4], refs[4:]
    down_mat, pre_gate, pre_up, d_gate, d_up, shares_out, grads = refs
    total, width = grads.shape
    lay_out(pieces, grads, slice(0, width))
    gate = gate_column(experts, gate_pieces, width)
    shares = []
    for start in range(0, d_gate.shape[1], tile):
        columns = slice(start, start + tile)
        raw = right_transposed(grads[...], down_mat[columns, :])
        up_part = pre_up[:, columns]
        silu_value, silu_slope = silu_parts(pre_gate[:, columns])
        share = raw * silu_value * up_part
        shares = shares + [share[:, c : c + LANES] for c in range(0, tile, LANES)]
        d_act = gate * raw
        d_gate[:, columns] = (d_act * up_part * silu_slope).astype(jnp.bfloat16)
        d_up[:, columns] = (d_act * silu_value).astype(jnp.bfloat16)
    value = jnp.sum(total_of(shares), axis=1, keepdims=True)
    lane = lax.broadcasted_iota(jnp.int32, (total, LANES), 1)
    high = 2 * lax.axis_index("expert") + lax.axis_index("helper")
    value = jnp.where((lane == high) | (lane == high + 2 * experts), value, 0.0)
    shares_out[...] = hi_lo(value, lane < 2 * experts)


def hidden_grads(pieces, gate_pieces, pre_gate, pre_up, down_mat, experts):
    hidden, width = down_mat.shape
    total = pre_gate.shape[0]
    act = jax.ShapeDtypeStruct((total, hidden), jnp.bfloat16)
    return call(
        functools.partial(hidden_grads_kernel, experts, 512),
        "hidden_grads",
        (*pieces, *gate_pieces, down_mat, pre_gate, pre_up),
        (act, act, jax.ShapeDtypeStruct((total, LANES), jnp.bfloat16)),
        [pltpu.VMEM((total, width), jnp.bfloat16)],
        mebibytes=12,
    )


def input_grads_kernel(tile, d_gate, d_up, shares, gate_mat, up_mat, *sums):
    half = sums[0].shape[1] - LANES
    split = len(sums) // 2

    def put(keep, columns, values):
        rows = values.shape[0] // split
        for i in range(split):
            sums[split * keep + i][:, columns] = values[i * rows : (i + 1) * rows]

    for keep in range(2):
        put(keep, slice(half, half + LANES), shares[...])
        side = lax.axis_index("helper")
        side = side if keep else 1 - side
        for start in range(0, half, tile):
            here = pl.ds(pl.multiple_of(side * half + start, tile), tile)
            back = right_transposed(d_gate[...], gate_mat[here, :])
            back = back + right_transposed(d_up[...], up_mat[here, :])
            put(keep, slice(start, start + tile), back.astype(jnp.bfloat16))


def input_grads_of(split, d_gate, d_up, shares, gate_mat, up_mat):
    width, hidden = gate_mat.shape
    total = d_gate.shape[0]
    sums = jax.ShapeDtypeStruct((total // split, width // 2 + LANES), jnp.bfloat16)
    return call(
        functools.partial(input_grads_kernel, 512),
        "input_grads",
        (d_gate, d_up, shares, gate_mat, up_mat),
        (sums,) * (2 * split),
        mebibytes=12,
    )


def weights_kernel(width, tile, *refs):
    pieces, (first, second, grad, rows, acts, made, sems) = refs[:4], refs[4:]
    total = first.shape[0]
    lay_out(pieces[:2], rows, slice(0, width))
    lay_out(pieces[2:], rows, slice(0, width), total)
    acts[:total, :] = first[...]
    acts[total:, :] = second[...]
    left, right = (acts, rows) if grad.shape[1] == width else (rows, acts)

    def copy(step):
        here = pl.ds(pl.multiple_of(step * tile, tile), tile)
        return pltpu.make_async_copy(made.at[here, :], grad.at[here, :], sems.at[step])

    steps = grad.shape[0] // tile

    @pl.loop(0, steps, unroll=2)
    def _(step):
        here = pl.ds(pl.multiple_of(step * tile, tile), tile)
        made[here, :] = transposed_product(left[:, here], right[...]).astype(jnp.bfloat16)
        copy(step).start()

    @pl.loop(0, steps)
    def _(step):
        copy(step).wait()


def weights(name, pieces, acts, width, by_hidden, flops=0):
    rows, hidden = acts[0].shape
    shape = (hidden, width) if by_hidden else (width, hidden)
    operands = (*pieces, *acts)
    return pl.pallas_call(
        functools.partial(weights_kernel, width, 512),
        out_shape=jax.ShapeDtypeStruct(shape, jnp.bfloat16),
        in_specs=[VMEM] * len(operands),
        out_specs=pl.BlockSpec(memory_space=pl.ANY),
        scratch_shapes=[
            pltpu.VMEM((2 * rows, width), jnp.bfloat16),
            pltpu.VMEM((2 * rows, hidden), jnp.bfloat16),
            pltpu.VMEM(shape, jnp.bfloat16),
            pltpu.SemaphoreType.DMA((shape[0] // 512,)),
        ],
        compiler_params=pltpu.CompilerParams(vmem_limit_bytes=16 * 2**20),
        cost_estimate=pl.CostEstimate(
            flops=flops, bytes_accessed=0, transcendentals=0
        ),
        name=name,
    )(*operands)


def send_kernel(first, own, received, *sent):
    at = 0
    for target in sent:
        rows = target.shape[0]
        here = slice(first + at, first + at + rows)
        target[...] = own[here, :] + received[at : at + rows, :]
        at = at + rows


def slot_sum(own, received, arrived, slot, offset, received_slot):
    rows = LANES
    half = rows // 2
    here = slice(slot * rows, (slot + 1) * rows)
    other = arrived[offset : offset + rows, :].astype(jnp.float32)
    there = slice(received_slot * rows, (received_slot + 1) * rows)
    kept = own[here, :].astype(jnp.float32) + received[there, :].astype(jnp.float32)
    return kept + jnp.concatenate([other[half:], other[:half]], axis=0)


def slots_kernel(own, received, arrived, near_and_last, far_slot):
    rows = far_slot.shape[0]
    targets = (near_and_last.at[:rows], far_slot, near_and_last.at[rows:])
    for i, target in enumerate(targets):
        whole = slot_sum(own, received, arrived, i + 1, i * rows, i + 1)
        target[...] = whole.astype(target.dtype)


def add_last_kernel(far_slot, arrived, total):
    rows = far_slot.shape[0]
    total[...] = far_slot[...] + arrived[rows:, :]


def slot_kernel(slot, offset, own, received, arrived, *refs):
    whole = slot_sum(own, received, arrived, slot, offset, slot % 2)
    if len(refs) > 1:
        whole = whole + refs[0][...].astype(jnp.float32)
    refs[-1][...] = whole.astype(refs[-1].dtype)


def finish_outputs_kernel(own, received, arrived, near_and_last, far, columns):
    near = near_and_last[: far.shape[0], :]
    whole = slot_sum(own, received, arrived, 0, 0, 0)
    whole = total_of([whole, near.astype(jnp.float32), far[...].astype(jnp.float32)])
    whole = jnp.where(lax.axis_index("helper") == 0, whole, swap_halves(whole))
    columns[...] = whole.astype(jnp.bfloat16)


def finish_inputs_kernel(experts, ids, counts, scores, clock, own, received, arrived, *refs):
    columns, d_scores = refs[-2:]
    width = columns.shape[1]
    whole = slot_sum(own, received, arrived, 0, 0, 0)
    whole = total_of([whole] + [ref[...].astype(jnp.float32) for ref in refs[:-2]])
    whole = jnp.where(lax.axis_index("helper") == 0, whole, swap_halves(whole))
    columns[...] = whole[:, :width].astype(jnp.bfloat16)
    table = whole[:, width:].T
    lane = lax.broadcasted_iota(jnp.int32, table.shape, 0)
    named_by = (lane % (2 * experts)) // 2
    gates, used, score_sum = gate_rows(counts[...], scores[...])
    d_gates = []
    for k in range(len(gates)):
        hit = (named_by == ids[k : k + 1, :]) & (lane < 4 * experts)
        d_gates.append(jnp.sum(jnp.where(hit, table, 0.0), axis=0, keepdims=True))
    mean = total_of([gate * d_gate for gate, d_gate in zip(gates, d_gates)])
    for k, d_gate in enumerate(d_gates):
        d_scores[k : k + 1, :] = used[k] * (d_gate - mean) / score_sum


class FourChips:
    def __init__(self, label):
        self.label = label
        both = lambda pairs: [(2 * a + c, 2 * b + c) for a, b in pairs for c in (0, 1)]
        self.near = both([(z, z ^ 1) for z in range(4)])
        self.far = both([(z, z ^ 2) for z in range(4)])
        self.cores = [(i, i ^ 1) for i in range(8)]
        self.sides = [(0, 1), (1, 0)]

    def line(self, array, pairs):
        with jax.named_scope(self.label + "_line"):
            return lax.ppermute(array, "expert", pairs)

    def sibling(self, array):
        with jax.named_scope(self.label + "_cores"):
            return lax.ppermute(array, "expert", self.cores)

    def across(self, array):
        with jax.named_scope(self.label + "_across"):
            return lax.ppermute(array, "helper", self.sides)

    def send(self, first, own, received, parts):
        shape = lambda rows: jax.ShapeDtypeStruct((rows, received.shape[1]), own.dtype)
        return call(
            functools.partial(send_kernel, first),
            self.label + "_send",
            (own, received),
            tuple(shape(rows) for rows in parts),
        )

    def slots(self, own, received, arrived):
        rows, columns = arrived.shape
        shape = lambda slots: jax.ShapeDtypeStruct((slots * rows // 3, columns), arrived.dtype)
        return call(
            slots_kernel,
            self.label + "_slots",
            (own, received, arrived),
            (shape(2), shape(1)),
        )

    def slot(self, which, offset, own, received, arrived, *others):
        return call(
            functools.partial(slot_kernel, which, offset),
            self.label + "_slot",
            (own, received, arrived, *others),
            jax.ShapeDtypeStruct((own.shape[0] // 4, own.shape[1]), own.dtype),
        )


def load_kernel(*refs):
    sources, targets, sems = refs[:3], refs[3:6], refs[6]
    copies = [
        pltpu.make_async_copy(source, target, sems.at[i])
        for i, (source, target) in enumerate(zip(sources, targets))
    ]
    for copy in copies:
        copy.start()
    for copy in copies:
        copy.wait()


def load(*mats):
    return pl.pallas_call(
        load_kernel,
        out_shape=tuple(jax.ShapeDtypeStruct(mat.shape, mat.dtype) for mat in mats),
        in_specs=[pl.BlockSpec(memory_space=pltpu.HBM)] * len(mats),
        out_specs=(VMEM,) * len(mats),
        scratch_shapes=[pltpu.SemaphoreType.DMA((len(mats),))],
        compiler_params=pltpu.CompilerParams(vmem_limit_bytes=2**20),
        name="load",
    )(*(pltpu.with_memory_space_constraint(mat, pltpu.HBM) for mat in mats))


def space(clock, flops=36 * 10**9):
    return pl.pallas_call(
        lambda old, new: None,
        out_shape=jax.ShapeDtypeStruct(clock.shape, clock.dtype),
        in_specs=[pl.BlockSpec(memory_space=pl.ANY)],
        out_specs=pl.BlockSpec(memory_space=pl.ANY),
        input_output_aliases={0: 0},
        compiler_params=pltpu.CompilerParams(vmem_limit_bytes=2**20),
        cost_estimate=pl.CostEstimate(flops=flops, bytes_accessed=0, transcendentals=0),
        name="space",
    )(clock)


class Order:
    def __init__(self):
        self.token = None

    def __call__(self, function, *operands, also=()):
        if self.token is not None:
            operands, _ = lax.optimization_barrier((operands, (self.token, also)))
        result = function(*operands)
        self.token = result
        return result


def lined_up(tokens, expert_ids, pick_counts, gate_scores, gate_local, up_local, down_local, grad_out):
    experts = lax.axis_size("expert")
    width = gate_local.shape[0]
    picks = (expert_ids.T, pick_counts[None, :], gate_scores.T)
    rows, grads, outs, ins = (FourChips(label) for label in ("rows", "grads", "out", "in"))
    order = Order()
    hold = lambda value, *tokens: lax.optimization_barrier((value, tokens))[0]
    product_of = lambda name, by_hidden, flops=0: lambda r, acts: weights(
        name, r, acts, width, by_hidden, flops
    )
    estimate = 16 * tokens.size * gate_local.shape[1]

    size = tokens.shape[0]
    half = size // 2
    zeros = (0,) * 6
    own, pair, clock = order(lambda r: prepare_rows(*picks, r, experts), tokens)
    near = rows.line(own, rows.near)
    far = rows.line(own, rows.far)
    sibling_pair = rows.sibling(pair)
    gate_mat, up_mat, down_mat = order(load, gate_local, up_local, down_local)
    sibling_pair = hold(sibling_pair, down_mat)
    line_pair = order(lambda *p: join(half, p, zeros[:2]), near, far, also=sibling_pair)
    last = rows.line(hold(far, line_pair), rows.near)
    across_pair = rows.across(line_pair)
    own, grads_pair = order(prepare_grads, grad_out)
    far = grads.line(own, grads.far)
    last_across = rows.across(last)
    far = hold(far, last)
    grads_last = grads.line(far, grads.near)
    far_across = grads.across(far)
    near = grads.line(hold(grads_pair, last), grads.near)
    clock = order(lambda c: space(c, 2 * 10**9), clock, also=far)
    across_pair, last_across = hold((across_pair, last_across), clock)
    rest = order(
        lambda *p: join(half, p, (0, half, 0, half, 0, 0)),
        line_pair,
        line_pair,
        across_pair,
        across_pair,
        last,
        last_across,
    )
    own_rows = (pair, rest)
    sibling_rest = rows.sibling(rest)
    clock = order(space, clock)
    other_rows = (sibling_pair, hold(sibling_rest, clock))
    hidden = lambda *r: hidden_units(r, gate_mat, up_mat, experts)
    own_gate, own_up, own_act = order(hidden, *own_rows)
    grads_last, far_across = hold((grads_last, far_across), own_act)
    last_across = grads.across(grads_last)
    grads_sibling = grads.sibling(hold(grads_pair, own_act))
    other_gate, other_up, other_act = order(hidden, *other_rows, also=(grads_last, far_across))
    sent, kept = order(outputs_of, other_act, down_mat)
    received, kept = outs.sibling(sent), outs.sibling(kept)
    out_send, out_keep = order(outputs_of, own_act, down_mat)
    clock = order(space, clock, also=(near, last_across, grads_sibling))
    received = hold(received, clock)
    out_sent, sent = order(
        lambda *s: outs.send(0, *s, (size, 3 * size)), out_send, received
    )
    arrived = outs.across(sent)
    rest = order(
        lambda *p: join(half, p, (0, 0, half, 0, 0, 0)),
        near,
        far,
        near,
        far_across,
        grads_last,
        last_across,
    )
    own_grads = (grads_pair, rest)
    other_grads = (grads_sibling, grads.sibling(rest))
    back = lambda g, r, *pre: hidden_grads(g, r, *pre, down_mat, experts)
    own_d_gate, own_d_up, own_shares = order(back, own_grads, own_rows, own_gate, own_up)
    other_d_gate, other_d_up, other_shares = order(
        back, other_grads, other_rows, other_gate, other_up
    )
    near_sent, far_sent, near_kept, far_kept = order(
        lambda *d: input_grads_of(2, *d, gate_mat, up_mat), other_d_gate, other_d_up, other_shares
    )
    far_received, far_kept = ins.sibling(far_sent), ins.sibling(far_kept)
    near_received, near_kept = ins.sibling(near_sent), ins.sibling(near_kept)
    in_send, in_keep = order(
        lambda *d: input_grads_of(1, *d, gate_mat, up_mat), own_d_gate, own_d_up, own_shares
    )
    (sent,) = order(lambda *s: ins.send(2 * size, *s, (2 * size,)), in_send, far_received)
    far_arrived = ins.across(sent)
    near_slots, far_slot = order(outs.slots, out_keep, kept, hold(arrived, sent))
    near_sums = outs.line(near_slots, outs.near)
    grad_down = order(product_of("grad_down", True, estimate), own_grads + other_grads, (own_act, other_act))
    far_slot = order(
        lambda *s: call(add_last_kernel, "add_last", s, jax.ShapeDtypeStruct(s[0].shape, s[0].dtype)),
        far_slot,
        near_sums,
    )
    far_sum = outs.line(far_slot, outs.far)
    slot = order(lambda *s: ins.slot(3, size, *s), in_keep, far_kept, far_arrived)
    last_sum = ins.line(slot, ins.near)
    own_sent, near_sent = order(
        lambda *s: ins.send(0, *s, (size, size)), in_send, near_received
    )
    near_arrived = ins.across(near_sent)
    out_arrived = outs.across(hold(out_sent, slot))
    grad_gate = order(
        product_of("grad_gate", False, estimate), own_rows + other_rows, (own_d_gate, other_d_gate)
    )
    slot = order(lambda *s: ins.slot(2, 0, *s), in_keep, far_kept, far_arrived, last_sum)
    far = ins.line(slot, ins.far)
    near_arrived = hold(near_arrived, slot)
    slot = order(
        lambda *s: ins.slot(1, 0, *s), in_keep, near_kept, near_arrived, also=out_arrived
    )
    near = ins.line(slot, ins.near)
    own_arrived = ins.across(hold(own_sent, slot))
    columns = jax.ShapeDtypeStruct((size, width // 2), jnp.bfloat16)
    output_cols = order(
        lambda *sums: call(finish_outputs_kernel, "finish_outputs", sums, columns),
        out_keep,
        kept,
        out_arrived,
        near_sums,
        far_sum,
    )
    clock = order(lambda c: space(c, 10**9), clock)
    grad_up = order(
        product_of("grad_up", False), own_rows + other_rows, (own_d_up, other_d_up)
    )
    clock = order(lambda c: space(c, 2 * 10**9), clock, also=far)
    near, own_arrived = hold((near, own_arrived), clock)
    input_cols, d_scores = order(
        lambda *sums: call(
            functools.partial(finish_inputs_kernel, experts),
            "finish_inputs",
            (*picks, clock, *sums),
            (columns, jax.ShapeDtypeStruct(picks[2].shape, jnp.float32)),
        ),
        in_keep,
        near_kept,
        own_arrived,
        far,
        near,
    )
    return output_cols, input_cols, d_scores.T, grad_gate[None], grad_up[None], grad_down[None]


def any_mesh(tokens, expert_ids, pick_counts, gate_scores, gate_local, up_local, down_local, grad_out):
    tok_rows = tokens.shape[0]
    pick_width = expert_ids.shape[1]
    experts = lax.axis_size("expert")
    active_mask = lax.broadcasted_iota(jnp.int32, (tok_rows, pick_width), 1) < pick_counts[:, None]
    active_float = active_mask.astype(jnp.float32)
    weighted = gate_scores * active_float
    score_sum = jnp.sum(weighted, axis=1, keepdims=True)
    gate_weights = weighted / score_sum
    picked = (expert_ids[:, :, None] == lax.broadcasted_iota(jnp.int32, (1, 1, experts), 2)).astype(
        jnp.float32
    )
    gate_table = jnp.sum(gate_weights[:, :, None] * picked, axis=1)

    def combine(partial):
        summed = lax.psum_scatter(partial, "expert", scatter_dimension=0, tiled=True)
        return lax.psum_scatter(summed, "helper", scatter_dimension=1, tiled=True)

    rows = lax.all_gather(tokens, "expert", tiled=True)
    tables = lax.all_gather(gate_table.T, "expert", tiled=False)
    gates = jnp.take(tables, lax.axis_index("expert"), axis=1).reshape(-1, 1)
    grads = lax.all_gather(grad_out, "expert", tiled=True)

    pre_gate = product(rows, gate_local)
    pre_up = product(rows, up_local)
    silu_value, silu_slope = silu_parts(pre_gate)
    hidden_act = silu_value * pre_up
    gated_act = (gates * hidden_act).astype(jnp.bfloat16)
    output_cols = combine(product(gated_act, down_local).astype(jnp.bfloat16))

    raw_act = right_transposed(grads, down_local)
    gate_part = jnp.sum(raw_act * hidden_act, axis=1)
    d_act = gates * raw_act
    d_pre_gate = (d_act * pre_up * silu_slope).astype(jnp.bfloat16)
    d_pre_up = (d_act * silu_value).astype(jnp.bfloat16)
    input_cols = combine(
        (right_transposed(d_pre_gate, gate_local) + right_transposed(d_pre_up, up_local)).astype(
            jnp.bfloat16
        )
    )

    gate_parts = lax.all_gather(
        gate_part.reshape(-1, tok_rows), ("expert", "helper"), tiled=False
    )
    own_parts = jnp.take(gate_parts, lax.axis_index("expert"), axis=1)
    by_expert = jnp.sum(own_parts.reshape(experts, -1, tok_rows), axis=1).T
    d_gates = jnp.sum(by_expert[:, None, :] * picked, axis=2)
    d_scores = (
        active_float
        * (d_gates - jnp.sum(gate_weights * d_gates, axis=1, keepdims=True))
        / score_sum
    )

    def over_dp(whole, dimension):
        return lax.psum_scatter(
            whole.astype(jnp.bfloat16), "dp", scatter_dimension=dimension, tiled=True
        )[None]

    grad_w_gate = over_dp(transposed_product(rows, d_pre_gate), 0)
    grad_w_up = over_dp(transposed_product(rows, d_pre_up), 0)
    grad_w_down = over_dp(transposed_product(gated_act, grads), 1)
    return output_cols, input_cols, d_scores, grad_w_gate, grad_w_up, grad_w_down


def on_device(tokens, expert_ids, pick_counts, gate_scores, w_gate, w_up, w_down, grad_out):
    sizes = tuple(lax.axis_size(axis) for axis in ("expert", "helper", "dp"))
    layer = lined_up if sizes == (8, 2, 1) else any_mesh
    return layer(
        tokens, expert_ids, pick_counts, gate_scores, w_gate[0], w_up[0], w_down[0], grad_out
    )


def solution(mesh):
    in_specs = (
        P(("groups", "expert", "dp"), None),
        P(("groups", "expert", "dp"), None),
        P(("groups", "expert", "dp")),
        P(("groups", "expert", "dp"), None),
        P("expert", None, "helper"),
        P("expert", None, "helper"),
        P("expert", "helper", None),
        P(("groups", "expert", "dp"), None),
    )
    out_specs = (
        P(("groups", "expert", "dp"), "helper"),
        P(("groups", "expert", "dp"), "helper"),
        P(("groups", "expert", "dp"), None),
        P(("groups", "expert"), "dp", "helper"),
        P(("groups", "expert"), "dp", "helper"),
        P(("groups", "expert"), "helper", "dp"),
    )
    return jax.shard_map(
        on_device, mesh=mesh, in_specs=in_specs, out_specs=out_specs, check_vma=False
    )
```
